32 devices in a mesh: dp: 8 (over z, x), table: 4 (over y, core).
Axes of the slice: x: 2, y: 2, z: 4, core: 2. Of those that a mesh axis runs over, the one named last changes fastest.
Arguments:
- touched_rows: bfloat16 [8192, 512], P(('dp', 'table')), may hold values from -6 to 6
- row_of_token: int32 [16384], P(('dp', 'table')), may hold values from 0 to 255
- row_owner: int32 [8192, 1], P(('dp', 'table')), may hold values from 0 to 31; in each aligned block of 256 rows (0 to 255, 256 to 511, ...) at most 16 rows name the same one
- owner_row: int32 [8192], P(('dp', 'table')), may hold values from 0 to 1023
- seq_blocks: int32 [256], P(('dp', 'table')), may hold values from 1 to 4, as said below
- seq_dest: int32 [256], P(('dp', 'table')), may hold values from 0 to 7, as said below
- grad_out: bfloat16 [8192, 512], P(('dp', 'table')), may hold values from -6 to 6
- w_in: bfloat16 [512, 2048], replicated, may hold values from -0.25 to 0.25
- w_out: bfloat16 [512, 512], replicated, may hold values from -0.25 to 0.25
- gain_in: float32 [512], replicated, may hold values from 0.25 to 1.75
- gain_out: float32 [512], replicated, may hold values from 0.25 to 1.75
Outputs:
- table_grad: float32 [32768, 512], P(('dp', 'table'))
- grad_w_in: float32 [512, 2048], replicated
- grad_w_out: float32 [512, 512], replicated
- grad_gain_in: float32 [512], replicated
- grad_gain_out: float32 [512], replicated
The draws below stay inside these ranges and needn't reach their ends.
Inputs may be any that keep to these rules, and one draw needn't show every extreme that they name: `seq_blocks`: lengths in blocks of 16 tokens. The sequences that one device receives total exactly 16 blocks, and among them one has exactly 4 blocks. `seq_dest`: the 8 slots of a device go to 8 different dp indices, so every device receives exactly one sequence from each device with its table index. `row_owner`: at most 16 of one device's touched rows have the same owner.
All inputs are finite; a program needn't handle non-finite values.
Results may differ from the reference program's by a relative error of at most 0.0091.
Values may be sent and summed in bfloat16 or wider, within the bound.
No kernel may reach another device: no remote copies, remote signals or barrier semaphores. Data moves between devices by JAX's collectives and lax.ppermute only.
A program may use at most 128 MiB of HBM per device.

```python
import math
import jax
import jax.numpy as jnp
import numpy as np
from jax import lax

D = 512
HEADS = 4
HDIM = 128
BLK = 16
LMAXB = 4
UNIQ = 256
ROWS_DEV = 1024
SLOT = 64
ARR_TOK = 512
BAL_TOK = 256
CAP = 16
TOTAL_TOK = 8192
UNIQ_ALL = 8192
ARR_ALL = 16384
N_DP = 8
N_TABLE = 4


def plan_tables(key):
    base_key = jax.random.fold_in(key, 4099)
    quarter = N_DP // 4

    def one_column(column_key):
        key_order, key_shift, key_wobble = jax.random.split(column_key, 3)
        ordering = jax.random.permutation(key_order, N_DP).astype(jnp.int32)
        ranking = jnp.zeros((N_DP,), jnp.int32).at[ordering].set(jnp.arange(N_DP, dtype=jnp.int32))
        slot_ids = jnp.arange(N_DP, dtype=jnp.int32)[None, :]
        source_rank = ranking[:, None]
        target_rank = (source_rank + slot_ids) % N_DP
        target = ordering[target_rank]
        cluster = slot_ids // 4
        shifts = jax.random.randint(key_shift, (N_DP, quarter), 0, LMAXB // 2)
        wobble = jax.random.randint(key_wobble, (N_DP, quarter), 0, 2)
        shift_here = jnp.where(cluster == target_rank % quarter, 0, shifts[target_rank, cluster])
        wobble_here = wobble[target_rank, cluster]
        source_role = source_rank % 4
        blocks = jnp.where(source_role == 0, LMAXB - shift_here, jnp.where(source_role == 3, 1 + shift_here, jnp.where(source_role == 1, 1 + wobble_here, 2 - wobble_here)))
        return (blocks.astype(jnp.int32), target.astype(jnp.int32))
    blocks, target = jax.vmap(one_column)(jax.random.split(base_key, N_TABLE))
    return (jnp.transpose(blocks, (1, 0, 2)).reshape(-1), jnp.transpose(target, (1, 0, 2)).reshape(-1))


def draw_seq_blocks(key, part):
    return plan_tables(key)[0]


def draw_seq_dest(key, part):
    return plan_tables(key)[1]


def set_ends(entries, own_key, least, high):
    shape = entries.shape
    index_at = [jax.random.randint(jax.random.fold_in(own_key, axis), (), 0, shape[axis]) for axis in range(len(shape))]
    entries = entries.at[tuple(index_at)].set(least)
    longest = shape.index(max(shape))
    index_at[longest] = (index_at[longest] + 1) % shape[longest]
    return entries.at[tuple(index_at)].set(high)


def shard_levels(key, extent, cuts, least, high):
    level, own = 1.0, jax.random.fold_in(key, 6)
    for dim, blocks in cuts:
        draws = jnp.exp(jax.random.uniform(jax.random.fold_in(own, dim), (blocks,), jnp.float32, least / len(cuts), high / len(cuts)))
        level = level * jnp.repeat(draws, extent[dim] // blocks).reshape([-1 if axis == dim else 1 for axis in range(len(extent))])
    return level


def rank_bounds(number_of, lean):
    loads = [(1 << 20) // math.isqrt(rank ** lean) + 1 for rank in range(1, number_of + 1)]
    deviation = 1 + sum(loads) // (1 << 30)
    return np.cumsum(np.array([max(1, weight // deviation) for weight in loads]))


def skewed_ids(stream_key, dims, number_of, skew):
    grid = rank_bounds(number_of, skew)
    ticket = jax.random.randint(jax.random.fold_in(stream_key, 1), dims, 0, int(grid[number_of - 1]))
    rank = jnp.searchsorted(jnp.asarray(grid, jnp.int32), ticket, side="right")
    return jax.random.permutation(jax.random.fold_in(stream_key, 2), number_of)[rank].astype(jnp.int32)


def shared_out(own_key, own, number, rows, amount, top, bound, slope):
    order = jax.random.permutation(own_key, amount)
    crowded, ordinary = portions_of(amount, rows * top, bound, slope, True), portions_of(amount, rows * top, bound, slope, False)
    places = jnp.arange(amount)

    def named(lengths, rotation):
        used = int((lengths > 0).sum())
        fixed = max(1, used // 4)
        moved = fixed + (places - fixed + rotation * (used - fixed)) % max(1, amount - fixed)
        return jnp.zeros((amount,), jnp.int32).at[order[jnp.where(places < fixed, places, moved)]].set(jnp.asarray(lengths, jnp.int32))

    lengths = jnp.where(number % 4 == 0, named(crowded, number // 4), named(ordinary, number - number // 4 - 1))
    mixed = jax.random.permutation(jax.random.fold_in(own, 3), amount)
    giver, taker = mixed[0:amount // 2 * 2:2], mixed[1:amount // 2 * 2:2]
    margin = jnp.minimum(lengths[giver] - 1, bound - lengths[taker]) // 2
    margin = jnp.where((giver == order[0]) | (taker == order[0]) | (lengths[taker] == 0), 0, jnp.maximum(margin, 0))
    moved = jax.random.randint(jax.random.fold_in(own, 4), (amount // 2,), 0, 1 << 20) % (margin + 1)
    lengths = lengths.at[giver].add(-moved).at[taker].add(moved)
    labels = jnp.searchsorted(jnp.cumsum(lengths), jnp.arange(rows * top), side="right").astype(jnp.int32)
    grid = labels.reshape(top, rows).T
    grid = grid[jax.random.permutation(jax.random.fold_in(own, 1), rows)]
    rotation = jax.random.randint(jax.random.fold_in(own, 2), (rows, 1), 0, top)
    return jnp.take_along_axis(grid, (jnp.arange(top)[None, :] + rotation) % top, axis=1)


def portions_of(number_of, total, limit, slope, full):
    portions = [(1 << 20) // math.isqrt(standing ** slope) + 1 for standing in range(1, number_of + 1)]
    largest = limit if full else min(limit, max(-(-total // number_of), total * portions[0] // sum(portions)))
    least = 1 if total - largest >= number_of - 1 else 0
    given, spare = [largest] + [least] * (number_of - 1), total - largest - least * (number_of - 1)
    while spare > 0:
        candidates = [i for i in range(1, number_of) if given[i] < largest] or [i for i in range(1, number_of) if given[i] < limit]
        whole, budget = sum([portions[i] for i in candidates]), spare
        for i in candidates:
            addition = min(limit - given[i], max(1, budget * portions[i] // whole), spare)
            given[i] = given[i] + addition
            spare = spare - addition
    return np.array(given)


def noise(stream_key, shape, deviation, bound, cuts=(), held_as=jnp.bfloat16):
    array = deviation * jax.random.normal(stream_key, shape, jnp.float32)
    if cuts:
        array = array * shard_levels(stream_key, shape, cuts, -0.22, 0.18)
    return jnp.clip(array, -bound, bound).astype(held_as)


def setup_inputs(seed: int = 0) -> dict:
    key_list = jax.random.split(jax.random.key(seed), 12)
    touched_rows = noise(key_list[0], (UNIQ_ALL, D), 1.0, 6.0, ((0, 32),))
    row_of_token = set_ends(skewed_ids(key_list[1], (ARR_ALL,), UNIQ, 2), jax.random.fold_in(key_list[1], 3), 0, UNIQ - 1).astype(jnp.int32)
    row_owner_keys = jax.random.split(jax.random.fold_in(key_list[2], 1), UNIQ_ALL // UNIQ)
    row_owner_turns = jax.random.permutation(jax.random.fold_in(key_list[2], 3), UNIQ_ALL // UNIQ)
    row_owner = jax.vmap(lambda own, number: shared_out(jax.random.fold_in(key_list[2], 2), own, number, UNIQ, N_DP * N_TABLE, 1, CAP, 1))(row_owner_keys, row_owner_turns).reshape((UNIQ_ALL, 1))
    owner_row = set_ends(jax.random.randint(key_list[3], (UNIQ_ALL,), 0, ROWS_DEV), jax.random.fold_in(key_list[3], 1), 0, ROWS_DEV - 1).astype(jnp.int32)
    seq_blocks = draw_seq_blocks(jax.random.fold_in(key_list[11], 71), 0)
    seq_dest = draw_seq_dest(jax.random.fold_in(key_list[11], 71), 0)
    grad_out = noise(key_list[6], (TOTAL_TOK, D), 1.0, 6.0, ((0, 32),))
    w_in = noise(key_list[7], (D, 4 * D), D ** -0.5, 0.25)
    w_out = noise(key_list[8], (D, D), D ** -0.5, 0.25)
    gain_in = jnp.clip(1.0 + 0.15 * jax.random.normal(key_list[9], (D,), jnp.float32), 0.25, 1.75)
    gain_out = jnp.clip(1.0 + 0.15 * jax.random.normal(key_list[10], (D,), jnp.float32), 0.25, 1.75)
    return {"touched_rows": touched_rows, "row_of_token": row_of_token, "row_owner": row_owner, "owner_row": owner_row, "seq_blocks": seq_blocks, "seq_dest": seq_dest, "grad_out": grad_out, "w_in": w_in, "w_out": w_out, "gain_in": gain_in, "gain_out": gain_out}


EPSILON = 1e-05

def norm_rows(values, row_gain):
    centre = lax.optimization_barrier(jnp.mean(values, axis=-1, keepdims=True))
    shifted = values - centre
    spread = lax.optimization_barrier(jnp.mean(shifted * shifted, axis=-1, keepdims=True))
    return shifted * lax.rsqrt(spread + EPSILON) * row_gain

def silu_slope(values):
    sigma_v = jax.nn.sigmoid(values)
    return sigma_v * (1.0 + values * (1.0 - sigma_v))

def head_scores(queries, keys_in):
    return jnp.einsum('qhd,khd->hqk', queries.astype(jnp.float32), keys_in.astype(jnp.float32)) * HDIM ** (-0.5)

def device_grads(tokens, grad_y, sequence, w_in, w_out, gain_in, gain_out):
    row_count = tokens.shape[0]
    positions = jnp.arange(row_count)
    allowed = (sequence[:, None] == sequence[None, :]) & (positions[:, None] >= positions[None, :])
    allowed = allowed[None]
    normed, back_in = jax.vjp(norm_rows, tokens.astype(jnp.float32), gain_in)
    normed_half = normed.astype(jnp.bfloat16)
    hidden = jnp.dot(normed_half, w_in, preferred_element_type=jnp.float32)
    active = hidden * jax.nn.sigmoid(hidden)
    gate_part = active[:, :D]
    head_shape = (row_count, HEADS, HDIM)
    values = active[:, D:2 * D].astype(jnp.bfloat16).reshape(head_shape)
    queries = active[:, 2 * D:3 * D].astype(jnp.bfloat16).reshape(head_shape)
    keys_in = active[:, 3 * D:].astype(jnp.bfloat16).reshape(head_shape)
    scores = head_scores(queries, keys_in)
    weights = jnp.where(allowed, scores * jax.nn.sigmoid(scores), 0.0).astype(jnp.bfloat16)
    attended = jnp.einsum('hqk,khd->qhd', weights.astype(jnp.float32), values.astype(jnp.float32)).reshape(row_count, D)
    out_norm, back_out = jax.vjp(norm_rows, attended, gain_out)
    mixed = (out_norm * gate_part).astype(jnp.bfloat16)
    grad_mixed = jnp.dot(grad_y, w_out.T, preferred_element_type=jnp.float32)
    sum_w_out = jnp.dot(mixed.T, grad_y, preferred_element_type=jnp.float32)
    grad_gate = grad_mixed * out_norm
    grad_attended, sum_gain_out = back_out(grad_mixed * gate_part)
    grad_att_half = grad_attended.astype(jnp.bfloat16).reshape(head_shape).astype(jnp.float32)
    grad_weight = jnp.einsum('qhd,khd->hqk', grad_att_half, values.astype(jnp.float32))
    grad_score = jnp.where(allowed, grad_weight * silu_slope(scores) * HDIM ** (-0.5), 0.0).astype(jnp.bfloat16).astype(jnp.float32)
    grad_queries = jnp.einsum('hqk,khd->qhd', grad_score, keys_in.astype(jnp.float32)).reshape(row_count, D)
    grad_keys = jnp.einsum('hqk,qhd->khd', grad_score, queries.astype(jnp.float32)).reshape(row_count, D)
    grad_values = jnp.einsum('hqk,qhd->khd', weights.astype(jnp.float32), grad_att_half).reshape(row_count, D)
    grad_active = jnp.concatenate([grad_gate, grad_values, grad_queries, grad_keys], axis=1)
    grad_hidden = (grad_active * silu_slope(hidden)).astype(jnp.bfloat16)
    sum_w_in = jnp.dot(normed_half.T, grad_hidden, preferred_element_type=jnp.float32)
    grad_normed = jnp.dot(grad_hidden, w_in.T, preferred_element_type=jnp.float32)
    grad_inner, sum_gain_in = back_in(grad_normed)
    grad_tokens = (grad_inner + grad_y.astype(jnp.float32)).astype(jnp.bfloat16)
    return (grad_tokens, (sum_w_in, sum_w_out, sum_gain_in, sum_gain_out))

def reference(touched_rows, row_of_token, row_owner, owner_row, seq_blocks, seq_dest, grad_out, w_in, w_out, gain_in, gain_out):
    groups = N_DP * N_TABLE
    blocks = seq_blocks.reshape(N_DP, N_TABLE, N_DP)
    target = seq_dest.reshape(N_DP, N_TABLE, N_DP)
    peers = jnp.arange(N_DP, dtype=jnp.int32)
    hits = (target[..., None] == peers).astype(jnp.int32)
    sent = lax.optimization_barrier(jnp.sum(blocks[..., None] * hits, axis=2))
    before = jnp.cumsum(sent, axis=0) - sent
    starts = lax.optimization_barrier(jnp.sum(hits * before[:, :, None, :], axis=3))
    table_ids = jnp.arange(N_TABLE, dtype=jnp.int32)[None, :, None]
    inner = jnp.arange(SLOT, dtype=jnp.int32)
    first_row = (target * N_TABLE + table_ids) * BAL_TOK + starts * BLK
    live = inner < (blocks * BLK)[..., None]
    landing_rows = jnp.where(live, first_row[..., None] + inner, TOTAL_TOK).reshape(-1).astype(jnp.int32)
    arrival_ids = jnp.arange(groups * ARR_TOK, dtype=jnp.int32)
    arrival_of = jnp.zeros((TOTAL_TOK,), jnp.int32).at[landing_rows].set(arrival_ids, mode='drop')
    device_of = arrival_of // ARR_TOK
    unique_of = (device_of * UNIQ + jnp.take(row_of_token, arrival_of)).astype(jnp.int32)
    sequence_of = (arrival_of // SLOT).astype(jnp.int32)
    tokens_all = jnp.take(touched_rows, unique_of, axis=0)
    zero_sums = (jnp.zeros((D, 4 * D), jnp.float32), jnp.zeros((D, D), jnp.float32), jnp.zeros((D,), jnp.float32), jnp.zeros((D,), jnp.float32))

    def per_device(running, inputs):
        tokens_here, grad_here, sequence_here = inputs
        grad_tokens, partial_sums = device_grads(tokens_here, grad_here, sequence_here, w_in, w_out, gain_in, gain_out)
        running = jax.tree.map(lambda first_sum, second_sum: first_sum + second_sum, running, partial_sums)
        return (running, grad_tokens)
    totals, grads_all = lax.scan(per_device, zero_sums, (tokens_all.reshape(groups, BAL_TOK, D), grad_out.reshape(groups, BAL_TOK, D), sequence_of.reshape(groups, BAL_TOK)))
    row_grad = jax.ops.segment_sum(grads_all.reshape(-1, D).astype(jnp.float32), unique_of, num_segments=UNIQ * groups)
    landing = (row_owner[:, 0] * ROWS_DEV + owner_row).astype(jnp.int32)
    table_grad = jax.ops.segment_sum(row_grad, landing, num_segments=ROWS_DEV * groups)
    factor = 1.0 / math.sqrt(TOTAL_TOK)
    return (table_grad, totals[0] * factor, totals[1] * factor, totals[2] * factor, totals[3] * factor)
```

```python
import functools
import math

import jax
import jax.numpy as jnp
from jax import lax
from jax.experimental import pallas as pl
from jax.experimental.pallas import tpu as pltpu
from jax.sharding import PartitionSpec as P

HEADS = 4
HDIM = 128
BLK = 16
LMAXB = 4
SLOT = LMAXB * BLK
ROWS_DEV = 1024
TILE = 2 * SLOT
EPSILON = 1e-05
F32 = jnp.float32
BF16 = jnp.bfloat16
VMEM = pl.BlockSpec(memory_space=pltpu.VMEM)
SMEM = pl.BlockSpec(memory_space=pltpu.SMEM)


def call(body, out_shape, in_specs, flops=0, moved=0, scratch=()):
    outs = jax.tree.map(lambda _: VMEM, out_shape)
    return pl.pallas_call(
        body,
        out_shape=out_shape,
        in_specs=in_specs,
        out_specs=outs,
        scratch_shapes=scratch,
        compiler_params=pltpu.CompilerParams(vmem_limit_bytes=40 * 1024 * 1024),
        cost_estimate=pl.CostEstimate(flops=flops, bytes_accessed=moved, transcendentals=0),
    )


def shape_of(dims, dtype):
    return jax.ShapeDtypeStruct(dims, dtype)


def sigmoid(values):
    return 0.5 * jnp.tanh(0.5 * values) + 0.5


def dot(left, right, contract=((1,), (0,))):
    return lax.dot_general(left, right, (contract, ((), ())), preferred_element_type=F32)


NT = ((1,), (1,))
TN = ((0,), (0,))


def send_body(packed_ref, me_ref, grad_ref, out_ref):
    peers, slots = packed_ref.shape
    blocks = grad_ref.shape[0] // BLK
    me = me_ref[0]
    begin = jnp.int32(0)
    for peer in range(peers):

        def find(slot, length):
            entry = packed_ref[peer, slot]
            return length + jnp.where(entry >> 3 == me, entry & 7, 0)

        length = lax.fori_loop(0, slots, find, jnp.int32(0), unroll=True)
        for inner in range(LMAXB):
            block = jnp.minimum(begin + inner, blocks - 1)
            rows = grad_ref[pl.ds(pl.multiple_of(block * BLK, BLK), BLK), :]
            live = jnp.full(rows.shape, inner, jnp.int32) < length
            out_ref[peer, inner * BLK : (inner + 1) * BLK, :] = jnp.where(
                live, rows.astype(F32), 0.0
            ).astype(BF16)
        begin = begin + length


def plan_body(capacity, owner_col_ref, owner_row_ref, rows_col_ref, place_ref, ids_ref):
    count = owner_col_ref.shape[0]
    places = ids_ref.shape[1]
    across = jnp.broadcast_to(owner_row_ref[...], (count, count))
    down = jnp.broadcast_to(owner_col_ref[...], (count, count))
    same = across == down
    sub = lax.broadcasted_iota(jnp.int32, (count, count), 0)
    lane = lax.broadcasted_iota(jnp.int32, (count, count), 1)
    before_row = jnp.sum(jnp.where(same & (sub < lane), 1.0, 0.0), axis=0, keepdims=True)
    before_col = jnp.sum(jnp.where(same & (lane < sub), 1.0, 0.0), axis=1, keepdims=True)
    place_ref[...] = owner_row_ref[...] * capacity + before_row.astype(jnp.int32)
    place_col = owner_col_ref[...] * capacity + before_col.astype(jnp.int32)
    spots = lax.broadcasted_iota(jnp.int32, (count, places), 1)
    hit = spots == jnp.broadcast_to(place_col, (count, places))
    numbers = jnp.broadcast_to(rows_col_ref[...], (count, places)) + 1
    found = jnp.sum(jnp.where(hit, numbers.astype(F32), 0.0), axis=0, keepdims=True)
    ids_ref[...] = found.astype(jnp.int32) - 1


def tile_mask():
    sub = lax.broadcasted_iota(jnp.int32, (TILE, TILE), 0)
    lane = lax.broadcasted_iota(jnp.int32, (TILE, TILE), 1)
    return (sub // SLOT == lane // SLOT) & (lane <= sub)


def forward_body(
    rows_ref,
    item_ref,
    w_in_ref,
    gain_in_ref,
    gain_out_ref,
    qkv_ref,
    gate_ref,
    hat_ref,
    hat_scale_ref,
    mixed_ref,
    weight_ref,
    slope_ref,
    normed_ref,
    rows_hat_ref,
    rows_scale_ref,
    rows_slope_ref,
):
    count, width = rows_ref.shape
    tokens = item_ref.shape[0]
    values = rows_ref[...].astype(F32)
    shifted = values - jnp.mean(values, axis=-1, keepdims=True)
    scale = lax.rsqrt(jnp.mean(shifted * shifted, axis=-1, keepdims=True) + EPSILON)
    hat = shifted * scale
    rows_hat_ref[...] = hat
    rows_scale_ref[...] = scale
    normed = (hat * gain_in_ref[...]).astype(BF16)
    normed_ref[...] = normed
    lane = lax.broadcasted_iota(jnp.int32, (tokens, count), 1)
    pick = jnp.where(lane == jnp.broadcast_to(item_ref[...], (tokens, count)), 1.0, 0.0)
    pick = pick.astype(BF16)
    for part in range(4):
        columns = slice(part * width, (part + 1) * width)
        hidden = dot(normed, w_in_ref[:, columns])
        sigma = sigmoid(hidden)
        active = hidden * sigma
        rows_slope_ref[:, columns] = sigma * (1.0 + hidden * (1.0 - sigma))
        if part == 0:
            high = active.astype(BF16)
            low = (active - high.astype(F32)).astype(BF16)
            gate_ref[...] = dot(pick, high) + dot(pick, low)
        else:
            qkv_ref[:, (part - 1) * width : part * width] = dot(pick, active.astype(BF16)).astype(
                BF16
            )
    mask = tile_mask()
    factor = HDIM ** (-0.5)
    for tile in range(tokens // TILE):
        rows = slice(tile * TILE, (tile + 1) * TILE)
        parts = []
        for head in range(HEADS):
            vals, queries, keys = (
                qkv_ref[rows, part * width + head * HDIM : part * width + (head + 1) * HDIM]
                for part in range(3)
            )
            score = dot(queries, keys, NT) * factor
            sigma = sigmoid(score)
            weight = jnp.where(mask, score * sigma, 0.0).astype(BF16)
            slope = sigma * (1.0 + score * (1.0 - sigma)) * factor
            slope_ref[tile * HEADS + head] = jnp.where(mask, slope, 0.0)
            weight_ref[tile * HEADS + head] = weight
            parts.append(dot(weight, vals))
        attended = jnp.concatenate(parts, axis=1)
        shifted = attended - jnp.mean(attended, axis=-1, keepdims=True)
        scale = lax.rsqrt(jnp.mean(shifted * shifted, axis=-1, keepdims=True) + EPSILON)
        hat = shifted * scale
        hat_ref[rows, :] = hat
        hat_scale_ref[rows, :] = scale
        mixed_ref[rows, :] = (hat * gain_out_ref[...] * gate_ref[rows, :]).astype(BF16)


def backward_body(
    total_factor,
    dest_ref,
    got_ref,
    item_ref,
    place_ref,
    w_in_ref,
    w_out_ref,
    gain_in_ref,
    gain_out_ref,
    qkv_ref,
    gate_ref,
    hat_ref,
    hat_scale_ref,
    mixed_ref,
    weight_ref,
    slope_ref,
    normed_ref,
    rows_hat_ref,
    rows_scale_ref,
    rows_slope_ref,
    sums_ref,
    table_ref,
    gains_ref,
    active_ref,
    grad_y_ref,
):
    count, width = rows_hat_ref.shape
    tokens = hat_ref.shape[0]
    for slot in range(got_ref.shape[0]):
        grad_y_ref[slot * SLOT : (slot + 1) * SLOT, :] = got_ref[dest_ref[slot]]
    gain_total = jnp.zeros((1, width), F32)
    for tile in range(tokens // TILE):
        rows = slice(tile * TILE, (tile + 1) * TILE)
        grad_mixed = dot(grad_y_ref[rows, :], w_out_ref[...], NT)
        hat = hat_ref[rows, :]
        active_ref[rows, :width] = (grad_mixed * hat * gain_out_ref[...]).astype(BF16)
        inner = grad_mixed * gate_ref[rows, :]
        gain_total = gain_total + jnp.sum(inner * hat, axis=0, keepdims=True)
        inner = inner * gain_out_ref[...]
        mean = jnp.mean(inner, axis=-1, keepdims=True)
        along = jnp.mean(inner * hat, axis=-1, keepdims=True)
        grad_att = ((inner - mean - hat * along) * hat_scale_ref[rows, :]).astype(BF16)
        for head in range(HEADS):
            columns = slice(head * HDIM, (head + 1) * HDIM)
            vals, queries, keys = (
                qkv_ref[rows, part * width + head * HDIM : part * width + (head + 1) * HDIM]
                for part in range(3)
            )
            grad_o = grad_att[:, columns]
            grad_weight = dot(grad_o, vals, NT)
            grad_score = (grad_weight * slope_ref[tile * HEADS + head]).astype(BF16)
            for part, value in (
                (1, dot(weight_ref[tile * HEADS + head], grad_o, TN)),
                (2, dot(grad_score, keys)),
                (3, dot(grad_score, queries, TN)),
            ):
                first = part * width + head * HDIM
                active_ref[rows, first : first + HDIM] = value.astype(BF16)
    gains_ref[1:2, :] = gain_total * total_factor
    grad_y = grad_y_ref[...]
    sums_ref[:, 4 * width :] = (dot(mixed_ref[...], grad_y, TN) * total_factor).astype(BF16)
    sub = lax.broadcasted_iota(jnp.int32, (count, tokens), 0)
    gather = jnp.where(sub == jnp.broadcast_to(item_ref[...], (count, tokens)), 1.0, 0.0)
    gather = gather.astype(BF16)
    grad_normed = jnp.zeros((count, width), F32)
    for part in range(4):
        columns = slice(part * width, (part + 1) * width)
        summed = dot(gather, active_ref[:, columns])
        grad_hidden = (summed * rows_slope_ref[:, columns]).astype(BF16)
        sums_ref[:, columns] = (dot(normed_ref[...], grad_hidden, TN) * total_factor).astype(BF16)
        grad_normed = grad_normed + dot(grad_hidden, w_in_ref[:, columns], NT)
    hat = rows_hat_ref[...]
    gains_ref[0:1, :] = jnp.sum(grad_normed * hat, axis=0, keepdims=True) * total_factor
    inner = grad_normed * gain_in_ref[...]
    mean = jnp.mean(inner, axis=-1, keepdims=True)
    along = jnp.mean(inner * hat, axis=-1, keepdims=True)
    row_grad = (inner - mean - hat * along) * rows_scale_ref[...] + dot(gather, grad_y)
    places = table_ref.shape[0]
    spots = lax.broadcasted_iota(jnp.int32, (places, count), 0)
    spread = jnp.where(spots == jnp.broadcast_to(place_ref[...], (places, count)), 1.0, 0.0)
    table_ref[...] = dot(spread.astype(BF16), row_grad.astype(BF16)).astype(BF16)


def table_body(got_ref, ids_ref, out_ref):
    places = got_ref.shape[0]
    step = 256
    for first in range(0, out_ref.shape[0], step):
        sub = lax.broadcasted_iota(jnp.int32, (step, places), 0) + first
        hit = jnp.where(sub == jnp.broadcast_to(ids_ref[...], (step, places)), 1.0, 0.0)
        out_ref[first : first + step, :] = dot(hit.astype(BF16), got_ref[...])


def widen_body(full_ref, w_in_ref, w_out_ref):
    split = w_in_ref.shape[1]
    w_in_ref[...] = full_ref[:, :split].astype(F32)
    w_out_ref[...] = full_ref[:, split:].astype(F32)


def on_device(
    touched_rows,
    row_of_token,
    row_owner,
    owner_row,
    seq_blocks,
    seq_dest,
    grad_out,
    w_in,
    w_out,
    gain_in,
    gain_out,
):
    dp_size = lax.axis_size("dp")
    devices_all = dp_size * lax.axis_size("table")
    both = ("dp", "table")
    count, width = touched_rows.shape
    tokens = row_of_token.shape[0]
    capacity = 2 * count // devices_all
    places = devices_all * capacity
    total_factor = 1.0 / math.sqrt(grad_out.shape[0] * devices_all)
    gain_in, gain_out = gain_in[None, :], gain_out[None, :]

    packed = lax.all_gather(seq_dest * 8 + seq_blocks, "dp")
    me = lax.axis_index("dp").astype(jnp.int32)[None]
    send = call(
        send_body,
        shape_of((dp_size, SLOT, width), BF16),
        [SMEM, SMEM, VMEM],
    )(packed, me, grad_out)
    got = lax.all_to_all(send, "dp", split_axis=0, concat_axis=0, tiled=True)

    place, ids = call(
        functools.partial(plan_body, capacity),
        (shape_of((1, count), jnp.int32), shape_of((1, places), jnp.int32)),
        [VMEM] * 3,
    )(row_owner, row_owner.reshape(1, count), owner_row.reshape(count, 1))
    got_ids = lax.all_to_all(
        ids.reshape(devices_all, capacity), both, split_axis=0, concat_axis=0, tiled=True
    ).reshape(1, places)

    pairs = tokens // TILE * HEADS
    saved = call(
        forward_body,
        (
            shape_of((tokens, 3 * width), BF16),
            shape_of((tokens, width), F32),
            shape_of((tokens, width), F32),
            shape_of((tokens, 1), F32),
            shape_of((tokens, width), BF16),
            shape_of((pairs, TILE, TILE), BF16),
            shape_of((pairs, TILE, TILE), F32),
            shape_of((count, width), BF16),
            shape_of((count, width), F32),
            shape_of((count, 1), F32),
            shape_of((count, 4 * width), F32),
        ),
        [VMEM] * 5,
        flops=4 * count * width * width * 8,
        moved=10_000_000,
    )(touched_rows, row_of_token.reshape(tokens, 1), w_in, gain_in, gain_out)

    sums, table_send, gains = call(
        functools.partial(backward_body, total_factor),
        (
            shape_of((width, 5 * width), BF16),
            shape_of((places, width), BF16),
            shape_of((2, width), F32),
        ),
        [SMEM] + [VMEM] * 18,
        flops=4 * count * width * width * 20,
        moved=12_000_000,
        scratch=[pltpu.VMEM((tokens, 4 * width), BF16), pltpu.VMEM((tokens, width), BF16)],
    )(
        seq_dest,
        got,
        row_of_token.reshape(1, tokens),
        place,
        w_in,
        w_out,
        gain_in,
        gain_out,
        *saved,
    )

    shard = lax.psum_scatter(sums, both, scatter_dimension=0, tiled=True)
    full = lax.all_gather(shard, both, axis=0, tiled=True)
    table_got = lax.all_to_all(
        table_send.reshape(devices_all, capacity, width),
        both,
        split_axis=0,
        concat_axis=0,
        tiled=True,
    )
    table_part = call(
        table_body,
        shape_of((ROWS_DEV, width), F32),
        [VMEM] * 2,
    )(table_got.reshape(places, width), got_ids)
    gain_sums = jnp.sum(lax.all_gather(gains, both), axis=0)
    grad_w_in, grad_w_out = call(
        widen_body,
        (shape_of(w_in.shape, F32), shape_of(w_out.shape, F32)),
        [VMEM],
    )(full)
    return (table_part, grad_w_in, grad_w_out, gain_sums[0], gain_sums[1])


def solution(mesh):
    rows = P(("dp", "table"), None)
    flat = P(("dp", "table"))
    in_specs = (rows, flat, rows, flat, flat, flat, rows, P(), P(), P(), P())
    out_specs = (rows, P(), P(), P(), P())
    return jax.shard_map(
        on_device, mesh=mesh, in_specs=in_specs, out_specs=out_specs, check_vma=False
    )
```

```python
import functools
import math

import jax
import jax.numpy as jnp
from jax import lax
from jax.experimental import pallas as pl
from jax.experimental.pallas import tpu as pltpu
from jax.sharding import PartitionSpec as P

HEADS = 4
HDIM = 128
BLK = 16
LMAXB = 4
SLOT = LMAXB * BLK
ROWS_DEV = 1024
TILE = 2 * SLOT
LANES = 128
CHUNK_ROWS = 16
EPSILON = 1e-05
F32 = jnp.float32
BF16 = jnp.bfloat16
VMEM = pl.BlockSpec(memory_space=pltpu.VMEM)
SMEM = pl.BlockSpec(memory_space=pltpu.SMEM)


def call(body, out_shape, in_specs, flops=0, moved=0, scratch=()):
    outs = jax.tree.map(lambda _: VMEM, out_shape)
    return pl.pallas_call(
        body,
        out_shape=out_shape,
        in_specs=in_specs,
        out_specs=outs,
        scratch_shapes=scratch,
        compiler_params=pltpu.CompilerParams(vmem_limit_bytes=24 * 1024 * 1024),
        cost_estimate=pl.CostEstimate(flops=flops, bytes_accessed=moved, transcendentals=0),
    )


def shape_of(dims, dtype):
    return jax.ShapeDtypeStruct(dims, dtype)


def sigmoid(values):
    return 0.5 * jnp.tanh(0.5 * values) + 0.5


def dot(left, right, contract=((1,), (0,))):
    return lax.dot_general(left, right, (contract, ((), ())), preferred_element_type=F32)


NT = ((1,), (1,))
TN = ((0,), (0,))


def send_body(table_size, me_ref, *refs):
    peers = (len(refs) - 2) // 2
    packed_refs, grad_ref, out_refs, lengths_ref = (
        refs[:peers],
        refs[peers],
        refs[peers + 1 : 2 * peers + 1],
        refs[-1],
    )
    blocks = grad_ref.shape[0] // BLK
    me = me_ref[0] // table_size
    for apart, packed_ref in enumerate(packed_refs):

        def find(slot, length, packed_ref=packed_ref):
            entry = packed_ref[slot]
            return length + jnp.where(entry >> 3 == me, entry & 7, 0)

        length = lax.fori_loop(0, peers, find, jnp.int32(0), unroll=True)
        lengths_ref[me ^ apart] = length
    for apart, out_ref in enumerate(out_refs):
        peer = me ^ apart

        def before(other, begin, peer=peer):
            return begin + jnp.where(other < peer, lengths_ref[other], 0)

        begin = lax.fori_loop(0, peers, before, jnp.int32(0), unroll=True)
        for inner in range(LMAXB):
            block = jnp.minimum(begin + inner, blocks - 1)
            rows = grad_ref[pl.ds(pl.multiple_of(block * BLK, BLK), BLK), :]
            live = jnp.full(rows.shape, inner, jnp.int32) < lengths_ref[peer]
            out_ref[inner * BLK : (inner + 1) * BLK, :] = jnp.where(
                live, rows.astype(F32), 0.0
            ).astype(BF16)


def tile_mask():
    sub = lax.broadcasted_iota(jnp.int32, (TILE, TILE), 0)
    lane = lax.broadcasted_iota(jnp.int32, (TILE, TILE), 1)
    return (sub // SLOT == lane // SLOT) & (lane <= sub)


def forward_body(
    rows_ref,
    item_ref,
    w_in_ref,
    gain_in_ref,
    gain_out_ref,
    owner_col_ref,
    owner_row_ref,
    number_ref,
    qkv_ref,
    gate_ref,
    hat_ref,
    hat_scale_ref,
    mixed_ref,
    weight_ref,
    slope_ref,
    normed_ref,
    rows_hat_ref,
    rows_scale_ref,
    rows_slope_ref,
    rank_ref,
    digits_ref,
):
    count, width = rows_ref.shape
    tokens = item_ref.shape[0]
    across = jnp.broadcast_to(owner_row_ref[...], (count, count))
    down = jnp.broadcast_to(owner_col_ref[...], (count, count))
    sub = lax.broadcasted_iota(jnp.int32, (count, count), 0)
    lane = lax.broadcasted_iota(jnp.int32, (count, count), 1)
    earlier = jnp.where((across == down) & (sub < lane), 1.0, 0.0)
    rank_ref[...] = jnp.sum(earlier, axis=0, keepdims=True).astype(jnp.int32)
    number = jnp.broadcast_to(number_ref[...], (count, LANES))
    lane = lax.broadcasted_iota(jnp.int32, (count, LANES), 1)
    digits = jnp.where(lane == 0, number >> 5, jnp.where(lane == 1, number & 31, 0))
    digits_ref[...] = digits.astype(F32).astype(BF16)
    values = rows_ref[...].astype(F32)
    shifted = values - jnp.mean(values, axis=-1, keepdims=True)
    scale = lax.rsqrt(jnp.mean(shifted * shifted, axis=-1, keepdims=True) + EPSILON)
    hat = shifted * scale
    rows_hat_ref[...] = hat
    rows_scale_ref[...] = scale
    normed = (hat * gain_in_ref[...]).astype(BF16)
    normed_ref[...] = normed
    lane = lax.broadcasted_iota(jnp.int32, (tokens, count), 1)
    pick = jnp.where(lane == jnp.broadcast_to(item_ref[...], (tokens, count)), 1.0, 0.0)
    pick = pick.astype(BF16)
    for part in range(4):
        columns = slice(part * width, (part + 1) * width)
        hidden = dot(normed, w_in_ref[:, columns])
        sigma = sigmoid(hidden)
        active = hidden * sigma
        rows_slope_ref[:, columns] = sigma * (1.0 + hidden * (1.0 - sigma))
        if part == 0:
            high = active.astype(BF16)
            low = (active - high.astype(F32)).astype(BF16)
            gate_ref[...] = dot(pick, high) + dot(pick, low)
        else:
            qkv_ref[:, (part - 1) * width : part * width] = dot(pick, active.astype(BF16)).astype(
                BF16
            )
    mask = tile_mask()
    factor = HDIM ** (-0.5)
    for tile in range(tokens // TILE):
        rows = slice(tile * TILE, (tile + 1) * TILE)
        parts = []
        for head in range(HEADS):
            vals, queries, keys = (
                qkv_ref[rows, part * width + head * HDIM : part * width + (head + 1) * HDIM]
                for part in range(3)
            )
            score = dot(queries, keys, NT) * factor
            sigma = sigmoid(score)
            weight = jnp.where(mask, score * sigma, 0.0).astype(BF16)
            slope = sigma * (1.0 + score * (1.0 - sigma)) * factor
            slope_ref[tile * HEADS + head] = jnp.where(mask, slope, 0.0)
            weight_ref[tile * HEADS + head] = weight
            parts.append(dot(weight, vals))
        attended = jnp.concatenate(parts, axis=1)
        shifted = attended - jnp.mean(attended, axis=-1, keepdims=True)
        scale = lax.rsqrt(jnp.mean(shifted * shifted, axis=-1, keepdims=True) + EPSILON)
        hat = shifted * scale
        hat_ref[rows, :] = hat
        hat_scale_ref[rows, :] = scale
        mixed_ref[rows, :] = (hat * gain_out_ref[...] * gate_ref[rows, :]).astype(BF16)


def backward_body(
    plan,
    total_factor,
    me_ref,
    dest_ref,
    item_ref,
    owner_row_ref,
    w_in_ref,
    w_out_ref,
    gain_in_ref,
    gain_out_ref,
    qkv_ref,
    gate_ref,
    hat_ref,
    hat_scale_ref,
    mixed_ref,
    weight_ref,
    slope_ref,
    normed_ref,
    rows_hat_ref,
    rows_scale_ref,
    rows_slope_ref,
    rank_ref,
    digits_ref,
    *refs,
):
    count, width = rows_hat_ref.shape
    tokens = hat_ref.shape[0]
    peers, table_size = plan.dp_size, plan.table_size
    got_refs, refs = refs[:peers], refs[peers:]
    table_refs, refs = refs[:table_size], refs[table_size:]
    part_refs, (sums_ref, active_ref, grad_y_ref, wide_ref) = refs[:4], refs[4:]
    me = me_ref[0]
    for slot in range(peers):
        wide_ref[me // table_size ^ slot] = got_refs[slot][...]
    for slot in range(peers):
        grad_y_ref[slot * SLOT : (slot + 1) * SLOT, :] = wide_ref[dest_ref[slot]]
    gain_total = jnp.zeros((1, width), F32)
    for tile in range(tokens // TILE):
        rows = slice(tile * TILE, (tile + 1) * TILE)
        grad_mixed = dot(grad_y_ref[rows, :], w_out_ref[...], NT)
        hat = hat_ref[rows, :]
        active_ref[rows, :width] = (grad_mixed * hat * gain_out_ref[...]).astype(BF16)
        inner = grad_mixed * gate_ref[rows, :]
        gain_total = gain_total + jnp.sum(inner * hat, axis=0, keepdims=True)
        inner = inner * gain_out_ref[...]
        mean = jnp.mean(inner, axis=-1, keepdims=True)
        along = jnp.mean(inner * hat, axis=-1, keepdims=True)
        grad_att = ((inner - mean - hat * along) * hat_scale_ref[rows, :]).astype(BF16)
        for head in range(HEADS):
            columns = slice(head * HDIM, (head + 1) * HDIM)
            vals, queries, keys = (
                qkv_ref[rows, part * width + head * HDIM : part * width + (head + 1) * HDIM]
                for part in range(3)
            )
            grad_o = grad_att[:, columns]
            grad_weight = dot(grad_o, vals, NT)
            grad_score = (grad_weight * slope_ref[tile * HEADS + head]).astype(BF16)
            for part, value in (
                (1, dot(weight_ref[tile * HEADS + head], grad_o, TN)),
                (2, dot(grad_score, keys)),
                (3, dot(grad_score, queries, TN)),
            ):
                first = part * width + head * HDIM
                active_ref[rows, first : first + HDIM] = value.astype(BF16)
    grad_y = grad_y_ref[...]
    sums_ref[:, 4 * width : 5 * width] = (dot(mixed_ref[...], grad_y, TN) * total_factor).astype(
        BF16
    )
    sub = lax.broadcasted_iota(jnp.int32, (count, tokens), 0)
    gather = jnp.where(sub == jnp.broadcast_to(item_ref[...], (count, tokens)), 1.0, 0.0)
    gather = gather.astype(BF16)
    grad_normed = jnp.zeros((count, width), F32)
    for part in range(4):
        columns = slice(part * width, (part + 1) * width)
        summed = dot(gather, active_ref[:, columns])
        grad_hidden = (summed * rows_slope_ref[:, columns]).astype(BF16)
        sums_ref[:, columns] = (dot(normed_ref[...], grad_hidden, TN) * total_factor).astype(BF16)
        grad_normed = grad_normed + dot(grad_hidden, w_in_ref[:, columns], NT)
    hat = rows_hat_ref[...]
    gain_rows = jnp.concatenate(
        [jnp.sum(grad_normed * hat, axis=0, keepdims=True), gain_total]
        + [jnp.zeros((14, width), F32)],
        axis=0,
    )
    gains = (gain_rows * total_factor).astype(BF16)
    sums_ref[:, 5 * width : 5 * width + LANES] = dot(gains, unit(16), TN).astype(BF16)
    if sums_ref.shape[1] > 5 * width + LANES:
        rest = sums_ref.shape[1] - 5 * width - LANES
        sums_ref[:, 5 * width + LANES :] = jnp.zeros((width, rest), BF16)
    inner = grad_normed * gain_in_ref[...]
    mean = jnp.mean(inner, axis=-1, keepdims=True)
    along = jnp.mean(inner * hat, axis=-1, keepdims=True)
    row_grad = (inner - mean - hat * along) * rows_scale_ref[...] + dot(gather, grad_y)
    owner = owner_row_ref[...] ^ me
    shift = table_size.bit_length() - 1
    place = (owner & (table_size - 1)) * peers + (owner >> shift)
    place = place * plan.capacity + rank_ref[...]
    row_grad = row_grad.astype(BF16)
    held = table_refs[0].shape[0]
    for apart, table_ref in enumerate(table_refs):
        spots = lax.broadcasted_iota(jnp.int32, (held, count), 0) + apart * held
        spread = jnp.where(spots == jnp.broadcast_to(place, (held, count)), 1.0, 0.0)
        spread = spread.astype(BF16)
        table_ref[:, :width] = dot(spread, row_grad).astype(BF16)
        table_ref[:, width:] = dot(spread, digits_ref[...]).astype(BF16)
    for half in range(2):
        for place_now in range(plan.chunks):
            out_ref = part_refs[2 * half + place_now // (plan.chunks // 2)]
            out_ref[place_now % (plan.chunks // 2)] = sums_ref[
                chunk_at(plan, me ^ plan.mask_of(half, place_now), half)
            ]


def unit(rows):
    sub = lax.broadcasted_iota(jnp.int32, (rows, LANES), 0)
    lane = lax.broadcasted_iota(jnp.int32, (rows, LANES), 1)
    return jnp.where(sub == lane, 1.0, 0.0).astype(BF16)


def chunk_at(plan, chunk, half):
    first = pl.multiple_of((chunk & (plan.row_groups - 1)) * CHUNK_ROWS, CHUNK_ROWS)
    begin, wide = plan.halves[half]
    if plan.column_groups == 1:
        return pl.ds(first, CHUNK_ROWS), slice(begin, begin + wide)
    group = chunk >> (plan.row_groups.bit_length() - 1)
    column = pl.multiple_of(group * wide + begin, LANES)
    return pl.ds(first, CHUNK_ROWS), pl.ds(column, wide)


class Plan:
    def __init__(self, dp_size, table_size, count, width):
        self.dp_size, self.table_size = dp_size, table_size
        self.chunks = dp_size * table_size
        self.capacity = 2 * count // self.chunks
        self.row_groups = min(self.chunks, width // CHUNK_ROWS)
        self.column_groups = self.chunks // self.row_groups
        block = self.column_groups * LANES
        blocks = -(-(5 * width + LANES) // block)
        left = -(-blocks // 2)
        self.columns = blocks * block
        self.halves = ((0, left * LANES), (left * block, (blocks - left) * LANES))
        table_bits = [1 << bit for bit in range(table_size.bit_length() - 1)]
        dp_bits = [table_size << bit for bit in range(dp_size.bit_length() - 1)]
        self.orders = (
            table_bits + dp_bits,
            table_bits[:1] + dp_bits[:1] + table_bits[1:] + dp_bits[1:],
        )

    def mask_of(self, half, place):
        order = self.orders[half]
        mask = 0
        for step, bit in enumerate(order):
            if place >> (len(order) - 1 - step) & 1:
                mask ^= bit
        return mask


def regroup_body(plan, *refs):
    in_refs, out_refs = refs[: plan.table_size], refs[plan.table_size :]
    rows = out_refs[0].shape[0]
    held = in_refs[0].shape[0]
    capacity = plan.capacity
    if capacity % 16 == 0:
        for apart, out_ref in enumerate(out_refs):
            for side, in_ref in enumerate(in_refs):
                out_ref[side * capacity : (side + 1) * capacity, :] = in_ref[
                    apart * capacity : (apart + 1) * capacity, :
                ]
        return
    for apart, out_ref in enumerate(out_refs):
        total = jnp.zeros(out_ref.shape, F32)
        for side, in_ref in enumerate(in_refs):
            sub = lax.broadcasted_iota(jnp.int32, (rows, held), 0) - side * capacity
            lane = lax.broadcasted_iota(jnp.int32, (rows, held), 1) - apart * capacity
            hit = (sub == lane) & (sub >= 0) & (sub < capacity)
            total = total + dot(jnp.where(hit, 1.0, 0.0).astype(BF16), in_ref[...])
        out_ref[...] = total.astype(BF16)


def table_body(*refs):
    got_refs, out_ref, full_ref = refs[:-2], refs[-2], refs[-1]
    held = got_refs[0].shape[0]
    for index, got_ref in enumerate(got_refs):
        full_ref[index * held : (index + 1) * held, :] = got_ref[...]
    places, width = full_ref.shape[0], out_ref.shape[1]
    lane = lax.broadcasted_iota(jnp.int32, (16, LANES), 1)
    scale = jnp.where(lane == 0, 32.0, jnp.where(lane == 1, 1.0, 0.0)).astype(BF16)
    numbers = dot(scale, full_ref[:, width:], NT)[0:1].astype(jnp.int32)
    step = 256
    for first in range(0, out_ref.shape[0], step):
        sub = lax.broadcasted_iota(jnp.int32, (step, places), 0) + first
        hit = jnp.where(sub == jnp.broadcast_to(numbers, (step, places)), 1.0, 0.0)
        out_ref[first : first + step, :] = dot(hit.astype(BF16), full_ref[:, :width])


def widen_body(plan, me_ref, *refs):
    part_refs, (w_in_ref, w_out_ref, gain_in_ref, gain_out_ref, sums_ref) = refs[:4], refs[4:]
    me = me_ref[0]
    for half in range(2):
        for place in range(plan.chunks):
            in_ref = part_refs[2 * half + place // (plan.chunks // 2)]
            sums_ref[chunk_at(plan, me ^ plan.mask_of(half, place), half)] = in_ref[
                place % (plan.chunks // 2)
            ]
    split, end = w_in_ref.shape[1], w_in_ref.shape[1] + w_out_ref.shape[1]
    w_in_ref[...] = sums_ref[:, :split].astype(F32)
    w_out_ref[...] = sums_ref[:, split:end].astype(F32)
    gains = dot(unit(16), sums_ref[:, end : end + LANES], NT)
    gain_in_ref[...] = gains[0:1]
    gain_out_ref[...] = gains[1:2]


def add(left, right):
    return (left.astype(F32) + right.astype(F32)).astype(BF16)


def on_device(
    touched_rows,
    row_of_token,
    row_owner,
    owner_row,
    seq_blocks,
    seq_dest,
    grad_out,
    w_in,
    w_out,
    gain_in,
    gain_out,
):
    dp_size, table_size = lax.axis_size("dp"), lax.axis_size("table")
    both = ("dp", "table")
    count, width = touched_rows.shape
    tokens = row_of_token.shape[0]
    plan = Plan(dp_size, table_size, count, width)
    devices_all = plan.chunks
    total_factor = 1.0 / math.sqrt(grad_out.shape[0] * devices_all)
    gain_in, gain_out = gain_in[None, :], gain_out[None, :]
    me = lax.axis_index(both).astype(jnp.int32)[None]

    def swap(values, mask):
        return lax.ppermute(values, both, [(here, here ^ mask) for here in range(devices_all)])

    packed = seq_dest * 8 + seq_blocks
    all_packed = [packed] + [swap(packed, apart * table_size) for apart in range(1, dp_size)]
    send = call(
        functools.partial(send_body, table_size),
        [shape_of((SLOT, width), BF16)] * dp_size,
        [SMEM] * (dp_size + 1) + [VMEM],
        scratch=[pltpu.SMEM((dp_size,), jnp.int32)],
    )(me, *all_packed, grad_out)
    got = [send[0]] + [swap(send[apart], apart * table_size) for apart in range(1, dp_size)]

    pairs = tokens // TILE * HEADS
    saved = call(
        forward_body,
        (
            shape_of((tokens, 3 * width), BF16),
            shape_of((tokens, width), F32),
            shape_of((tokens, width), F32),
            shape_of((tokens, 1), F32),
            shape_of((tokens, width), BF16),
            shape_of((pairs, TILE, TILE), BF16),
            shape_of((pairs, TILE, TILE), F32),
            shape_of((count, width), BF16),
            shape_of((count, width), F32),
            shape_of((count, 1), F32),
            shape_of((count, 4 * width), F32),
            shape_of((1, count), jnp.int32),
            shape_of((count, LANES), BF16),
        ),
        [VMEM] * 8,
        flops=4 * count * width * width * 8,
        moved=10_000_000,
    )(
        touched_rows,
        row_of_token.reshape(tokens, 1),
        w_in,
        gain_in,
        gain_out,
        row_owner,
        row_owner.reshape(1, count),
        owner_row.reshape(count, 1),
    )

    half_shapes = [
        shape_of((devices_all // 2, CHUNK_ROWS, wide), BF16) for _, wide in plan.halves
    ]
    held = dp_size * plan.capacity
    outs = call(
        functools.partial(backward_body, plan, total_factor),
        [shape_of((held, width + LANES), BF16)] * table_size
        + [half_shapes[0], half_shapes[0], half_shapes[1], half_shapes[1]],
        [SMEM] * 2 + [VMEM] * (19 + dp_size),
        flops=4 * count * width * width * 20,
        moved=12_000_000,
        scratch=[
            pltpu.VMEM((width, plan.columns), BF16),
            pltpu.VMEM((tokens, 4 * width), BF16),
            pltpu.VMEM((tokens, width), BF16),
            pltpu.VMEM((dp_size, SLOT, width), BF16),
        ],
    )(
        me,
        seq_dest,
        row_of_token.reshape(1, tokens),
        row_owner.reshape(1, count),
        w_in,
        w_out,
        gain_in,
        gain_out,
        *saved,
        *got,
    )
    table_send, parts = outs[:table_size], outs[table_size:]

    steps = len(plan.orders[0])
    kept, sent = [parts[0], parts[2]], [parts[1], parts[3]]
    for step in range(steps):
        came = [swap(sent[half], plan.orders[half][step]) for half in range(2)]
        middle = kept[0].shape[0] // 2
        for half in range(2):
            if middle:
                sent[half] = add(kept[half][middle:], came[half][middle:])
                kept[half] = add(kept[half][:middle], came[half][:middle])
            else:
                kept[half] = add(kept[half], came[half])
    for step in reversed(range(steps)):
        came = [swap(kept[half], plan.orders[half][step]) for half in range(2)]
        if step:
            kept = [jnp.concatenate([kept[half], came[half]]) for half in range(2)]

    table_mid = [table_send[0]] + [swap(table_send[apart], apart) for apart in range(1, table_size)]
    table_mid = call(
        functools.partial(regroup_body, plan),
        [shape_of((table_size * plan.capacity, width + LANES), BF16)] * dp_size,
        [VMEM] * table_size,
    )(*table_mid)
    table_got = [table_mid[0]] + [
        swap(table_mid[apart], apart * table_size) for apart in range(1, dp_size)
    ]
    table_part = call(
        table_body,
        shape_of((ROWS_DEV, width), F32),
        [VMEM] * dp_size,
        scratch=[pltpu.VMEM((devices_all * plan.capacity, width + LANES), BF16)],
    )(*table_got)
    grad_w_in, grad_w_out, grad_gain_in, grad_gain_out = call(
        functools.partial(widen_body, plan),
        (
            shape_of(w_in.shape, F32),
            shape_of(w_out.shape, F32),
            shape_of((1, width), F32),
            shape_of((1, width), F32),
        ),
        [SMEM] + [VMEM] * 4,
        scratch=[pltpu.VMEM((width, plan.columns), BF16)],
    )(me, kept[0], came[0], kept[1], came[1])
    return (table_part, grad_w_in, grad_w_out, grad_gain_in[0], grad_gain_out[0])


def solution(mesh):
    rows = P(("dp", "table"), None)
    flat = P(("dp", "table"))
    in_specs = (rows, flat, rows, flat, flat, flat, rows, P(), P(), P(), P())
    out_specs = (rows, P(), P(), P(), P())
    return jax.shard_map(
        on_device, mesh=mesh, in_specs=in_specs, out_specs=out_specs, check_vma=False
    )
```

```python
import functools
import math

import jax
import jax.numpy as jnp
from jax import lax
from jax.experimental import pallas as pl
from jax.experimental.pallas import tpu as pltpu
from jax.sharding import PartitionSpec as P

HEADS = 4
HDIM = 128
BLK = 16
LMAXB = 4
SLOT = LMAXB * BLK
ROWS_DEV = 1024
TILE = 2 * SLOT
LANES = 128
CHUNK_ROWS = 16
EPSILON = 1e-05
F32 = jnp.float32
BF16 = jnp.bfloat16
VMEM = pl.BlockSpec(memory_space=pltpu.VMEM)
SMEM = pl.BlockSpec(memory_space=pltpu.SMEM)


def call(body, out_shape, in_specs, flops=0, moved=0, scratch=()):
    outs = jax.tree.map(lambda _: VMEM, out_shape)
    return pl.pallas_call(
        body,
        out_shape=out_shape,
        in_specs=in_specs,
        out_specs=outs,
        scratch_shapes=scratch,
        compiler_params=pltpu.CompilerParams(vmem_limit_bytes=24 * 1024 * 1024),
        cost_estimate=pl.CostEstimate(flops=flops, bytes_accessed=moved, transcendentals=0),
    )


def shape_of(dims, dtype):
    return jax.ShapeDtypeStruct(dims, dtype)


def sigmoid(values):
    return 0.5 * jnp.tanh(0.5 * values) + 0.5


def dot(left, right, contract=((1,), (0,))):
    return lax.dot_general(left, right, (contract, ((), ())), preferred_element_type=F32)


NT = ((1,), (1,))
TN = ((0,), (0,))


def send_body(table_size, me_ref, packed_ref, grad_ref, out_ref):
    peers = out_ref.shape[0]
    blocks = grad_ref.shape[0] // BLK
    me = me_ref[0] // table_size
    begin = jnp.int32(0)
    for peer in range(peers):

        def find(slot, length, peer=peer):
            entry = packed_ref[peer, 0, slot]
            return length + jnp.where(entry >> 3 == me, entry & 7, 0)

        length = lax.fori_loop(0, peers, find, jnp.int32(0), unroll=True)
        for inner in range(LMAXB):
            block = jnp.minimum(begin + inner, blocks - 1)
            rows = grad_ref[pl.ds(pl.multiple_of(block * BLK, BLK), BLK), :]
            live = jnp.full(rows.shape, inner, jnp.int32) < length
            out_ref[peer, inner * BLK : (inner + 1) * BLK, :] = jnp.where(
                live, rows.astype(F32), 0.0
            ).astype(BF16)
        begin = begin + length


def tile_mask():
    sub = lax.broadcasted_iota(jnp.int32, (TILE, TILE), 0)
    lane = lax.broadcasted_iota(jnp.int32, (TILE, TILE), 1)
    return (sub // SLOT == lane // SLOT) & (lane <= sub)


def forward_body(
    rows_ref,
    item_ref,
    w_in_ref,
    gain_in_ref,
    gain_out_ref,
    owner_col_ref,
    owner_row_ref,
    number_ref,
    qkv_ref,
    gate_ref,
    hat_ref,
    hat_scale_ref,
    mixed_ref,
    weight_ref,
    slope_ref,
    normed_ref,
    rows_hat_ref,
    rows_scale_ref,
    rows_slope_ref,
    rank_ref,
    digits_ref,
):
    count, width = rows_ref.shape
    tokens = item_ref.shape[0]
    across = jnp.broadcast_to(owner_row_ref[...], (count, count))
    down = jnp.broadcast_to(owner_col_ref[...], (count, count))
    sub = lax.broadcasted_iota(jnp.int32, (count, count), 0)
    lane = lax.broadcasted_iota(jnp.int32, (count, count), 1)
    earlier = jnp.where((across == down) & (sub < lane), 1.0, 0.0)
    rank_ref[...] = jnp.sum(earlier, axis=0, keepdims=True).astype(jnp.int32)
    number = jnp.broadcast_to(number_ref[...], (count, LANES))
    lane = lax.broadcasted_iota(jnp.int32, (count, LANES), 1)
    digits = jnp.where(lane == 0, number >> 5, jnp.where(lane == 1, number & 31, 0))
    digits_ref[...] = digits.astype(F32).astype(BF16)
    values = rows_ref[...].astype(F32)
    shifted = values - jnp.mean(values, axis=-1, keepdims=True)
    scale = lax.rsqrt(jnp.mean(shifted * shifted, axis=-1, keepdims=True) + EPSILON)
    hat = shifted * scale
    rows_hat_ref[...] = hat
    rows_scale_ref[...] = scale
    normed = (hat * gain_in_ref[...]).astype(BF16)
    normed_ref[...] = normed
    lane = lax.broadcasted_iota(jnp.int32, (tokens, count), 1)
    pick = jnp.where(lane == jnp.broadcast_to(item_ref[...], (tokens, count)), 1.0, 0.0)
    pick = pick.astype(BF16)
    for part in range(4):
        columns = slice(part * width, (part + 1) * width)
        hidden = dot(normed, w_in_ref[:, columns])
        sigma = sigmoid(hidden)
        active = hidden * sigma
        rows_slope_ref[:, columns] = sigma * (1.0 + hidden * (1.0 - sigma))
        if part == 0:
            high = active.astype(BF16)
            low = (active - high.astype(F32)).astype(BF16)
            gate_ref[...] = dot(pick, high) + dot(pick, low)
        else:
            qkv_ref[:, (part - 1) * width : part * width] = dot(pick, active.astype(BF16)).astype(
                BF16
            )
    mask = tile_mask()
    factor = HDIM ** (-0.5)
    for tile in range(tokens // TILE):
        rows = slice(tile * TILE, (tile + 1) * TILE)
        parts = []
        for head in range(HEADS):
            vals, queries, keys = (
                qkv_ref[rows, part * width + head * HDIM : part * width + (head + 1) * HDIM]
                for part in range(3)
            )
            score = dot(queries, keys, NT) * factor
            sigma = sigmoid(score)
            weight = jnp.where(mask, score * sigma, 0.0).astype(BF16)
            slope = sigma * (1.0 + score * (1.0 - sigma)) * factor
            slope_ref[tile * HEADS + head] = jnp.where(mask, slope, 0.0)
            weight_ref[tile * HEADS + head] = weight
            parts.append(dot(weight, vals))
        attended = jnp.concatenate(parts, axis=1)
        shifted = attended - jnp.mean(attended, axis=-1, keepdims=True)
        scale = lax.rsqrt(jnp.mean(shifted * shifted, axis=-1, keepdims=True) + EPSILON)
        hat = shifted * scale
        hat_ref[rows, :] = hat
        hat_scale_ref[rows, :] = scale
        mixed_ref[rows, :] = (hat * gain_out_ref[...] * gate_ref[rows, :]).astype(BF16)


def backward_body(
    plan,
    total_factor,
    me_ref,
    dest_ref,
    item_ref,
    owner_row_ref,
    w_in_ref,
    w_out_ref,
    gain_in_ref,
    gain_out_ref,
    qkv_ref,
    gate_ref,
    hat_ref,
    hat_scale_ref,
    mixed_ref,
    weight_ref,
    slope_ref,
    normed_ref,
    rows_hat_ref,
    rows_scale_ref,
    rows_slope_ref,
    rank_ref,
    digits_ref,
    got_ref,
    table_ref,
    keep_ref,
    give_ref,
    sums_ref,
    active_ref,
    grad_y_ref,
):
    count, width = rows_hat_ref.shape
    tokens = hat_ref.shape[0]
    me = me_ref[0]
    for slot in range(got_ref.shape[0]):
        grad_y_ref[slot * SLOT : (slot + 1) * SLOT, :] = got_ref[dest_ref[slot]]
    gain_total = jnp.zeros((1, width), F32)
    for tile in range(tokens // TILE):
        rows = slice(tile * TILE, (tile + 1) * TILE)
        grad_mixed = dot(grad_y_ref[rows, :], w_out_ref[...], NT)
        hat = hat_ref[rows, :]
        active_ref[rows, :width] = (grad_mixed * hat * gain_out_ref[...]).astype(BF16)
        inner = grad_mixed * gate_ref[rows, :]
        gain_total = gain_total + jnp.sum(inner * hat, axis=0, keepdims=True)
        inner = inner * gain_out_ref[...]
        mean = jnp.mean(inner, axis=-1, keepdims=True)
        along = jnp.mean(inner * hat, axis=-1, keepdims=True)
        grad_att = ((inner - mean - hat * along) * hat_scale_ref[rows, :]).astype(BF16)
        for head in range(HEADS):
            columns = slice(head * HDIM, (head + 1) * HDIM)
            vals, queries, keys = (
                qkv_ref[rows, part * width + head * HDIM : part * width + (head + 1) * HDIM]
                for part in range(3)
            )
            grad_o = grad_att[:, columns]
            grad_weight = dot(grad_o, vals, NT)
            grad_score = (grad_weight * slope_ref[tile * HEADS + head]).astype(BF16)
            for part, value in (
                (1, dot(weight_ref[tile * HEADS + head], grad_o, TN)),
                (2, dot(grad_score, keys)),
                (3, dot(grad_score, queries, TN)),
            ):
                first = part * width + head * HDIM
                active_ref[rows, first : first + HDIM] = value.astype(BF16)
    grad_y = grad_y_ref[...]
    sums_ref[:, 4 * width : 5 * width] = (dot(mixed_ref[...], grad_y, TN) * total_factor).astype(
        BF16
    )
    sub = lax.broadcasted_iota(jnp.int32, (count, tokens), 0)
    gather = jnp.where(sub == jnp.broadcast_to(item_ref[...], (count, tokens)), 1.0, 0.0)
    gather = gather.astype(BF16)
    grad_normed = jnp.zeros((count, width), F32)
    for part in range(4):
        columns = slice(part * width, (part + 1) * width)
        summed = dot(gather, active_ref[:, columns])
        grad_hidden = (summed * rows_slope_ref[:, columns]).astype(BF16)
        sums_ref[:, columns] = (dot(normed_ref[...], grad_hidden, TN) * total_factor).astype(BF16)
        grad_normed = grad_normed + dot(grad_hidden, w_in_ref[:, columns], NT)
    hat = rows_hat_ref[...]
    gain_rows = jnp.concatenate(
        [jnp.sum(grad_normed * hat, axis=0, keepdims=True), gain_total]
        + [jnp.zeros((14, width), F32)],
        axis=0,
    )
    gains = (gain_rows * total_factor).astype(BF16)
    sums_ref[:, 5 * width : 5 * width + LANES] = dot(gains, unit(16), TN).astype(BF16)
    if sums_ref.shape[1] > 5 * width + LANES:
        rest = sums_ref.shape[1] - 5 * width - LANES
        sums_ref[:, 5 * width + LANES :] = jnp.zeros((width, rest), BF16)
    inner = grad_normed * gain_in_ref[...]
    mean = jnp.mean(inner, axis=-1, keepdims=True)
    along = jnp.mean(inner * hat, axis=-1, keepdims=True)
    row_grad = (inner - mean - hat * along) * rows_scale_ref[...] + dot(gather, grad_y)
    places = table_ref.shape[0]
    place = owner_row_ref[...] * plan.capacity + rank_ref[...]
    spots = lax.broadcasted_iota(jnp.int32, (places, count), 0)
    spread = jnp.where(spots == jnp.broadcast_to(place, (places, count)), 1.0, 0.0).astype(BF16)
    table_ref[:, :width] = dot(spread, row_grad.astype(BF16)).astype(BF16)
    table_ref[:, width:] = dot(spread, digits_ref[...]).astype(BF16)
    for place_now in range(plan.chunks):
        out_ref = (keep_ref, give_ref)[place_now // (plan.chunks // 2)]
        out_ref[place_now % (plan.chunks // 2)] = sums_ref[plan.chunk_at(me, place_now)]


def unit(rows):
    sub = lax.broadcasted_iota(jnp.int32, (rows, LANES), 0)
    lane = lax.broadcasted_iota(jnp.int32, (rows, LANES), 1)
    return jnp.where(sub == lane, 1.0, 0.0).astype(BF16)


class Plan:
    def __init__(self, dp_size, table_size, count, width):
        self.chunks = dp_size * table_size
        self.capacity = 2 * count // self.chunks
        self.row_groups = min(self.chunks, width // CHUNK_ROWS)
        self.column_groups = self.chunks // self.row_groups
        block = self.column_groups * LANES
        blocks = -(-(5 * width + LANES) // block)
        self.columns = blocks * block
        self.wide = blocks * LANES
        table_bits = [1 << bit for bit in range(1, table_size.bit_length() - 1)]
        dp_bits = [table_size << bit for bit in range(dp_size.bit_length() - 1)]
        self.orders = (table_bits + dp_bits, dp_bits[:2] + table_bits + dp_bits[2:])
        self.steps = len(self.orders[0])

    def low_mask(self, core, place):
        mask = 0
        for step, bit in enumerate(self.orders[core]):
            if place >> (self.steps - 1 - step) & 1:
                mask ^= bit
        return mask

    def chunk_at(self, me, place):
        top, low = divmod(place, self.chunks // 2)
        masks = [top ^ self.low_mask(core ^ top, low) for core in range(2)]
        chunk = me ^ jnp.where((me & 1) == 0, masks[0], masks[1])
        first = pl.multiple_of((chunk & (self.row_groups - 1)) * CHUNK_ROWS, CHUNK_ROWS)
        if self.column_groups == 1:
            return pl.ds(first, CHUNK_ROWS), slice(0, self.wide)
        group = chunk >> (self.row_groups.bit_length() - 1)
        return pl.ds(first, CHUNK_ROWS), pl.ds(pl.multiple_of(group * self.wide, LANES), self.wide)


def table_body(got_ref, out_ref):
    places, width = got_ref.shape[0], out_ref.shape[1]
    lane = lax.broadcasted_iota(jnp.int32, (16, LANES), 1)
    scale = jnp.where(lane == 0, 32.0, jnp.where(lane == 1, 1.0, 0.0)).astype(BF16)
    numbers = dot(scale, got_ref[:, width:], NT)[0:1].astype(jnp.int32)
    step = 256
    for first in range(0, out_ref.shape[0], step):
        sub = lax.broadcasted_iota(jnp.int32, (step, places), 0) + first
        hit = jnp.where(sub == jnp.broadcast_to(numbers, (step, places)), 1.0, 0.0)
        out_ref[first : first + step, :] = dot(hit.astype(BF16), got_ref[:, :width])


def widen_body(
    plan, me_ref, own_ref, came_ref, w_in_ref, w_out_ref, gain_in_ref, gain_out_ref, sums_ref
):
    me = me_ref[0]
    for place in range(plan.chunks):
        in_ref = (own_ref, came_ref)[place // (plan.chunks // 2)]
        sums_ref[plan.chunk_at(me, place)] = in_ref[place % (plan.chunks // 2)]
    split, end = w_in_ref.shape[1], w_in_ref.shape[1] + w_out_ref.shape[1]
    w_in_ref[...] = sums_ref[:, :split].astype(F32)
    w_out_ref[...] = sums_ref[:, split:end].astype(F32)
    gains = dot(unit(16), sums_ref[:, end : end + LANES], NT)
    gain_in_ref[...] = gains[0:1]
    gain_out_ref[...] = gains[1:2]


def add(left, right):
    return (left.astype(F32) + right.astype(F32)).astype(BF16)


def on_device(
    touched_rows,
    row_of_token,
    row_owner,
    owner_row,
    seq_blocks,
    seq_dest,
    grad_out,
    w_in,
    w_out,
    gain_in,
    gain_out,
):
    dp_size, table_size = lax.axis_size("dp"), lax.axis_size("table")
    both = ("dp", "table")
    count, width = touched_rows.shape
    tokens = row_of_token.shape[0]
    plan = Plan(dp_size, table_size, count, width)
    devices_all = plan.chunks
    total_factor = 1.0 / math.sqrt(grad_out.shape[0] * devices_all)
    gain_in, gain_out = gain_in[None, :], gain_out[None, :]
    me = lax.axis_index(both).astype(jnp.int32)[None]

    def swap(values, masks):
        pairs = [(here, here ^ masks[here & 1]) for here in range(devices_all)]
        return lax.ppermute(values, both, pairs)

    def exchange(values, axes):
        return lax.all_to_all(values, axes, split_axis=0, concat_axis=0, tiled=True)

    packed = jnp.broadcast_to(seq_dest * 8 + seq_blocks, (dp_size, 1, dp_size))
    send = call(
        functools.partial(send_body, table_size),
        shape_of((dp_size, SLOT, width), BF16),
        [SMEM] * 2 + [VMEM],
    )(me, exchange(packed, "dp"), grad_out)
    got = exchange(send, "dp")

    pairs = tokens // TILE * HEADS
    saved = call(
        forward_body,
        (
            shape_of((tokens, 3 * width), BF16),
            shape_of((tokens, width), F32),
            shape_of((tokens, width), F32),
            shape_of((tokens, 1), F32),
            shape_of((tokens, width), BF16),
            shape_of((pairs, TILE, TILE), BF16),
            shape_of((pairs, TILE, TILE), F32),
            shape_of((count, width), BF16),
            shape_of((count, width), F32),
            shape_of((count, 1), F32),
            shape_of((count, 4 * width), F32),
            shape_of((1, count), jnp.int32),
            shape_of((count, LANES), BF16),
        ),
        [VMEM] * 8,
        flops=4 * count * width * width * 8,
        moved=10_000_000,
    )(
        touched_rows,
        row_of_token.reshape(tokens, 1),
        w_in,
        gain_in,
        gain_out,
        row_owner,
        row_owner.reshape(1, count),
        owner_row.reshape(count, 1),
    )

    half = shape_of((devices_all // 2, CHUNK_ROWS, plan.wide), BF16)
    table_send, kept, sent = call(
        functools.partial(backward_body, plan, total_factor),
        [shape_of((devices_all * plan.capacity, width + LANES), BF16), half, half],
        [SMEM] * 2 + [VMEM] * 20,
        flops=4 * count * width * width * 20,
        moved=12_000_000,
        scratch=[
            pltpu.VMEM((width, plan.columns), BF16),
            pltpu.VMEM((tokens, 4 * width), BF16),
            pltpu.VMEM((tokens, width), BF16),
        ],
    )(
        me,
        seq_dest,
        row_of_token.reshape(1, tokens),
        row_owner.reshape(1, count),
        w_in,
        w_out,
        gain_in,
        gain_out,
        *saved,
        got,
    )

    kept = add(kept, swap(sent, (1, 1)))
    for masks in zip(*plan.orders):
        middle = kept.shape[0] // 2
        came = swap(kept[middle:], masks)
        kept = add(kept[:middle], came)
    for masks in reversed(list(zip(*plan.orders))):
        kept = jnp.concatenate([kept, swap(kept, masks)])
    came = swap(kept, (1, 1))

    table_got = exchange(table_send.reshape(devices_all, plan.capacity, width + LANES), both)
    table_part = call(
        table_body,
        shape_of((ROWS_DEV, width), F32),
        [VMEM],
    )(table_got.reshape(devices_all * plan.capacity, width + LANES))
    grad_w_in, grad_w_out, grad_gain_in, grad_gain_out = call(
        functools.partial(widen_body, plan),
        (
            shape_of(w_in.shape, F32),
            shape_of(w_out.shape, F32),
            shape_of((1, width), F32),
            shape_of((1, width), F32),
        ),
        [SMEM] + [VMEM] * 2,
        scratch=[pltpu.VMEM((width, plan.columns), BF16)],
    )(me, kept, came)
    return (table_part, grad_w_in, grad_w_out, grad_gain_in[0], grad_gain_out[0])


def solution(mesh):
    rows = P(("dp", "table"), None)
    flat = P(("dp", "table"))
    in_specs = (rows, flat, rows, flat, flat, flat, rows, P(), P(), P(), P())
    out_specs = (rows, P(), P(), P(), P())
    return jax.shard_map(
        on_device, mesh=mesh, in_specs=in_specs, out_specs=out_specs, check_vma=False
    )
```

```python
import functools
import math

import jax
import jax.numpy as jnp
from jax import lax
from jax.experimental import pallas as pl
from jax.experimental.pallas import tpu as pltpu
from jax.sharding import PartitionSpec as P

HEADS = 4
HDIM = 128
BLK = 16
LMAXB = 4
SLOT = LMAXB * BLK
ROWS_DEV = 1024
TILE = 2 * SLOT
LANES = 128
CHUNK_ROWS = 16
EPSILON = 1e-05
F32 = jnp.float32
BF16 = jnp.bfloat16
VMEM = pl.BlockSpec(memory_space=pltpu.VMEM)
SMEM = pl.BlockSpec(memory_space=pltpu.SMEM)
HBM = pl.BlockSpec(memory_space=pltpu.HBM)


def call(body, out_shape, in_specs, flops=0, moved=0, scratch=(), out_space=VMEM, mebibytes=24):
    outs = jax.tree.map(lambda _: out_space, out_shape)
    return pl.pallas_call(
        body,
        out_shape=out_shape,
        in_specs=in_specs,
        out_specs=outs,
        scratch_shapes=scratch,
        compiler_params=pltpu.CompilerParams(vmem_limit_bytes=mebibytes * 1024 * 1024),
        cost_estimate=pl.CostEstimate(flops=flops, bytes_accessed=moved, transcendentals=0),
    )


def shape_of(dims, dtype):
    return jax.ShapeDtypeStruct(dims, dtype)


def sigmoid(values):
    return 0.5 * jnp.tanh(0.5 * values) + 0.5


def dot(left, right, contract=((1,), (0,))):
    return lax.dot_general(left, right, (contract, ((), ())), preferred_element_type=F32)


NT = ((1,), (1,))
TN = ((0,), (0,))


def send_body(table_size, me_ref, packed_ref, grad_ref, out_ref):
    peers = out_ref.shape[0]
    blocks = grad_ref.shape[0] // BLK
    me = me_ref[0] // table_size
    begin = jnp.int32(0)
    for peer in range(peers):

        def find(slot, length, peer=peer):
            entry = packed_ref[peer, 0, slot]
            return length + jnp.where(entry >> 3 == me, entry & 7, 0)

        length = lax.fori_loop(0, peers, find, jnp.int32(0), unroll=True)
        for inner in range(LMAXB):
            block = jnp.minimum(begin + inner, blocks - 1)
            rows = grad_ref[pl.ds(pl.multiple_of(block * BLK, BLK), BLK), :]
            live = jnp.full(rows.shape, inner, jnp.int32) < length
            out_ref[peer, inner * BLK : (inner + 1) * BLK, :] = jnp.where(
                live, rows.astype(F32), 0.0
            ).astype(BF16)
        begin = begin + length


def tile_mask():
    sub = lax.broadcasted_iota(jnp.int32, (TILE, TILE), 0)
    lane = lax.broadcasted_iota(jnp.int32, (TILE, TILE), 1)
    return (sub // SLOT == lane // SLOT) & (lane <= sub)


SAVED = (
    "gate",
    "hat",
    "hat_scale",
    "qkv",
    "slope",
    "weight",
    "mixed",
    "normed",
    "rows_slope",
    "rows_hat",
    "rows_scale",
    "place",
    "digits",
)


def saved_shapes(tokens, count, width):
    pairs = tokens // TILE * HEADS
    return dict(
        gate=shape_of((tokens, width), F32),
        hat=shape_of((tokens, width), F32),
        hat_scale=shape_of((tokens, 1), F32),
        qkv=shape_of((tokens, 3 * width), BF16),
        slope=shape_of((pairs, TILE, TILE), F32),
        weight=shape_of((pairs, TILE, TILE), BF16),
        mixed=shape_of((tokens, width), BF16),
        normed=shape_of((count, width), BF16),
        rows_slope=shape_of((count, 4 * width), F32),
        rows_hat=shape_of((count, width), F32),
        rows_scale=shape_of((count, 1), F32),
        place=shape_of((1, count), jnp.int32),
        digits=shape_of((count, LANES), BF16),
    )


def forward_body(
    capacity,
    rows_ref,
    item_ref,
    w_in_ref,
    gain_in_ref,
    gain_out_ref,
    owner_col_ref,
    owner_row_ref,
    number_ref,
    *refs,
):
    size = len(SAVED)
    held = dict(zip(SAVED, refs[size : 2 * size]))
    sems = refs[-1]
    copies = {
        name: pltpu.make_async_copy(held[name], refs[index], sems.at[index])
        for index, name in enumerate(SAVED)
    }
    gate_ref, hat_ref, hat_scale_ref, qkv_ref, slope_ref, weight_ref, mixed_ref = (
        held[name] for name in SAVED[:7]
    )
    normed_ref, rows_slope_ref, rows_hat_ref, rows_scale_ref, place_ref, digits_ref = (
        held[name] for name in SAVED[7:]
    )
    count, width = rows_ref.shape
    tokens = item_ref.shape[0]
    across = jnp.broadcast_to(owner_row_ref[...], (count, count))
    down = jnp.broadcast_to(owner_col_ref[...], (count, count))
    sub = lax.broadcasted_iota(jnp.int32, (count, count), 0)
    lane = lax.broadcasted_iota(jnp.int32, (count, count), 1)
    earlier = jnp.where((across == down) & (sub < lane), 1.0, 0.0)
    rank = jnp.sum(earlier, axis=0, keepdims=True).astype(jnp.int32)
    place_ref[...] = owner_row_ref[...] * capacity + rank
    number = jnp.broadcast_to(number_ref[...], (count, LANES))
    lane = lax.broadcasted_iota(jnp.int32, (count, LANES), 1)
    digits = jnp.where(lane == 0, number >> 5, jnp.where(lane == 1, number & 31, 0))
    digits_ref[...] = digits.astype(F32).astype(BF16)
    copies["place"].start()
    copies["digits"].start()
    values = rows_ref[...].astype(F32)
    shifted = values - jnp.mean(values, axis=-1, keepdims=True)
    scale = lax.rsqrt(jnp.mean(shifted * shifted, axis=-1, keepdims=True) + EPSILON)
    hat = shifted * scale
    rows_hat_ref[...] = hat
    rows_scale_ref[...] = scale
    normed = (hat * gain_in_ref[...]).astype(BF16)
    normed_ref[...] = normed
    for name in ("rows_hat", "rows_scale", "normed"):
        copies[name].start()
    lane = lax.broadcasted_iota(jnp.int32, (tokens, count), 1)
    pick = jnp.where(lane == jnp.broadcast_to(item_ref[...], (tokens, count)), 1.0, 0.0)
    pick = pick.astype(BF16)
    for part in range(4):
        columns = slice(part * width, (part + 1) * width)
        hidden = dot(normed, w_in_ref[:, columns])
        sigma = sigmoid(hidden)
        active = hidden * sigma
        rows_slope_ref[:, columns] = sigma * (1.0 + hidden * (1.0 - sigma))
        if part == 0:
            high = active.astype(BF16)
            low = (active - high.astype(F32)).astype(BF16)
            gate_ref[...] = dot(pick, high) + dot(pick, low)
        else:
            qkv_ref[:, (part - 1) * width : part * width] = dot(pick, active.astype(BF16)).astype(
                BF16
            )
    for name in ("gate", "qkv", "rows_slope"):
        copies[name].start()
    mask = tile_mask()
    factor = HDIM ** (-0.5)
    for tile in range(tokens // TILE):
        rows = slice(tile * TILE, (tile + 1) * TILE)
        parts = []
        for head in range(HEADS):
            vals, queries, keys = (
                qkv_ref[rows, part * width + head * HDIM : part * width + (head + 1) * HDIM]
                for part in range(3)
            )
            score = dot(queries, keys, NT) * factor
            sigma = sigmoid(score)
            weight = jnp.where(mask, score * sigma, 0.0).astype(BF16)
            slope = sigma * (1.0 + score * (1.0 - sigma)) * factor
            slope_ref[tile * HEADS + head] = jnp.where(mask, slope, 0.0)
            weight_ref[tile * HEADS + head] = weight
            parts.append(dot(weight, vals))
        attended = jnp.concatenate(parts, axis=1)
        shifted = attended - jnp.mean(attended, axis=-1, keepdims=True)
        scale = lax.rsqrt(jnp.mean(shifted * shifted, axis=-1, keepdims=True) + EPSILON)
        hat = shifted * scale
        hat_ref[rows, :] = hat
        hat_scale_ref[rows, :] = scale
        mixed_ref[rows, :] = (hat * gain_out_ref[...] * gate_ref[rows, :]).astype(BF16)
    for name in ("hat", "hat_scale", "slope", "weight", "mixed"):
        copies[name].start()
    for copy in copies.values():
        copy.wait()


def backward_body(
    plan, total_factor, me_ref, dest_ref, item_ref, gain_in_ref, gain_out_ref, got_ref, *refs
):
    size = len(SAVED) + 2
    far_refs, (table_ref, keep_ref, give_ref), near_refs = (
        refs[:size],
        refs[size : size + 3],
        refs[size + 3 : 2 * size + 3],
    )
    sums_ref, active_ref, grad_y_ref, sems = refs[2 * size + 3 :]
    copies = [
        pltpu.make_async_copy(far, near, sems.at[index])
        for index, (far, near) in enumerate(zip(far_refs, near_refs))
    ]
    for copy in copies:
        copy.start()
    w_out_ref, gate_ref, hat_ref, hat_scale_ref, qkv_ref, slope_ref, weight_ref = near_refs[:7]
    mixed_ref, normed_ref, rows_slope_ref, rows_hat_ref, rows_scale_ref = near_refs[7:12]
    place_ref, digits_ref, w_in_ref = near_refs[12:]
    count, width = rows_hat_ref.shape
    tokens = hat_ref.shape[0]
    me = me_ref[0]
    for slot in range(got_ref.shape[0]):
        grad_y_ref[slot * SLOT : (slot + 1) * SLOT, :] = got_ref[dest_ref[slot]]
    for copy in copies[:7]:
        copy.wait()
    gain_total = jnp.zeros((1, width), F32)
    for tile in range(tokens // TILE):
        rows = slice(tile * TILE, (tile + 1) * TILE)
        grad_mixed = dot(grad_y_ref[rows, :], w_out_ref[...], NT)
        hat = hat_ref[rows, :]
        active_ref[rows, :width] = (grad_mixed * hat * gain_out_ref[...]).astype(BF16)
        inner = grad_mixed * gate_ref[rows, :]
        gain_total = gain_total + jnp.sum(inner * hat, axis=0, keepdims=True)
        inner = inner * gain_out_ref[...]
        mean = jnp.mean(inner, axis=-1, keepdims=True)
        along = jnp.mean(inner * hat, axis=-1, keepdims=True)
        grad_att = ((inner - mean - hat * along) * hat_scale_ref[rows, :]).astype(BF16)
        for head in range(HEADS):
            columns = slice(head * HDIM, (head + 1) * HDIM)
            vals, queries, keys = (
                qkv_ref[rows, part * width + head * HDIM : part * width + (head + 1) * HDIM]
                for part in range(3)
            )
            grad_o = grad_att[:, columns]
            grad_weight = dot(grad_o, vals, NT)
            grad_score = (grad_weight * slope_ref[tile * HEADS + head]).astype(BF16)
            for part, value in (
                (1, dot(weight_ref[tile * HEADS + head], grad_o, TN)),
                (2, dot(grad_score, keys)),
                (3, dot(grad_score, queries, TN)),
            ):
                first = part * width + head * HDIM
                active_ref[rows, first : first + HDIM] = value.astype(BF16)
    for copy in copies[7:]:
        copy.wait()
    grad_y = grad_y_ref[...]
    sums_ref[:, 4 * width : 5 * width] = (dot(mixed_ref[...], grad_y, TN) * total_factor).astype(
        BF16
    )
    sub = lax.broadcasted_iota(jnp.int32, (count, tokens), 0)
    gather = jnp.where(sub == jnp.broadcast_to(item_ref[...], (count, tokens)), 1.0, 0.0)
    gather = gather.astype(BF16)
    grad_normed = jnp.zeros((count, width), F32)
    for part in range(4):
        columns = slice(part * width, (part + 1) * width)
        summed = dot(gather, active_ref[:, columns])
        grad_hidden = (summed * rows_slope_ref[:, columns]).astype(BF16)
        sums_ref[:, columns] = (dot(normed_ref[...], grad_hidden, TN) * total_factor).astype(BF16)
        grad_normed = grad_normed + dot(grad_hidden, w_in_ref[:, columns], NT)
    hat = rows_hat_ref[...]
    gain_rows = jnp.concatenate(
        [jnp.sum(grad_normed * hat, axis=0, keepdims=True), gain_total]
        + [jnp.zeros((14, width), F32)],
        axis=0,
    )
    gains = (gain_rows * total_factor).astype(BF16)
    sums_ref[:, 5 * width : 5 * width + LANES] = dot(gains, unit(16), TN).astype(BF16)
    if sums_ref.shape[1] > 5 * width + LANES:
        rest = sums_ref.shape[1] - 5 * width - LANES
        sums_ref[:, 5 * width + LANES :] = jnp.zeros((width, rest), BF16)
    inner = grad_normed * gain_in_ref[...]
    mean = jnp.mean(inner, axis=-1, keepdims=True)
    along = jnp.mean(inner * hat, axis=-1, keepdims=True)
    row_grad = (inner - mean - hat * along) * rows_scale_ref[...] + dot(gather, grad_y)
    places = table_ref.shape[0]
    place = place_ref[...]
    spots = lax.broadcasted_iota(jnp.int32, (places, count), 0)
    spread = jnp.where(spots == jnp.broadcast_to(place, (places, count)), 1.0, 0.0).astype(BF16)
    table_ref[:, :width] = dot(spread, row_grad.astype(BF16)).astype(BF16)
    table_ref[:, width:] = dot(spread, digits_ref[...]).astype(BF16)
    for place_now in range(plan.chunks):
        out_ref = (keep_ref, give_ref)[place_now // (plan.chunks // 2)]
        out_ref[place_now % (plan.chunks // 2)] = sums_ref[plan.chunk_at(me, place_now)]


def unit(rows):
    sub = lax.broadcasted_iota(jnp.int32, (rows, LANES), 0)
    lane = lax.broadcasted_iota(jnp.int32, (rows, LANES), 1)
    return jnp.where(sub == lane, 1.0, 0.0).astype(BF16)


class Plan:
    def __init__(self, dp_size, table_size, count, width):
        self.chunks = dp_size * table_size
        self.capacity = 2 * count // self.chunks
        self.row_groups = min(self.chunks, width // CHUNK_ROWS)
        self.column_groups = self.chunks // self.row_groups
        block = self.column_groups * LANES
        blocks = -(-(5 * width + LANES) // block)
        self.columns = blocks * block
        self.wide = blocks * LANES
        table_bits = [1 << bit for bit in range(1, table_size.bit_length() - 1)]
        dp_bits = [table_size << bit for bit in range(dp_size.bit_length() - 1)]
        self.orders = (table_bits + dp_bits, dp_bits[:2] + table_bits + dp_bits[2:])
        self.steps = len(self.orders[0])

    def low_mask(self, core, place):
        mask = 0
        for step, bit in enumerate(self.orders[core]):
            if place >> (self.steps - 1 - step) & 1:
                mask ^= bit
        return mask

    def chunk_at(self, me, place):
        top, low = divmod(place, self.chunks // 2)
        masks = [top ^ self.low_mask(core ^ top, low) for core in range(2)]
        chunk = me ^ jnp.where((me & 1) == 0, masks[0], masks[1])
        first = pl.multiple_of((chunk & (self.row_groups - 1)) * CHUNK_ROWS, CHUNK_ROWS)
        if self.column_groups == 1:
            return pl.ds(first, CHUNK_ROWS), slice(0, self.wide)
        group = chunk >> (self.row_groups.bit_length() - 1)
        return pl.ds(first, CHUNK_ROWS), pl.ds(pl.multiple_of(group * self.wide, LANES), self.wide)


def table_body(got_ref, out_ref):
    places, width = got_ref.shape[0], out_ref.shape[1]
    lane = lax.broadcasted_iota(jnp.int32, (16, LANES), 1)
    scale = jnp.where(lane == 0, 32.0, jnp.where(lane == 1, 1.0, 0.0)).astype(BF16)
    numbers = dot(scale, got_ref[:, width:], NT)[0:1].astype(jnp.int32)
    step = 256
    for first in range(0, out_ref.shape[0], step):
        sub = lax.broadcasted_iota(jnp.int32, (step, places), 0) + first
        hit = jnp.where(sub == jnp.broadcast_to(numbers, (step, places)), 1.0, 0.0)
        out_ref[first : first + step, :] = dot(hit.astype(BF16), got_ref[:, :width])


def widen_body(
    plan, me_ref, own_ref, came_ref, w_in_ref, w_out_ref, gain_in_ref, gain_out_ref, sums_ref
):
    me = me_ref[0]
    for place in range(plan.chunks):
        in_ref = (own_ref, came_ref)[place // (plan.chunks // 2)]
        sums_ref[plan.chunk_at(me, place)] = in_ref[place % (plan.chunks // 2)]
    split, end = w_in_ref.shape[1], w_in_ref.shape[1] + w_out_ref.shape[1]
    w_in_ref[...] = sums_ref[:, :split].astype(F32)
    w_out_ref[...] = sums_ref[:, split:end].astype(F32)
    gains = dot(unit(16), sums_ref[:, end : end + LANES], NT)
    gain_in_ref[...] = gains[0:1]
    gain_out_ref[...] = gains[1:2]


def add(left, right):
    return (left.astype(F32) + right.astype(F32)).astype(BF16)


def on_device(
    touched_rows,
    row_of_token,
    row_owner,
    owner_row,
    seq_blocks,
    seq_dest,
    grad_out,
    w_in,
    w_out,
    gain_in,
    gain_out,
):
    dp_size, table_size = lax.axis_size("dp"), lax.axis_size("table")
    both = ("dp", "table")
    count, width = touched_rows.shape
    tokens = row_of_token.shape[0]
    plan = Plan(dp_size, table_size, count, width)
    devices_all = plan.chunks
    total_factor = 1.0 / math.sqrt(grad_out.shape[0] * devices_all)
    gain_in, gain_out = gain_in[None, :], gain_out[None, :]
    me = lax.axis_index(both).astype(jnp.int32)[None]

    def swap(values, masks):
        pairs = [(here, here ^ masks[here & 1]) for here in range(devices_all)]
        return lax.ppermute(values, both, pairs)

    def exchange(values, axes):
        return lax.all_to_all(values, axes, split_axis=0, concat_axis=0, tiled=True)

    packed = jnp.broadcast_to(seq_dest * 8 + seq_blocks, (dp_size, 1, dp_size))
    send = call(
        functools.partial(send_body, table_size),
        shape_of((dp_size, SLOT, width), BF16),
        [SMEM] * 2 + [VMEM],
    )(me, exchange(packed, "dp"), grad_out)
    got = exchange(send, "dp")

    shapes = saved_shapes(tokens, count, width)
    shapes = [shapes[name] for name in SAVED]
    held = [pltpu.VMEM(item.shape, item.dtype) for item in shapes]
    saved = call(
        functools.partial(forward_body, plan.capacity),
        shapes,
        [VMEM] * 8,
        flops=4 * count * width * width * 8,
        moved=10_000_000,
        mebibytes=12 + tokens // 32,
        scratch=held + [pltpu.SemaphoreType.DMA((len(SAVED),))],
        out_space=HBM,
    )(
        touched_rows,
        row_of_token.reshape(tokens, 1),
        w_in,
        gain_in,
        gain_out,
        row_owner,
        row_owner.reshape(1, count),
        owner_row.reshape(count, 1),
    )

    half = shape_of((devices_all // 2, CHUNK_ROWS, plan.wide), BF16)
    table_send, kept, sent = call(
        functools.partial(backward_body, plan, total_factor),
        [shape_of((devices_all * plan.capacity, width + LANES), BF16), half, half],
        [SMEM] * 2 + [VMEM] * 4 + [HBM] * (len(SAVED) + 2),
        flops=4 * count * width * width * 20,
        moved=12_000_000,
        mebibytes=12 + tokens // 32,
        scratch=[pltpu.VMEM(w_out.shape, BF16)]
        + held
        + [
            pltpu.VMEM(w_in.shape, BF16),
            pltpu.VMEM((width, plan.columns), BF16),
            pltpu.VMEM((tokens, 4 * width), BF16),
            pltpu.VMEM((tokens, width), BF16),
            pltpu.SemaphoreType.DMA((len(SAVED) + 2,)),
        ],
    )(
        me,
        seq_dest,
        row_of_token.reshape(1, tokens),
        gain_in,
        gain_out,
        got,
        w_out,
        *saved,
        w_in,
    )

    kept = add(kept, swap(sent, (1, 1)))
    for masks in zip(*plan.orders):
        middle = kept.shape[0] // 2
        came = swap(kept[middle:], masks)
        kept = add(kept[:middle], came)
    table_got = exchange(table_send.reshape(devices_all, plan.capacity, width + LANES), both)
    kept, table_got = lax.optimization_barrier((kept, table_got))
    for masks in reversed(list(zip(*plan.orders))):
        kept = jnp.concatenate([kept, swap(kept, masks)])
    table_part = call(
        table_body,
        shape_of((ROWS_DEV, width), F32),
        [VMEM],
    )(table_got.reshape(devices_all * plan.capacity, width + LANES))
    came = swap(kept, (1, 1))

    grad_w_in, grad_w_out, grad_gain_in, grad_gain_out = call(
        functools.partial(widen_body, plan),
        (
            shape_of(w_in.shape, F32),
            shape_of(w_out.shape, F32),
            shape_of((1, width), F32),
            shape_of((1, width), F32),
        ),
        [SMEM] + [VMEM] * 2,
        scratch=[pltpu.VMEM((width, plan.columns), BF16)],
    )(me, kept, came)
    return (table_part, grad_w_in, grad_w_out, grad_gain_in[0], grad_gain_out[0])


def solution(mesh):
    rows = P(("dp", "table"), None)
    flat = P(("dp", "table"))
    in_specs = (rows, flat, rows, flat, flat, flat, rows, P(), P(), P(), P())
    out_specs = (rows, P(), P(), P(), P())
    return jax.shard_map(
        on_device, mesh=mesh, in_specs=in_specs, out_specs=out_specs, check_vma=False
    )
```

```python
import functools
import math

import jax
import jax.numpy as jnp
from jax import lax
from jax.experimental import pallas as pl
from jax.experimental.pallas import tpu as pltpu
from jax.sharding import PartitionSpec as P

HEADS = 4
HDIM = 128
BLK = 16
LMAXB = 4
SLOT = LMAXB * BLK
ROWS_DEV = 1024
TILE = 2 * SLOT
LANES = 128
CHUNK_ROWS = 16
EPSILON = 1e-05
F32 = jnp.float32
BF16 = jnp.bfloat16
VMEM = pl.BlockSpec(memory_space=pltpu.VMEM)
SMEM = pl.BlockSpec(memory_space=pltpu.SMEM)
HBM = pl.BlockSpec(memory_space=pltpu.HBM)


def call(body, out_shape, in_specs, flops=0, moved=0, scratch=(), out_space=VMEM, mebibytes=24):
    outs = jax.tree.map(lambda _: out_space, out_shape)
    return pl.pallas_call(
        body,
        out_shape=out_shape,
        in_specs=in_specs,
        out_specs=outs,
        scratch_shapes=scratch,
        compiler_params=pltpu.CompilerParams(vmem_limit_bytes=mebibytes * 1024 * 1024),
        cost_estimate=pl.CostEstimate(flops=flops, bytes_accessed=moved, transcendentals=0),
    )


def shape_of(dims, dtype):
    return jax.ShapeDtypeStruct(dims, dtype)


def sigmoid(values):
    return 0.5 * jnp.tanh(0.5 * values) + 0.5


def dot(left, right, contract=((1,), (0,))):
    return lax.dot_general(left, right, (contract, ((), ())), preferred_element_type=F32)


NT = ((1,), (1,))
TN = ((0,), (0,))


def send_body(table_size, me_ref, packed_ref, grad_ref, out_ref):
    peers = out_ref.shape[0]
    blocks = grad_ref.shape[0] // BLK
    me = me_ref[0] // table_size
    begin = jnp.int32(0)
    for peer in range(peers):

        def find(slot, length, peer=peer):
            entry = packed_ref[peer, 0, slot]
            return length + jnp.where(entry >> 3 == me, entry & 7, 0)

        length = lax.fori_loop(0, peers, find, jnp.int32(0), unroll=True)
        for inner in range(LMAXB):
            block = jnp.minimum(begin + inner, blocks - 1)
            rows = grad_ref[pl.ds(pl.multiple_of(block * BLK, BLK), BLK), :]
            live = jnp.full(rows.shape, inner, jnp.int32) < length
            out_ref[peer, inner * BLK : (inner + 1) * BLK, :] = jnp.where(
                live, rows.astype(F32), 0.0
            ).astype(BF16)
        begin = begin + length


def tile_mask():
    sub = lax.broadcasted_iota(jnp.int32, (TILE, TILE), 0)
    lane = lax.broadcasted_iota(jnp.int32, (TILE, TILE), 1)
    return (sub // SLOT == lane // SLOT) & (lane <= sub)


SAVED = (
    "gate",
    "hat",
    "hat_scale",
    "qkv",
    "slope",
    "weight",
    "mixed",
    "normed",
    "rows_slope",
    "rows_hat",
    "rows_scale",
    "place",
    "digits",
)


def saved_shapes(tokens, count, width):
    pairs = tokens // TILE * HEADS
    return dict(
        gate=shape_of((tokens, width), F32),
        hat=shape_of((tokens, width), F32),
        hat_scale=shape_of((tokens, 1), F32),
        qkv=shape_of((tokens, 3 * width), BF16),
        slope=shape_of((pairs, TILE, TILE), F32),
        weight=shape_of((pairs, TILE, TILE), BF16),
        mixed=shape_of((tokens, width), BF16),
        normed=shape_of((count, width), BF16),
        rows_slope=shape_of((count, 4 * width), F32),
        rows_hat=shape_of((count, width), F32),
        rows_scale=shape_of((count, 1), F32),
        place=shape_of((1, count), jnp.int32),
        digits=shape_of((count, LANES), BF16),
    )


def forward_body(
    capacity,
    rows_ref,
    item_ref,
    w_in_ref,
    gain_in_ref,
    gain_out_ref,
    owner_col_ref,
    owner_row_ref,
    number_ref,
    *refs,
):
    size = len(SAVED)
    held = dict(zip(SAVED, refs[size : 2 * size]))
    sems = refs[-1]
    copies = {
        name: pltpu.make_async_copy(held[name], refs[index], sems.at[index])
        for index, name in enumerate(SAVED)
    }
    gate_ref, hat_ref, hat_scale_ref, qkv_ref, slope_ref, weight_ref, mixed_ref = (
        held[name] for name in SAVED[:7]
    )
    normed_ref, rows_slope_ref, rows_hat_ref, rows_scale_ref, place_ref, digits_ref = (
        held[name] for name in SAVED[7:]
    )
    count, width = rows_ref.shape
    tokens = item_ref.shape[0]
    across = jnp.broadcast_to(owner_row_ref[...], (count, count))
    down = jnp.broadcast_to(owner_col_ref[...], (count, count))
    sub = lax.broadcasted_iota(jnp.int32, (count, count), 0)
    lane = lax.broadcasted_iota(jnp.int32, (count, count), 1)
    earlier = jnp.where((across == down) & (sub < lane), 1.0, 0.0)
    rank = jnp.sum(earlier, axis=0, keepdims=True).astype(jnp.int32)
    place_ref[...] = owner_row_ref[...] * capacity + rank
    number = jnp.broadcast_to(number_ref[...], (count, LANES))
    lane = lax.broadcasted_iota(jnp.int32, (count, LANES), 1)
    digits = jnp.where(lane == 0, number >> 5, jnp.where(lane == 1, number & 31, 0))
    digits_ref[...] = digits.astype(F32).astype(BF16)
    copies["place"].start()
    copies["digits"].start()
    values = rows_ref[...].astype(F32)
    shifted = values - jnp.mean(values, axis=-1, keepdims=True)
    scale = lax.rsqrt(jnp.mean(shifted * shifted, axis=-1, keepdims=True) + EPSILON)
    hat = shifted * scale
    rows_hat_ref[...] = hat
    rows_scale_ref[...] = scale
    normed = (hat * gain_in_ref[...]).astype(BF16)
    normed_ref[...] = normed
    for name in ("rows_hat", "rows_scale", "normed"):
        copies[name].start()
    lane = lax.broadcasted_iota(jnp.int32, (tokens, count), 1)
    pick = jnp.where(lane == jnp.broadcast_to(item_ref[...], (tokens, count)), 1.0, 0.0)
    pick = pick.astype(BF16)
    for part in range(4):
        columns = slice(part * width, (part + 1) * width)
        hidden = dot(normed, w_in_ref[:, columns])
        sigma = sigmoid(hidden)
        active = hidden * sigma
        rows_slope_ref[:, columns] = sigma * (1.0 + hidden * (1.0 - sigma))
        if part == 0:
            high = active.astype(BF16)
            low = (active - high.astype(F32)).astype(BF16)
            gate_ref[...] = dot(pick, high) + dot(pick, low)
        else:
            qkv_ref[:, (part - 1) * width : part * width] = dot(pick, active.astype(BF16)).astype(
                BF16
            )
    for name in ("gate", "qkv", "rows_slope"):
        copies[name].start()
    mask = tile_mask()
    factor = HDIM ** (-0.5)
    for tile in range(tokens // TILE):
        rows = slice(tile * TILE, (tile + 1) * TILE)
        parts = []
        for head in range(HEADS):
            vals, queries, keys = (
                qkv_ref[rows, part * width + head * HDIM : part * width + (head + 1) * HDIM]
                for part in range(3)
            )
            score = dot(queries, keys, NT) * factor
            sigma = sigmoid(score)
            weight = jnp.where(mask, score * sigma, 0.0).astype(BF16)
            slope = sigma * (1.0 + score * (1.0 - sigma)) * factor
            slope_ref[tile * HEADS + head] = jnp.where(mask, slope, 0.0)
            weight_ref[tile * HEADS + head] = weight
            parts.append(dot(weight, vals))
        attended = jnp.concatenate(parts, axis=1)
        shifted = attended - jnp.mean(attended, axis=-1, keepdims=True)
        scale = lax.rsqrt(jnp.mean(shifted * shifted, axis=-1, keepdims=True) + EPSILON)
        hat = shifted * scale
        hat_ref[rows, :] = hat
        hat_scale_ref[rows, :] = scale
        mixed_ref[rows, :] = (hat * gain_out_ref[...] * gate_ref[rows, :]).astype(BF16)
    for name in ("hat", "hat_scale", "slope", "weight", "mixed"):
        copies[name].start()
    for copy in copies.values():
        copy.wait()


def backward_body(
    plan, total_factor, me_ref, dest_ref, item_ref, gain_in_ref, gain_out_ref, got_ref, *refs
):
    size = len(SAVED) + 2
    far_refs, (table_ref, keep_ref, give_ref), near_refs = (
        refs[:size],
        refs[size : size + 3],
        refs[size + 3 : 2 * size + 3],
    )
    sums_ref, active_ref, grad_y_ref, sems = refs[2 * size + 3 :]
    copies = [
        pltpu.make_async_copy(far, near, sems.at[index])
        for index, (far, near) in enumerate(zip(far_refs, near_refs))
    ]
    for copy in copies:
        copy.start()
    w_out_ref, gate_ref, hat_ref, hat_scale_ref, qkv_ref, slope_ref, weight_ref = near_refs[:7]
    mixed_ref, normed_ref, rows_slope_ref, rows_hat_ref, rows_scale_ref = near_refs[7:12]
    place_ref, digits_ref, w_in_ref = near_refs[12:]
    count, width = rows_hat_ref.shape
    tokens = hat_ref.shape[0]
    me = me_ref[0]
    for slot in range(got_ref.shape[0]):
        grad_y_ref[slot * SLOT : (slot + 1) * SLOT, :] = got_ref[dest_ref[slot]]
    for copy in copies[:7]:
        copy.wait()
    gain_total = jnp.zeros((1, width), F32)
    for tile in range(tokens // TILE):
        rows = slice(tile * TILE, (tile + 1) * TILE)
        grad_mixed = dot(grad_y_ref[rows, :], w_out_ref[...], NT)
        hat = hat_ref[rows, :]
        active_ref[rows, :width] = (grad_mixed * hat * gain_out_ref[...]).astype(BF16)
        inner = grad_mixed * gate_ref[rows, :]
        gain_total = gain_total + jnp.sum(inner * hat, axis=0, keepdims=True)
        inner = inner * gain_out_ref[...]
        mean = jnp.mean(inner, axis=-1, keepdims=True)
        along = jnp.mean(inner * hat, axis=-1, keepdims=True)
        grad_att = ((inner - mean - hat * along) * hat_scale_ref[rows, :]).astype(BF16)
        for head in range(HEADS):
            columns = slice(head * HDIM, (head + 1) * HDIM)
            vals, queries, keys = (
                qkv_ref[rows, part * width + head * HDIM : part * width + (head + 1) * HDIM]
                for part in range(3)
            )
            grad_o = grad_att[:, columns]
            grad_weight = dot(grad_o, vals, NT)
            grad_score = (grad_weight * slope_ref[tile * HEADS + head]).astype(BF16)
            for part, value in (
                (1, dot(weight_ref[tile * HEADS + head], grad_o, TN)),
                (2, dot(grad_score, keys)),
                (3, dot(grad_score, queries, TN)),
            ):
                first = part * width + head * HDIM
                active_ref[rows, first : first + HDIM] = value.astype(BF16)
    for copy in copies[7:]:
        copy.wait()
    grad_y = grad_y_ref[...]
    sums_ref[:, 4 * width : 5 * width] = (dot(mixed_ref[...], grad_y, TN) * total_factor).astype(
        BF16
    )
    sub = lax.broadcasted_iota(jnp.int32, (count, tokens), 0)
    gather = jnp.where(sub == jnp.broadcast_to(item_ref[...], (count, tokens)), 1.0, 0.0)
    gather = gather.astype(BF16)
    grad_normed = jnp.zeros((count, width), F32)
    for part in range(4):
        columns = slice(part * width, (part + 1) * width)
        summed = dot(gather, active_ref[:, columns])
        grad_hidden = (summed * rows_slope_ref[:, columns]).astype(BF16)
        sums_ref[:, columns] = (dot(normed_ref[...], grad_hidden, TN) * total_factor).astype(BF16)
        grad_normed = grad_normed + dot(grad_hidden, w_in_ref[:, columns], NT)
    hat = rows_hat_ref[...]
    gain_rows = jnp.concatenate(
        [jnp.sum(grad_normed * hat, axis=0, keepdims=True), gain_total]
        + [jnp.zeros((14, width), F32)],
        axis=0,
    )
    gains = (gain_rows * total_factor).astype(BF16)
    sums_ref[:, 5 * width : 5 * width + LANES] = dot(gains, unit(16), TN).astype(BF16)
    if sums_ref.shape[1] > 5 * width + LANES:
        rest = sums_ref.shape[1] - 5 * width - LANES
        sums_ref[:, 5 * width + LANES :] = jnp.zeros((width, rest), BF16)
    inner = grad_normed * gain_in_ref[...]
    mean = jnp.mean(inner, axis=-1, keepdims=True)
    along = jnp.mean(inner * hat, axis=-1, keepdims=True)
    row_grad = (inner - mean - hat * along) * rows_scale_ref[...] + dot(gather, grad_y)
    places = table_ref.shape[0]
    place = place_ref[...]
    spots = lax.broadcasted_iota(jnp.int32, (places, count), 0)
    spread = jnp.where(spots == jnp.broadcast_to(place, (places, count)), 1.0, 0.0).astype(BF16)
    table_ref[:, :width] = dot(spread, row_grad.astype(BF16)).astype(BF16)
    table_ref[:, width:] = dot(spread, digits_ref[...]).astype(BF16)
    for place_now in range(plan.chunks):
        out_ref = (keep_ref, give_ref)[place_now // (plan.chunks // 2)]
        out_ref[place_now % (plan.chunks // 2)] = sums_ref[plan.chunk_at(me, place_now)]


def unit(rows):
    sub = lax.broadcasted_iota(jnp.int32, (rows, LANES), 0)
    lane = lax.broadcasted_iota(jnp.int32, (rows, LANES), 1)
    return jnp.where(sub == lane, 1.0, 0.0).astype(BF16)


class Plan:
    def __init__(self, dp_size, table_size, count, width):
        self.chunks = dp_size * table_size
        self.capacity = 2 * count // self.chunks
        self.row_groups = min(self.chunks, width // CHUNK_ROWS)
        self.column_groups = self.chunks // self.row_groups
        block = self.column_groups * LANES
        blocks = -(-(5 * width + LANES) // block)
        self.columns = blocks * block
        self.wide = blocks * LANES
        table_bits = [1 << bit for bit in range(1, table_size.bit_length() - 1)]
        dp_bits = [table_size << bit for bit in range(dp_size.bit_length() - 1)]
        self.orders = (table_bits + dp_bits, dp_bits[:2] + table_bits + dp_bits[2:])
        self.steps = len(self.orders[0])

    def low_mask(self, core, place):
        mask = 0
        for step, bit in enumerate(self.orders[core]):
            if place >> (self.steps - 1 - step) & 1:
                mask ^= bit
        return mask

    def chunk_at(self, me, place):
        top, low = divmod(place, self.chunks // 2)
        masks = [top ^ self.low_mask(core ^ top, low) for core in range(2)]
        chunk = me ^ jnp.where((me & 1) == 0, masks[0], masks[1])
        first = pl.multiple_of((chunk & (self.row_groups - 1)) * CHUNK_ROWS, CHUNK_ROWS)
        if self.column_groups == 1:
            return pl.ds(first, CHUNK_ROWS), slice(0, self.wide)
        group = chunk >> (self.row_groups.bit_length() - 1)
        return pl.ds(first, CHUNK_ROWS), pl.ds(pl.multiple_of(group * self.wide, LANES), self.wide)


def table_body(got_ref, out_ref):
    places, width = got_ref.shape[0], out_ref.shape[1]
    lane = lax.broadcasted_iota(jnp.int32, (16, LANES), 1)
    scale = jnp.where(lane == 0, 32.0, jnp.where(lane == 1, 1.0, 0.0)).astype(BF16)
    numbers = dot(scale, got_ref[:, width:], NT)[0:1].astype(jnp.int32)
    step = 256
    for first in range(0, out_ref.shape[0], step):
        sub = lax.broadcasted_iota(jnp.int32, (step, places), 0) + first
        hit = jnp.where(sub == jnp.broadcast_to(numbers, (step, places)), 1.0, 0.0)
        out_ref[first : first + step, :] = dot(hit.astype(BF16), got_ref[:, :width])


def widen_body(
    plan, me_ref, own_ref, came_ref, w_in_ref, w_out_ref, gain_in_ref, gain_out_ref, sums_ref
):
    me = me_ref[0]
    for place in range(plan.chunks):
        in_ref = (own_ref, came_ref)[place // (plan.chunks // 2)]
        sums_ref[plan.chunk_at(me, place)] = in_ref[place % (plan.chunks // 2)]
    split, end = w_in_ref.shape[1], w_in_ref.shape[1] + w_out_ref.shape[1]
    w_in_ref[...] = sums_ref[:, :split].astype(F32)
    w_out_ref[...] = sums_ref[:, split:end].astype(F32)
    gains = dot(unit(16), sums_ref[:, end : end + LANES], NT)
    gain_in_ref[...] = gains[0:1]
    gain_out_ref[...] = gains[1:2]


def add(left, right):
    return (left.astype(F32) + right.astype(F32)).astype(BF16)


def on_device(
    touched_rows,
    row_of_token,
    row_owner,
    owner_row,
    seq_blocks,
    seq_dest,
    grad_out,
    w_in,
    w_out,
    gain_in,
    gain_out,
):
    dp_size, table_size = lax.axis_size("dp"), lax.axis_size("table")
    both = ("dp", "table")
    count, width = touched_rows.shape
    tokens = row_of_token.shape[0]
    plan = Plan(dp_size, table_size, count, width)
    devices_all = plan.chunks
    total_factor = 1.0 / math.sqrt(grad_out.shape[0] * devices_all)
    gain_in, gain_out = gain_in[None, :], gain_out[None, :]
    me = lax.axis_index(both).astype(jnp.int32)[None]

    def swap(values, masks):
        pairs = [(here, here ^ masks[here & 1]) for here in range(devices_all)]
        return lax.ppermute(values, both, pairs)

    def exchange(values, axes):
        return lax.all_to_all(values, axes, split_axis=0, concat_axis=0, tiled=True)

    packed = jnp.broadcast_to(seq_dest * 8 + seq_blocks, (dp_size, 1, dp_size))
    send = call(
        functools.partial(send_body, table_size),
        shape_of((dp_size, SLOT, width), BF16),
        [SMEM] * 2 + [VMEM],
    )(me, exchange(packed, "dp"), grad_out)
    got = exchange(send, "dp")

    shapes = saved_shapes(tokens, count, width)
    shapes = [shapes[name] for name in SAVED]
    held = [pltpu.VMEM(item.shape, item.dtype) for item in shapes]
    saved = call(
        functools.partial(forward_body, plan.capacity),
        shapes,
        [VMEM] * 8,
        flops=4 * count * width * width * 8,
        moved=10_000_000,
        mebibytes=58,
        scratch=held + [pltpu.SemaphoreType.DMA((len(SAVED),))],
        out_space=HBM,
    )(
        touched_rows,
        row_of_token.reshape(tokens, 1),
        w_in,
        gain_in,
        gain_out,
        row_owner,
        row_owner.reshape(1, count),
        owner_row.reshape(count, 1),
    )

    half = shape_of((devices_all // 2, CHUNK_ROWS, plan.wide), BF16)
    table_send, kept, sent = call(
        functools.partial(backward_body, plan, total_factor),
        [shape_of((devices_all * plan.capacity, width + LANES), BF16), half, half],
        [SMEM] * 2 + [VMEM] * 4 + [HBM] * (len(SAVED) + 2),
        flops=4 * count * width * width * 20,
        moved=12_000_000,
        mebibytes=58,
        scratch=[pltpu.VMEM(w_out.shape, BF16)]
        + held
        + [
            pltpu.VMEM(w_in.shape, BF16),
            pltpu.VMEM((width, plan.columns), BF16),
            pltpu.VMEM((tokens, 4 * width), BF16),
            pltpu.VMEM((tokens, width), BF16),
            pltpu.SemaphoreType.DMA((len(SAVED) + 2,)),
        ],
    )(
        me,
        seq_dest,
        row_of_token.reshape(1, tokens),
        gain_in,
        gain_out,
        got,
        w_out,
        *saved,
        w_in,
    )

    kept = add(kept, swap(sent, (1, 1)))
    table_got = exchange(table_send.reshape(devices_all, plan.capacity, width + LANES), both)
    for step, masks in enumerate(zip(*plan.orders)):
        if step == 2:
            kept, table_got = lax.optimization_barrier((kept, table_got))
        middle = kept.shape[0] // 2
        came = swap(kept[middle:], masks)
        kept = add(kept[:middle], came)
    for masks in reversed(list(zip(*plan.orders))):
        kept = jnp.concatenate([kept, swap(kept, masks)])
    table_part = call(
        table_body,
        shape_of((ROWS_DEV, width), F32),
        [VMEM],
    )(table_got.reshape(devices_all * plan.capacity, width + LANES))
    came = swap(kept, (1, 1))

    grad_w_in, grad_w_out, grad_gain_in, grad_gain_out = call(
        functools.partial(widen_body, plan),
        (
            shape_of(w_in.shape, F32),
            shape_of(w_out.shape, F32),
            shape_of((1, width), F32),
            shape_of((1, width), F32),
        ),
        [SMEM] + [VMEM] * 2,
        scratch=[pltpu.VMEM((width, plan.columns), BF16)],
    )(me, kept, came)
    return (table_part, grad_w_in, grad_w_out, grad_gain_in[0], grad_gain_out[0])


def solution(mesh):
    rows = P(("dp", "table"), None)
    flat = P(("dp", "table"))
    in_specs = (rows, flat, rows, flat, flat, flat, rows, P(), P(), P(), P())
    out_specs = (rows, P(), P(), P(), P())
    return jax.shard_map(
        on_device, mesh=mesh, in_specs=in_specs, out_specs=out_specs, check_vma=False
    )
```

```python
import functools
import math

import jax
import jax.numpy as jnp
from jax import lax
from jax.experimental import pallas as pl
from jax.experimental.pallas import tpu as pltpu
from jax.sharding import PartitionSpec as P

HEADS = 4
HDIM = 128
BLK = 16
LMAXB = 4
SLOT = LMAXB * BLK
ROWS_DEV = 1024
TILE = 2 * SLOT
LANES = 128
CHUNK_ROWS = 16
EPSILON = 1e-05
F32 = jnp.float32
BF16 = jnp.bfloat16
VMEM = pl.BlockSpec(memory_space=pltpu.VMEM)
SMEM = pl.BlockSpec(memory_space=pltpu.SMEM)
HBM = pl.BlockSpec(memory_space=pltpu.HBM)


def call(body, out_shape, in_specs, flops=0, moved=0, scratch=(), out_space=VMEM, mebibytes=24):
    outs = jax.tree.map(lambda _: out_space, out_shape)
    return pl.pallas_call(
        body,
        out_shape=out_shape,
        in_specs=in_specs,
        out_specs=outs,
        scratch_shapes=scratch,
        compiler_params=pltpu.CompilerParams(vmem_limit_bytes=mebibytes * 1024 * 1024),
        cost_estimate=pl.CostEstimate(flops=flops, bytes_accessed=moved, transcendentals=0),
    )


def shape_of(dims, dtype):
    return jax.ShapeDtypeStruct(dims, dtype)


def sigmoid(values):
    return 0.5 * jnp.tanh(0.5 * values) + 0.5


def dot(left, right, contract=((1,), (0,))):
    return lax.dot_general(left, right, (contract, ((), ())), preferred_element_type=F32)


NT = ((1,), (1,))
TN = ((0,), (0,))


def send_body(table_size, me_ref, packed_ref, grad_ref, out_ref):
    peers = out_ref.shape[0]
    blocks = grad_ref.shape[0] // BLK
    me = me_ref[0] // table_size
    begin = jnp.int32(0)
    for peer in range(peers):

        def find(slot, length, peer=peer):
            entry = packed_ref[peer, 0, slot]
            return length + jnp.where(entry >> 3 == me, entry & 7, 0)

        length = lax.fori_loop(0, peers, find, jnp.int32(0), unroll=True)
        for inner in range(LMAXB):
            block = jnp.minimum(begin + inner, blocks - 1)
            rows = grad_ref[pl.ds(pl.multiple_of(block * BLK, BLK), BLK), :]
            live = jnp.full(rows.shape, inner, jnp.int32) < length
            out_ref[peer, inner * BLK : (inner + 1) * BLK, :] = jnp.where(
                live, rows.astype(F32), 0.0
            ).astype(BF16)
        begin = begin + length


def tile_mask():
    sub = lax.broadcasted_iota(jnp.int32, (TILE, TILE), 0)
    lane = lax.broadcasted_iota(jnp.int32, (TILE, TILE), 1)
    return (sub // SLOT == lane // SLOT) & (lane <= sub)


SAVED = (
    "gate",
    "hat",
    "hat_scale",
    "qkv",
    "slope",
    "weight",
    "mixed",
    "normed",
    "rows_slope",
    "rows_hat",
    "rows_scale",
    "place",
    "digits",
)


def saved_shapes(tokens, count, width):
    pairs = tokens // TILE * HEADS
    return dict(
        gate=shape_of((tokens, width), F32),
        hat=shape_of((tokens, width), F32),
        hat_scale=shape_of((tokens, 1), F32),
        qkv=shape_of((tokens, 3 * width), BF16),
        slope=shape_of((pairs, TILE, TILE), BF16),
        weight=shape_of((pairs, TILE, TILE), BF16),
        mixed=shape_of((tokens, width), BF16),
        normed=shape_of((count, width), BF16),
        rows_slope=shape_of((count, 4 * width), BF16),
        rows_hat=shape_of((count, width), F32),
        rows_scale=shape_of((count, 1), F32),
        place=shape_of((1, count), jnp.int32),
        digits=shape_of((count, LANES), BF16),
    )


def forward_body(
    capacity,
    rows_ref,
    item_ref,
    w_in_ref,
    gain_in_ref,
    gain_out_ref,
    owner_col_ref,
    owner_row_ref,
    number_ref,
    *refs,
):
    size = len(SAVED)
    held = dict(zip(SAVED, refs[size : 2 * size]))
    sems = refs[-1]
    copies = {
        name: pltpu.make_async_copy(held[name], refs[index], sems.at[index])
        for index, name in enumerate(SAVED)
    }
    gate_ref, hat_ref, hat_scale_ref, qkv_ref, slope_ref, weight_ref, mixed_ref = (
        held[name] for name in SAVED[:7]
    )
    normed_ref, rows_slope_ref, rows_hat_ref, rows_scale_ref, place_ref, digits_ref = (
        held[name] for name in SAVED[7:]
    )
    count, width = rows_ref.shape
    tokens = item_ref.shape[0]
    across = jnp.broadcast_to(owner_row_ref[...], (count, count))
    down = jnp.broadcast_to(owner_col_ref[...], (count, count))
    sub = lax.broadcasted_iota(jnp.int32, (count, count), 0)
    lane = lax.broadcasted_iota(jnp.int32, (count, count), 1)
    earlier = jnp.where((across == down) & (sub < lane), 1.0, 0.0)
    rank = jnp.sum(earlier, axis=0, keepdims=True).astype(jnp.int32)
    place_ref[...] = owner_row_ref[...] * capacity + rank
    number = jnp.broadcast_to(number_ref[...], (count, LANES))
    lane = lax.broadcasted_iota(jnp.int32, (count, LANES), 1)
    digits = jnp.where(lane == 0, number >> 5, jnp.where(lane == 1, number & 31, 0))
    digits_ref[...] = digits.astype(F32).astype(BF16)
    copies["place"].start()
    copies["digits"].start()
    values = rows_ref[...].astype(F32)
    shifted = values - jnp.mean(values, axis=-1, keepdims=True)
    scale = lax.rsqrt(jnp.mean(shifted * shifted, axis=-1, keepdims=True) + EPSILON)
    hat = shifted * scale
    rows_hat_ref[...] = hat
    rows_scale_ref[...] = scale
    normed = (hat * gain_in_ref[...]).astype(BF16)
    normed_ref[...] = normed
    for name in ("rows_hat", "rows_scale", "normed"):
        copies[name].start()
    lane = lax.broadcasted_iota(jnp.int32, (tokens, count), 1)
    pick = jnp.where(lane == jnp.broadcast_to(item_ref[...], (tokens, count)), 1.0, 0.0)
    pick = pick.astype(BF16)
    for part in range(4):
        columns = slice(part * width, (part + 1) * width)
        hidden = dot(normed, w_in_ref[:, columns])
        sigma = sigmoid(hidden)
        active = hidden * sigma
        slope = sigma * (1.0 + hidden * (1.0 - sigma))
        rows_slope_ref[:, columns] = slope.astype(BF16)
        if part == 0:
            high = active.astype(BF16)
            low = (active - high.astype(F32)).astype(BF16)
            gate_ref[...] = dot(pick, high) + dot(pick, low)
        else:
            qkv_ref[:, (part - 1) * width : part * width] = dot(pick, active.astype(BF16)).astype(
                BF16
            )
    for name in ("gate", "qkv", "rows_slope"):
        copies[name].start()
    mask = tile_mask()
    factor = HDIM ** (-0.5)
    for tile in range(tokens // TILE):
        rows = slice(tile * TILE, (tile + 1) * TILE)
        parts = []
        for head in range(HEADS):
            vals, queries, keys = (
                qkv_ref[rows, part * width + head * HDIM : part * width + (head + 1) * HDIM]
                for part in range(3)
            )
            score = dot(queries, keys, NT) * factor
            sigma = sigmoid(score)
            weight = jnp.where(mask, score * sigma, 0.0).astype(BF16)
            slope = sigma * (1.0 + score * (1.0 - sigma)) * factor
            slope_ref[tile * HEADS + head] = jnp.where(mask, slope, 0.0).astype(BF16)
            weight_ref[tile * HEADS + head] = weight
            parts.append(dot(weight, vals))
        attended = jnp.concatenate(parts, axis=1)
        shifted = attended - jnp.mean(attended, axis=-1, keepdims=True)
        scale = lax.rsqrt(jnp.mean(shifted * shifted, axis=-1, keepdims=True) + EPSILON)
        hat = shifted * scale
        hat_ref[rows, :] = hat
        hat_scale_ref[rows, :] = scale
        mixed_ref[rows, :] = (hat * gain_out_ref[...] * gate_ref[rows, :]).astype(BF16)
    for name in ("hat", "hat_scale", "slope", "weight", "mixed"):
        copies[name].start()
    for copy in copies.values():
        copy.wait()


def backward_body(
    plan, total_factor, me_ref, dest_ref, item_ref, gain_in_ref, gain_out_ref, got_ref, *refs
):
    size = len(SAVED) + 2
    far_refs, (table_ref, keep_ref, give_ref), near_refs = (
        refs[:size],
        refs[size : size + 3],
        refs[size + 3 : 2 * size + 3],
    )
    sums_ref, active_ref, grad_y_ref, sems = refs[2 * size + 3 :]
    copies = [
        pltpu.make_async_copy(far, near, sems.at[index])
        for index, (far, near) in enumerate(zip(far_refs, near_refs))
    ]
    for copy in copies:
        copy.start()
    w_out_ref, gate_ref, hat_ref, hat_scale_ref, qkv_ref, slope_ref, weight_ref = near_refs[:7]
    mixed_ref, normed_ref, rows_slope_ref, rows_hat_ref, rows_scale_ref = near_refs[7:12]
    place_ref, digits_ref, w_in_ref = near_refs[12:]
    count, width = rows_hat_ref.shape
    tokens = hat_ref.shape[0]
    me = me_ref[0]
    for slot in range(got_ref.shape[0]):
        grad_y_ref[slot * SLOT : (slot + 1) * SLOT, :] = got_ref[dest_ref[slot]]
    for copy in copies[:4]:
        copy.wait()
    gain_total = jnp.zeros((1, width), F32)
    for tile in range(tokens // TILE):
        rows = slice(tile * TILE, (tile + 1) * TILE)
        grad_mixed = dot(grad_y_ref[rows, :], w_out_ref[...], NT)
        hat = hat_ref[rows, :]
        active_ref[rows, :width] = (grad_mixed * hat * gain_out_ref[...]).astype(BF16)
        inner = grad_mixed * gate_ref[rows, :]
        gain_total = gain_total + jnp.sum(inner * hat, axis=0, keepdims=True)
        inner = inner * gain_out_ref[...]
        mean = jnp.mean(inner, axis=-1, keepdims=True)
        along = jnp.mean(inner * hat, axis=-1, keepdims=True)
        grad_att = ((inner - mean - hat * along) * hat_scale_ref[rows, :]).astype(BF16)
        if tile == 0:
            for copy in copies[4:7]:
                copy.wait()
        for head in range(HEADS):
            columns = slice(head * HDIM, (head + 1) * HDIM)
            vals, queries, keys = (
                qkv_ref[rows, part * width + head * HDIM : part * width + (head + 1) * HDIM]
                for part in range(3)
            )
            grad_o = grad_att[:, columns]
            grad_weight = dot(grad_o, vals, NT)
            grad_score = (grad_weight * slope_ref[tile * HEADS + head].astype(F32)).astype(
                BF16
            )
            for part, value in (
                (1, dot(weight_ref[tile * HEADS + head], grad_o, TN)),
                (2, dot(grad_score, keys)),
                (3, dot(grad_score, queries, TN)),
            ):
                first = part * width + head * HDIM
                active_ref[rows, first : first + HDIM] = value.astype(BF16)
    for copy in copies[7:]:
        copy.wait()
    grad_y = grad_y_ref[...]
    sums_ref[:, 4 * width : 5 * width] = (dot(mixed_ref[...], grad_y, TN) * total_factor).astype(
        BF16
    )
    sub = lax.broadcasted_iota(jnp.int32, (count, tokens), 0)
    gather = jnp.where(sub == jnp.broadcast_to(item_ref[...], (count, tokens)), 1.0, 0.0)
    gather = gather.astype(BF16)
    grad_normed = jnp.zeros((count, width), F32)
    for part in range(4):
        columns = slice(part * width, (part + 1) * width)
        summed = dot(gather, active_ref[:, columns])
        grad_hidden = (summed * rows_slope_ref[:, columns].astype(F32)).astype(BF16)
        sums_ref[:, columns] = (dot(normed_ref[...], grad_hidden, TN) * total_factor).astype(BF16)
        grad_normed = grad_normed + dot(grad_hidden, w_in_ref[:, columns], NT)
    hat = rows_hat_ref[...]
    gain_rows = jnp.concatenate(
        [jnp.sum(grad_normed * hat, axis=0, keepdims=True), gain_total]
        + [jnp.zeros((14, width), F32)],
        axis=0,
    )
    gains = (gain_rows * total_factor).astype(BF16)
    sums_ref[:, 5 * width : 5 * width + LANES] = dot(gains, unit(16), TN).astype(BF16)
    if sums_ref.shape[1] > 5 * width + LANES:
        rest = sums_ref.shape[1] - 5 * width - LANES
        sums_ref[:, 5 * width + LANES :] = jnp.zeros((width, rest), BF16)
    inner = grad_normed * gain_in_ref[...]
    mean = jnp.mean(inner, axis=-1, keepdims=True)
    along = jnp.mean(inner * hat, axis=-1, keepdims=True)
    row_grad = (inner - mean - hat * along) * rows_scale_ref[...] + dot(gather, grad_y)
    places = table_ref.shape[0]
    place = place_ref[...]
    spots = lax.broadcasted_iota(jnp.int32, (places, count), 0)
    spread = jnp.where(spots == jnp.broadcast_to(place, (places, count)), 1.0, 0.0).astype(BF16)
    table_ref[:, :width] = dot(spread, row_grad.astype(BF16)).astype(BF16)
    table_ref[:, width:] = dot(spread, digits_ref[...]).astype(BF16)
    for place_now in range(plan.chunks):
        out_ref = (keep_ref, give_ref)[place_now // (plan.chunks // 2)]
        out_ref[place_now % (plan.chunks // 2)] = sums_ref[plan.chunk_at(me, place_now)]


def unit(rows):
    sub = lax.broadcasted_iota(jnp.int32, (rows, LANES), 0)
    lane = lax.broadcasted_iota(jnp.int32, (rows, LANES), 1)
    return jnp.where(sub == lane, 1.0, 0.0).astype(BF16)


class Plan:
    def __init__(self, dp_size, table_size, count, width):
        self.chunks = dp_size * table_size
        self.capacity = 2 * count // self.chunks
        self.row_groups = min(self.chunks, width // CHUNK_ROWS)
        self.column_groups = self.chunks // self.row_groups
        block = self.column_groups * LANES
        blocks = -(-(5 * width + LANES) // block)
        self.columns = blocks * block
        self.wide = blocks * LANES
        table_bits = [1 << bit for bit in range(1, table_size.bit_length() - 1)]
        dp_bits = [table_size << bit for bit in range(dp_size.bit_length() - 1)]
        self.orders = (table_bits + dp_bits, dp_bits[:1] + table_bits + dp_bits[1:])
        self.steps = len(self.orders[0])

    def low_mask(self, core, place):
        mask = 0
        for step, bit in enumerate(self.orders[core]):
            if place >> (self.steps - 1 - step) & 1:
                mask ^= bit
        return mask

    def chunk_at(self, me, place):
        top, low = divmod(place, self.chunks // 2)
        masks = [top ^ self.low_mask(core ^ top, low) for core in range(2)]
        chunk = me ^ jnp.where((me & 1) == 0, masks[0], masks[1])
        first = pl.multiple_of((chunk & (self.row_groups - 1)) * CHUNK_ROWS, CHUNK_ROWS)
        if self.column_groups == 1:
            return pl.ds(first, CHUNK_ROWS), slice(0, self.wide)
        group = chunk >> (self.row_groups.bit_length() - 1)
        return pl.ds(first, CHUNK_ROWS), pl.ds(pl.multiple_of(group * self.wide, LANES), self.wide)


def table_body(got_ref, out_ref):
    places, width = got_ref.shape[0], out_ref.shape[1]
    lane = lax.broadcasted_iota(jnp.int32, (16, LANES), 1)
    scale = jnp.where(lane == 0, 32.0, jnp.where(lane == 1, 1.0, 0.0)).astype(BF16)
    numbers = dot(scale, got_ref[:, width:], NT)[0:1].astype(jnp.int32)
    step = 256
    for first in range(0, out_ref.shape[0], step):
        sub = lax.broadcasted_iota(jnp.int32, (step, places), 0) + first
        hit = jnp.where(sub == jnp.broadcast_to(numbers, (step, places)), 1.0, 0.0)
        out_ref[first : first + step, :] = dot(hit.astype(BF16), got_ref[:, :width])


def widen_body(
    plan, me_ref, own_ref, came_ref, w_in_ref, w_out_ref, gain_in_ref, gain_out_ref, sums_ref
):
    me = me_ref[0]
    for place in range(plan.chunks):
        in_ref = (own_ref, came_ref)[place // (plan.chunks // 2)]
        sums_ref[plan.chunk_at(me, place)] = in_ref[place % (plan.chunks // 2)]
    split, end = w_in_ref.shape[1], w_in_ref.shape[1] + w_out_ref.shape[1]
    w_in_ref[...] = sums_ref[:, :split].astype(F32)
    w_out_ref[...] = sums_ref[:, split:end].astype(F32)
    gains = dot(unit(16), sums_ref[:, end : end + LANES], NT)
    gain_in_ref[...] = gains[0:1]
    gain_out_ref[...] = gains[1:2]


def add(left, right):
    return (left.astype(F32) + right.astype(F32)).astype(BF16)


def on_device(
    touched_rows,
    row_of_token,
    row_owner,
    owner_row,
    seq_blocks,
    seq_dest,
    grad_out,
    w_in,
    w_out,
    gain_in,
    gain_out,
):
    dp_size, table_size = lax.axis_size("dp"), lax.axis_size("table")
    both = ("dp", "table")
    count, width = touched_rows.shape
    tokens = row_of_token.shape[0]
    plan = Plan(dp_size, table_size, count, width)
    devices_all = plan.chunks
    total_factor = 1.0 / math.sqrt(grad_out.shape[0] * devices_all)
    gain_in, gain_out = gain_in[None, :], gain_out[None, :]
    me = lax.axis_index(both).astype(jnp.int32)[None]

    def swap(values, masks):
        pairs = [(here, here ^ masks[here & 1]) for here in range(devices_all)]
        return lax.ppermute(values, both, pairs)

    def exchange(values, axes):
        return lax.all_to_all(values, axes, split_axis=0, concat_axis=0, tiled=True)

    packed = jnp.broadcast_to(seq_dest * 8 + seq_blocks, (dp_size, 1, dp_size))
    send = call(
        functools.partial(send_body, table_size),
        shape_of((dp_size, SLOT, width), BF16),
        [SMEM] * 2 + [VMEM],
    )(me, exchange(packed, "dp"), grad_out)
    got = exchange(send, "dp")

    shapes = saved_shapes(tokens, count, width)
    shapes = [shapes[name] for name in SAVED]
    held = [pltpu.VMEM(item.shape, item.dtype) for item in shapes]
    saved = call(
        functools.partial(forward_body, plan.capacity),
        shapes,
        [VMEM] * 8,
        flops=4 * count * width * width * 8,
        moved=10_000_000,
        mebibytes=58,
        scratch=held + [pltpu.SemaphoreType.DMA((len(SAVED),))],
        out_space=HBM,
    )(
        touched_rows,
        row_of_token.reshape(tokens, 1),
        w_in,
        gain_in,
        gain_out,
        row_owner,
        row_owner.reshape(1, count),
        owner_row.reshape(count, 1),
    )

    half = shape_of((devices_all // 2, CHUNK_ROWS, plan.wide), BF16)
    table_send, kept, sent = call(
        functools.partial(backward_body, plan, total_factor),
        [shape_of((devices_all * plan.capacity, width + LANES), BF16), half, half],
        [SMEM] * 2 + [VMEM] * 4 + [HBM] * (len(SAVED) + 2),
        flops=4 * count * width * width * 20,
        moved=12_000_000,
        mebibytes=58,
        scratch=[pltpu.VMEM(w_out.shape, BF16)]
        + held
        + [
            pltpu.VMEM(w_in.shape, BF16),
            pltpu.VMEM((width, plan.columns), BF16),
            pltpu.VMEM((tokens, 4 * width), BF16),
            pltpu.VMEM((tokens, width), BF16),
            pltpu.SemaphoreType.DMA((len(SAVED) + 2,)),
        ],
    )(
        me,
        seq_dest,
        row_of_token.reshape(1, tokens),
        gain_in,
        gain_out,
        got,
        w_out,
        *saved,
        w_in,
    )

    kept = add(kept, swap(sent, (1, 1)))
    table_got = exchange(table_send.reshape(devices_all, plan.capacity, width + LANES), both)
    for step, masks in enumerate(zip(*plan.orders)):
        if step == 2:
            kept, table_got = lax.optimization_barrier((kept, table_got))
        middle = kept.shape[0] // 2
        came = swap(kept[middle:], masks)
        kept = add(kept[:middle], came)
    table_part = call(
        table_body,
        shape_of((ROWS_DEV, width), F32),
        [VMEM],
    )(table_got.reshape(devices_all * plan.capacity, width + LANES))
    for step, masks in reversed(list(enumerate(zip(*plan.orders)))):
        if step == 0:
            kept, table_part = lax.optimization_barrier((kept, table_part))
        kept = jnp.concatenate([kept, swap(kept, masks)])
    came = swap(kept, (1, 1))

    grad_w_in, grad_w_out, grad_gain_in, grad_gain_out = call(
        functools.partial(widen_body, plan),
        (
            shape_of(w_in.shape, F32),
            shape_of(w_out.shape, F32),
            shape_of((1, width), F32),
            shape_of((1, width), F32),
        ),
        [SMEM] + [VMEM] * 2,
        scratch=[pltpu.VMEM((width, plan.columns), BF16)],
    )(me, kept, came)
    return (table_part, grad_w_in, grad_w_out, grad_gain_in[0], grad_gain_out[0])


def solution(mesh):
    rows = P(("dp", "table"), None)
    flat = P(("dp", "table"))
    in_specs = (rows, flat, rows, flat, flat, flat, rows, P(), P(), P(), P())
    out_specs = (rows, P(), P(), P(), P())
    return jax.shard_map(
        on_device, mesh=mesh, in_specs=in_specs, out_specs=out_specs, check_vma=False
    )
```

```python
import functools
import math

import jax
import jax.numpy as jnp
from jax import lax
from jax.experimental import pallas as pl
from jax.experimental.pallas import tpu as pltpu
from jax.sharding import PartitionSpec as P

HEADS = 4
HDIM = 128
BLK = 16
LMAXB = 4
SLOT = LMAXB * BLK
ROWS_DEV = 1024
TILE = 2 * SLOT
LANES = 128
CHUNK_ROWS = 16
EPSILON = 1e-05
F32 = jnp.float32
BF16 = jnp.bfloat16
VMEM = pl.BlockSpec(memory_space=pltpu.VMEM)
SMEM = pl.BlockSpec(memory_space=pltpu.SMEM)
HBM = pl.BlockSpec(memory_space=pltpu.HBM)


def call(body, out_shape, in_specs, flops=0, moved=0, scratch=(), out_space=VMEM, mebibytes=24):
    outs = jax.tree.map(lambda _: out_space, out_shape)
    return pl.pallas_call(
        body,
        out_shape=out_shape,
        in_specs=in_specs,
        out_specs=outs,
        scratch_shapes=scratch,
        compiler_params=pltpu.CompilerParams(vmem_limit_bytes=mebibytes * 1024 * 1024),
        cost_estimate=pl.CostEstimate(flops=flops, bytes_accessed=moved, transcendentals=0),
    )


def shape_of(dims, dtype):
    return jax.ShapeDtypeStruct(dims, dtype)


def sigmoid(values):
    return 0.5 * jnp.tanh(0.5 * values) + 0.5


def dot(left, right, contract=((1,), (0,))):
    return lax.dot_general(left, right, (contract, ((), ())), preferred_element_type=F32)


NT = ((1,), (1,))
TN = ((0,), (0,))


def send_body(table_size, me_ref, packed_ref, grad_ref, out_ref):
    peers = out_ref.shape[0]
    blocks = grad_ref.shape[0] // BLK
    me = me_ref[0] // table_size
    begin = jnp.int32(0)
    for peer in range(peers):

        def find(slot, length, peer=peer):
            entry = packed_ref[peer, 0, slot]
            return length + jnp.where(entry >> 3 == me, entry & 7, 0)

        length = lax.fori_loop(0, peers, find, jnp.int32(0), unroll=True)
        for inner in range(LMAXB):
            block = jnp.minimum(begin + inner, blocks - 1)
            rows = grad_ref[pl.ds(pl.multiple_of(block * BLK, BLK), BLK), :]
            live = jnp.full(rows.shape, inner, jnp.int32) < length
            out_ref[peer, inner * BLK : (inner + 1) * BLK, :] = jnp.where(
                live, rows.astype(F32), 0.0
            ).astype(BF16)
        begin = begin + length


def tile_mask():
    sub = lax.broadcasted_iota(jnp.int32, (TILE, TILE), 0)
    lane = lax.broadcasted_iota(jnp.int32, (TILE, TILE), 1)
    return (sub // SLOT == lane // SLOT) & (lane <= sub)


SAVED = (
    "gate",
    "hat",
    "hat_scale",
    "qkv",
    "slope",
    "weight",
    "mixed",
    "normed",
    "rows_slope",
    "rows_hat",
    "rows_scale",
    "place",
    "digits",
)


def saved_shapes(tokens, count, width):
    pairs = tokens // TILE * HEADS
    return dict(
        gate=shape_of((tokens, width), F32),
        hat=shape_of((tokens, width), F32),
        hat_scale=shape_of((tokens, 1), F32),
        qkv=shape_of((tokens, 3 * width), BF16),
        slope=shape_of((pairs, TILE, TILE), BF16),
        weight=shape_of((pairs, TILE, TILE), BF16),
        mixed=shape_of((tokens, width), BF16),
        normed=shape_of((count, width), BF16),
        rows_slope=shape_of((count, 4 * width), BF16),
        rows_hat=shape_of((count, width), F32),
        rows_scale=shape_of((count, 1), F32),
        place=shape_of((1, count), jnp.int32),
        digits=shape_of((count, LANES), BF16),
    )


def forward_body(
    capacity,
    rows_ref,
    item_ref,
    w_in_ref,
    gain_in_ref,
    gain_out_ref,
    owner_col_ref,
    owner_row_ref,
    number_ref,
    *refs,
):
    size = len(SAVED)
    held = dict(zip(SAVED, refs[size : 2 * size]))
    sems = refs[-1]
    copies = {
        name: pltpu.make_async_copy(held[name], refs[index], sems.at[index])
        for index, name in enumerate(SAVED)
    }
    gate_ref, hat_ref, hat_scale_ref, qkv_ref, slope_ref, weight_ref, mixed_ref = (
        held[name] for name in SAVED[:7]
    )
    normed_ref, rows_slope_ref, rows_hat_ref, rows_scale_ref, place_ref, digits_ref = (
        held[name] for name in SAVED[7:]
    )
    count, width = rows_ref.shape
    tokens = item_ref.shape[0]
    across = jnp.broadcast_to(owner_row_ref[...], (count, count))
    down = jnp.broadcast_to(owner_col_ref[...], (count, count))
    sub = lax.broadcasted_iota(jnp.int32, (count, count), 0)
    lane = lax.broadcasted_iota(jnp.int32, (count, count), 1)
    earlier = jnp.where((across == down) & (sub < lane), 1.0, 0.0)
    rank = jnp.sum(earlier, axis=0, keepdims=True).astype(jnp.int32)
    place_ref[...] = owner_row_ref[...] * capacity + rank
    number = jnp.broadcast_to(number_ref[...], (count, LANES))
    lane = lax.broadcasted_iota(jnp.int32, (count, LANES), 1)
    digits = jnp.where(lane == 0, number >> 5, jnp.where(lane == 1, number & 31, 0))
    digits_ref[...] = digits.astype(F32).astype(BF16)
    copies["place"].start()
    copies["digits"].start()
    values = rows_ref[...].astype(F32)
    shifted = values - jnp.mean(values, axis=-1, keepdims=True)
    scale = lax.rsqrt(jnp.mean(shifted * shifted, axis=-1, keepdims=True) + EPSILON)
    hat = shifted * scale
    rows_hat_ref[...] = hat
    rows_scale_ref[...] = scale
    normed = (hat * gain_in_ref[...]).astype(BF16)
    normed_ref[...] = normed
    for name in ("rows_hat", "rows_scale", "normed"):
        copies[name].start()
    lane = lax.broadcasted_iota(jnp.int32, (tokens, count), 1)
    pick = jnp.where(lane == jnp.broadcast_to(item_ref[...], (tokens, count)), 1.0, 0.0)
    pick = pick.astype(BF16)
    for part in range(4):
        columns = slice(part * width, (part + 1) * width)
        hidden = dot(normed, w_in_ref[:, columns])
        sigma = sigmoid(hidden)
        active = hidden * sigma
        slope = sigma * (1.0 + hidden * (1.0 - sigma))
        rows_slope_ref[:, columns] = slope.astype(BF16)
        if part == 0:
            high = active.astype(BF16)
            low = (active - high.astype(F32)).astype(BF16)
            gate_ref[...] = dot(pick, high) + dot(pick, low)
        else:
            qkv_ref[:, (part - 1) * width : part * width] = dot(pick, active.astype(BF16)).astype(
                BF16
            )
    for name in ("gate", "qkv", "rows_slope"):
        copies[name].start()
    mask = tile_mask()
    factor = HDIM ** (-0.5)
    for tile in range(tokens // TILE):
        rows = slice(tile * TILE, (tile + 1) * TILE)
        parts = []
        for head in range(HEADS):
            vals, queries, keys = (
                qkv_ref[rows, part * width + head * HDIM : part * width + (head + 1) * HDIM]
                for part in range(3)
            )
            score = dot(queries, keys, NT) * factor
            sigma = sigmoid(score)
            weight = jnp.where(mask, score * sigma, 0.0).astype(BF16)
            slope = sigma * (1.0 + score * (1.0 - sigma)) * factor
            slope_ref[tile * HEADS + head] = jnp.where(mask, slope, 0.0).astype(BF16)
            weight_ref[tile * HEADS + head] = weight
            parts.append(dot(weight, vals))
        attended = jnp.concatenate(parts, axis=1)
        shifted = attended - jnp.mean(attended, axis=-1, keepdims=True)
        scale = lax.rsqrt(jnp.mean(shifted * shifted, axis=-1, keepdims=True) + EPSILON)
        hat = shifted * scale
        hat_ref[rows, :] = hat
        hat_scale_ref[rows, :] = scale
        mixed_ref[rows, :] = (hat * gain_out_ref[...] * gate_ref[rows, :]).astype(BF16)
    for name in ("hat", "hat_scale", "slope", "weight", "mixed"):
        copies[name].start()
    for copy in copies.values():
        copy.wait()


def fetch(names, far_refs, near_refs, sems):
    copies = {}
    for index, name in enumerate(names):
        copies[name] = pltpu.make_async_copy(far_refs[index], near_refs[index], sems.at[index])
        copies[name].start()

    def get(name):
        copies[name].wait()
        return near_refs[names.index(name)]

    return get


def gather_of(item_ref, count):
    tokens = item_ref.shape[1]
    sub = lax.broadcasted_iota(jnp.int32, (count, tokens), 0)
    hit = sub == jnp.broadcast_to(item_ref[...], (count, tokens))
    return jnp.where(hit, 1.0, 0.0).astype(BF16)


FIRST = ("w_out", "gate", "hat", "hat_scale", "mixed", "normed", "rows_slope")
SECOND = (
    "grad_att",
    "qkv",
    "slope",
    "weight",
    "normed",
    "rows_slope",
    "grad_hidden",
    "w_in",
    "rows_hat",
    "rows_scale",
    "grad_y",
    "place",
    "digits",
)


def first_body(plan, factor, me_ref, dest_ref, item_ref, gain_out_ref, got_ref, *refs):
    size = len(FIRST)
    far_refs, refs = refs[:size], refs[size:]
    keep_ref, give_ref, grad_att_ref, grad_hidden_ref, grad_y_ref, gain_ref = refs[:6]
    near_refs, (sums_ref, active_ref, sems) = refs[6 : 6 + size], refs[6 + size :]
    get = fetch(FIRST, far_refs, near_refs, sems)
    tokens, width = grad_att_ref.shape
    count = grad_hidden_ref.shape[0]
    for slot in range(got_ref.shape[0]):
        grad_y_ref[slot * SLOT : (slot + 1) * SLOT, :] = got_ref[dest_ref[slot]]
    w_out_ref, gate_ref, hat_ref, hat_scale_ref = (get(name) for name in FIRST[:4])
    gain_total = jnp.zeros((1, width), F32)
    for tile in range(tokens // TILE):
        rows = slice(tile * TILE, (tile + 1) * TILE)
        grad_mixed = dot(grad_y_ref[rows, :], w_out_ref[...], NT)
        hat = hat_ref[rows, :]
        active_ref[rows, :] = (grad_mixed * hat * gain_out_ref[...]).astype(BF16)
        inner = grad_mixed * gate_ref[rows, :]
        gain_total = gain_total + jnp.sum(inner * hat, axis=0, keepdims=True)
        inner = inner * gain_out_ref[...]
        mean = jnp.mean(inner, axis=-1, keepdims=True)
        along = jnp.mean(inner * hat, axis=-1, keepdims=True)
        grad_att_ref[rows, :] = ((inner - mean - hat * along) * hat_scale_ref[rows, :]).astype(BF16)
    gain_ref[...] = gain_total
    mixed_ref, normed_ref, slope_ref = (get(name) for name in FIRST[4:])
    sums_ref[:, :width] = (dot(mixed_ref[...], grad_y_ref[...], TN) * factor).astype(BF16)
    summed = dot(gather_of(item_ref, count), active_ref[...])
    grad_hidden = (summed * slope_ref[...].astype(F32)).astype(BF16)
    grad_hidden_ref[...] = grad_hidden
    sums_ref[:, width:] = (dot(normed_ref[...], grad_hidden, TN) * factor).astype(BF16)
    plan.write(me_ref[0], plan.first, sums_ref, keep_ref, give_ref)


def second_body(plan, factor, me_ref, item_ref, gain_in_ref, gain_ref, *refs):
    size = len(SECOND)
    far_refs, refs = refs[:size], refs[size:]
    (table_ref, keep_ref, give_ref), near_refs = refs[:3], refs[3 : 3 + size]
    sums_ref, active_ref, sems = refs[3 + size :]
    get = fetch(SECOND, far_refs, near_refs, sems)
    grad_att_ref, qkv_ref, slope_ref, weight_ref = (get(name) for name in SECOND[:4])
    tokens, width = grad_att_ref.shape
    for tile in range(tokens // TILE):
        rows = slice(tile * TILE, (tile + 1) * TILE)
        for head in range(HEADS):
            vals, queries, keys = (
                qkv_ref[rows, part * width + head * HDIM : part * width + (head + 1) * HDIM]
                for part in range(3)
            )
            grad_o = grad_att_ref[rows, head * HDIM : (head + 1) * HDIM]
            grad_weight = dot(grad_o, vals, NT)
            grad_score = (grad_weight * slope_ref[tile * HEADS + head].astype(F32)).astype(BF16)
            for part, value in (
                (0, dot(weight_ref[tile * HEADS + head], grad_o, TN)),
                (1, dot(grad_score, keys)),
                (2, dot(grad_score, queries, TN)),
            ):
                first = part * width + head * HDIM
                active_ref[rows, first : first + HDIM] = value.astype(BF16)
    normed_ref, rows_slope_ref, grad_hidden_ref, w_in_ref = (get(name) for name in SECOND[4:8])
    count = normed_ref.shape[0]
    gather = gather_of(item_ref, count)
    grad_normed = dot(grad_hidden_ref[...], w_in_ref[:, :width], NT)
    for part in range(3):
        columns = slice(part * width, (part + 1) * width)
        inside = slice((part + 1) * width, (part + 2) * width)
        summed = dot(gather, active_ref[:, columns])
        grad_hidden = (summed * rows_slope_ref[:, inside].astype(F32)).astype(BF16)
        sums_ref[:, columns] = (dot(normed_ref[...], grad_hidden, TN) * factor).astype(BF16)
        grad_normed = grad_normed + dot(grad_hidden, w_in_ref[:, inside], NT)
    rows_hat_ref, rows_scale_ref, grad_y_ref, place_ref, digits_ref = (
        get(name) for name in SECOND[8:]
    )
    hat = rows_hat_ref[...]
    gain_rows = jnp.concatenate(
        [jnp.sum(grad_normed * hat, axis=0, keepdims=True), gain_ref[...]]
        + [jnp.zeros((14, width), F32)],
        axis=0,
    )
    gains = (gain_rows * factor).astype(BF16)
    end = 3 * width + LANES
    sums_ref[:, 3 * width : end] = dot(gains, unit(16), TN).astype(BF16)
    if sums_ref.shape[1] > end:
        sums_ref[:, end:] = jnp.zeros((width, sums_ref.shape[1] - end), BF16)
    inner = grad_normed * gain_in_ref[...]
    mean = jnp.mean(inner, axis=-1, keepdims=True)
    along = jnp.mean(inner * hat, axis=-1, keepdims=True)
    row_grad = (inner - mean - hat * along) * rows_scale_ref[...] + dot(gather, grad_y_ref[...])
    places = table_ref.shape[0]
    spots = lax.broadcasted_iota(jnp.int32, (places, count), 0)
    hit = spots == jnp.broadcast_to(place_ref[...], (places, count))
    spread = jnp.where(hit, 1.0, 0.0).astype(BF16)
    table_ref[:, :width] = dot(spread, row_grad.astype(BF16)).astype(BF16)
    table_ref[:, width:] = dot(spread, digits_ref[...]).astype(BF16)
    plan.write(me_ref[0], plan.second, sums_ref, keep_ref, give_ref)


def unit(rows):
    sub = lax.broadcasted_iota(jnp.int32, (rows, LANES), 0)
    lane = lax.broadcasted_iota(jnp.int32, (rows, LANES), 1)
    return jnp.where(sub == lane, 1.0, 0.0).astype(BF16)


class Plan:
    def __init__(self, dp_size, table_size, count, width):
        self.chunks = dp_size * table_size
        self.capacity = 2 * count // self.chunks
        self.row_groups = min(self.chunks, width // CHUNK_ROWS)
        self.column_groups = self.chunks // self.row_groups
        block = self.column_groups * LANES
        self.left = 2 * width // self.column_groups
        self.right = -(-(3 * width + LANES) // block) * LANES
        self.split = -(-(self.left + self.right) // (2 * LANES)) * LANES
        table_bits = [1 << bit for bit in range(1, table_size.bit_length() - 1)]
        dp_bits = [table_size << bit for bit in range(dp_size.bit_length() - 1)]
        far, near = table_bits + dp_bits[:1], dp_bits[:1] + table_bits
        self.near_steps = len(far)
        last = (dp_bits[1:], dp_bits[:0:-1])
        self.first = (far + last[0], far + last[1])
        self.second = (far + last[0], near + last[1])
        self.third = (near + last[0], near + last[1])

    def chunk(self, me, orders, place):
        top, low = divmod(place, self.chunks // 2)
        steps = len(orders[0])
        masks = []
        for core in range(2):
            mask = top
            for step, bit in enumerate(orders[core ^ top]):
                if low >> (steps - 1 - step) & 1:
                    mask ^= bit
            masks.append(mask)
        return me ^ jnp.where((me & 1) == 0, masks[0], masks[1])

    def rows(self, chunk):
        first = (chunk & (self.row_groups - 1)) * CHUNK_ROWS
        return pl.ds(pl.multiple_of(first, CHUNK_ROWS), CHUNK_ROWS)

    def columns(self, chunk, begin, group_width, first, size):
        if self.column_groups == 1:
            return slice(begin + first, begin + first + size)
        group = chunk >> (self.row_groups.bit_length() - 1)
        return pl.ds(pl.multiple_of(group * group_width + begin + first, LANES), size)

    def write(self, me, orders, sums_ref, keep_ref, give_ref):
        half, _, wide = keep_ref.shape
        for place in range(self.chunks):
            chunk = self.chunk(me, orders, place)
            columns = self.columns(chunk, 0, wide, 0, wide)
            (keep_ref, give_ref)[place // half][place % half] = sums_ref[self.rows(chunk), columns]

    def read(self, me, left_refs, right_refs, sums_ref):
        half = self.chunks // 2
        whole = self.left * self.column_groups
        over = self.split - self.left
        for place in range(self.chunks):
            chunk = self.chunk(me, self.first, place)
            rows = self.rows(chunk)
            piece = left_refs[place // half].at[place % half]
            sums_ref[rows, self.columns(chunk, 0, self.left, 0, self.left)] = piece[:, : self.left]
            sums_ref[rows, self.columns(chunk, whole, self.right, 0, over)] = piece[:, self.left :]
            chunk = self.chunk(me, self.third, place)
            columns = self.columns(chunk, whole, self.right, over, self.right - over)
            sums_ref[self.rows(chunk), columns] = right_refs[place // half][place % half]


def table_body(got_ref, out_ref):
    places, width = got_ref.shape[0], out_ref.shape[1]
    lane = lax.broadcasted_iota(jnp.int32, (16, LANES), 1)
    scale = jnp.where(lane == 0, 32.0, jnp.where(lane == 1, 1.0, 0.0)).astype(BF16)
    numbers = dot(scale, got_ref[:, width:], NT)[0:1].astype(jnp.int32)
    step = 256
    for first in range(0, out_ref.shape[0], step):
        sub = lax.broadcasted_iota(jnp.int32, (step, places), 0) + first
        hit = jnp.where(sub == jnp.broadcast_to(numbers, (step, places)), 1.0, 0.0)
        out_ref[first : first + step, :] = dot(hit.astype(BF16), got_ref[:, :width])


def widen_body(plan, me_ref, *refs):
    left_refs, right_refs, (w_in_ref, w_out_ref, gain_in_ref, gain_out_ref, sums_ref) = (
        refs[:2],
        refs[2:4],
        refs[4:],
    )
    plan.read(me_ref[0], left_refs, right_refs, sums_ref)
    width = w_out_ref.shape[0]
    w_out_ref[...] = sums_ref[:, :width].astype(F32)
    w_in_ref[...] = sums_ref[:, width : 5 * width].astype(F32)
    gains = dot(unit(16), sums_ref[:, 5 * width : 5 * width + LANES], NT)
    gain_in_ref[...] = gains[0:1]
    gain_out_ref[...] = gains[1:2]


def add(left, right):
    return (left.astype(F32) + right.astype(F32)).astype(BF16)


def on_device(
    touched_rows,
    row_of_token,
    row_owner,
    owner_row,
    seq_blocks,
    seq_dest,
    grad_out,
    w_in,
    w_out,
    gain_in,
    gain_out,
):
    dp_size, table_size = lax.axis_size("dp"), lax.axis_size("table")
    both = ("dp", "table")
    count, width = touched_rows.shape
    tokens = row_of_token.shape[0]
    plan = Plan(dp_size, table_size, count, width)
    devices_all = plan.chunks
    total_factor = 1.0 / math.sqrt(grad_out.shape[0] * devices_all)
    gain_in, gain_out = gain_in[None, :], gain_out[None, :]
    me = lax.axis_index(both).astype(jnp.int32)[None]

    def swap(values, masks):
        pairs = [(here, here ^ masks[here & 1]) for here in range(devices_all)]
        return lax.ppermute(values, both, pairs)

    def exchange(values, axes):
        return lax.all_to_all(values, axes, split_axis=0, concat_axis=0, tiled=True)

    packed = jnp.broadcast_to(seq_dest * 8 + seq_blocks, (dp_size, 1, dp_size))
    send = call(
        functools.partial(send_body, table_size),
        shape_of((dp_size, SLOT, width), BF16),
        [SMEM] * 2 + [VMEM],
    )(me, exchange(packed, "dp"), grad_out)
    got = exchange(send, "dp")

    shapes = saved_shapes(tokens, count, width)
    shapes = [shapes[name] for name in SAVED]
    held = [pltpu.VMEM(item.shape, item.dtype) for item in shapes]
    saved = call(
        functools.partial(forward_body, plan.capacity),
        shapes,
        [VMEM] * 8,
        flops=4 * count * width * width * 8,
        moved=10_000_000,
        mebibytes=58,
        scratch=held + [pltpu.SemaphoreType.DMA((len(SAVED),))],
        out_space=HBM,
    )(
        touched_rows,
        row_of_token.reshape(tokens, 1),
        w_in,
        gain_in,
        gain_out,
        row_owner,
        row_owner.reshape(1, count),
        owner_row.reshape(count, 1),
    )

    saved = dict(zip(SAVED, saved), w_in=w_in, w_out=w_out)
    items = row_of_token.reshape(1, tokens)

    def near(names, **arrays):
        arrays = saved | arrays
        return [pltpu.VMEM(arrays[name].shape, arrays[name].dtype) for name in names] + [
            pltpu.SemaphoreType.DMA((len(names),))
        ]

    def halves(wide):
        return [shape_of((devices_all // 2, CHUNK_ROWS, wide), BF16)] * 2

    first = dict(saved, rows_slope=saved["rows_slope"][:, :width])
    scratch = near(FIRST, **first)
    keep_left, give_left, grad_att, grad_hidden, grad_y, gain_total = call(
        functools.partial(first_body, plan, total_factor),
        halves(plan.left)
        + [
            shape_of((tokens, width), BF16),
            shape_of((count, width), BF16),
            shape_of((tokens, width), BF16),
            shape_of((1, width), F32),
        ],
        [SMEM] * 2 + [VMEM] * 3 + [HBM] * len(FIRST),
        flops=4 * count * width * width * 10,
        moved=6_000_000,
        mebibytes=58,
        scratch=scratch[:-1]
        + [pltpu.VMEM((width, 2 * width), BF16), pltpu.VMEM((tokens, width), BF16)]
        + scratch[-1:],
    )(me, seq_dest, items, gain_out, got, *(first[name] for name in FIRST))

    left = add(keep_left, swap(give_left, (1, 1)))
    left, grad_att = lax.optimization_barrier((left, grad_att))
    second = dict(saved, grad_att=grad_att, grad_hidden=grad_hidden, grad_y=grad_y)
    scratch = near(SECOND, **second)
    table_send, keep_right, give_right = call(
        functools.partial(second_body, plan, total_factor),
        [shape_of((devices_all * plan.capacity, width + LANES), BF16)] + halves(plan.right),
        [SMEM] + [VMEM] * 3 + [HBM] * len(SECOND),
        flops=4 * count * width * width * 30,
        moved=8_000_000,
        mebibytes=58,
        scratch=scratch[:-1]
        + [
            pltpu.VMEM((width, plan.column_groups * plan.right), BF16),
            pltpu.VMEM((tokens, 3 * width), BF16),
        ]
        + scratch[-1:],
    )(me, items, gain_in, gain_total, *(second[name] for name in SECOND))

    def reduced(kept, masks):
        middle = kept.shape[0] // 2
        return add(kept[:middle], swap(kept[middle:], masks))

    def gathered(kept, masks):
        return jnp.concatenate([kept, swap(kept, masks)])

    table_got = exchange(table_send.reshape(devices_all, plan.capacity, width + LANES), both)
    right = add(keep_right, swap(give_right, (1, 1)))
    rounds = [list(zip(*orders)) for orders in (plan.first, plan.second, plan.third)]
    for step in range(plan.near_steps):
        left = reduced(left, rounds[0][step])
        right = reduced(right, rounds[1][step])
    kept = jnp.concatenate([left, right], axis=2)
    kept, table_got = lax.optimization_barrier((kept, table_got))
    table_part = call(
        table_body,
        shape_of((ROWS_DEV, width), F32),
        [VMEM],
    )(table_got.reshape(devices_all * plan.capacity, width + LANES))
    for masks in rounds[0][plan.near_steps :]:
        kept = reduced(kept, masks)
    for masks in reversed(rounds[0][plan.near_steps :]):
        kept = gathered(kept, masks)
    left, right = kept[..., : plan.split], kept[..., plan.split :]
    for step in reversed(range(plan.near_steps)):
        if step == 0:
            left, right, table_part = lax.optimization_barrier((left, right, table_part))
        left = gathered(left, rounds[0][step])
        right = gathered(right, rounds[2][step])
    grad_w_in, grad_w_out, grad_gain_in, grad_gain_out = call(
        functools.partial(widen_body, plan),
        (
            shape_of(w_in.shape, F32),
            shape_of(w_out.shape, F32),
            shape_of((1, width), F32),
            shape_of((1, width), F32),
        ),
        [SMEM] + [VMEM] * 4,
        scratch=[pltpu.VMEM((width, plan.column_groups * (plan.left + plan.right)), BF16)],
    )(me, left, swap(left, (1, 1)), right, swap(right, (1, 1)))
    return (table_part, grad_w_in, grad_w_out, grad_gain_in[0], grad_gain_out[0])


def solution(mesh):
    rows = P(("dp", "table"), None)
    flat = P(("dp", "table"))
    in_specs = (rows, flat, rows, flat, flat, flat, rows, P(), P(), P(), P())
    out_specs = (rows, P(), P(), P(), P())
    return jax.shard_map(
        on_device, mesh=mesh, in_specs=in_specs, out_specs=out_specs, check_vma=False
    )
```

```python
import functools
import math

import jax
import jax.numpy as jnp
from jax import lax
from jax.experimental import pallas as pl
from jax.experimental.pallas import tpu as pltpu
from jax.sharding import PartitionSpec as P

HEADS = 4
HDIM = 128
BLK = 16
LMAXB = 4
SLOT = LMAXB * BLK
ROWS_DEV = 1024
TILE = 2 * SLOT
LANES = 128
CHUNK_ROWS = 16
EPSILON = 1e-05
F32 = jnp.float32
BF16 = jnp.bfloat16
VMEM = pl.BlockSpec(memory_space=pltpu.VMEM)
SMEM = pl.BlockSpec(memory_space=pltpu.SMEM)
HBM = pl.BlockSpec(memory_space=pltpu.HBM)


def call(body, out_shape, in_specs, flops=0, moved=0, scratch=(), out_space=VMEM, mebibytes=24):
    outs = jax.tree.map(lambda _: out_space, out_shape)
    return pl.pallas_call(
        body,
        out_shape=out_shape,
        in_specs=in_specs,
        out_specs=outs,
        scratch_shapes=scratch,
        compiler_params=pltpu.CompilerParams(vmem_limit_bytes=mebibytes * 1024 * 1024),
        cost_estimate=pl.CostEstimate(flops=flops, bytes_accessed=moved, transcendentals=0),
    )


def shape_of(dims, dtype):
    return jax.ShapeDtypeStruct(dims, dtype)


def sigmoid(values):
    return 0.5 * jnp.tanh(0.5 * values) + 0.5


def dot(left, right, contract=((1,), (0,))):
    return lax.dot_general(left, right, (contract, ((), ())), preferred_element_type=F32)


NT = ((1,), (1,))
TN = ((0,), (0,))


def send_body(table_size, me_ref, packed_ref, grad_ref, out_ref):
    peers = out_ref.shape[0]
    blocks = grad_ref.shape[0] // BLK
    me = me_ref[0] // table_size
    begin = jnp.int32(0)
    for peer in range(peers):

        def find(slot, length, peer=peer):
            entry = packed_ref[peer, 0, slot]
            return length + jnp.where(entry >> 3 == me, entry & 7, 0)

        length = lax.fori_loop(0, peers, find, jnp.int32(0), unroll=True)
        for inner in range(LMAXB):
            block = jnp.minimum(begin + inner, blocks - 1)
            rows = grad_ref[pl.ds(pl.multiple_of(block * BLK, BLK), BLK), :]
            live = jnp.full(rows.shape, inner, jnp.int32) < length
            out_ref[peer, inner * BLK : (inner + 1) * BLK, :] = jnp.where(
                live, rows.astype(F32), 0.0
            ).astype(BF16)
        begin = begin + length


def tile_mask():
    sub = lax.broadcasted_iota(jnp.int32, (TILE, TILE), 0)
    lane = lax.broadcasted_iota(jnp.int32, (TILE, TILE), 1)
    return (sub // SLOT == lane // SLOT) & (lane <= sub)


SAVED = (
    "gate",
    "hat",
    "hat_scale",
    "qkv",
    "slope",
    "weight",
    "mixed",
    "normed",
    "rows_slope",
    "rows_hat",
    "rows_scale",
    "place",
    "digits",
)


def saved_shapes(tokens, count, width):
    pairs = tokens // TILE * HEADS
    return dict(
        gate=shape_of((tokens, width), F32),
        hat=shape_of((tokens, width), F32),
        hat_scale=shape_of((tokens, 1), F32),
        qkv=shape_of((tokens, 3 * width), BF16),
        slope=shape_of((pairs, TILE, TILE), BF16),
        weight=shape_of((pairs, TILE, TILE), BF16),
        mixed=shape_of((tokens, width), BF16),
        normed=shape_of((count, width), BF16),
        rows_slope=shape_of((count, 4 * width), BF16),
        rows_hat=shape_of((count, width), F32),
        rows_scale=shape_of((count, 1), F32),
        place=shape_of((1, count), jnp.int32),
        digits=shape_of((count, LANES), BF16),
    )


def forward_body(
    capacity,
    rows_ref,
    item_ref,
    w_in_ref,
    gain_in_ref,
    gain_out_ref,
    owner_col_ref,
    owner_row_ref,
    number_ref,
    *refs,
):
    size = len(SAVED)
    held = dict(zip(SAVED, refs[size : 2 * size]))
    sems = refs[-1]
    copies = {
        name: pltpu.make_async_copy(held[name], refs[index], sems.at[index])
        for index, name in enumerate(SAVED)
    }
    gate_ref, hat_ref, hat_scale_ref, qkv_ref, slope_ref, weight_ref, mixed_ref = (
        held[name] for name in SAVED[:7]
    )
    normed_ref, rows_slope_ref, rows_hat_ref, rows_scale_ref, place_ref, digits_ref = (
        held[name] for name in SAVED[7:]
    )
    count, width = rows_ref.shape
    tokens = item_ref.shape[0]
    across = jnp.broadcast_to(owner_row_ref[...], (count, count))
    down = jnp.broadcast_to(owner_col_ref[...], (count, count))
    sub = lax.broadcasted_iota(jnp.int32, (count, count), 0)
    lane = lax.broadcasted_iota(jnp.int32, (count, count), 1)
    earlier = jnp.where((across == down) & (sub < lane), 1.0, 0.0)
    rank = jnp.sum(earlier, axis=0, keepdims=True).astype(jnp.int32)
    place_ref[...] = owner_row_ref[...] * capacity + rank
    number = jnp.broadcast_to(number_ref[...], (count, LANES))
    lane = lax.broadcasted_iota(jnp.int32, (count, LANES), 1)
    digits = jnp.where(lane == 0, number >> 5, jnp.where(lane == 1, number & 31, 0))
    digits_ref[...] = digits.astype(F32).astype(BF16)
    copies["place"].start()
    copies["digits"].start()
    values = rows_ref[...].astype(F32)
    shifted = values - jnp.mean(values, axis=-1, keepdims=True)
    scale = lax.rsqrt(jnp.mean(shifted * shifted, axis=-1, keepdims=True) + EPSILON)
    hat = shifted * scale
    rows_hat_ref[...] = hat
    rows_scale_ref[...] = scale
    normed = (hat * gain_in_ref[...]).astype(BF16)
    normed_ref[...] = normed
    for name in ("rows_hat", "rows_scale", "normed"):
        copies[name].start()
    lane = lax.broadcasted_iota(jnp.int32, (tokens, count), 1)
    pick = jnp.where(lane == jnp.broadcast_to(item_ref[...], (tokens, count)), 1.0, 0.0)
    pick = pick.astype(BF16)
    for part in range(4):
        columns = slice(part * width, (part + 1) * width)
        hidden = dot(normed, w_in_ref[:, columns])
        sigma = sigmoid(hidden)
        active = hidden * sigma
        slope = sigma * (1.0 + hidden * (1.0 - sigma))
        rows_slope_ref[:, columns] = slope.astype(BF16)
        if part == 0:
            high = active.astype(BF16)
            low = (active - high.astype(F32)).astype(BF16)
            gate_ref[...] = dot(pick, high) + dot(pick, low)
        else:
            qkv_ref[:, (part - 1) * width : part * width] = dot(pick, active.astype(BF16)).astype(
                BF16
            )
    for name in ("gate", "qkv", "rows_slope"):
        copies[name].start()
    mask = tile_mask()
    factor = HDIM ** (-0.5)
    for tile in range(tokens // TILE):
        rows = slice(tile * TILE, (tile + 1) * TILE)
        parts = []
        for head in range(HEADS):
            vals, queries, keys = (
                qkv_ref[rows, part * width + head * HDIM : part * width + (head + 1) * HDIM]
                for part in range(3)
            )
            score = dot(queries, keys, NT) * factor
            sigma = sigmoid(score)
            weight = jnp.where(mask, score * sigma, 0.0).astype(BF16)
            slope = sigma * (1.0 + score * (1.0 - sigma)) * factor
            slope_ref[tile * HEADS + head] = jnp.where(mask, slope, 0.0).astype(BF16)
            weight_ref[tile * HEADS + head] = weight
            parts.append(dot(weight, vals))
        attended = jnp.concatenate(parts, axis=1)
        shifted = attended - jnp.mean(attended, axis=-1, keepdims=True)
        scale = lax.rsqrt(jnp.mean(shifted * shifted, axis=-1, keepdims=True) + EPSILON)
        hat = shifted * scale
        hat_ref[rows, :] = hat
        hat_scale_ref[rows, :] = scale
        mixed_ref[rows, :] = (hat * gain_out_ref[...] * gate_ref[rows, :]).astype(BF16)
    for name in ("hat", "hat_scale", "slope", "weight", "mixed"):
        copies[name].start()
    for copy in copies.values():
        copy.wait()


def fetch(names, far_refs, near_refs, sems):
    copies = {}
    for index, name in enumerate(names):
        copies[name] = pltpu.make_async_copy(far_refs[index], near_refs[index], sems.at[index])
        copies[name].start()

    def get(name):
        copies[name].wait()
        return near_refs[names.index(name)]

    return get


def gather_of(item_ref, count):
    tokens = item_ref.shape[1]
    sub = lax.broadcasted_iota(jnp.int32, (count, tokens), 0)
    hit = sub == jnp.broadcast_to(item_ref[...], (count, tokens))
    return jnp.where(hit, 1.0, 0.0).astype(BF16)


FETCHED = (
    "got",
    "w_out",
    "hat",
    "gate",
    "hat_scale",
    "qkv",
    "slope",
    "weight",
    "mixed",
    "normed",
    "rows_slope",
    "w_in",
    "rows_hat",
    "rows_scale",
    "place",
    "digits",
)


def backward_body(plan, factor, me_ref, dest_ref, item_ref, gain_in_ref, gain_out_ref, *refs):
    size = len(FETCHED)
    far_refs, out_refs, refs = refs[:size], refs[size : size + 5], refs[size + 5 :]
    near_refs, stage_refs, refs = refs[:size], refs[size : size + 5], refs[size + 5 :]
    sums_ref, active_ref, grad_y_ref, in_sems, out_sems = refs
    get = fetch(FETCHED, far_refs, near_refs, in_sems)
    sends = [
        pltpu.make_async_copy(stage, out, out_sems.at[index])
        for index, (stage, out) in enumerate(zip(stage_refs, out_refs))
    ]
    got_ref = get("got")
    for slot in range(got_ref.shape[0]):
        grad_y_ref[slot * SLOT : (slot + 1) * SLOT, :] = got_ref[dest_ref[slot]]
    w_out_ref = get("w_out")
    tokens, width = grad_y_ref.shape
    gain_total = jnp.zeros((1, width), F32)
    for tile in range(tokens // TILE):
        rows = slice(tile * TILE, (tile + 1) * TILE)
        grad_mixed = dot(grad_y_ref[rows, :], w_out_ref[...], NT)
        if tile == 0:
            hat_ref, gate_ref, hat_scale_ref = get("hat"), get("gate"), get("hat_scale")
        hat = hat_ref[rows, :]
        active_ref[rows, :width] = (grad_mixed * hat * gain_out_ref[...]).astype(BF16)
        inner = grad_mixed * gate_ref[rows, :]
        gain_total = gain_total + jnp.sum(inner * hat, axis=0, keepdims=True)
        inner = inner * gain_out_ref[...]
        mean = jnp.mean(inner, axis=-1, keepdims=True)
        along = jnp.mean(inner * hat, axis=-1, keepdims=True)
        grad_att = ((inner - mean - hat * along) * hat_scale_ref[rows, :]).astype(BF16)
        if tile == 0:
            qkv_ref, slope_ref, weight_ref = get("qkv"), get("slope"), get("weight")
        for head in range(HEADS):
            vals, queries, keys = (
                qkv_ref[rows, part * width + head * HDIM : part * width + (head + 1) * HDIM]
                for part in range(3)
            )
            grad_o = grad_att[:, head * HDIM : (head + 1) * HDIM]
            grad_weight = dot(grad_o, vals, NT)
            grad_score = (grad_weight * slope_ref[tile * HEADS + head].astype(F32)).astype(BF16)
            for part, value in (
                (1, dot(weight_ref[tile * HEADS + head], grad_o, TN)),
                (2, dot(grad_score, keys)),
                (3, dot(grad_score, queries, TN)),
            ):
                first = part * width + head * HDIM
                active_ref[rows, first : first + HDIM] = value.astype(BF16)
    mixed_ref = get("mixed")
    sums_ref[:, :width] = (dot(mixed_ref[...], grad_y_ref[...], TN) * factor).astype(BF16)
    normed_ref, rows_slope_ref, w_in_ref = get("normed"), get("rows_slope"), get("w_in")
    count = normed_ref.shape[0]
    gather = gather_of(item_ref, count)
    grad_normed = jnp.zeros((count, width), F32)
    for part in range(4):
        columns = slice(part * width, (part + 1) * width)
        summed = dot(gather, active_ref[:, columns])
        grad_hidden = (summed * rows_slope_ref[:, columns].astype(F32)).astype(BF16)
        sums_ref[:, (part + 1) * width : (part + 2) * width] = (
            dot(normed_ref[...], grad_hidden, TN) * factor
        ).astype(BF16)
        grad_normed = grad_normed + dot(grad_hidden, w_in_ref[:, columns], NT)
    rows_hat_ref, rows_scale_ref, place_ref, digits_ref = (get(name) for name in FETCHED[12:])
    hat = rows_hat_ref[...]
    gain_rows = jnp.concatenate(
        [jnp.sum(grad_normed * hat, axis=0, keepdims=True), gain_total]
        + [jnp.zeros((14, width), F32)],
        axis=0,
    )
    gains = (gain_rows * factor).astype(BF16)
    end = 5 * width + LANES
    sums_ref[:, 5 * width : end] = dot(gains, unit(16), TN).astype(BF16)
    if sums_ref.shape[1] > end:
        sums_ref[:, end:] = jnp.zeros((width, sums_ref.shape[1] - end), BF16)
    plan.write(me_ref[0], sums_ref, stage_refs[1:])
    for copy in sends[1:]:
        copy.start()
    inner = grad_normed * gain_in_ref[...]
    mean = jnp.mean(inner, axis=-1, keepdims=True)
    along = jnp.mean(inner * hat, axis=-1, keepdims=True)
    row_grad = (inner - mean - hat * along) * rows_scale_ref[...] + dot(gather, grad_y_ref[...])
    table_ref = stage_refs[0]
    places = table_ref.shape[0]
    spots = lax.broadcasted_iota(jnp.int32, (places, count), 0)
    hit = spots == jnp.broadcast_to(place_ref[...], (places, count))
    spread = jnp.where(hit, 1.0, 0.0).astype(BF16)
    table_ref[:, :width] = dot(spread, row_grad.astype(BF16)).astype(BF16)
    table_ref[:, width:] = dot(spread, digits_ref[...]).astype(BF16)
    sends[0].start()
    for copy in sends:
        copy.wait()


def unit(rows):
    sub = lax.broadcasted_iota(jnp.int32, (rows, LANES), 0)
    lane = lax.broadcasted_iota(jnp.int32, (rows, LANES), 1)
    return jnp.where(sub == lane, 1.0, 0.0).astype(BF16)


class Plan:
    def __init__(self, dp_size, table_size, count, width):
        self.chunks = dp_size * table_size
        self.capacity = 2 * count // self.chunks
        self.row_groups = min(self.chunks, width // CHUNK_ROWS)
        self.column_groups = self.chunks // self.row_groups
        block = self.column_groups * LANES
        self.wide = -(-(5 * width + LANES) // block) * LANES
        self.split = -(-self.wide // (2 * LANES)) * LANES
        self.sides = ((0, self.split), (self.split, self.wide - self.split))
        table_bits = [1 << bit for bit in range(1, table_size.bit_length() - 1)]
        dp_bits = [table_size << bit for bit in range(dp_size.bit_length() - 1)]
        self.near_steps = len(table_bits) + 1
        self.orders = (table_bits + dp_bits, dp_bits[:1] + table_bits + dp_bits[1:])

    def chunk_at(self, me, side, place):
        order = [1] + self.orders[side]
        mask = 0
        for step, bit in enumerate(order):
            if place >> (len(order) - 1 - step) & 1:
                mask ^= bit
        chunk = me ^ mask
        begin, size = self.sides[side]
        first = (chunk & (self.row_groups - 1)) * CHUNK_ROWS
        rows = pl.ds(pl.multiple_of(first, CHUNK_ROWS), CHUNK_ROWS)
        if self.column_groups == 1:
            return rows, slice(begin, begin + size)
        group = chunk >> (self.row_groups.bit_length() - 1)
        return rows, pl.ds(pl.multiple_of(group * self.wide + begin, LANES), size)

    def write(self, me, sums_ref, part_refs):
        half = self.chunks // 2
        for side in range(2):
            for place in range(self.chunks):
                out_ref = part_refs[2 * side + place // half]
                out_ref[place % half] = sums_ref[self.chunk_at(me, side, place)]

    def read(self, me, part_refs, sums_ref):
        half = self.chunks // 2
        for side in range(2):
            for place in range(self.chunks):
                in_ref = part_refs[2 * side + place // half]
                sums_ref[self.chunk_at(me, side, place)] = in_ref[place % half]


def table_body(got_ref, out_ref):
    places, width = got_ref.shape[0], out_ref.shape[1]
    lane = lax.broadcasted_iota(jnp.int32, (16, LANES), 1)
    scale = jnp.where(lane == 0, 32.0, jnp.where(lane == 1, 1.0, 0.0)).astype(BF16)
    numbers = dot(scale, got_ref[:, width:], NT)[0:1].astype(jnp.int32)
    step = 256
    for first in range(0, out_ref.shape[0], step):
        sub = lax.broadcasted_iota(jnp.int32, (step, places), 0) + first
        hit = jnp.where(sub == jnp.broadcast_to(numbers, (step, places)), 1.0, 0.0)
        out_ref[first : first + step, :] = dot(hit.astype(BF16), got_ref[:, :width])


def widen_body(plan, me_ref, *refs):
    w_in_ref, w_out_ref, gain_in_ref, gain_out_ref, sums_ref = refs[4:]
    plan.read(me_ref[0], refs[:4], sums_ref)
    width = w_out_ref.shape[0]
    w_out_ref[...] = sums_ref[:, :width].astype(F32)
    w_in_ref[...] = sums_ref[:, width : 5 * width].astype(F32)
    gains = dot(unit(16), sums_ref[:, 5 * width : 5 * width + LANES], NT)
    gain_in_ref[...] = gains[0:1]
    gain_out_ref[...] = gains[1:2]


def add(left, right):
    return (left.astype(F32) + right.astype(F32)).astype(BF16)


def on_device(
    touched_rows,
    row_of_token,
    row_owner,
    owner_row,
    seq_blocks,
    seq_dest,
    grad_out,
    w_in,
    w_out,
    gain_in,
    gain_out,
):
    dp_size, table_size = lax.axis_size("dp"), lax.axis_size("table")
    both = ("dp", "table")
    count, width = touched_rows.shape
    tokens = row_of_token.shape[0]
    plan = Plan(dp_size, table_size, count, width)
    devices_all = plan.chunks
    total_factor = 1.0 / math.sqrt(grad_out.shape[0] * devices_all)
    gain_in, gain_out = gain_in[None, :], gain_out[None, :]
    me = lax.axis_index(both).astype(jnp.int32)[None]

    def swap(values, mask):
        return lax.ppermute(values, both, [(here, here ^ mask) for here in range(devices_all)])

    def exchange(values, axes):
        return lax.all_to_all(values, axes, split_axis=0, concat_axis=0, tiled=True)

    packed = jnp.broadcast_to(seq_dest * 8 + seq_blocks, (dp_size, 1, dp_size))
    send = call(
        functools.partial(send_body, table_size),
        shape_of((dp_size, SLOT, width), BF16),
        [SMEM] * 2 + [VMEM],
    )(me, exchange(packed, "dp"), grad_out)
    got = exchange(send, "dp")

    shapes = saved_shapes(tokens, count, width)
    shapes = [shapes[name] for name in SAVED]
    held = [pltpu.VMEM(item.shape, item.dtype) for item in shapes]
    saved = call(
        functools.partial(forward_body, plan.capacity),
        shapes,
        [VMEM] * 8,
        flops=4 * count * width * width * 8,
        moved=10_000_000,
        mebibytes=58,
        scratch=held + [pltpu.SemaphoreType.DMA((len(SAVED),))],
        out_space=HBM,
    )(
        touched_rows,
        row_of_token.reshape(tokens, 1),
        w_in,
        gain_in,
        gain_out,
        row_owner,
        row_owner.reshape(1, count),
        owner_row.reshape(count, 1),
    )

    saved = dict(zip(SAVED, saved), w_in=w_in, w_out=w_out)
    saved = dict(saved, got=got)
    fetched = [saved[name] for name in FETCHED]
    outs = [shape_of((devices_all * plan.capacity, width + LANES), BF16)]
    for _, wide in plan.sides:
        outs += [shape_of((devices_all // 2, CHUNK_ROWS, wide), BF16)] * 2
    table_send, *parts = call(
        functools.partial(backward_body, plan, total_factor),
        outs,
        [SMEM] * 2 + [VMEM] * 3 + [HBM] * len(FETCHED),
        flops=4 * count * width * width * 40,
        moved=12_000_000,
        mebibytes=58,
        out_space=HBM,
        scratch=[pltpu.VMEM(item.shape, item.dtype) for item in fetched + outs]
        + [
            pltpu.VMEM((width, plan.column_groups * plan.wide), BF16),
            pltpu.VMEM((tokens, 4 * width), BF16),
            pltpu.VMEM((tokens, width), BF16),
            pltpu.SemaphoreType.DMA((len(FETCHED),)),
            pltpu.SemaphoreType.DMA((len(outs),)),
        ],
    )(me, seq_dest, row_of_token.reshape(1, tokens), gain_in, gain_out, *fetched)

    def reduced(kept, mask):
        middle = kept.shape[0] // 2
        return add(kept[:middle], swap(kept[middle:], mask))

    def gathered(kept, mask):
        return jnp.concatenate([kept, swap(kept, mask)])

    table_got = exchange(table_send.reshape(devices_all, plan.capacity, width + LANES), both)
    sides = [add(parts[2 * side], swap(parts[2 * side + 1], 1)) for side in range(2)]
    for step in range(plan.near_steps):
        sides = [reduced(sides[side], plan.orders[side][step]) for side in range(2)]
    kept = jnp.concatenate(sides, axis=2)
    kept, table_got = lax.optimization_barrier((kept, table_got))
    table_part = call(
        table_body,
        shape_of((ROWS_DEV, width), F32),
        [VMEM],
    )(table_got.reshape(devices_all * plan.capacity, width + LANES))
    for mask in plan.orders[0][plan.near_steps :]:
        kept = reduced(kept, mask)
    for mask in reversed(plan.orders[0][plan.near_steps :]):
        kept = gathered(kept, mask)
    kept, table_part = lax.optimization_barrier((kept, table_part))
    sides = [kept[..., : plan.split], kept[..., plan.split :]]
    for step in reversed(range(plan.near_steps)):
        sides = [gathered(sides[side], plan.orders[side][step]) for side in range(2)]
    grad_w_in, grad_w_out, grad_gain_in, grad_gain_out = call(
        functools.partial(widen_body, plan),
        (
            shape_of(w_in.shape, F32),
            shape_of(w_out.shape, F32),
            shape_of((1, width), F32),
            shape_of((1, width), F32),
        ),
        [SMEM] + [VMEM] * 4,
        scratch=[pltpu.VMEM((width, plan.column_groups * plan.wide), BF16)],
    )(me, sides[0], swap(sides[0], 1), sides[1], swap(sides[1], 1))
    return (table_part, grad_w_in, grad_w_out, grad_gain_in[0], grad_gain_out[0])


def solution(mesh):
    rows = P(("dp", "table"), None)
    flat = P(("dp", "table"))
    in_specs = (rows, flat, rows, flat, flat, flat, rows, P(), P(), P(), P())
    out_specs = (rows, P(), P(), P(), P())
    return jax.shard_map(
        on_device, mesh=mesh, in_specs=in_specs, out_specs=out_specs, check_vma=False
    )
```

```python
import functools
import math

import jax
import jax.numpy as jnp
from jax import lax
from jax.experimental import pallas as pl
from jax.experimental.pallas import tpu as pltpu
from jax.sharding import PartitionSpec as P

HEADS = 4
HDIM = 128
BLK = 16
LMAXB = 4
SLOT = LMAXB * BLK
ROWS_DEV = 1024
TILE = 2 * SLOT
LANES = 128
CHUNK_ROWS = 16
GAIN_AT = 64
EPSILON = 1e-05
F32 = jnp.float32
BF16 = jnp.bfloat16
VMEM = pl.BlockSpec(memory_space=pltpu.VMEM)
SMEM = pl.BlockSpec(memory_space=pltpu.SMEM)
HBM = pl.BlockSpec(memory_space=pltpu.HBM)
ANY = pl.BlockSpec(memory_space=pl.ANY)


def call(body, out_shape, in_specs, flops=0, moved=0, scratch=(), out_space=VMEM, mebibytes=24):
    outs = jax.tree.map(lambda _: out_space, out_shape)
    return pl.pallas_call(
        body,
        out_shape=out_shape,
        in_specs=in_specs,
        out_specs=outs,
        scratch_shapes=scratch,
        compiler_params=pltpu.CompilerParams(vmem_limit_bytes=mebibytes * 1024 * 1024),
        cost_estimate=pl.CostEstimate(flops=flops, bytes_accessed=moved, transcendentals=0),
    )


def shape_of(dims, dtype):
    return jax.ShapeDtypeStruct(dims, dtype)


def sigmoid(values):
    return 0.5 * jnp.tanh(0.5 * values) + 0.5


def dot(left, right, contract=((1,), (0,))):
    return lax.dot_general(left, right, (contract, ((), ())), preferred_element_type=F32)


NT = ((1,), (1,))
TN = ((0,), (0,))


def send_body(lengths_ref, grad_ref, out_ref, sems):
    peers = out_ref.shape[0]
    blocks = grad_ref.shape[0] // BLK
    begin = jnp.int32(0)
    copies = []
    for peer in range(peers):
        for inner in range(LMAXB):
            block = jnp.minimum(begin + inner, blocks - 1)
            copies.append(
                pltpu.make_async_copy(
                    grad_ref.at[pl.ds(pl.multiple_of(block * BLK, BLK), BLK)],
                    out_ref.at[peer, pl.ds(inner * BLK, BLK)],
                    sems.at[peer, inner],
                )
            )
            copies[-1].start()
        for slot in range(peers):
            begin = begin + lengths_ref[peer, 0, slot]
    for copy in copies:
        copy.wait()


def tile_mask():
    sub = lax.broadcasted_iota(jnp.int32, (TILE, TILE), 0)
    lane = lax.broadcasted_iota(jnp.int32, (TILE, TILE), 1)
    return (sub // SLOT == lane // SLOT) & (lane <= sub)


SAVED = (
    "gate",
    "hat",
    "hat_scale",
    "qkv",
    "slope",
    "slope_t",
    "weight_t",
    "mixed_t",
    "normed_t",
    "rows_slope",
    "rows_hat",
    "rows_scale",
    "place",
    "digits",
)


def saved_shapes(tokens, count, width):
    pairs = tokens // TILE * HEADS
    return dict(
        gate=shape_of((tokens, width), F32),
        hat=shape_of((tokens, width), F32),
        hat_scale=shape_of((tokens, 1), F32),
        qkv=shape_of((tokens, 3 * width), BF16),
        slope=shape_of((pairs, TILE, TILE), BF16),
        slope_t=shape_of((pairs, TILE, TILE), BF16),
        weight_t=shape_of((pairs, TILE, TILE), BF16),
        mixed_t=shape_of((width, tokens), BF16),
        normed_t=shape_of((width, count), BF16),
        rows_slope=shape_of((count, 4 * width), BF16),
        rows_hat=shape_of((count, width), F32),
        rows_scale=shape_of((count, 1), F32),
        place=shape_of((1, count), jnp.int32),
        digits=shape_of((count, LANES), BF16),
    )


def forward_body(
    capacity,
    rows_ref,
    item_ref,
    w_in_ref,
    gain_in_ref,
    gain_out_ref,
    owner_col_ref,
    owner_row_ref,
    number_ref,
    *refs,
):
    size = len(SAVED)
    held = dict(zip(SAVED, refs[size : 2 * size]))
    sems = refs[-1]
    copies = {
        name: pltpu.make_async_copy(held[name], refs[index], sems.at[index])
        for index, name in enumerate(SAVED)
    }
    gate_ref, hat_ref, hat_scale_ref, qkv_ref, slope_ref, slope_t_ref = (
        held[name] for name in SAVED[:6]
    )
    weight_t_ref, mixed_t_ref, normed_t_ref, rows_slope_ref = (held[name] for name in SAVED[6:10])
    rows_hat_ref, rows_scale_ref, place_ref, digits_ref = (held[name] for name in SAVED[10:])
    count, width = rows_ref.shape
    tokens = item_ref.shape[0]
    across = jnp.broadcast_to(owner_row_ref[...], (count, count))
    down = jnp.broadcast_to(owner_col_ref[...], (count, count))
    sub = lax.broadcasted_iota(jnp.int32, (count, count), 0)
    lane = lax.broadcasted_iota(jnp.int32, (count, count), 1)
    earlier = jnp.where((across == down) & (sub < lane), 1.0, 0.0)
    rank = jnp.sum(earlier, axis=0, keepdims=True).astype(jnp.int32)
    place_ref[...] = owner_row_ref[...] * capacity + rank
    number = jnp.broadcast_to(number_ref[...], (count, LANES))
    lane = lax.broadcasted_iota(jnp.int32, (count, LANES), 1)
    digits = jnp.where(lane == 0, number >> 5, jnp.where(lane == 1, number & 31, 0))
    digits_ref[...] = digits.astype(F32).astype(BF16)
    copies["place"].start()
    copies["digits"].start()
    values = rows_ref[...].astype(F32)
    shifted = values - jnp.mean(values, axis=-1, keepdims=True)
    scale = lax.rsqrt(jnp.mean(shifted * shifted, axis=-1, keepdims=True) + EPSILON)
    hat = shifted * scale
    rows_hat_ref[...] = hat
    rows_scale_ref[...] = scale
    normed = hat * gain_in_ref[...]
    normed_t_ref[...] = normed.T.astype(BF16)
    normed = normed.astype(BF16)
    for name in ("rows_hat", "rows_scale", "normed_t"):
        copies[name].start()
    lane = lax.broadcasted_iota(jnp.int32, (tokens, count), 1)
    pick = jnp.where(lane == jnp.broadcast_to(item_ref[...], (tokens, count)), 1.0, 0.0)
    pick = pick.astype(BF16)
    for part in range(4):
        columns = slice(part * width, (part + 1) * width)
        hidden = dot(normed, w_in_ref[:, columns])
        sigma = sigmoid(hidden)
        active = hidden * sigma
        slope = sigma * (1.0 + hidden * (1.0 - sigma))
        rows_slope_ref[:, columns] = slope.astype(BF16)
        if part == 0:
            high = active.astype(BF16)
            low = (active - high.astype(F32)).astype(BF16)
            gate_ref[...] = dot(pick, high) + dot(pick, low)
        else:
            qkv_ref[:, (part - 1) * width : part * width] = dot(pick, active.astype(BF16)).astype(
                BF16
            )
    for name in ("gate", "qkv", "rows_slope"):
        copies[name].start()
    mask = tile_mask()
    factor = HDIM ** (-0.5)
    for tile in range(tokens // TILE):
        rows = slice(tile * TILE, (tile + 1) * TILE)
        parts = []
        for head in range(HEADS):
            vals, queries, keys = (
                qkv_ref[rows, part * width + head * HDIM : part * width + (head + 1) * HDIM]
                for part in range(3)
            )
            score = dot(queries, keys, NT) * factor
            sigma = sigmoid(score)
            weight = jnp.where(mask, score * sigma, 0.0)
            slope = sigma * (1.0 + score * (1.0 - sigma)) * factor
            slope = jnp.where(mask, slope, 0.0)
            slope_ref[tile * HEADS + head] = slope.astype(BF16)
            slope_t_ref[tile * HEADS + head] = slope.T.astype(BF16)
            weight_t_ref[tile * HEADS + head] = weight.T.astype(BF16)
            parts.append(dot(weight.astype(BF16), vals))
        attended = jnp.concatenate(parts, axis=1)
        shifted = attended - jnp.mean(attended, axis=-1, keepdims=True)
        scale = lax.rsqrt(jnp.mean(shifted * shifted, axis=-1, keepdims=True) + EPSILON)
        hat = shifted * scale
        hat_ref[rows, :] = hat
        hat_scale_ref[rows, :] = scale
        mixed = hat * gain_out_ref[...] * gate_ref[rows, :]
        mixed_t_ref[:, rows] = mixed.T.astype(BF16)
    for name in ("hat", "hat_scale", "slope", "slope_t", "weight_t", "mixed_t"):
        copies[name].start()
    for copy in copies.values():
        copy.wait()


def fetch(names, far_refs, near_refs, sems):
    copies = {}
    for index, name in enumerate(names):
        copies[name] = pltpu.make_async_copy(far_refs[index], near_refs[index], sems.at[index])
        copies[name].start()

    def get(name):
        copies[name].wait()
        return near_refs[names.index(name)]

    return get


def gather_of(item_ref, count):
    tokens = item_ref.shape[1]
    sub = lax.broadcasted_iota(jnp.int32, (count, tokens), 0)
    hit = sub == jnp.broadcast_to(item_ref[...], (count, tokens))
    return jnp.where(hit, 1.0, 0.0).astype(BF16)


FETCHED = (
    "got",
    "w_out",
    "hat",
    "gate",
    "hat_scale",
    "qkv",
    "slope",
    "slope_t",
    "weight_t",
    "mixed_t",
    "normed_t",
    "rows_slope",
    "w_in",
    "rows_hat",
    "rows_scale",
    "place",
    "digits",
)


def backward_body(
    plan, factor, me_ref, dest_ref, blocks_ref, item_ref, gain_in_ref, gain_out_ref, *refs
):
    size = len(FETCHED)
    far_refs, out_refs, refs = refs[:size], refs[size : size + 5], refs[size + 5 :]
    near_refs, stage_refs, refs = refs[:size], refs[size : size + 5], refs[size + 5 :]
    sums_ref, active_ref, grad_y_ref, in_sems, out_sems = refs
    get = fetch(FETCHED, far_refs, near_refs, in_sems)
    sends = [
        pltpu.make_async_copy(stage, out, out_sems.at[index])
        for index, (stage, out) in enumerate(zip(stage_refs, out_refs))
    ]
    got_ref = get("got")
    for slot in range(got_ref.shape[0]):
        rows = got_ref[dest_ref[slot]]
        live = lax.broadcasted_iota(jnp.int32, rows.shape, 0) < blocks_ref[slot] * BLK
        rows = jnp.where(live, rows.astype(F32), 0.0).astype(BF16)
        grad_y_ref[slot * SLOT : (slot + 1) * SLOT, :] = rows
    w_out_ref = get("w_out")
    tokens, width = grad_y_ref.shape
    gain_total = jnp.zeros((1, width), F32)
    for tile in range(tokens // TILE):
        rows = slice(tile * TILE, (tile + 1) * TILE)
        grad_mixed = dot(grad_y_ref[rows, :], w_out_ref[...], NT)
        if tile == 0:
            hat_ref, gate_ref, hat_scale_ref = get("hat"), get("gate"), get("hat_scale")
        hat = hat_ref[rows, :]
        active_ref[rows, :width] = (grad_mixed * hat * gain_out_ref[...]).astype(BF16)
        inner = grad_mixed * gate_ref[rows, :]
        gain_total = gain_total + jnp.sum(inner * hat, axis=0, keepdims=True)
        inner = inner * gain_out_ref[...]
        mean = jnp.mean(inner, axis=-1, keepdims=True)
        along = jnp.mean(inner * hat, axis=-1, keepdims=True)
        grad_att = ((inner - mean - hat * along) * hat_scale_ref[rows, :]).astype(BF16)
        if tile == 0:
            qkv_ref, slope_ref, slope_t_ref, weight_t_ref = (get(name) for name in FETCHED[5:9])
        for head in range(HEADS):
            vals, queries, keys = (
                qkv_ref[rows, part * width + head * HDIM : part * width + (head + 1) * HDIM]
                for part in range(3)
            )
            grad_o = grad_att[:, head * HDIM : (head + 1) * HDIM]
            grad_weight = dot(grad_o, vals, NT)
            grad_score = (grad_weight * slope_ref[tile * HEADS + head].astype(F32)).astype(BF16)
            weight_t = dot(vals, grad_o, NT)
            score_t = (weight_t * slope_t_ref[tile * HEADS + head].astype(F32)).astype(BF16)
            for part, value in (
                (1, dot(weight_t_ref[tile * HEADS + head], grad_o)),
                (2, dot(grad_score, keys)),
                (3, dot(score_t, queries)),
            ):
                first = part * width + head * HDIM
                active_ref[rows, first : first + HDIM] = value.astype(BF16)
    mixed_t_ref = get("mixed_t")
    sums_ref[:, :width] = (dot(mixed_t_ref[...], grad_y_ref[...]) * factor).astype(BF16)
    normed_t_ref, rows_slope_ref, w_in_ref = get("normed_t"), get("rows_slope"), get("w_in")
    count = normed_t_ref.shape[1]
    gather = gather_of(item_ref, count)
    grad_normed = jnp.zeros((count, width), F32)
    for part in range(4):
        columns = slice(part * width, (part + 1) * width)
        summed = dot(gather, active_ref[:, columns])
        grad_hidden = (summed * rows_slope_ref[:, columns].astype(F32)).astype(BF16)
        sums_ref[:, (part + 1) * width : (part + 2) * width] = (
            dot(normed_t_ref[...], grad_hidden) * factor
        ).astype(BF16)
        grad_normed = grad_normed + dot(grad_hidden, w_in_ref[:, columns], NT)
    rows_hat_ref, rows_scale_ref, place_ref, digits_ref = (get(name) for name in FETCHED[13:])
    hat = rows_hat_ref[...]
    gains = (jnp.sum(grad_normed * hat, axis=0, keepdims=True) * factor, gain_total * factor)
    plan.write(me_ref[0], sums_ref, stage_refs[1:])
    for copy in sends[1:]:
        copy.start()
    inner = grad_normed * gain_in_ref[...]
    mean = jnp.mean(inner, axis=-1, keepdims=True)
    along = jnp.mean(inner * hat, axis=-1, keepdims=True)
    row_grad = (inner - mean - hat * along) * rows_scale_ref[...] + dot(gather, grad_y_ref[...])
    table_ref = stage_refs[0]
    places = table_ref.shape[0]
    spots = lax.broadcasted_iota(jnp.int32, (places, count), 0)
    hit = spots == jnp.broadcast_to(place_ref[...], (places, count))
    spread = jnp.where(hit, 1.0, 0.0).astype(BF16)
    table_ref[:, :width] = dot(spread, row_grad.astype(BF16)).astype(BF16)
    extra = plan.extra
    lanes = []
    for row in range(plan.capacity):
        first = row * plan.gain_lanes
        gain = gains[first // width][:, first % width : first % width + plan.gain_lanes]
        rest = extra - GAIN_AT - plan.gain_lanes
        row_parts = [jnp.zeros((1, GAIN_AT), F32), gain]
        lanes.append(jnp.concatenate(row_parts + [jnp.zeros((1, rest), F32)] * (rest > 0), axis=1))
    lanes = jnp.concatenate(lanes, axis=0).astype(BF16)
    repeat = lax.broadcasted_iota(jnp.int32, (places, plan.capacity), 0) % plan.capacity
    lane = lax.broadcasted_iota(jnp.int32, (places, plan.capacity), 1)
    repeat = jnp.where(repeat == lane, 1.0, 0.0).astype(BF16)
    table_ref[:, width:] = dot(repeat, lanes).astype(BF16)
    table_ref[:, width : width + LANES] += dot(spread, digits_ref[...]).astype(BF16)
    sends[0].start()
    for copy in sends:
        copy.wait()


class Plan:
    def __init__(self, dp_size, table_size, count, width):
        self.chunks = dp_size * table_size
        self.capacity = 2 * count // self.chunks
        self.row_groups = min(self.chunks, width // CHUNK_ROWS)
        self.column_groups = self.chunks // self.row_groups
        block = self.column_groups * LANES
        self.wide = -(-5 * width // block) * LANES
        self.gain_lanes = 2 * width // self.capacity
        self.extra = -(-(GAIN_AT + self.gain_lanes) // LANES) * LANES
        self.split = -(-self.wide // (2 * LANES)) * LANES
        self.sides = ((0, self.split), (self.split, self.wide - self.split))
        table_bits = [1 << bit for bit in range(1, table_size.bit_length() - 1)]
        dp_bits = [table_size << bit for bit in range(dp_size.bit_length() - 1)]
        self.near_steps = len(table_bits) + 1
        self.orders = (table_bits + dp_bits, dp_bits[:1] + table_bits + dp_bits[1:])

    def chunk_at(self, me, side, place):
        order = [1] + self.orders[side]
        mask = 0
        for step, bit in enumerate(order):
            if place >> (len(order) - 1 - step) & 1:
                mask ^= bit
        chunk = me ^ mask
        begin, size = self.sides[side]
        first = (chunk & (self.row_groups - 1)) * CHUNK_ROWS
        rows = pl.ds(pl.multiple_of(first, CHUNK_ROWS), CHUNK_ROWS)
        if self.column_groups == 1:
            return rows, slice(begin, begin + size)
        group = chunk >> (self.row_groups.bit_length() - 1)
        return rows, pl.ds(pl.multiple_of(group * self.wide + begin, LANES), size)

    def write(self, me, sums_ref, part_refs):
        half = self.chunks // 2
        for side in range(2):
            for place in range(self.chunks):
                out_ref = part_refs[2 * side + place // half]
                out_ref[place % half] = sums_ref[self.chunk_at(me, side, place)]

    def read(self, me, part_refs, sums_ref):
        half = self.chunks // 2
        for side in range(2):
            for place in range(self.chunks):
                in_ref = part_refs[2 * side + place // half]
                sums_ref[self.chunk_at(me, side, place)] = in_ref[place % half]


def table_body(plan, got_ref, out_ref, gain_in_ref, gain_out_ref):
    places, width = got_ref.shape[0], out_ref.shape[1]
    lane = lax.broadcasted_iota(jnp.int32, (16, LANES), 1)
    scale = jnp.where(lane == 0, 32.0, jnp.where(lane == 1, 1.0, 0.0)).astype(BF16)
    numbers = dot(scale, got_ref[:, width : width + LANES], NT)[0:1].astype(jnp.int32)
    step = 256
    for first in range(0, out_ref.shape[0], step):
        sub = lax.broadcasted_iota(jnp.int32, (step, places), 0) + first
        hit = jnp.where(sub == jnp.broadcast_to(numbers, (step, places)), 1.0, 0.0)
        out_ref[first : first + step, :] = dot(hit.astype(BF16), got_ref[:, :width])
    sub = lax.broadcasted_iota(jnp.int32, (16, places), 0)
    lane = lax.broadcasted_iota(jnp.int32, (16, places), 1) % plan.capacity
    total = dot(jnp.where(sub == lane, 1.0, 0.0).astype(BF16), got_ref[:, width:])
    for row in range(plan.capacity):
        first = row * plan.gain_lanes
        gain_ref = (gain_in_ref, gain_out_ref)[first // width]
        gain_ref[:, first % width : first % width + plan.gain_lanes] = total[
            row : row + 1, GAIN_AT : GAIN_AT + plan.gain_lanes
        ]


def widen_body(plan, me_ref, *refs):
    w_in_ref, w_out_ref, sums_ref = refs[4:]
    plan.read(me_ref[0], refs[:4], sums_ref)
    width = w_out_ref.shape[0]
    w_out_ref[...] = sums_ref[:, :width].astype(F32)
    w_in_ref[...] = sums_ref[:, width : 5 * width].astype(F32)


def add(left, right):
    return (left.astype(F32) + right.astype(F32)).astype(BF16)


def on_device(
    touched_rows,
    row_of_token,
    row_owner,
    owner_row,
    seq_blocks,
    seq_dest,
    grad_out,
    w_in,
    w_out,
    gain_in,
    gain_out,
):
    dp_size, table_size = lax.axis_size("dp"), lax.axis_size("table")
    both = ("dp", "table")
    count, width = touched_rows.shape
    tokens = row_of_token.shape[0]
    plan = Plan(dp_size, table_size, count, width)
    devices_all = plan.chunks
    total_factor = 1.0 / math.sqrt(grad_out.shape[0] * devices_all)
    gain_in, gain_out = gain_in[None, :], gain_out[None, :]
    me = lax.axis_index(both).astype(jnp.int32)[None]

    def swap(values, mask):
        return lax.ppermute(values, both, [(here, here ^ mask) for here in range(devices_all)])

    def exchange(values, axes):
        return lax.all_to_all(values, axes, split_axis=0, concat_axis=0, tiled=True)

    peers = jnp.arange(dp_size, dtype=jnp.int32)[:, None, None]
    lengths = jnp.where(seq_dest[None, None, :] == peers, seq_blocks[None, None, :], 0)
    send = call(
        send_body,
        shape_of((dp_size, SLOT, width), BF16),
        [SMEM, HBM],
        mebibytes=58,
        out_space=HBM,
        scratch=[pltpu.SemaphoreType.DMA((dp_size, LMAXB))],
    )(exchange(lengths, "dp"), grad_out)
    got = exchange(send, "dp")

    shapes = saved_shapes(tokens, count, width)
    shapes = [shapes[name] for name in SAVED]
    held = [pltpu.VMEM(item.shape, item.dtype) for item in shapes]
    saved = call(
        functools.partial(forward_body, plan.capacity),
        shapes,
        [VMEM] * 8,
        flops=4 * count * width * width * 8,
        moved=10_000_000,
        mebibytes=58,
        scratch=held + [pltpu.SemaphoreType.DMA((len(SAVED),))],
        out_space=HBM,
    )(
        touched_rows,
        row_of_token.reshape(tokens, 1),
        w_in,
        gain_in,
        gain_out,
        row_owner,
        row_owner.reshape(1, count),
        owner_row.reshape(count, 1),
    )

    saved = dict(zip(SAVED, saved), w_in=w_in, w_out=w_out)
    saved = dict(saved, got=got)
    fetched = [saved[name] for name in FETCHED]
    outs = [shape_of((devices_all * plan.capacity, width + plan.extra), BF16)]
    for _, wide in plan.sides:
        outs += [shape_of((devices_all // 2, CHUNK_ROWS, wide), BF16)] * 2
    table_send, *parts = call(
        functools.partial(backward_body, plan, total_factor),
        outs,
        [SMEM] * 3 + [VMEM] * 3 + [ANY] + [HBM] * (len(FETCHED) - 1),
        flops=4 * count * width * width * 40,
        moved=12_000_000,
        mebibytes=58,
        out_space=HBM,
        scratch=[pltpu.VMEM(item.shape, item.dtype) for item in fetched + outs]
        + [
            pltpu.VMEM((width, plan.column_groups * plan.wide), BF16),
            pltpu.VMEM((tokens, 4 * width), BF16),
            pltpu.VMEM((tokens, width), BF16),
            pltpu.SemaphoreType.DMA((len(FETCHED),)),
            pltpu.SemaphoreType.DMA((len(outs),)),
        ],
    )(me, seq_dest, seq_blocks, row_of_token.reshape(1, tokens), gain_in, gain_out, *fetched)

    def reduced(kept, mask):
        middle = kept.shape[0] // 2
        return add(kept[:middle], swap(kept[middle:], mask))

    def gathered(kept, mask):
        return jnp.concatenate([kept, swap(kept, mask)])

    sides = [add(parts[2 * side], swap(parts[2 * side + 1], 1)) for side in range(2)]
    *sides, table_send = lax.optimization_barrier((*sides, table_send))
    table_got = exchange(table_send.reshape(devices_all, plan.capacity, -1), both)
    for step in range(plan.near_steps):
        sides = [reduced(sides[side], plan.orders[side][step]) for side in range(2)]
    kept = jnp.concatenate(sides, axis=2)
    kept, table_got = lax.optimization_barrier((kept, table_got))
    table_part, grad_gain_in, grad_gain_out = call(
        functools.partial(table_body, plan),
        (
            shape_of((ROWS_DEV, width), F32),
            shape_of((1, width), F32),
            shape_of((1, width), F32),
        ),
        [VMEM],
    )(table_got.reshape(devices_all * plan.capacity, -1))
    for mask in plan.orders[0][plan.near_steps :]:
        kept = reduced(kept, mask)
    for mask in reversed(plan.orders[0][plan.near_steps :]):
        kept = gathered(kept, mask)
    kept, table_part = lax.optimization_barrier((kept, table_part))
    sides = [kept[..., : plan.split], kept[..., plan.split :]]
    for step in reversed(range(plan.near_steps)):
        sides = [gathered(sides[side], plan.orders[side][step]) for side in range(2)]
    grad_w_in, grad_w_out = call(
        functools.partial(widen_body, plan),
        (shape_of(w_in.shape, F32), shape_of(w_out.shape, F32)),
        [SMEM] + [VMEM] * 4,
        scratch=[pltpu.VMEM((width, plan.column_groups * plan.wide), BF16)],
    )(me, sides[0], swap(sides[0], 1), sides[1], swap(sides[1], 1))
    return (table_part, grad_w_in, grad_w_out, grad_gain_in[0], grad_gain_out[0])


def solution(mesh):
    rows = P(("dp", "table"), None)
    flat = P(("dp", "table"))
    in_specs = (rows, flat, rows, flat, flat, flat, rows, P(), P(), P(), P())
    out_specs = (rows, P(), P(), P(), P())
    return jax.shard_map(
        on_device, mesh=mesh, in_specs=in_specs, out_specs=out_specs, check_vma=False
    )
```

```python
import functools
import math

import jax
import jax.numpy as jnp
from jax import lax
from jax.experimental import pallas as pl
from jax.experimental.pallas import tpu as pltpu
from jax.sharding import PartitionSpec as P

HEADS = 4
HDIM = 128
BLK = 16
LMAXB = 4
SLOT = LMAXB * BLK
ROWS_DEV = 1024
TILE = 2 * SLOT
LANES = 128
CHUNK_ROWS = 16
GAIN_AT = 64
EPSILON = 1e-05
F32 = jnp.float32
BF16 = jnp.bfloat16
VMEM = pl.BlockSpec(memory_space=pltpu.VMEM)
SMEM = pl.BlockSpec(memory_space=pltpu.SMEM)


def call(body, out_shape, in_specs, flops=0, moved=0, scratch=(), mebibytes=24):
    outs = jax.tree.map(lambda _: VMEM, out_shape)
    return pl.pallas_call(
        body,
        out_shape=out_shape,
        in_specs=in_specs,
        out_specs=outs,
        scratch_shapes=scratch,
        compiler_params=pltpu.CompilerParams(vmem_limit_bytes=mebibytes * 1024 * 1024),
        cost_estimate=pl.CostEstimate(flops=flops, bytes_accessed=moved, transcendentals=0),
    )


def shape_of(dims, dtype):
    return jax.ShapeDtypeStruct(dims, dtype)


def sigmoid(values):
    return 0.5 * jnp.tanh(0.5 * values) + 0.5


def dot(left, right, contract=((1,), (0,))):
    return lax.dot_general(left, right, (contract, ((), ())), preferred_element_type=F32)


NT = ((1,), (1,))
TN = ((0,), (0,))


def send_body(table_size, me_ref, lengths_ref, grad_ref, *refs):
    out_refs, begin_ref = refs[:-1], refs[-1]
    peers = len(out_refs)
    blocks = grad_ref.shape[0] // BLK
    begin = jnp.int32(0)
    for peer in range(peers):
        begin_ref[peer] = begin
        for slot in range(peers):
            begin = begin + lengths_ref[peer, 0, slot]
    me = me_ref[0] // table_size
    for apart, out_ref in enumerate(out_refs):
        begin = begin_ref[me ^ apart]
        for inner in range(LMAXB):
            block = jnp.minimum(begin + inner, blocks - 1)
            rows = grad_ref[pl.ds(pl.multiple_of(block * BLK, BLK), BLK), :]
            out_ref[inner * BLK : (inner + 1) * BLK, :] = rows


def tile_mask():
    sub = lax.broadcasted_iota(jnp.int32, (TILE, TILE), 0)
    lane = lax.broadcasted_iota(jnp.int32, (TILE, TILE), 1)
    return (sub // SLOT == lane // SLOT) & (lane <= sub)


SAVED = (
    "gate",
    "hat",
    "hat_scale",
    "qkv",
    "slope",
    "slope_t",
    "weight_t",
    "mixed_t",
    "normed_t",
    "rows_slope",
    "rows_hat",
    "rows_scale",
    "place",
    "digits",
)


def saved_shapes(tokens, count, width):
    pairs = tokens // TILE * HEADS
    return dict(
        gate=shape_of((tokens, width), F32),
        hat=shape_of((tokens, width), F32),
        hat_scale=shape_of((tokens, 1), F32),
        qkv=shape_of((tokens, 3 * width), BF16),
        slope=shape_of((pairs, TILE, TILE), BF16),
        slope_t=shape_of((pairs, TILE, TILE), BF16),
        weight_t=shape_of((pairs, TILE, TILE), BF16),
        mixed_t=shape_of((width, tokens), BF16),
        normed_t=shape_of((width, count), BF16),
        rows_slope=shape_of((count, 4 * width), BF16),
        rows_hat=shape_of((count, width), F32),
        rows_scale=shape_of((count, 1), F32),
        place=shape_of((1, count), jnp.int32),
        digits=shape_of((count, LANES), BF16),
    )


def forward_body(
    capacity,
    rows_ref,
    item_ref,
    w_in_ref,
    gain_in_ref,
    gain_out_ref,
    owner_col_ref,
    owner_row_ref,
    number_ref,
    *refs,
):
    held = dict(zip(SAVED, refs))
    gate_ref, hat_ref, hat_scale_ref, qkv_ref, slope_ref, slope_t_ref = (
        held[name] for name in SAVED[:6]
    )
    weight_t_ref, mixed_t_ref, normed_t_ref, rows_slope_ref = (held[name] for name in SAVED[6:10])
    rows_hat_ref, rows_scale_ref, place_ref, digits_ref = (held[name] for name in SAVED[10:])
    count, width = rows_ref.shape
    tokens = item_ref.shape[0]
    across = jnp.broadcast_to(owner_row_ref[...], (count, count))
    down = jnp.broadcast_to(owner_col_ref[...], (count, count))
    sub = lax.broadcasted_iota(jnp.int32, (count, count), 0)
    lane = lax.broadcasted_iota(jnp.int32, (count, count), 1)
    earlier = jnp.where((across == down) & (sub < lane), 1.0, 0.0)
    rank = jnp.sum(earlier, axis=0, keepdims=True).astype(jnp.int32)
    place_ref[...] = owner_row_ref[...] * capacity + rank
    number = jnp.broadcast_to(number_ref[...], (count, LANES))
    lane = lax.broadcasted_iota(jnp.int32, (count, LANES), 1)
    digits = jnp.where(lane == 0, number >> 5, jnp.where(lane == 1, number & 31, 0))
    digits_ref[...] = digits.astype(F32).astype(BF16)
    values = rows_ref[...].astype(F32)
    shifted = values - jnp.mean(values, axis=-1, keepdims=True)
    scale = lax.rsqrt(jnp.mean(shifted * shifted, axis=-1, keepdims=True) + EPSILON)
    hat = shifted * scale
    rows_hat_ref[...] = hat
    rows_scale_ref[...] = scale
    normed = hat * gain_in_ref[...]
    normed_t_ref[...] = normed.T.astype(BF16)
    normed = normed.astype(BF16)
    lane = lax.broadcasted_iota(jnp.int32, (tokens, count), 1)
    pick = jnp.where(lane == jnp.broadcast_to(item_ref[...], (tokens, count)), 1.0, 0.0)
    pick = pick.astype(BF16)
    for part in range(4):
        columns = slice(part * width, (part + 1) * width)
        hidden = dot(normed, w_in_ref[:, columns])
        sigma = sigmoid(hidden)
        active = hidden * sigma
        slope = sigma * (1.0 + hidden * (1.0 - sigma))
        rows_slope_ref[:, columns] = slope.astype(BF16)
        if part == 0:
            high = active.astype(BF16)
            low = (active - high.astype(F32)).astype(BF16)
            gate_ref[...] = dot(pick, high) + dot(pick, low)
        else:
            qkv_ref[:, (part - 1) * width : part * width] = dot(pick, active.astype(BF16)).astype(
                BF16
            )
    mask = tile_mask()
    factor = HDIM ** (-0.5)
    for tile in range(tokens // TILE):
        rows = slice(tile * TILE, (tile + 1) * TILE)
        parts = []
        for head in range(HEADS):
            vals, queries, keys = (
                qkv_ref[rows, part * width + head * HDIM : part * width + (head + 1) * HDIM]
                for part in range(3)
            )
            score = dot(queries, keys, NT) * factor
            sigma = sigmoid(score)
            weight = jnp.where(mask, score * sigma, 0.0)
            slope = sigma * (1.0 + score * (1.0 - sigma)) * factor
            slope = jnp.where(mask, slope, 0.0)
            slope_ref[tile * HEADS + head] = slope.astype(BF16)
            slope_t_ref[tile * HEADS + head] = slope.T.astype(BF16)
            weight_t_ref[tile * HEADS + head] = weight.T.astype(BF16)
            parts.append(dot(weight.astype(BF16), vals))
        attended = jnp.concatenate(parts, axis=1)
        shifted = attended - jnp.mean(attended, axis=-1, keepdims=True)
        scale = lax.rsqrt(jnp.mean(shifted * shifted, axis=-1, keepdims=True) + EPSILON)
        hat = shifted * scale
        hat_ref[rows, :] = hat
        hat_scale_ref[rows, :] = scale
        mixed = hat * gain_out_ref[...] * gate_ref[rows, :]
        mixed_t_ref[:, rows] = mixed.T.astype(BF16)


def gather_of(item_ref, count):
    tokens = item_ref.shape[1]
    sub = lax.broadcasted_iota(jnp.int32, (count, tokens), 0)
    hit = sub == jnp.broadcast_to(item_ref[...], (count, tokens))
    return jnp.where(hit, 1.0, 0.0).astype(BF16)


USED = (
    "w_out",
    "hat",
    "gate",
    "hat_scale",
    "qkv",
    "slope",
    "slope_t",
    "weight_t",
    "mixed_t",
    "normed_t",
    "rows_slope",
    "w_in",
    "rows_hat",
    "rows_scale",
    "place",
    "digits",
)


def backward_body(
    plan,
    table_size,
    factor,
    me_ref,
    dest_ref,
    blocks_ref,
    item_ref,
    gain_in_ref,
    gain_out_ref,
    *refs,
):
    used, refs = dict(zip(USED, refs)), refs[len(USED) :]
    got_refs, (table_ref, *part_refs), (wide_ref, sums_ref, active_ref, grad_y_ref) = (
        refs[:-9],
        refs[-9:-4],
        refs[-4:],
    )
    w_out_ref, hat_ref, gate_ref, hat_scale_ref, qkv_ref, slope_ref, slope_t_ref = (
        used[name] for name in USED[:7]
    )
    weight_t_ref, mixed_t_ref, normed_t_ref, rows_slope_ref, w_in_ref = (
        used[name] for name in USED[7:12]
    )
    rows_hat_ref, rows_scale_ref, place_ref, digits_ref = (used[name] for name in USED[12:])
    for apart, got_ref in enumerate(got_refs):
        wide_ref[apart] = got_ref[...]
    for slot in range(len(got_refs)):
        rows = wide_ref[dest_ref[slot] ^ (me_ref[0] // table_size)]
        live = lax.broadcasted_iota(jnp.int32, rows.shape, 0) < blocks_ref[slot] * BLK
        rows = jnp.where(live, rows.astype(F32), 0.0).astype(BF16)
        grad_y_ref[slot * SLOT : (slot + 1) * SLOT, :] = rows
    tokens, width = grad_y_ref.shape
    count = normed_t_ref.shape[1]
    gain_total = jnp.zeros((1, width), F32)
    for tile in range(tokens // TILE):
        rows = slice(tile * TILE, (tile + 1) * TILE)
        grad_mixed = dot(grad_y_ref[rows, :], w_out_ref[...], NT)
        hat = hat_ref[rows, :]
        active_ref[rows, :width] = (grad_mixed * hat * gain_out_ref[...]).astype(BF16)
        inner = grad_mixed * gate_ref[rows, :]
        gain_total = gain_total + jnp.sum(inner * hat, axis=0, keepdims=True)
        inner = inner * gain_out_ref[...]
        mean = jnp.mean(inner, axis=-1, keepdims=True)
        along = jnp.mean(inner * hat, axis=-1, keepdims=True)
        grad_att = ((inner - mean - hat * along) * hat_scale_ref[rows, :]).astype(BF16)
        for head in range(HEADS):
            vals, queries, keys = (
                qkv_ref[rows, part * width + head * HDIM : part * width + (head + 1) * HDIM]
                for part in range(3)
            )
            grad_o = grad_att[:, head * HDIM : (head + 1) * HDIM]
            grad_weight = dot(grad_o, vals, NT)
            grad_score = (grad_weight * slope_ref[tile * HEADS + head].astype(F32)).astype(BF16)
            weight_t = dot(vals, grad_o, NT)
            score_t = (weight_t * slope_t_ref[tile * HEADS + head].astype(F32)).astype(BF16)
            for part, value in (
                (1, dot(weight_t_ref[tile * HEADS + head], grad_o)),
                (2, dot(grad_score, keys)),
                (3, dot(score_t, queries)),
            ):
                first = part * width + head * HDIM
                active_ref[rows, first : first + HDIM] = value.astype(BF16)
    sums_ref[:, :width] = (dot(mixed_t_ref[...], grad_y_ref[...]) * factor).astype(BF16)
    gather = gather_of(item_ref, count)
    grad_normed = jnp.zeros((count, width), F32)
    for part in range(4):
        columns = slice(part * width, (part + 1) * width)
        summed = dot(gather, active_ref[:, columns])
        grad_hidden = (summed * rows_slope_ref[:, columns].astype(F32)).astype(BF16)
        sums_ref[:, (part + 1) * width : (part + 2) * width] = (
            dot(normed_t_ref[...], grad_hidden) * factor
        ).astype(BF16)
        grad_normed = grad_normed + dot(grad_hidden, w_in_ref[:, columns], NT)
    hat = rows_hat_ref[...]
    gains = (jnp.sum(grad_normed * hat, axis=0, keepdims=True) * factor, gain_total * factor)
    plan.write(me_ref[0], sums_ref, part_refs)
    inner = grad_normed * gain_in_ref[...]
    mean = jnp.mean(inner, axis=-1, keepdims=True)
    along = jnp.mean(inner * hat, axis=-1, keepdims=True)
    row_grad = (inner - mean - hat * along) * rows_scale_ref[...] + dot(gather, grad_y_ref[...])
    places = table_ref.shape[0]
    spots = lax.broadcasted_iota(jnp.int32, (places, count), 0)
    hit = spots == jnp.broadcast_to(place_ref[...], (places, count))
    spread = jnp.where(hit, 1.0, 0.0).astype(BF16)
    table_ref[:, :width] = dot(spread, row_grad.astype(BF16)).astype(BF16)
    extra = plan.extra
    lanes = []
    for row in range(plan.capacity):
        first = row * plan.gain_lanes
        gain = gains[first // width][:, first % width : first % width + plan.gain_lanes]
        rest = extra - GAIN_AT - plan.gain_lanes
        row_parts = [jnp.zeros((1, GAIN_AT), F32), gain]
        lanes.append(jnp.concatenate(row_parts + [jnp.zeros((1, rest), F32)] * (rest > 0), axis=1))
    lanes = jnp.concatenate(lanes, axis=0).astype(BF16)
    repeat = lax.broadcasted_iota(jnp.int32, (places, plan.capacity), 0) % plan.capacity
    lane = lax.broadcasted_iota(jnp.int32, (places, plan.capacity), 1)
    repeat = jnp.where(repeat == lane, 1.0, 0.0).astype(BF16)
    table_ref[:, width:] = dot(repeat, lanes).astype(BF16)
    table_ref[:, width : width + LANES] += dot(spread, digits_ref[...]).astype(BF16)


class Plan:
    def __init__(self, dp_size, table_size, count, width):
        self.chunks = dp_size * table_size
        self.capacity = 2 * count // self.chunks
        self.row_groups = min(self.chunks, width // CHUNK_ROWS)
        self.column_groups = self.chunks // self.row_groups
        block = self.column_groups * LANES
        self.wide = -(-5 * width // block) * LANES
        self.gain_lanes = 2 * width // self.capacity
        self.extra = -(-(GAIN_AT + self.gain_lanes) // LANES) * LANES
        self.split = -(-self.wide // (2 * LANES)) * LANES
        self.sides = ((0, self.split), (self.split, self.wide - self.split))
        table_bits = [1 << bit for bit in range(1, table_size.bit_length() - 1)]
        dp_bits = [table_size << bit for bit in range(dp_size.bit_length() - 1)]
        self.near_steps = len(table_bits) + 1
        self.orders = (table_bits + dp_bits, dp_bits[:1] + table_bits + dp_bits[1:])

    def chunk_at(self, me, side, place):
        order = [1] + self.orders[side]
        mask = 0
        for step, bit in enumerate(order):
            if place >> (len(order) - 1 - step) & 1:
                mask ^= bit
        chunk = me ^ mask
        begin, size = self.sides[side]
        first = (chunk & (self.row_groups - 1)) * CHUNK_ROWS
        rows = pl.ds(pl.multiple_of(first, CHUNK_ROWS), CHUNK_ROWS)
        if self.column_groups == 1:
            return rows, slice(begin, begin + size)
        group = chunk >> (self.row_groups.bit_length() - 1)
        return rows, pl.ds(pl.multiple_of(group * self.wide + begin, LANES), size)

    def write(self, me, sums_ref, part_refs):
        half = self.chunks // 2
        for side in range(2):
            for place in range(self.chunks):
                out_ref = part_refs[2 * side + place // half]
                out_ref[place % half] = sums_ref[self.chunk_at(me, side, place)]

    def read(self, me, part_refs, sums_ref):
        half = self.chunks // 2
        for side in range(2):
            for place in range(self.chunks):
                in_ref = part_refs[2 * side + place // half]
                sums_ref[self.chunk_at(me, side, place)] = in_ref[place % half]


def table_body(plan, got_ref, out_ref, gain_in_ref, gain_out_ref):
    places, width = got_ref.shape[0], out_ref.shape[1]
    lane = lax.broadcasted_iota(jnp.int32, (16, LANES), 1)
    scale = jnp.where(lane == 0, 32.0, jnp.where(lane == 1, 1.0, 0.0)).astype(BF16)
    numbers = dot(scale, got_ref[:, width : width + LANES], NT)[0:1].astype(jnp.int32)
    step = 256
    for first in range(0, out_ref.shape[0], step):
        sub = lax.broadcasted_iota(jnp.int32, (step, places), 0) + first
        hit = jnp.where(sub == jnp.broadcast_to(numbers, (step, places)), 1.0, 0.0)
        out_ref[first : first + step, :] = dot(hit.astype(BF16), got_ref[:, :width])
    sub = lax.broadcasted_iota(jnp.int32, (16, places), 0)
    lane = lax.broadcasted_iota(jnp.int32, (16, places), 1) % plan.capacity
    total = dot(jnp.where(sub == lane, 1.0, 0.0).astype(BF16), got_ref[:, width:])
    for row in range(plan.capacity):
        first = row * plan.gain_lanes
        gain_ref = (gain_in_ref, gain_out_ref)[first // width]
        gain_ref[:, first % width : first % width + plan.gain_lanes] = total[
            row : row + 1, GAIN_AT : GAIN_AT + plan.gain_lanes
        ]


def widen_body(plan, me_ref, *refs):
    w_in_ref, w_out_ref, sums_ref = refs[4:]
    plan.read(me_ref[0], refs[:4], sums_ref)
    width = w_out_ref.shape[0]
    w_out_ref[...] = sums_ref[:, :width].astype(F32)
    w_in_ref[...] = sums_ref[:, width : 5 * width].astype(F32)


def add(left, right):
    return (left.astype(F32) + right.astype(F32)).astype(BF16)


def on_device(
    touched_rows,
    row_of_token,
    row_owner,
    owner_row,
    seq_blocks,
    seq_dest,
    grad_out,
    w_in,
    w_out,
    gain_in,
    gain_out,
):
    dp_size, table_size = lax.axis_size("dp"), lax.axis_size("table")
    both = ("dp", "table")
    count, width = touched_rows.shape
    tokens = row_of_token.shape[0]
    plan = Plan(dp_size, table_size, count, width)
    devices_all = plan.chunks
    total_factor = 1.0 / math.sqrt(grad_out.shape[0] * devices_all)
    gain_in, gain_out = gain_in[None, :], gain_out[None, :]
    me = lax.axis_index(both).astype(jnp.int32)[None]

    def swap(values, mask):
        return lax.ppermute(values, both, [(here, here ^ mask) for here in range(devices_all)])

    def exchange(values, axes):
        return lax.all_to_all(values, axes, split_axis=0, concat_axis=0, tiled=True)

    peers = jnp.arange(dp_size, dtype=jnp.int32)[:, None, None]
    lengths = jnp.where(seq_dest[None, None, :] == peers, seq_blocks[None, None, :], 0)
    send = call(
        functools.partial(send_body, table_size),
        [shape_of((SLOT, width), BF16)] * dp_size,
        [SMEM] * 2 + [VMEM],
        scratch=[pltpu.SMEM((dp_size,), jnp.int32)],
    )(me, exchange(lengths, "dp"), grad_out)
    got = list(send)
    far = [apart for apart in range(1, dp_size) if 2 * apart >= dp_size]
    for apart in far:
        got[apart] = swap(send[apart], apart * table_size)
    *near, touched_rows = lax.optimization_barrier((*send[: far[0]], touched_rows))

    shapes = saved_shapes(tokens, count, width)
    saved = call(
        functools.partial(forward_body, plan.capacity),
        [shapes[name] for name in SAVED],
        [VMEM] * 8,
        flops=4 * count * width * width * 20,
        moved=10_000_000,
        mebibytes=12 + tokens // 32,
    )(
        touched_rows,
        row_of_token.reshape(tokens, 1),
        w_in,
        gain_in,
        gain_out,
        row_owner,
        row_owner.reshape(1, count),
        owner_row.reshape(count, 1),
    )
    *near, gate = lax.optimization_barrier((*near, saved[0]))
    saved = [gate, *saved[1:]]
    got[0] = near[0]
    for apart in range(1, far[0]):
        got[apart] = swap(near[apart], apart * table_size)
    saved = dict(zip(SAVED, saved), w_in=w_in, w_out=w_out)
    outs = [shape_of((devices_all * plan.capacity, width + plan.extra), BF16)]
    for _, wide in plan.sides:
        outs += [shape_of((devices_all // 2, CHUNK_ROWS, wide), BF16)] * 2
    table_send, *parts = call(
        functools.partial(backward_body, plan, table_size, total_factor),
        outs,
        [SMEM] * 3 + [VMEM] * (3 + len(USED) + dp_size),
        flops=4 * count * width * width * 40,
        moved=12_000_000,
        mebibytes=12 + tokens // 32,
        scratch=[
            pltpu.VMEM((dp_size, SLOT, width), BF16),
            pltpu.VMEM((width, plan.column_groups * plan.wide), BF16),
            pltpu.VMEM((tokens, 4 * width), BF16),
            pltpu.VMEM((tokens, width), BF16),
        ],
    )(
        me,
        seq_dest,
        seq_blocks,
        row_of_token.reshape(1, tokens),
        gain_in,
        gain_out,
        *(saved[name] for name in USED),
        *got,
    )

    def reduced(kept, mask):
        middle = kept.shape[0] // 2
        return add(kept[:middle], swap(kept[middle:], mask))

    def gathered(kept, mask):
        return jnp.concatenate([kept, swap(kept, mask)])

    sides = [add(parts[2 * side], swap(parts[2 * side + 1], 1)) for side in range(2)]
    table_got = exchange(table_send.reshape(devices_all, plan.capacity, -1), both)
    for step in range(plan.near_steps):
        sides = [reduced(sides[side], plan.orders[side][step]) for side in range(2)]
    kept = jnp.concatenate(sides, axis=2)
    kept, table_got = lax.optimization_barrier((kept, table_got))
    table_part, grad_gain_in, grad_gain_out = call(
        functools.partial(table_body, plan),
        (
            shape_of((ROWS_DEV, width), F32),
            shape_of((1, width), F32),
            shape_of((1, width), F32),
        ),
        [VMEM],
    )(table_got.reshape(devices_all * plan.capacity, -1))
    for mask in plan.orders[0][plan.near_steps :]:
        kept = reduced(kept, mask)
    for mask in reversed(plan.orders[0][plan.near_steps :]):
        kept = gathered(kept, mask)
    kept, table_part = lax.optimization_barrier((kept, table_part))
    sides = [kept[..., : plan.split], kept[..., plan.split :]]
    for step in reversed(range(plan.near_steps)):
        sides = [gathered(sides[side], plan.orders[side][step]) for side in range(2)]
    grad_w_in, grad_w_out = call(
        functools.partial(widen_body, plan),
        (shape_of(w_in.shape, F32), shape_of(w_out.shape, F32)),
        [SMEM] + [VMEM] * 4,
        scratch=[pltpu.VMEM((width, plan.column_groups * plan.wide), BF16)],
    )(me, sides[0], swap(sides[0], 1), sides[1], swap(sides[1], 1))
    return (table_part, grad_w_in, grad_w_out, grad_gain_in[0], grad_gain_out[0])


def solution(mesh):
    rows = P(("dp", "table"), None)
    flat = P(("dp", "table"))
    in_specs = (rows, flat, rows, flat, flat, flat, rows, P(), P(), P(), P())
    out_specs = (rows, P(), P(), P(), P())
    return jax.shard_map(
        on_device, mesh=mesh, in_specs=in_specs, out_specs=out_specs, check_vma=False
    )
```

```python
import functools
import math

import jax
import jax.numpy as jnp
from jax import lax
from jax.experimental import pallas as pl
from jax.experimental.pallas import tpu as pltpu
from jax.sharding import PartitionSpec as P

HEADS = 4
HDIM = 128
BLK = 16
LMAXB = 4
SLOT = LMAXB * BLK
ROWS_DEV = 1024
TILE = 2 * SLOT
LANES = 128
CHUNK_ROWS = 16
GAIN_AT = 64
EPSILON = 1e-05
F32 = jnp.float32
BF16 = jnp.bfloat16
VMEM = pl.BlockSpec(memory_space=pltpu.VMEM)
SMEM = pl.BlockSpec(memory_space=pltpu.SMEM)


def call(body, out_shape, in_specs, flops=0, moved=0, scratch=(), mebibytes=24):
    outs = jax.tree.map(lambda _: VMEM, out_shape)
    return pl.pallas_call(
        body,
        out_shape=out_shape,
        in_specs=in_specs,
        out_specs=outs,
        scratch_shapes=scratch,
        compiler_params=pltpu.CompilerParams(vmem_limit_bytes=mebibytes * 1024 * 1024),
        cost_estimate=pl.CostEstimate(flops=flops, bytes_accessed=moved, transcendentals=0),
    )


def shape_of(dims, dtype):
    return jax.ShapeDtypeStruct(dims, dtype)


def sigmoid(values):
    return 0.5 * jnp.tanh(0.5 * values) + 0.5


def dot(left, right, contract=((1,), (0,))):
    return lax.dot_general(left, right, (contract, ((), ())), preferred_element_type=F32)


NT = ((1,), (1,))
TN = ((0,), (0,))


def send_body(table_size, me_ref, lengths_ref, grad_ref, *refs):
    out_refs, begin_ref = refs[:-1], refs[-1]
    peers = len(out_refs)
    blocks = grad_ref.shape[0] // BLK
    me = me_ref[0] // table_size
    begin = jnp.int32(0)
    for peer in range(peers):
        begin_ref[peer] = begin
        begin = begin + lengths_ref[peer, me]
    for apart, out_ref in enumerate(out_refs):
        begin = begin_ref[me ^ apart]
        for inner in range(LMAXB):
            block = jnp.minimum(begin + inner, blocks - 1)
            rows = grad_ref[pl.ds(pl.multiple_of(block * BLK, BLK), BLK), :]
            out_ref[inner * BLK : (inner + 1) * BLK, :] = rows


def tile_mask():
    sub = lax.broadcasted_iota(jnp.int32, (TILE, TILE), 0)
    lane = lax.broadcasted_iota(jnp.int32, (TILE, TILE), 1)
    return (sub // SLOT == lane // SLOT) & (lane <= sub)


SAVED = (
    "gate",
    "hat",
    "hat_scale",
    "qkv",
    "slope",
    "slope_t",
    "weight_t",
    "mixed_t",
    "normed_t",
    "rows_slope",
    "rows_hat",
    "rows_scale",
    "place",
    "digits",
)


def saved_shapes(tokens, count, width):
    pairs = tokens // TILE * HEADS
    return dict(
        gate=shape_of((tokens, width), F32),
        hat=shape_of((tokens, width), F32),
        hat_scale=shape_of((tokens, 1), F32),
        qkv=shape_of((tokens, 3 * width), BF16),
        slope=shape_of((pairs, TILE, TILE), BF16),
        slope_t=shape_of((pairs, TILE, TILE), BF16),
        weight_t=shape_of((pairs, TILE, TILE), BF16),
        mixed_t=shape_of((width, tokens), BF16),
        normed_t=shape_of((width, count), BF16),
        rows_slope=shape_of((count, 4 * width), BF16),
        rows_hat=shape_of((count, width), F32),
        rows_scale=shape_of((count, 1), F32),
        place=shape_of((1, count), jnp.int32),
        digits=shape_of((count, LANES), BF16),
    )


def forward_body(
    capacity,
    rows_ref,
    item_ref,
    w_in_ref,
    gains_ref,
    owner_col_ref,
    ints_ref,
    number_ref,
    *refs,
):
    held = dict(zip(SAVED, refs))
    gate_ref, hat_ref, hat_scale_ref, qkv_ref, slope_ref, slope_t_ref = (
        held[name] for name in SAVED[:6]
    )
    weight_t_ref, mixed_t_ref, normed_t_ref, rows_slope_ref = (held[name] for name in SAVED[6:10])
    rows_hat_ref, rows_scale_ref, place_ref, digits_ref = (held[name] for name in SAVED[10:])
    count, width = rows_ref.shape
    tokens = item_ref.shape[0]
    gain_in, gain_out = gains_ref[0:1, :], gains_ref[1:2, :]
    owner_row = ints_ref[:, tokens:]
    across = jnp.broadcast_to(owner_row, (count, count))
    down = jnp.broadcast_to(owner_col_ref[...], (count, count))
    sub = lax.broadcasted_iota(jnp.int32, (count, count), 0)
    lane = lax.broadcasted_iota(jnp.int32, (count, count), 1)
    earlier = jnp.where((across == down) & (sub < lane), 1.0, 0.0)
    rank = jnp.sum(earlier, axis=0, keepdims=True).astype(jnp.int32)
    place_ref[...] = owner_row * capacity + rank
    number = jnp.broadcast_to(number_ref[...], (count, LANES))
    lane = lax.broadcasted_iota(jnp.int32, (count, LANES), 1)
    digits = jnp.where(lane == 0, number >> 5, jnp.where(lane == 1, number & 31, 0))
    digits_ref[...] = digits.astype(F32).astype(BF16)
    values = rows_ref[...].astype(F32)
    shifted = values - jnp.mean(values, axis=-1, keepdims=True)
    scale = lax.rsqrt(jnp.mean(shifted * shifted, axis=-1, keepdims=True) + EPSILON)
    hat = shifted * scale
    rows_hat_ref[...] = hat
    rows_scale_ref[...] = scale
    normed = hat * gain_in
    normed_t_ref[...] = normed.T.astype(BF16)
    normed = normed.astype(BF16)
    lane = lax.broadcasted_iota(jnp.int32, (tokens, count), 1)
    pick = jnp.where(lane == jnp.broadcast_to(item_ref[...], (tokens, count)), 1.0, 0.0)
    pick = pick.astype(BF16)
    for part in range(4):
        columns = slice(part * width, (part + 1) * width)
        hidden = dot(normed, w_in_ref[:, columns])
        sigma = sigmoid(hidden)
        active = hidden * sigma
        slope = sigma * (1.0 + hidden * (1.0 - sigma))
        rows_slope_ref[:, columns] = slope.astype(BF16)
        if part == 0:
            high = active.astype(BF16)
            low = (active - high.astype(F32)).astype(BF16)
            gate_ref[...] = dot(pick, high) + dot(pick, low)
        else:
            qkv_ref[:, (part - 1) * width : part * width] = dot(pick, active.astype(BF16)).astype(
                BF16
            )
    mask = tile_mask()
    factor = HDIM ** (-0.5)
    for tile in range(tokens // TILE):
        rows = slice(tile * TILE, (tile + 1) * TILE)
        parts = []
        for head in range(HEADS):
            vals, queries, keys = (
                qkv_ref[rows, part * width + head * HDIM : part * width + (head + 1) * HDIM]
                for part in range(3)
            )
            score = dot(queries, keys, NT) * factor
            sigma = sigmoid(score)
            weight = jnp.where(mask, score * sigma, 0.0)
            slope = sigma * (1.0 + score * (1.0 - sigma)) * factor
            slope = jnp.where(mask, slope, 0.0)
            slope_ref[tile * HEADS + head] = slope.astype(BF16)
            slope_t_ref[tile * HEADS + head] = slope.T.astype(BF16)
            weight_t_ref[tile * HEADS + head] = weight.T.astype(BF16)
            parts.append(dot(weight.astype(BF16), vals))
        attended = jnp.concatenate(parts, axis=1)
        shifted = attended - jnp.mean(attended, axis=-1, keepdims=True)
        scale = lax.rsqrt(jnp.mean(shifted * shifted, axis=-1, keepdims=True) + EPSILON)
        hat = shifted * scale
        hat_ref[rows, :] = hat
        hat_scale_ref[rows, :] = scale
        mixed = hat * gain_out * gate_ref[rows, :]
        mixed_t_ref[:, rows] = mixed.T.astype(BF16)


def gather_of(items, count):
    tokens = items.shape[1]
    sub = lax.broadcasted_iota(jnp.int32, (count, tokens), 0)
    hit = sub == jnp.broadcast_to(items, (count, tokens))
    return jnp.where(hit, 1.0, 0.0).astype(BF16)


USED = (
    "w_out",
    "hat",
    "gate",
    "hat_scale",
    "qkv",
    "slope",
    "slope_t",
    "weight_t",
    "mixed_t",
    "normed_t",
    "rows_slope",
    "w_in",
    "rows_hat",
    "rows_scale",
    "place",
    "digits",
)


def backward_body(
    plan,
    table_size,
    factor,
    me_ref,
    dest_ref,
    blocks_ref,
    ints_ref,
    gains_ref,
    *refs,
):
    used, refs = dict(zip(USED, refs)), refs[len(USED) :]
    got_refs, (table_ref, *part_refs), (wide_ref, sums_ref, active_ref, grad_y_ref) = (
        refs[:-9],
        refs[-9:-4],
        refs[-4:],
    )
    w_out_ref, hat_ref, gate_ref, hat_scale_ref, qkv_ref, slope_ref, slope_t_ref = (
        used[name] for name in USED[:7]
    )
    weight_t_ref, mixed_t_ref, normed_t_ref, rows_slope_ref, w_in_ref = (
        used[name] for name in USED[7:12]
    )
    rows_hat_ref, rows_scale_ref, place_ref, digits_ref = (used[name] for name in USED[12:])
    for apart, got_ref in enumerate(got_refs):
        wide_ref[apart] = got_ref[...]
    for slot in range(len(got_refs)):
        rows = wide_ref[dest_ref[slot] ^ (me_ref[0] // table_size)]
        live = lax.broadcasted_iota(jnp.int32, rows.shape, 0) < blocks_ref[slot] * BLK
        rows = jnp.where(live, rows.astype(F32), 0.0).astype(BF16)
        grad_y_ref[slot * SLOT : (slot + 1) * SLOT, :] = rows
    tokens, width = grad_y_ref.shape
    count = normed_t_ref.shape[1]
    gain_in, gain_out = gains_ref[0:1, :], gains_ref[1:2, :]
    gain_total = jnp.zeros((1, width), F32)
    for tile in range(tokens // TILE):
        rows = slice(tile * TILE, (tile + 1) * TILE)
        grad_mixed = dot(grad_y_ref[rows, :], w_out_ref[...], NT)
        hat = hat_ref[rows, :]
        active_ref[rows, :width] = (grad_mixed * hat * gain_out).astype(BF16)
        inner = grad_mixed * gate_ref[rows, :]
        gain_total = gain_total + jnp.sum(inner * hat, axis=0, keepdims=True)
        inner = inner * gain_out
        mean = jnp.mean(inner, axis=-1, keepdims=True)
        along = jnp.mean(inner * hat, axis=-1, keepdims=True)
        grad_att = ((inner - mean - hat * along) * hat_scale_ref[rows, :]).astype(BF16)
        for head in range(HEADS):
            vals, queries, keys = (
                qkv_ref[rows, part * width + head * HDIM : part * width + (head + 1) * HDIM]
                for part in range(3)
            )
            grad_o = grad_att[:, head * HDIM : (head + 1) * HDIM]
            grad_weight = dot(grad_o, vals, NT)
            grad_score = (grad_weight * slope_ref[tile * HEADS + head].astype(F32)).astype(BF16)
            weight_t = dot(vals, grad_o, NT)
            score_t = (weight_t * slope_t_ref[tile * HEADS + head].astype(F32)).astype(BF16)
            for part, value in (
                (1, dot(weight_t_ref[tile * HEADS + head], grad_o)),
                (2, dot(grad_score, keys)),
                (3, dot(score_t, queries)),
            ):
                first = part * width + head * HDIM
                active_ref[rows, first : first + HDIM] = value.astype(BF16)
    sums_ref[:, :width] = (dot(mixed_t_ref[...], grad_y_ref[...]) * factor).astype(BF16)
    gather = gather_of(ints_ref[:, :tokens], count)
    grad_normed = jnp.zeros((count, width), F32)
    for part in range(4):
        columns = slice(part * width, (part + 1) * width)
        summed = dot(gather, active_ref[:, columns])
        grad_hidden = (summed * rows_slope_ref[:, columns].astype(F32)).astype(BF16)
        sums_ref[:, (part + 1) * width : (part + 2) * width] = (
            dot(normed_t_ref[...], grad_hidden) * factor
        ).astype(BF16)
        grad_normed = grad_normed + dot(grad_hidden, w_in_ref[:, columns], NT)
    hat = rows_hat_ref[...]
    gains = (jnp.sum(grad_normed * hat, axis=0, keepdims=True) * factor, gain_total * factor)
    plan.write(me_ref[0], sums_ref, part_refs)
    inner = grad_normed * gain_in
    mean = jnp.mean(inner, axis=-1, keepdims=True)
    along = jnp.mean(inner * hat, axis=-1, keepdims=True)
    row_grad = (inner - mean - hat * along) * rows_scale_ref[...] + dot(gather, grad_y_ref[...])
    places = table_ref.shape[0]
    spots = lax.broadcasted_iota(jnp.int32, (places, count), 0)
    hit = spots == jnp.broadcast_to(place_ref[...], (places, count))
    spread = jnp.where(hit, 1.0, 0.0).astype(BF16)
    table_ref[:, :width] = dot(spread, row_grad.astype(BF16)).astype(BF16)
    extra = plan.extra
    lanes = []
    for row in range(plan.capacity):
        first = row * plan.gain_lanes
        gain = gains[first // width][:, first % width : first % width + plan.gain_lanes]
        rest = extra - GAIN_AT - plan.gain_lanes
        row_parts = [jnp.zeros((1, GAIN_AT), F32), gain]
        lanes.append(jnp.concatenate(row_parts + [jnp.zeros((1, rest), F32)] * (rest > 0), axis=1))
    lanes = jnp.concatenate(lanes, axis=0).astype(BF16)
    repeat = lax.broadcasted_iota(jnp.int32, (places, plan.capacity), 0) % plan.capacity
    lane = lax.broadcasted_iota(jnp.int32, (places, plan.capacity), 1)
    repeat = jnp.where(repeat == lane, 1.0, 0.0).astype(BF16)
    table_ref[:, width:] = dot(repeat, lanes).astype(BF16)
    table_ref[:, width : width + LANES] += dot(spread, digits_ref[...]).astype(BF16)


class Plan:
    def __init__(self, dp_size, table_size, count, width):
        self.chunks = dp_size * table_size
        self.capacity = 2 * count // self.chunks
        self.row_groups = min(self.chunks, width // CHUNK_ROWS)
        self.column_groups = self.chunks // self.row_groups
        block = self.column_groups * LANES
        self.wide = -(-5 * width // block) * LANES
        self.gain_lanes = 2 * width // self.capacity
        self.extra = -(-(GAIN_AT + self.gain_lanes) // LANES) * LANES
        self.split = -(-self.wide // (2 * LANES)) * LANES
        self.sides = ((0, self.split), (self.split, self.wide - self.split))
        table_bits = [1 << bit for bit in range(1, table_size.bit_length() - 1)]
        dp_bits = [table_size << bit for bit in range(dp_size.bit_length() - 1)]
        self.near_steps = len(table_bits) + 1
        self.orders = (table_bits + dp_bits, dp_bits[:1] + table_bits + dp_bits[1:])

    def chunk_at(self, me, side, place):
        order = [1] + self.orders[side]
        mask = 0
        for step, bit in enumerate(order):
            if place >> (len(order) - 1 - step) & 1:
                mask ^= bit
        chunk = me ^ mask
        begin, size = self.sides[side]
        first = (chunk & (self.row_groups - 1)) * CHUNK_ROWS
        rows = pl.ds(pl.multiple_of(first, CHUNK_ROWS), CHUNK_ROWS)
        if self.column_groups == 1:
            return rows, slice(begin, begin + size)
        group = chunk >> (self.row_groups.bit_length() - 1)
        return rows, pl.ds(pl.multiple_of(group * self.wide + begin, LANES), size)

    def write(self, me, sums_ref, part_refs):
        half = self.chunks // 2
        for side in range(2):
            for place in range(self.chunks):
                out_ref = part_refs[2 * side + place // half]
                out_ref[place % half] = sums_ref[self.chunk_at(me, side, place)]

    def read(self, me, part_refs, sums_ref):
        half = self.chunks // 2
        for side in range(2):
            for place in range(self.chunks):
                in_ref = part_refs[2 * side + place // half]
                sums_ref[self.chunk_at(me, side, place)] = in_ref[place % half]


def table_body(plan, got_ref, out_ref, gain_in_ref, gain_out_ref):
    places, width = got_ref.shape[0], out_ref.shape[1]
    lane = lax.broadcasted_iota(jnp.int32, (16, LANES), 1)
    scale = jnp.where(lane == 0, 32.0, jnp.where(lane == 1, 1.0, 0.0)).astype(BF16)
    numbers = dot(scale, got_ref[:, width : width + LANES], NT)[0:1].astype(jnp.int32)
    step = 256
    for first in range(0, out_ref.shape[0], step):
        sub = lax.broadcasted_iota(jnp.int32, (step, places), 0) + first
        hit = jnp.where(sub == jnp.broadcast_to(numbers, (step, places)), 1.0, 0.0)
        out_ref[first : first + step, :] = dot(hit.astype(BF16), got_ref[:, :width])
    sub = lax.broadcasted_iota(jnp.int32, (16, places), 0)
    lane = lax.broadcasted_iota(jnp.int32, (16, places), 1) % plan.capacity
    total = dot(jnp.where(sub == lane, 1.0, 0.0).astype(BF16), got_ref[:, width:])
    for row in range(plan.capacity):
        first = row * plan.gain_lanes
        gain_ref = (gain_in_ref, gain_out_ref)[first // width]
        gain_ref[:, first % width : first % width + plan.gain_lanes] = total[
            row : row + 1, GAIN_AT : GAIN_AT + plan.gain_lanes
        ]


def widen_body(plan, me_ref, *refs):
    w_in_ref, w_out_ref, sums_ref = refs[4:]
    plan.read(me_ref[0], refs[:4], sums_ref)
    width = w_out_ref.shape[0]
    w_out_ref[...] = sums_ref[:, :width].astype(F32)
    w_in_ref[...] = sums_ref[:, width : 5 * width].astype(F32)


def add(left, right):
    return (left.astype(F32) + right.astype(F32)).astype(BF16)


def on_device(
    touched_rows,
    row_of_token,
    row_owner,
    owner_row,
    seq_blocks,
    seq_dest,
    grad_out,
    w_in,
    w_out,
    gain_in,
    gain_out,
):
    dp_size, table_size = lax.axis_size("dp"), lax.axis_size("table")
    both = ("dp", "table")
    count, width = touched_rows.shape
    tokens = row_of_token.shape[0]
    plan = Plan(dp_size, table_size, count, width)
    devices_all = plan.chunks
    total_factor = 1.0 / math.sqrt(grad_out.shape[0] * devices_all)
    gain_rows = jnp.stack([gain_in, gain_out])
    ints = jnp.concatenate([row_of_token, row_owner[:, 0]])[None, :]
    me = lax.axis_index(both).astype(jnp.int32)[None]

    def swap(values, mask):
        return lax.ppermute(values, both, [(here, here ^ mask) for here in range(devices_all)])

    def exchange(values, axes):
        return lax.all_to_all(values, axes, split_axis=0, concat_axis=0, tiled=True)

    peers = jnp.arange(dp_size, dtype=jnp.int32)
    own = jnp.sum(jnp.where(seq_dest[:, None] == peers, seq_blocks[:, None], 0), axis=0)
    lengths = jnp.where(peers[:, None] == lax.axis_index("dp"), own, 0)
    for bit in range(dp_size.bit_length() - 1):
        lengths = lengths + swap(lengths, table_size << bit)
    send = call(
        functools.partial(send_body, table_size),
        [shape_of((SLOT, width), BF16)] * dp_size,
        [SMEM] * 2 + [VMEM],
        scratch=[pltpu.SMEM((dp_size,), jnp.int32)],
    )(me, lengths, grad_out)
    got = list(send)
    far = [apart for apart in range(1, dp_size) if 2 * apart >= dp_size]
    for apart in far:
        got[apart] = swap(send[apart], apart * table_size)
    *near, ints = lax.optimization_barrier((*send[: far[0]], ints))

    shapes = saved_shapes(tokens, count, width)
    saved = call(
        functools.partial(forward_body, plan.capacity),
        [shapes[name] for name in SAVED],
        [VMEM] * 7,
        flops=4 * count * width * width * 20,
        moved=10_000_000,
        mebibytes=12 + tokens // 32,
    )(
        touched_rows,
        row_of_token.reshape(tokens, 1),
        w_in,
        gain_rows,
        row_owner,
        ints,
        owner_row.reshape(count, 1),
    )
    *near, gate = lax.optimization_barrier((*near, saved[0]))
    saved = [gate, *saved[1:]]
    got[0] = near[0]
    for apart in range(1, far[0]):
        got[apart] = swap(near[apart], apart * table_size)
    saved = dict(zip(SAVED, saved), w_in=w_in, w_out=w_out)
    outs = [shape_of((devices_all * plan.capacity, width + plan.extra), BF16)]
    for _, wide in plan.sides:
        outs += [shape_of((devices_all // 2, CHUNK_ROWS, wide), BF16)] * 2
    table_send, *parts = call(
        functools.partial(backward_body, plan, table_size, total_factor),
        outs,
        [SMEM] * 3 + [VMEM] * (2 + len(USED) + dp_size),
        flops=4 * count * width * width * 40,
        moved=12_000_000,
        mebibytes=12 + tokens // 32,
        scratch=[
            pltpu.VMEM((dp_size, SLOT, width), BF16),
            pltpu.VMEM((width, plan.column_groups * plan.wide), BF16),
            pltpu.VMEM((tokens, 4 * width), BF16),
            pltpu.VMEM((tokens, width), BF16),
        ],
    )(
        me,
        seq_dest,
        seq_blocks,
        ints,
        gain_rows,
        *(saved[name] for name in USED),
        *got,
    )

    def reduced(kept, mask):
        middle = kept.shape[0] // 2
        return add(kept[:middle], swap(kept[middle:], mask))

    def gathered(kept, mask):
        return jnp.concatenate([kept, swap(kept, mask)])

    sides = [add(parts[2 * side], swap(parts[2 * side + 1], 1)) for side in range(2)]
    table_got = exchange(table_send.reshape(devices_all, plan.capacity, -1), both)
    for step in range(plan.near_steps):
        sides = [reduced(sides[side], plan.orders[side][step]) for side in range(2)]
    kept = jnp.concatenate(sides, axis=2)
    kept, table_got = lax.optimization_barrier((kept, table_got))
    table_part, grad_gain_in, grad_gain_out = call(
        functools.partial(table_body, plan),
        (
            shape_of((ROWS_DEV, width), F32),
            shape_of((1, width), F32),
            shape_of((1, width), F32),
        ),
        [VMEM],
    )(table_got.reshape(devices_all * plan.capacity, -1))
    for mask in plan.orders[0][plan.near_steps :]:
        kept = reduced(kept, mask)
    for mask in reversed(plan.orders[0][plan.near_steps :]):
        kept = gathered(kept, mask)
    kept, table_part = lax.optimization_barrier((kept, table_part))
    sides = [kept[..., : plan.split], kept[..., plan.split :]]
    for step in reversed(range(plan.near_steps)):
        sides = [gathered(sides[side], plan.orders[side][step]) for side in range(2)]
    grad_w_in, grad_w_out = call(
        functools.partial(widen_body, plan),
        (shape_of(w_in.shape, F32), shape_of(w_out.shape, F32)),
        [SMEM] + [VMEM] * 4,
        scratch=[pltpu.VMEM((width, plan.column_groups * plan.wide), BF16)],
    )(me, sides[0], swap(sides[0], 1), sides[1], swap(sides[1], 1))
    return (table_part, grad_w_in, grad_w_out, grad_gain_in[0], grad_gain_out[0])


def solution(mesh):
    rows = P(("dp", "table"), None)
    flat = P(("dp", "table"))
    in_specs = (rows, flat, rows, flat, flat, flat, rows, P(), P(), P(), P())
    out_specs = (rows, P(), P(), P(), P())
    return jax.shard_map(
        on_device, mesh=mesh, in_specs=in_specs, out_specs=out_specs, check_vma=False
    )
```

```python
import functools
import math

import jax
import jax.numpy as jnp
from jax import lax
from jax.experimental import pallas as pl
from jax.experimental.pallas import tpu as pltpu
from jax.sharding import PartitionSpec as P

HEADS = 4
HDIM = 128
BLK = 16
LMAXB = 4
SLOT = LMAXB * BLK
ROWS_DEV = 1024
TILE = 2 * SLOT
LANES = 128
CHUNK_ROWS = 16
GAIN_AT = 64
EPSILON = 1e-05
F32 = jnp.float32
BF16 = jnp.bfloat16
VMEM = pl.BlockSpec(memory_space=pltpu.VMEM)
SMEM = pl.BlockSpec(memory_space=pltpu.SMEM)


def call(body, out_shape, in_specs, flops=0, moved=0, scratch=(), mebibytes=24):
    outs = jax.tree.map(lambda _: VMEM, out_shape)
    return pl.pallas_call(
        body,
        out_shape=out_shape,
        in_specs=in_specs,
        out_specs=outs,
        scratch_shapes=scratch,
        compiler_params=pltpu.CompilerParams(vmem_limit_bytes=mebibytes * 1024 * 1024),
        cost_estimate=pl.CostEstimate(flops=flops, bytes_accessed=moved, transcendentals=0),
    )


def shape_of(dims, dtype):
    return jax.ShapeDtypeStruct(dims, dtype)


def sigmoid(values):
    return 0.5 * jnp.tanh(0.5 * values) + 0.5


def dot(left, right, contract=((1,), (0,))):
    return lax.dot_general(left, right, (contract, ((), ())), preferred_element_type=F32)


NT = ((1,), (1,))
TN = ((0,), (0,))


def send_body(table_size, me_ref, lengths_ref, grad_ref, *refs):
    out_refs, begin_ref = refs[:-1], refs[-1]
    peers = len(out_refs)
    blocks = grad_ref.shape[0] // BLK
    me = me_ref[0] // table_size
    begin = jnp.int32(0)
    for peer in range(peers):
        begin_ref[peer] = begin
        begin = begin + lengths_ref[peer, me]
    for apart, out_ref in enumerate(out_refs):
        begin = begin_ref[me ^ apart]
        for inner in range(LMAXB):
            block = jnp.minimum(begin + inner, blocks - 1)
            rows = grad_ref[pl.ds(pl.multiple_of(block * BLK, BLK), BLK), :]
            out_ref[inner * BLK : (inner + 1) * BLK, :] = rows


def tile_mask():
    sub = lax.broadcasted_iota(jnp.int32, (TILE, TILE), 0)
    lane = lax.broadcasted_iota(jnp.int32, (TILE, TILE), 1)
    return (sub // SLOT == lane // SLOT) & (lane <= sub)


SAVED = (
    "gate",
    "hat",
    "hat_scale",
    "qkv",
    "slope",
    "slope_t",
    "weight_t",
    "mixed_t",
    "normed_t",
    "rows_slope",
    "rows_hat",
    "rows_scale",
    "place",
    "digits",
)


def saved_shapes(tokens, count, width):
    pairs = tokens // TILE * HEADS
    return dict(
        gate=shape_of((tokens, width), F32),
        hat=shape_of((tokens, width), F32),
        hat_scale=shape_of((tokens, 1), F32),
        qkv=shape_of((tokens, 3 * width), BF16),
        slope=shape_of((pairs, TILE, TILE), BF16),
        slope_t=shape_of((pairs, TILE, TILE), BF16),
        weight_t=shape_of((pairs, TILE, TILE), BF16),
        mixed_t=shape_of((width, tokens), BF16),
        normed_t=shape_of((width, count), BF16),
        rows_slope=shape_of((count, 4 * width), BF16),
        rows_hat=shape_of((count, width), F32),
        rows_scale=shape_of((count, 1), F32),
        place=shape_of((1, count), jnp.int32),
        digits=shape_of((count, LANES), BF16),
    )


def forward_body(
    capacity,
    rows_ref,
    w_in_ref,
    gains_ref,
    ints_ref,
    *refs,
):
    held = dict(zip(SAVED, refs))
    gate_ref, hat_ref, hat_scale_ref, qkv_ref, slope_ref, slope_t_ref = (
        held[name] for name in SAVED[:6]
    )
    weight_t_ref, mixed_t_ref, normed_t_ref, rows_slope_ref = (held[name] for name in SAVED[6:10])
    rows_hat_ref, rows_scale_ref, place_ref, digits_ref = (held[name] for name in SAVED[10:])
    count, width = rows_ref.shape
    tokens = ints_ref.shape[1] - 2 * count
    gain_in, gain_out = gains_ref[0:1, :], gains_ref[1:2, :]
    columns = jnp.broadcast_to(ints_ref[...].astype(F32), (8, ints_ref.shape[1])).T
    columns = columns[:, 0:1].astype(jnp.int32)
    items, owners, numbers = (
        columns[:tokens],
        columns[tokens : tokens + count],
        columns[tokens + count :],
    )
    owner_row = ints_ref[:, tokens : tokens + count]
    across = jnp.broadcast_to(owner_row, (count, count))
    down = jnp.broadcast_to(owners, (count, count))
    sub = lax.broadcasted_iota(jnp.int32, (count, count), 0)
    lane = lax.broadcasted_iota(jnp.int32, (count, count), 1)
    earlier = jnp.where((across == down) & (sub < lane), 1.0, 0.0)
    rank = jnp.sum(earlier, axis=0, keepdims=True).astype(jnp.int32)
    place_ref[...] = owner_row * capacity + rank
    number = jnp.broadcast_to(numbers, (count, LANES))
    lane = lax.broadcasted_iota(jnp.int32, (count, LANES), 1)
    digits = jnp.where(lane == 0, number >> 5, jnp.where(lane == 1, number & 31, 0))
    digits_ref[...] = digits.astype(F32).astype(BF16)
    values = rows_ref[...].astype(F32)
    shifted = values - jnp.mean(values, axis=-1, keepdims=True)
    scale = lax.rsqrt(jnp.mean(shifted * shifted, axis=-1, keepdims=True) + EPSILON)
    hat = shifted * scale
    rows_hat_ref[...] = hat
    rows_scale_ref[...] = scale
    normed = hat * gain_in
    normed_t_ref[...] = normed.T.astype(BF16)
    normed = normed.astype(BF16)
    lane = lax.broadcasted_iota(jnp.int32, (tokens, count), 1)
    pick = jnp.where(lane == jnp.broadcast_to(items, (tokens, count)), 1.0, 0.0)
    pick = pick.astype(BF16)
    for part in range(4):
        columns = slice(part * width, (part + 1) * width)
        hidden = dot(normed, w_in_ref[:, columns])
        sigma = sigmoid(hidden)
        active = hidden * sigma
        slope = sigma * (1.0 + hidden * (1.0 - sigma))
        rows_slope_ref[:, columns] = slope.astype(BF16)
        if part == 0:
            high = active.astype(BF16)
            low = (active - high.astype(F32)).astype(BF16)
            gate_ref[...] = dot(pick, high) + dot(pick, low)
        else:
            qkv_ref[:, (part - 1) * width : part * width] = dot(pick, active.astype(BF16)).astype(
                BF16
            )
    mask = tile_mask()
    factor = HDIM ** (-0.5)
    for tile in range(tokens // TILE):
        rows = slice(tile * TILE, (tile + 1) * TILE)
        parts = []
        for head in range(HEADS):
            vals, queries, keys = (
                qkv_ref[rows, part * width + head * HDIM : part * width + (head + 1) * HDIM]
                for part in range(3)
            )
            score = dot(queries, keys, NT) * factor
            sigma = sigmoid(score)
            weight = jnp.where(mask, score * sigma, 0.0)
            slope = sigma * (1.0 + score * (1.0 - sigma)) * factor
            slope = jnp.where(mask, slope, 0.0)
            slope_ref[tile * HEADS + head] = slope.astype(BF16)
            slope_t_ref[tile * HEADS + head] = slope.T.astype(BF16)
            weight_t_ref[tile * HEADS + head] = weight.T.astype(BF16)
            parts.append(dot(weight.astype(BF16), vals))
        attended = jnp.concatenate(parts, axis=1)
        shifted = attended - jnp.mean(attended, axis=-1, keepdims=True)
        scale = lax.rsqrt(jnp.mean(shifted * shifted, axis=-1, keepdims=True) + EPSILON)
        hat = shifted * scale
        hat_ref[rows, :] = hat
        hat_scale_ref[rows, :] = scale
        mixed = hat * gain_out * gate_ref[rows, :]
        mixed_t_ref[:, rows] = mixed.T.astype(BF16)


def gather_of(items, count):
    tokens = items.shape[1]
    sub = lax.broadcasted_iota(jnp.int32, (count, tokens), 0)
    hit = sub == jnp.broadcast_to(items, (count, tokens))
    return jnp.where(hit, 1.0, 0.0).astype(BF16)


USED = (
    "w_out",
    "hat",
    "gate",
    "hat_scale",
    "qkv",
    "slope",
    "slope_t",
    "weight_t",
    "mixed_t",
    "normed_t",
    "rows_slope",
    "w_in",
    "rows_hat",
    "rows_scale",
    "place",
    "digits",
)


def backward_body(
    plan,
    table_size,
    factor,
    me_ref,
    dest_ref,
    blocks_ref,
    ints_ref,
    gains_ref,
    *refs,
):
    used, refs = dict(zip(USED, refs)), refs[len(USED) :]
    got_refs, (table_ref, *part_refs), (wide_ref, sums_ref, active_ref, grad_y_ref) = (
        refs[:-9],
        refs[-9:-4],
        refs[-4:],
    )
    w_out_ref, hat_ref, gate_ref, hat_scale_ref, qkv_ref, slope_ref, slope_t_ref = (
        used[name] for name in USED[:7]
    )
    weight_t_ref, mixed_t_ref, normed_t_ref, rows_slope_ref, w_in_ref = (
        used[name] for name in USED[7:12]
    )
    rows_hat_ref, rows_scale_ref, place_ref, digits_ref = (used[name] for name in USED[12:])
    for apart, got_ref in enumerate(got_refs):
        wide_ref[apart] = got_ref[...]
    for slot in range(len(got_refs)):
        rows = wide_ref[dest_ref[slot] ^ (me_ref[0] // table_size)]
        live = lax.broadcasted_iota(jnp.int32, rows.shape, 0) < blocks_ref[slot] * BLK
        rows = jnp.where(live, rows.astype(F32), 0.0).astype(BF16)
        grad_y_ref[slot * SLOT : (slot + 1) * SLOT, :] = rows
    tokens, width = grad_y_ref.shape
    count = normed_t_ref.shape[1]
    gain_in, gain_out = gains_ref[0:1, :], gains_ref[1:2, :]
    gain_total = jnp.zeros((1, width), F32)
    for tile in range(tokens // TILE):
        rows = slice(tile * TILE, (tile + 1) * TILE)
        grad_mixed = dot(grad_y_ref[rows, :], w_out_ref[...], NT)
        hat = hat_ref[rows, :]
        active_ref[rows, :width] = (grad_mixed * hat * gain_out).astype(BF16)
        inner = grad_mixed * gate_ref[rows, :]
        gain_total = gain_total + jnp.sum(inner * hat, axis=0, keepdims=True)
        inner = inner * gain_out
        mean = jnp.mean(inner, axis=-1, keepdims=True)
        along = jnp.mean(inner * hat, axis=-1, keepdims=True)
        grad_att = ((inner - mean - hat * along) * hat_scale_ref[rows, :]).astype(BF16)
        for head in range(HEADS):
            vals, queries, keys = (
                qkv_ref[rows, part * width + head * HDIM : part * width + (head + 1) * HDIM]
                for part in range(3)
            )
            grad_o = grad_att[:, head * HDIM : (head + 1) * HDIM]
            grad_weight = dot(grad_o, vals, NT)
            grad_score = (grad_weight * slope_ref[tile * HEADS + head].astype(F32)).astype(BF16)
            weight_t = dot(vals, grad_o, NT)
            score_t = (weight_t * slope_t_ref[tile * HEADS + head].astype(F32)).astype(BF16)
            for part, value in (
                (1, dot(weight_t_ref[tile * HEADS + head], grad_o)),
                (2, dot(grad_score, keys)),
                (3, dot(score_t, queries)),
            ):
                first = part * width + head * HDIM
                active_ref[rows, first : first + HDIM] = value.astype(BF16)
    sums_ref[:, :width] = (dot(mixed_t_ref[...], grad_y_ref[...]) * factor).astype(BF16)
    gather = gather_of(ints_ref[:, :tokens], count)
    grad_normed = jnp.zeros((count, width), F32)
    for part in range(4):
        columns = slice(part * width, (part + 1) * width)
        summed = dot(gather, active_ref[:, columns])
        grad_hidden = (summed * rows_slope_ref[:, columns].astype(F32)).astype(BF16)
        sums_ref[:, (part + 1) * width : (part + 2) * width] = (
            dot(normed_t_ref[...], grad_hidden) * factor
        ).astype(BF16)
        grad_normed = grad_normed + dot(grad_hidden, w_in_ref[:, columns], NT)
    hat = rows_hat_ref[...]
    gains = (jnp.sum(grad_normed * hat, axis=0, keepdims=True) * factor, gain_total * factor)
    plan.write(me_ref[0], sums_ref, part_refs)
    inner = grad_normed * gain_in
    mean = jnp.mean(inner, axis=-1, keepdims=True)
    along = jnp.mean(inner * hat, axis=-1, keepdims=True)
    row_grad = (inner - mean - hat * along) * rows_scale_ref[...] + dot(gather, grad_y_ref[...])
    places = table_ref.shape[0]
    spots = lax.broadcasted_iota(jnp.int32, (places, count), 0)
    hit = spots == jnp.broadcast_to(place_ref[...], (places, count))
    spread = jnp.where(hit, 1.0, 0.0).astype(BF16)
    table_ref[:, :width] = dot(spread, row_grad.astype(BF16)).astype(BF16)
    extra = plan.extra
    lanes = []
    for row in range(plan.capacity):
        first = row * plan.gain_lanes
        gain = gains[first // width][:, first % width : first % width + plan.gain_lanes]
        rest = extra - GAIN_AT - plan.gain_lanes
        row_parts = [jnp.zeros((1, GAIN_AT), F32), gain]
        lanes.append(jnp.concatenate(row_parts + [jnp.zeros((1, rest), F32)] * (rest > 0), axis=1))
    lanes = jnp.concatenate(lanes, axis=0).astype(BF16)
    repeat = lax.broadcasted_iota(jnp.int32, (places, plan.capacity), 0) % plan.capacity
    lane = lax.broadcasted_iota(jnp.int32, (places, plan.capacity), 1)
    repeat = jnp.where(repeat == lane, 1.0, 0.0).astype(BF16)
    table_ref[:, width:] = dot(repeat, lanes).astype(BF16)
    table_ref[:, width : width + LANES] += dot(spread, digits_ref[...]).astype(BF16)


class Plan:
    def __init__(self, dp_size, table_size, count, width):
        self.chunks = dp_size * table_size
        self.capacity = 2 * count // self.chunks
        self.row_groups = min(self.chunks, width // CHUNK_ROWS)
        self.column_groups = self.chunks // self.row_groups
        block = self.column_groups * LANES
        self.wide = -(-5 * width // block) * LANES
        self.gain_lanes = 2 * width // self.capacity
        self.extra = -(-(GAIN_AT + self.gain_lanes) // LANES) * LANES
        self.split = -(-self.wide // (2 * LANES)) * LANES
        self.sides = ((0, self.split), (self.split, self.wide - self.split))
        table_bits = [1 << bit for bit in range(1, table_size.bit_length() - 1)]
        dp_bits = [table_size << bit for bit in range(dp_size.bit_length() - 1)]
        self.near_steps = len(table_bits) + 1
        self.orders = (table_bits + dp_bits, dp_bits[:1] + table_bits + dp_bits[1:])

    def chunk_at(self, me, side, place):
        order = [1] + self.orders[side]
        mask = 0
        for step, bit in enumerate(order):
            if place >> (len(order) - 1 - step) & 1:
                mask ^= bit
        chunk = me ^ mask
        begin, size = self.sides[side]
        first = (chunk & (self.row_groups - 1)) * CHUNK_ROWS
        rows = pl.ds(pl.multiple_of(first, CHUNK_ROWS), CHUNK_ROWS)
        if self.column_groups == 1:
            return rows, slice(begin, begin + size)
        group = chunk >> (self.row_groups.bit_length() - 1)
        return rows, pl.ds(pl.multiple_of(group * self.wide + begin, LANES), size)

    def write(self, me, sums_ref, part_refs):
        half = self.chunks // 2
        for side in range(2):
            for place in range(self.chunks):
                out_ref = part_refs[2 * side + place // half]
                out_ref[place % half] = sums_ref[self.chunk_at(me, side, place)]

    def read(self, me, part_refs, sums_ref):
        half = self.chunks // 2
        for side in range(2):
            for place in range(self.chunks):
                in_ref = part_refs[2 * side + place // half]
                sums_ref[self.chunk_at(me, side, place)] = in_ref[place % half]


def table_body(plan, got_ref, out_ref, gain_in_ref, gain_out_ref):
    places, width = got_ref.shape[0], out_ref.shape[1]
    lane = lax.broadcasted_iota(jnp.int32, (16, LANES), 1)
    scale = jnp.where(lane == 0, 32.0, jnp.where(lane == 1, 1.0, 0.0)).astype(BF16)
    numbers = dot(scale, got_ref[:, width : width + LANES], NT)[0:1].astype(jnp.int32)
    step = 256
    for first in range(0, out_ref.shape[0], step):
        sub = lax.broadcasted_iota(jnp.int32, (step, places), 0) + first
        hit = jnp.where(sub == jnp.broadcast_to(numbers, (step, places)), 1.0, 0.0)
        out_ref[first : first + step, :] = dot(hit.astype(BF16), got_ref[:, :width])
    sub = lax.broadcasted_iota(jnp.int32, (16, places), 0)
    lane = lax.broadcasted_iota(jnp.int32, (16, places), 1) % plan.capacity
    total = dot(jnp.where(sub == lane, 1.0, 0.0).astype(BF16), got_ref[:, width:])
    for row in range(plan.capacity):
        first = row * plan.gain_lanes
        gain_ref = (gain_in_ref, gain_out_ref)[first // width]
        gain_ref[:, first % width : first % width + plan.gain_lanes] = total[
            row : row + 1, GAIN_AT : GAIN_AT + plan.gain_lanes
        ]


def widen_body(plan, me_ref, *refs):
    w_in_ref, w_out_ref, sums_ref = refs[4:]
    plan.read(me_ref[0], refs[:4], sums_ref)
    width = w_out_ref.shape[0]
    w_out_ref[...] = sums_ref[:, :width].astype(F32)
    w_in_ref[...] = sums_ref[:, width : 5 * width].astype(F32)


def add(left, right):
    return (left.astype(F32) + right.astype(F32)).astype(BF16)


def on_device(
    touched_rows,
    row_of_token,
    row_owner,
    owner_row,
    seq_blocks,
    seq_dest,
    grad_out,
    w_in,
    w_out,
    gain_in,
    gain_out,
):
    dp_size, table_size = lax.axis_size("dp"), lax.axis_size("table")
    both = ("dp", "table")
    count, width = touched_rows.shape
    tokens = row_of_token.shape[0]
    plan = Plan(dp_size, table_size, count, width)
    devices_all = plan.chunks
    total_factor = 1.0 / math.sqrt(grad_out.shape[0] * devices_all)
    gain_rows = jnp.stack([gain_in, gain_out])
    ints = jnp.concatenate([row_of_token, row_owner[:, 0], owner_row])[None, :]
    me = lax.axis_index(both).astype(jnp.int32)[None]

    def swap(values, mask):
        return lax.ppermute(values, both, [(here, here ^ mask) for here in range(devices_all)])

    def exchange(values, axes, groups):
        return lax.all_to_all(
            values, axes, split_axis=0, concat_axis=0, tiled=True, axis_index_groups=groups
        )

    peers = jnp.arange(dp_size, dtype=jnp.int32)
    own = jnp.sum(jnp.where(seq_dest[:, None] == peers, seq_blocks[:, None], 0), axis=0)
    lengths = jnp.where(peers[:, None] == lax.axis_index("dp"), own, 0)
    for bit in range(dp_size.bit_length() - 1):
        lengths = lengths + swap(lengths, table_size << bit)
    send = call(
        functools.partial(send_body, table_size),
        [shape_of((SLOT, width), BF16)] * dp_size,
        [SMEM] * 2 + [VMEM],
        scratch=[pltpu.SMEM((dp_size,), jnp.int32)],
    )(me, lengths, grad_out)
    got = list(send)
    far = [apart for apart in range(1, dp_size) if 2 * apart >= dp_size]
    for apart in far:
        got[apart] = swap(send[apart], apart * table_size)
    *near, ints = lax.optimization_barrier((*send[: far[0]], ints))

    shapes = saved_shapes(tokens, count, width)
    saved = call(
        functools.partial(forward_body, plan.capacity),
        [shapes[name] for name in SAVED],
        [VMEM] * 4,
        flops=4 * count * width * width * 20,
        moved=10_000_000,
        mebibytes=12 + tokens // 32,
    )(
        touched_rows,
        w_in,
        gain_rows,
        ints,
    )
    *near, gate = lax.optimization_barrier((*near, saved[0]))
    saved = [gate, *saved[1:]]
    got[0] = near[0]
    for apart in range(1, far[0]):
        got[apart] = swap(near[apart], apart * table_size)
    saved = dict(zip(SAVED, saved), w_in=w_in, w_out=w_out)
    outs = [shape_of((devices_all * plan.capacity, width + plan.extra), BF16)]
    for _, wide in plan.sides:
        outs += [shape_of((devices_all // 2, CHUNK_ROWS, wide), BF16)] * 2
    table_send, *parts = call(
        functools.partial(backward_body, plan, table_size, total_factor),
        outs,
        [SMEM] * 3 + [VMEM] * (2 + len(USED) + dp_size),
        flops=4 * count * width * width * 40,
        moved=12_000_000,
        mebibytes=12 + tokens // 32,
        scratch=[
            pltpu.VMEM((dp_size, SLOT, width), BF16),
            pltpu.VMEM((width, plan.column_groups * plan.wide), BF16),
            pltpu.VMEM((tokens, 4 * width), BF16),
            pltpu.VMEM((tokens, width), BF16),
        ],
    )(
        me,
        seq_dest,
        seq_blocks,
        ints,
        gain_rows,
        *(saved[name] for name in USED),
        *got,
    )

    def reduced(kept, mask):
        middle = kept.shape[0] // 2
        return add(kept[:middle], swap(kept[middle:], mask))

    def gathered(kept, mask):
        return jnp.concatenate([kept, swap(kept, mask)])

    low = min(2, dp_size)
    high, inside = dp_size // low, low * table_size
    groups = [[upper * low + lower for upper in range(high)] for lower in range(low)]
    table_got = exchange(table_send.reshape(high, inside, plan.capacity, -1), "dp", groups)
    sides = [add(parts[2 * side], swap(parts[2 * side + 1], 1)) for side in range(2)]
    for step in range(plan.near_steps):
        sides = [reduced(sides[side], plan.orders[side][step]) for side in range(2)]
    kept = jnp.concatenate(sides, axis=2)
    kept, table_got = lax.optimization_barrier((kept, table_got))
    groups = [[upper * inside + lower for lower in range(inside)] for upper in range(high)]
    table_got = exchange(jnp.swapaxes(table_got, 0, 1), both, groups)
    table_part, grad_gain_in, grad_gain_out = call(
        functools.partial(table_body, plan),
        (
            shape_of((ROWS_DEV, width), F32),
            shape_of((1, width), F32),
            shape_of((1, width), F32),
        ),
        [VMEM],
    )(table_got.reshape(devices_all * plan.capacity, -1))
    for mask in plan.orders[0][plan.near_steps :]:
        kept = reduced(kept, mask)
    for mask in reversed(plan.orders[0][plan.near_steps :]):
        kept = gathered(kept, mask)
    kept, table_part = lax.optimization_barrier((kept, table_part))
    sides = [kept[..., : plan.split], kept[..., plan.split :]]
    for step in reversed(range(plan.near_steps)):
        sides = [gathered(sides[side], plan.orders[side][step]) for side in range(2)]
    grad_w_in, grad_w_out = call(
        functools.partial(widen_body, plan),
        (shape_of(w_in.shape, F32), shape_of(w_out.shape, F32)),
        [SMEM] + [VMEM] * 4,
        scratch=[pltpu.VMEM((width, plan.column_groups * plan.wide), BF16)],
    )(me, sides[0], swap(sides[0], 1), sides[1], swap(sides[1], 1))
    return (table_part, grad_w_in, grad_w_out, grad_gain_in[0], grad_gain_out[0])


def solution(mesh):
    rows = P(("dp", "table"), None)
    flat = P(("dp", "table"))
    in_specs = (rows, flat, rows, flat, flat, flat, rows, P(), P(), P(), P())
    out_specs = (rows, P(), P(), P(), P())
    return jax.shard_map(
        on_device, mesh=mesh, in_specs=in_specs, out_specs=out_specs, check_vma=False
    )
```

```python
import functools
import math

import jax
import jax.numpy as jnp
from jax import lax
from jax.experimental import pallas as pl
from jax.experimental.pallas import tpu as pltpu
from jax.sharding import PartitionSpec as P

HEADS = 4
HDIM = 128
BLK = 16
LMAXB = 4
SLOT = LMAXB * BLK
ROWS_DEV = 1024
TILE = 2 * SLOT
LANES = 128
CHUNK_ROWS = 16
GAIN_AT = 64
EPSILON = 1e-05
F32 = jnp.float32
BF16 = jnp.bfloat16
VMEM = pl.BlockSpec(memory_space=pltpu.VMEM)
SMEM = pl.BlockSpec(memory_space=pltpu.SMEM)


def call(body, out_shape, in_specs, flops=0, moved=0, scratch=(), mebibytes=24):
    outs = jax.tree.map(lambda _: VMEM, out_shape)
    return pl.pallas_call(
        body,
        out_shape=out_shape,
        in_specs=in_specs,
        out_specs=outs,
        scratch_shapes=scratch,
        compiler_params=pltpu.CompilerParams(vmem_limit_bytes=mebibytes * 1024 * 1024),
        cost_estimate=pl.CostEstimate(flops=flops, bytes_accessed=moved, transcendentals=0),
    )


def shape_of(dims, dtype):
    return jax.ShapeDtypeStruct(dims, dtype)


def sigmoid(values):
    return 0.5 * jnp.tanh(0.5 * values) + 0.5


def dot(left, right, contract=((1,), (0,))):
    return lax.dot_general(left, right, (contract, ((), ())), preferred_element_type=F32)


NT = ((1,), (1,))
TN = ((0,), (0,))


def send_body(table_size, me_ref, lengths_ref, grad_ref, *refs):
    out_refs, begin_ref = refs[:-1], refs[-1]
    peers = len(out_refs)
    blocks = grad_ref.shape[0] // BLK
    me = me_ref[0] // table_size
    begin = jnp.int32(0)
    for peer in range(peers):
        begin_ref[peer] = begin
        begin = begin + lengths_ref[peer, me]
    for apart, out_ref in enumerate(out_refs):
        begin = begin_ref[me ^ apart]
        for inner in range(LMAXB):
            block = jnp.minimum(begin + inner, blocks - 1)
            rows = grad_ref[pl.ds(pl.multiple_of(block * BLK, BLK), BLK), :]
            out_ref[inner * BLK : (inner + 1) * BLK, :] = rows


def tile_mask():
    sub = lax.broadcasted_iota(jnp.int32, (TILE, TILE), 0)
    lane = lax.broadcasted_iota(jnp.int32, (TILE, TILE), 1)
    return (sub // SLOT == lane // SLOT) & (lane <= sub)


SAVED = (
    "gate",
    "hat",
    "hat_scale",
    "qkv",
    "slope",
    "slope_t",
    "weight_t",
    "mixed_t",
    "normed_t",
    "rows_slope",
    "rows_hat",
    "rows_scale",
    "place",
    "digits",
)


def saved_shapes(tokens, count, width):
    pairs = tokens // TILE * HEADS
    return dict(
        gate=shape_of((tokens, width), F32),
        hat=shape_of((tokens, width), F32),
        hat_scale=shape_of((tokens, 1), F32),
        qkv=shape_of((tokens, 3 * width), BF16),
        slope=shape_of((pairs, TILE, TILE), BF16),
        slope_t=shape_of((pairs, TILE, TILE), BF16),
        weight_t=shape_of((pairs, TILE, TILE), BF16),
        mixed_t=shape_of((width, tokens), BF16),
        normed_t=shape_of((width, count), BF16),
        rows_slope=shape_of((count, 4 * width), BF16),
        rows_hat=shape_of((count, width), F32),
        rows_scale=shape_of((count, 1), F32),
        place=shape_of((1, count), jnp.int32),
        digits=shape_of((count, LANES), BF16),
    )


def forward_body(
    capacity,
    rows_ref,
    w_in_ref,
    gains_ref,
    ints_ref,
    *refs,
):
    held = dict(zip(SAVED, refs))
    gate_ref, hat_ref, hat_scale_ref, qkv_ref, slope_ref, slope_t_ref = (
        held[name] for name in SAVED[:6]
    )
    weight_t_ref, mixed_t_ref, normed_t_ref, rows_slope_ref = (held[name] for name in SAVED[6:10])
    rows_hat_ref, rows_scale_ref, place_ref, digits_ref = (held[name] for name in SAVED[10:])
    count, width = rows_ref.shape
    tokens = ints_ref.shape[1] - 2 * count
    gain_in, gain_out = gains_ref[0:1, :], gains_ref[1:2, :]
    columns = jnp.broadcast_to(ints_ref[...].astype(F32), (8, ints_ref.shape[1])).T
    columns = columns[:, 0:1].astype(jnp.int32)
    items, owners, numbers = (
        columns[:tokens],
        columns[tokens : tokens + count],
        columns[tokens + count :],
    )
    owner_row = ints_ref[:, tokens : tokens + count]
    across = jnp.broadcast_to(owner_row, (count, count))
    down = jnp.broadcast_to(owners, (count, count))
    sub = lax.broadcasted_iota(jnp.int32, (count, count), 0)
    lane = lax.broadcasted_iota(jnp.int32, (count, count), 1)
    earlier = jnp.where((across == down) & (sub < lane), 1.0, 0.0)
    rank = jnp.sum(earlier, axis=0, keepdims=True).astype(jnp.int32)
    place_ref[...] = owner_row * capacity + rank
    number = jnp.broadcast_to(numbers, (count, LANES))
    lane = lax.broadcasted_iota(jnp.int32, (count, LANES), 1)
    digits = jnp.where(lane == 0, number >> 5, jnp.where(lane == 1, number & 31, 0))
    digits_ref[...] = digits.astype(F32).astype(BF16)
    values = rows_ref[...].astype(F32)
    shifted = values - jnp.mean(values, axis=-1, keepdims=True)
    scale = lax.rsqrt(jnp.mean(shifted * shifted, axis=-1, keepdims=True) + EPSILON)
    hat = shifted * scale
    rows_hat_ref[...] = hat
    rows_scale_ref[...] = scale
    normed = hat * gain_in
    normed_t_ref[...] = normed.T.astype(BF16)
    normed = normed.astype(BF16)
    lane = lax.broadcasted_iota(jnp.int32, (tokens, count), 1)
    pick = jnp.where(lane == jnp.broadcast_to(items, (tokens, count)), 1.0, 0.0)
    pick = pick.astype(BF16)
    for part in range(4):
        columns = slice(part * width, (part + 1) * width)
        hidden = dot(normed, w_in_ref[:, columns])
        sigma = sigmoid(hidden)
        active = hidden * sigma
        slope = sigma * (1.0 + hidden * (1.0 - sigma))
        rows_slope_ref[:, columns] = slope.astype(BF16)
        if part == 0:
            high = active.astype(BF16)
            low = (active - high.astype(F32)).astype(BF16)
            gate_ref[...] = dot(pick, high) + dot(pick, low)
        else:
            qkv_ref[:, (part - 1) * width : part * width] = dot(pick, active.astype(BF16)).astype(
                BF16
            )
    mask = tile_mask()
    factor = HDIM ** (-0.5)
    for tile in range(tokens // TILE):
        rows = slice(tile * TILE, (tile + 1) * TILE)
        parts = []
        for head in range(HEADS):
            vals, queries, keys = (
                qkv_ref[rows, part * width + head * HDIM : part * width + (head + 1) * HDIM]
                for part in range(3)
            )
            score = dot(queries, keys, NT) * factor
            sigma = sigmoid(score)
            weight = jnp.where(mask, score * sigma, 0.0)
            slope = sigma * (1.0 + score * (1.0 - sigma)) * factor
            slope = jnp.where(mask, slope, 0.0)
            slope_ref[tile * HEADS + head] = slope.astype(BF16)
            slope_t_ref[tile * HEADS + head] = slope.T.astype(BF16)
            weight_t_ref[tile * HEADS + head] = weight.T.astype(BF16)
            parts.append(dot(weight.astype(BF16), vals))
        attended = jnp.concatenate(parts, axis=1)
        shifted = attended - jnp.mean(attended, axis=-1, keepdims=True)
        scale = lax.rsqrt(jnp.mean(shifted * shifted, axis=-1, keepdims=True) + EPSILON)
        hat = shifted * scale
        hat_ref[rows, :] = hat
        hat_scale_ref[rows, :] = scale
        mixed = hat * gain_out * gate_ref[rows, :]
        mixed_t_ref[:, rows] = mixed.T.astype(BF16)


def gather_of(items, count):
    tokens = items.shape[1]
    sub = lax.broadcasted_iota(jnp.int32, (count, tokens), 0)
    hit = sub == jnp.broadcast_to(items, (count, tokens))
    return jnp.where(hit, 1.0, 0.0).astype(BF16)


USED = (
    "w_out",
    "hat",
    "gate",
    "hat_scale",
    "qkv",
    "slope",
    "slope_t",
    "weight_t",
    "mixed_t",
    "normed_t",
    "rows_slope",
    "w_in",
    "rows_hat",
    "rows_scale",
    "place",
    "digits",
)


def backward_body(
    plan,
    table_size,
    factor,
    me_ref,
    dest_ref,
    blocks_ref,
    ints_ref,
    gains_ref,
    *refs,
):
    used, refs = dict(zip(USED, refs)), refs[len(USED) :]
    got_refs, (table_ref, *part_refs), (wide_ref, sums_ref, active_ref, grad_y_ref) = (
        refs[:-9],
        refs[-9:-4],
        refs[-4:],
    )
    w_out_ref, hat_ref, gate_ref, hat_scale_ref, qkv_ref, slope_ref, slope_t_ref = (
        used[name] for name in USED[:7]
    )
    weight_t_ref, mixed_t_ref, normed_t_ref, rows_slope_ref, w_in_ref = (
        used[name] for name in USED[7:12]
    )
    rows_hat_ref, rows_scale_ref, place_ref, digits_ref = (used[name] for name in USED[12:])
    for apart, got_ref in enumerate(got_refs):
        wide_ref[apart] = got_ref[...]
    for slot in range(len(got_refs)):
        rows = wide_ref[dest_ref[slot] ^ (me_ref[0] // table_size)]
        live = lax.broadcasted_iota(jnp.int32, rows.shape, 0) < blocks_ref[slot] * BLK
        rows = jnp.where(live, rows.astype(F32), 0.0).astype(BF16)
        grad_y_ref[slot * SLOT : (slot + 1) * SLOT, :] = rows
    tokens, width = grad_y_ref.shape
    count = normed_t_ref.shape[1]
    gain_in, gain_out = gains_ref[0:1, :], gains_ref[1:2, :]
    gain_total = jnp.zeros((1, width), F32)
    for tile in range(tokens // TILE):
        rows = slice(tile * TILE, (tile + 1) * TILE)
        grad_mixed = dot(grad_y_ref[rows, :], w_out_ref[...], NT)
        hat = hat_ref[rows, :]
        active_ref[rows, :width] = (grad_mixed * hat * gain_out).astype(BF16)
        inner = grad_mixed * gate_ref[rows, :]
        gain_total = gain_total + jnp.sum(inner * hat, axis=0, keepdims=True)
        inner = inner * gain_out
        mean = jnp.mean(inner, axis=-1, keepdims=True)
        along = jnp.mean(inner * hat, axis=-1, keepdims=True)
        grad_att = ((inner - mean - hat * along) * hat_scale_ref[rows, :]).astype(BF16)
        for head in range(HEADS):
            vals, queries, keys = (
                qkv_ref[rows, part * width + head * HDIM : part * width + (head + 1) * HDIM]
                for part in range(3)
            )
            grad_o = grad_att[:, head * HDIM : (head + 1) * HDIM]
            grad_weight = dot(grad_o, vals, NT)
            grad_score = (grad_weight * slope_ref[tile * HEADS + head].astype(F32)).astype(BF16)
            weight_t = dot(vals, grad_o, NT)
            score_t = (weight_t * slope_t_ref[tile * HEADS + head].astype(F32)).astype(BF16)
            for part, value in (
                (1, dot(weight_t_ref[tile * HEADS + head], grad_o)),
                (2, dot(grad_score, keys)),
                (3, dot(score_t, queries)),
            ):
                first = part * width + head * HDIM
                active_ref[rows, first : first + HDIM] = value.astype(BF16)
    sums_ref[:, :width] = (dot(mixed_t_ref[...], grad_y_ref[...]) * factor).astype(BF16)
    gather = gather_of(ints_ref[:, :tokens], count)
    grad_normed = jnp.zeros((count, width), F32)
    for part in range(4):
        columns = slice(part * width, (part + 1) * width)
        summed = dot(gather, active_ref[:, columns])
        grad_hidden = (summed * rows_slope_ref[:, columns].astype(F32)).astype(BF16)
        sums_ref[:, (part + 1) * width : (part + 2) * width] = (
            dot(normed_t_ref[...], grad_hidden) * factor
        ).astype(BF16)
        grad_normed = grad_normed + dot(grad_hidden, w_in_ref[:, columns], NT)
    hat = rows_hat_ref[...]
    gains = (jnp.sum(grad_normed * hat, axis=0, keepdims=True) * factor, gain_total * factor)
    plan.write(me_ref[0], sums_ref, part_refs)
    inner = grad_normed * gain_in
    mean = jnp.mean(inner, axis=-1, keepdims=True)
    along = jnp.mean(inner * hat, axis=-1, keepdims=True)
    row_grad = (inner - mean - hat * along) * rows_scale_ref[...] + dot(gather, grad_y_ref[...])
    places = table_ref.shape[0]
    spots = lax.broadcasted_iota(jnp.int32, (places, count), 0)
    hit = spots == jnp.broadcast_to(place_ref[...], (places, count))
    spread = jnp.where(hit, 1.0, 0.0).astype(BF16)
    table_ref[:, :width] = dot(spread, row_grad.astype(BF16)).astype(BF16)
    extra = plan.extra
    lanes = []
    for row in range(plan.capacity):
        first = row * plan.gain_lanes
        gain = gains[first // width][:, first % width : first % width + plan.gain_lanes]
        rest = extra - GAIN_AT - plan.gain_lanes
        row_parts = [jnp.zeros((1, GAIN_AT), F32), gain]
        lanes.append(jnp.concatenate(row_parts + [jnp.zeros((1, rest), F32)] * (rest > 0), axis=1))
    lanes = jnp.concatenate(lanes, axis=0).astype(BF16)
    repeat = lax.broadcasted_iota(jnp.int32, (places, plan.capacity), 0) % plan.capacity
    lane = lax.broadcasted_iota(jnp.int32, (places, plan.capacity), 1)
    repeat = jnp.where(repeat == lane, 1.0, 0.0).astype(BF16)
    table_ref[:, width:] = dot(repeat, lanes).astype(BF16)
    table_ref[:, width : width + LANES] += dot(spread, digits_ref[...]).astype(BF16)


class Plan:
    def __init__(self, dp_size, table_size, count, width):
        self.chunks = dp_size * table_size
        self.capacity = 2 * count // self.chunks
        self.row_groups = min(self.chunks, width // CHUNK_ROWS)
        self.column_groups = self.chunks // self.row_groups
        block = self.column_groups * LANES
        self.wide = -(-5 * width // block) * LANES
        self.gain_lanes = 2 * width // self.capacity
        self.extra = -(-(GAIN_AT + self.gain_lanes) // LANES) * LANES
        self.split = -(-self.wide // (2 * LANES)) * LANES
        self.sides = ((0, self.split), (self.split, self.wide - self.split))
        table_bits = [1 << bit for bit in range(1, table_size.bit_length() - 1)]
        dp_bits = [table_size << bit for bit in range(dp_size.bit_length() - 1)]
        self.near_steps = len(table_bits) + 1
        self.orders = (table_bits + dp_bits, dp_bits[:1] + table_bits + dp_bits[1:])

    def chunk_at(self, me, side, place):
        order = [1] + self.orders[side]
        mask = 0
        for step, bit in enumerate(order):
            if place >> (len(order) - 1 - step) & 1:
                mask ^= bit
        chunk = me ^ mask
        begin, size = self.sides[side]
        first = (chunk & (self.row_groups - 1)) * CHUNK_ROWS
        rows = pl.ds(pl.multiple_of(first, CHUNK_ROWS), CHUNK_ROWS)
        if self.column_groups == 1:
            return rows, slice(begin, begin + size)
        group = chunk >> (self.row_groups.bit_length() - 1)
        return rows, pl.ds(pl.multiple_of(group * self.wide + begin, LANES), size)

    def write(self, me, sums_ref, part_refs):
        half = self.chunks // 2
        for side in range(2):
            for place in range(self.chunks):
                out_ref = part_refs[2 * side + place // half]
                out_ref[place % half] = sums_ref[self.chunk_at(me, side, place)]

    def read(self, me, part_refs, sums_ref):
        half = self.chunks // 2
        for side in range(2):
            for place in range(self.chunks):
                in_ref = part_refs[2 * side + place // half]
                sums_ref[self.chunk_at(me, side, place)] = in_ref[place % half]


def table_body(plan, got_ref, out_ref, gain_in_ref, gain_out_ref):
    places, width = got_ref.shape[0], out_ref.shape[1]
    lane = lax.broadcasted_iota(jnp.int32, (16, LANES), 1)
    scale = jnp.where(lane == 0, 32.0, jnp.where(lane == 1, 1.0, 0.0)).astype(BF16)
    numbers = dot(scale, got_ref[:, width : width + LANES], NT)[0:1].astype(jnp.int32)
    step = 256
    for first in range(0, out_ref.shape[0], step):
        sub = lax.broadcasted_iota(jnp.int32, (step, places), 0) + first
        hit = jnp.where(sub == jnp.broadcast_to(numbers, (step, places)), 1.0, 0.0)
        out_ref[first : first + step, :] = dot(hit.astype(BF16), got_ref[:, :width])
    sub = lax.broadcasted_iota(jnp.int32, (16, places), 0)
    lane = lax.broadcasted_iota(jnp.int32, (16, places), 1) % plan.capacity
    total = dot(jnp.where(sub == lane, 1.0, 0.0).astype(BF16), got_ref[:, width:])
    for row in range(plan.capacity):
        first = row * plan.gain_lanes
        gain_ref = (gain_in_ref, gain_out_ref)[first // width]
        gain_ref[:, first % width : first % width + plan.gain_lanes] = total[
            row : row + 1, GAIN_AT : GAIN_AT + plan.gain_lanes
        ]


def widen_body(plan, me_ref, *refs):
    w_in_ref, w_out_ref, sums_ref = refs[4:]
    plan.read(me_ref[0], refs[:4], sums_ref)
    width = w_out_ref.shape[0]
    w_out_ref[...] = sums_ref[:, :width].astype(F32)
    w_in_ref[...] = sums_ref[:, width : 5 * width].astype(F32)


def add(left, right):
    return (left.astype(F32) + right.astype(F32)).astype(BF16)


def on_device(
    touched_rows,
    row_of_token,
    row_owner,
    owner_row,
    seq_blocks,
    seq_dest,
    grad_out,
    w_in,
    w_out,
    gain_in,
    gain_out,
):
    dp_size, table_size = lax.axis_size("dp"), lax.axis_size("table")
    both = ("dp", "table")
    count, width = touched_rows.shape
    tokens = row_of_token.shape[0]
    plan = Plan(dp_size, table_size, count, width)
    devices_all = plan.chunks
    total_factor = 1.0 / math.sqrt(grad_out.shape[0] * devices_all)
    gain_rows = jnp.stack([gain_in, gain_out])
    ints = jnp.concatenate([row_of_token, row_owner[:, 0], owner_row])[None, :]
    me = lax.axis_index(both).astype(jnp.int32)[None]

    def swap(values, mask):
        return lax.ppermute(values, both, [(here, here ^ mask) for here in range(devices_all)])

    def exchange(values, axes, groups):
        return lax.all_to_all(
            values, axes, split_axis=0, concat_axis=0, tiled=True, axis_index_groups=groups
        )

    peers = jnp.arange(dp_size, dtype=jnp.int32)
    own = jnp.sum(jnp.where(seq_dest[:, None] == peers, seq_blocks[:, None], 0), axis=0)
    lengths = jnp.where(peers[:, None] == lax.axis_index("dp"), own, 0)
    for bit in range(dp_size.bit_length() - 1):
        lengths = lengths + swap(lengths, table_size << bit)
    send = call(
        functools.partial(send_body, table_size),
        [shape_of((SLOT, width), BF16)] * dp_size,
        [SMEM] * 2 + [VMEM],
        scratch=[pltpu.SMEM((dp_size,), jnp.int32)],
    )(me, lengths, grad_out)
    got = list(send)
    for apart in reversed(range(1, dp_size)):
        got[apart] = swap(send[apart], apart * table_size)
    got[0], ints = lax.optimization_barrier((got[0], ints))

    shapes = saved_shapes(tokens, count, width)
    saved = call(
        functools.partial(forward_body, plan.capacity),
        [shapes[name] for name in SAVED],
        [VMEM] * 4,
        flops=4 * count * width * width * 20,
        moved=10_000_000,
        mebibytes=12 + tokens // 32,
    )(
        touched_rows,
        w_in,
        gain_rows,
        ints,
    )
    saved = dict(zip(SAVED, saved), w_in=w_in, w_out=w_out)
    outs = [shape_of((devices_all * plan.capacity, width + plan.extra), BF16)]
    for _, wide in plan.sides:
        outs += [shape_of((devices_all // 2, CHUNK_ROWS, wide), BF16)] * 2
    table_send, *parts = call(
        functools.partial(backward_body, plan, table_size, total_factor),
        outs,
        [SMEM] * 3 + [VMEM] * (2 + len(USED) + dp_size),
        flops=4 * count * width * width * 40,
        moved=12_000_000,
        mebibytes=12 + tokens // 32,
        scratch=[
            pltpu.VMEM((dp_size, SLOT, width), BF16),
            pltpu.VMEM((width, plan.column_groups * plan.wide), BF16),
            pltpu.VMEM((tokens, 4 * width), BF16),
            pltpu.VMEM((tokens, width), BF16),
        ],
    )(
        me,
        seq_dest,
        seq_blocks,
        ints,
        gain_rows,
        *(saved[name] for name in USED),
        *got,
    )

    def reduced(kept, mask):
        middle = kept.shape[0] // 2
        return add(kept[:middle], swap(kept[middle:], mask))

    def gathered(kept, mask):
        return jnp.concatenate([kept, swap(kept, mask)])

    low = min(2, dp_size)
    high, inside = dp_size // low, low * table_size
    groups = [[upper * low + lower for upper in range(high)] for lower in range(low)]
    table_got = exchange(table_send.reshape(high, inside, plan.capacity, -1), "dp", groups)
    sides = [add(parts[2 * side], swap(parts[2 * side + 1], 1)) for side in range(2)]
    for step in range(plan.near_steps):
        sides = [reduced(sides[side], plan.orders[side][step]) for side in range(2)]
    kept = jnp.concatenate(sides, axis=2)
    kept, table_got = lax.optimization_barrier((kept, table_got))
    groups = [[upper * inside + lower for lower in range(inside)] for upper in range(high)]
    table_got = exchange(jnp.swapaxes(table_got, 0, 1), both, groups)
    for mask in plan.orders[0][plan.near_steps :]:
        kept = reduced(kept, mask)
    back = plan.orders[0][: plan.near_steps - 1 : -1]
    kept = gathered(kept, back[0])
    kept, table_got = lax.optimization_barrier((kept, table_got))
    table_part, grad_gain_in, grad_gain_out = call(
        functools.partial(table_body, plan),
        (
            shape_of((ROWS_DEV, width), F32),
            shape_of((1, width), F32),
            shape_of((1, width), F32),
        ),
        [VMEM],
    )(table_got.reshape(devices_all * plan.capacity, -1))
    for mask in back[1:]:
        kept = gathered(kept, mask)
    kept, table_part = lax.optimization_barrier((kept, table_part))
    sides = [kept[..., : plan.split], kept[..., plan.split :]]
    for step in reversed(range(plan.near_steps)):
        sides = [gathered(sides[side], plan.orders[side][step]) for side in range(2)]
    grad_w_in, grad_w_out = call(
        functools.partial(widen_body, plan),
        (shape_of(w_in.shape, F32), shape_of(w_out.shape, F32)),
        [SMEM] + [VMEM] * 4,
        scratch=[pltpu.VMEM((width, plan.column_groups * plan.wide), BF16)],
    )(me, sides[0], swap(sides[0], 1), sides[1], swap(sides[1], 1))
    return (table_part, grad_w_in, grad_w_out, grad_gain_in[0], grad_gain_out[0])


def solution(mesh):
    rows = P(("dp", "table"), None)
    flat = P(("dp", "table"))
    in_specs = (rows, flat, rows, flat, flat, flat, rows, P(), P(), P(), P())
    out_specs = (rows, P(), P(), P(), P())
    return jax.shard_map(
        on_device, mesh=mesh, in_specs=in_specs, out_specs=out_specs, check_vma=False
    )
```

```python
import functools
import math

import jax
import jax.numpy as jnp
from jax import lax
from jax.experimental import pallas as pl
from jax.experimental.pallas import tpu as pltpu
from jax.sharding import PartitionSpec as P

HEADS = 4
HDIM = 128
BLK = 16
LMAXB = 4
SLOT = LMAXB * BLK
ROWS_DEV = 1024
TILE = 2 * SLOT
LANES = 128
CHUNK_ROWS = 16
GAIN_AT = 64
EPSILON = 1e-05
F32 = jnp.float32
BF16 = jnp.bfloat16
VMEM = pl.BlockSpec(memory_space=pltpu.VMEM)
SMEM = pl.BlockSpec(memory_space=pltpu.SMEM)


def call(body, out_shape, in_specs, flops=0, moved=0, scratch=(), mebibytes=24):
    outs = jax.tree.map(lambda _: VMEM, out_shape)
    return pl.pallas_call(
        body,
        out_shape=out_shape,
        in_specs=in_specs,
        out_specs=outs,
        scratch_shapes=scratch,
        compiler_params=pltpu.CompilerParams(vmem_limit_bytes=mebibytes * 1024 * 1024),
        cost_estimate=pl.CostEstimate(flops=flops, bytes_accessed=moved, transcendentals=0),
    )


def shape_of(dims, dtype):
    return jax.ShapeDtypeStruct(dims, dtype)


def sigmoid(values):
    return 0.5 * jnp.tanh(0.5 * values) + 0.5


def dot(left, right, contract=((1,), (0,))):
    return lax.dot_general(left, right, (contract, ((), ())), preferred_element_type=F32)


NT = ((1,), (1,))
TN = ((0,), (0,))


def send_body(table_size, count, me_ref, lengths_ref, rows_ref, *refs):
    out_refs, begin_ref = refs[:-1], refs[-1]
    peers = len(out_refs)
    blocks = (rows_ref.shape[0] - count) // BLK
    me = me_ref[0] // table_size
    begin = jnp.int32(0)
    for peer in range(peers):
        begin_ref[peer] = begin
        begin = begin + lengths_ref[peer, me]
    for apart, out_ref in enumerate(out_refs):
        begin = begin_ref[me ^ apart]
        for inner in range(LMAXB):
            block = jnp.minimum(begin + inner, blocks - 1)
            rows = rows_ref[pl.ds(pl.multiple_of(count + block * BLK, BLK), BLK), :]
            out_ref[inner * BLK : (inner + 1) * BLK, :] = rows


def tile_mask():
    sub = lax.broadcasted_iota(jnp.int32, (TILE, TILE), 0)
    lane = lax.broadcasted_iota(jnp.int32, (TILE, TILE), 1)
    return (sub // SLOT == lane // SLOT) & (lane <= sub)


def row_shapes(count, width):
    return dict(
        rows_active=shape_of((count, 5 * width), BF16),
        normed_t=shape_of((width, count), BF16),
        rows_slope=shape_of((count, 4 * width), BF16),
        rows_hat=shape_of((count, width), F32),
        rows_scale=shape_of((count, 1), F32),
        place=shape_of((1, count), jnp.int32),
        digits=shape_of((count, LANES), BF16),
    )


def token_shapes(tokens, width):
    pairs = tokens // TILE * HEADS
    return dict(
        gate=shape_of((tokens, width), F32),
        hat=shape_of((tokens, width), F32),
        hat_scale=shape_of((tokens, 1), F32),
        qkv=shape_of((tokens, 3 * width), BF16),
        slope=shape_of((pairs, TILE, TILE), BF16),
        slope_t=shape_of((pairs, TILE, TILE), BF16),
        weight_t=shape_of((pairs, TILE, TILE), BF16),
        mixed_t=shape_of((width, tokens), BF16),
    )


def column_of(row):
    wide = jnp.broadcast_to(row.astype(F32), (8, row.shape[1])).T
    return wide[:, 0:1].astype(jnp.int32)


def rows_body(
    capacity,
    rows_ref,
    weights_ref,
    gains_ref,
    ints_ref,
    rows_active_ref,
    normed_t_ref,
    rows_slope_ref,
    rows_hat_ref,
    rows_scale_ref,
    place_ref,
    digits_ref,
):
    count, width = rows_hat_ref.shape
    tokens = ints_ref.shape[1] - 2 * count
    owner_row = ints_ref[:, tokens : tokens + count]
    across = jnp.broadcast_to(owner_row, (count, count))
    down = jnp.broadcast_to(column_of(owner_row), (count, count))
    sub = lax.broadcasted_iota(jnp.int32, (count, count), 0)
    lane = lax.broadcasted_iota(jnp.int32, (count, count), 1)
    earlier = jnp.where((across == down) & (sub < lane), 1.0, 0.0)
    rank = jnp.sum(earlier, axis=0, keepdims=True).astype(jnp.int32)
    place_ref[...] = owner_row * capacity + rank
    number = jnp.broadcast_to(column_of(ints_ref[:, tokens + count :]), (count, LANES))
    lane = lax.broadcasted_iota(jnp.int32, (count, LANES), 1)
    digits = jnp.where(lane == 0, number >> 5, jnp.where(lane == 1, number & 31, 0))
    digits_ref[...] = digits.astype(F32).astype(BF16)
    values = rows_ref[:count, :].astype(F32)
    shifted = values - jnp.mean(values, axis=-1, keepdims=True)
    scale = lax.rsqrt(jnp.mean(shifted * shifted, axis=-1, keepdims=True) + EPSILON)
    hat = shifted * scale
    rows_hat_ref[...] = hat
    rows_scale_ref[...] = scale
    normed = hat * gains_ref[0:1, :]
    normed_t_ref[...] = normed.T.astype(BF16)
    normed = normed.astype(BF16)
    for part in range(4):
        columns = slice(part * width, (part + 1) * width)
        hidden = dot(normed, weights_ref[:, columns])
        sigma = sigmoid(hidden)
        active = hidden * sigma
        slope = sigma * (1.0 + hidden * (1.0 - sigma))
        rows_slope_ref[:, columns] = slope.astype(BF16)
        high = active.astype(BF16)
        rows_active_ref[:, columns] = high
        if part == 0:
            rows_active_ref[:, 4 * width :] = (active - high.astype(F32)).astype(BF16)


def forward_body(
    rows_active_ref,
    gains_ref,
    ints_ref,
    gate_ref,
    hat_ref,
    hat_scale_ref,
    qkv_ref,
    slope_ref,
    slope_t_ref,
    weight_t_ref,
    mixed_t_ref,
):
    count = rows_active_ref.shape[0]
    tokens, width = gate_ref.shape
    items = column_of(ints_ref[:, :tokens])
    lane = lax.broadcasted_iota(jnp.int32, (tokens, count), 1)
    pick = jnp.where(lane == jnp.broadcast_to(items, (tokens, count)), 1.0, 0.0).astype(BF16)
    gate_ref[...] = dot(pick, rows_active_ref[:, :width]) + dot(
        pick, rows_active_ref[:, 4 * width :]
    )
    for part in range(3):
        columns = slice((part + 1) * width, (part + 2) * width)
        qkv_ref[:, part * width : (part + 1) * width] = dot(pick, rows_active_ref[:, columns]).astype(
            BF16
        )
    gain_out = gains_ref[1:2, :]
    mask = tile_mask()
    factor = HDIM ** (-0.5)
    for tile in range(tokens // TILE):
        rows = slice(tile * TILE, (tile + 1) * TILE)
        parts = []
        for head in range(HEADS):
            vals, queries, keys = (
                qkv_ref[rows, part * width + head * HDIM : part * width + (head + 1) * HDIM]
                for part in range(3)
            )
            score = dot(queries, keys, NT) * factor
            sigma = sigmoid(score)
            weight = jnp.where(mask, score * sigma, 0.0)
            slope = sigma * (1.0 + score * (1.0 - sigma)) * factor
            slope = jnp.where(mask, slope, 0.0)
            slope_ref[tile * HEADS + head] = slope.astype(BF16)
            slope_t_ref[tile * HEADS + head] = slope.T.astype(BF16)
            weight_t_ref[tile * HEADS + head] = weight.T.astype(BF16)
            parts.append(dot(weight.astype(BF16), vals))
        attended = jnp.concatenate(parts, axis=1)
        shifted = attended - jnp.mean(attended, axis=-1, keepdims=True)
        scale = lax.rsqrt(jnp.mean(shifted * shifted, axis=-1, keepdims=True) + EPSILON)
        hat = shifted * scale
        hat_ref[rows, :] = hat
        hat_scale_ref[rows, :] = scale
        mixed = hat * gain_out * gate_ref[rows, :]
        mixed_t_ref[:, rows] = mixed.T.astype(BF16)


def gather_of(items, count):
    tokens = items.shape[1]
    sub = lax.broadcasted_iota(jnp.int32, (count, tokens), 0)
    hit = sub == jnp.broadcast_to(items, (count, tokens))
    return jnp.where(hit, 1.0, 0.0).astype(BF16)


USED = (
    "weights",
    "hat",
    "gate",
    "hat_scale",
    "qkv",
    "slope",
    "slope_t",
    "weight_t",
    "mixed_t",
    "normed_t",
    "rows_slope",
    "rows_hat",
    "rows_scale",
    "place",
    "digits",
)


def backward_body(
    plan,
    table_size,
    factor,
    me_ref,
    dest_ref,
    blocks_ref,
    ints_ref,
    gains_ref,
    *refs,
):
    used, refs = dict(zip(USED, refs)), refs[len(USED) :]
    got_refs, (table_ref, *part_refs), (wide_ref, sums_ref, active_ref, grad_y_ref) = (
        refs[:-9],
        refs[-9:-4],
        refs[-4:],
    )
    weights_ref, hat_ref, gate_ref, hat_scale_ref, qkv_ref, slope_ref, slope_t_ref = (
        used[name] for name in USED[:7]
    )
    weight_t_ref, mixed_t_ref, normed_t_ref, rows_slope_ref = (used[name] for name in USED[7:11])
    rows_hat_ref, rows_scale_ref, place_ref, digits_ref = (used[name] for name in USED[11:])
    for apart, got_ref in enumerate(got_refs):
        wide_ref[apart] = got_ref[...]
    for slot in range(len(got_refs)):
        rows = wide_ref[dest_ref[slot] ^ (me_ref[0] // table_size)]
        live = lax.broadcasted_iota(jnp.int32, rows.shape, 0) < blocks_ref[slot] * BLK
        rows = jnp.where(live, rows.astype(F32), 0.0).astype(BF16)
        grad_y_ref[slot * SLOT : (slot + 1) * SLOT, :] = rows
    tokens, width = grad_y_ref.shape
    count = normed_t_ref.shape[1]
    gain_in, gain_out = gains_ref[0:1, :], gains_ref[1:2, :]
    gain_total = jnp.zeros((1, width), F32)
    for tile in range(tokens // TILE):
        rows = slice(tile * TILE, (tile + 1) * TILE)
        grad_mixed = dot(grad_y_ref[rows, :], weights_ref[:, 4 * width :], NT)
        hat = hat_ref[rows, :]
        active_ref[rows, :width] = (grad_mixed * hat * gain_out).astype(BF16)
        inner = grad_mixed * gate_ref[rows, :]
        gain_total = gain_total + jnp.sum(inner * hat, axis=0, keepdims=True)
        inner = inner * gain_out
        mean = jnp.mean(inner, axis=-1, keepdims=True)
        along = jnp.mean(inner * hat, axis=-1, keepdims=True)
        grad_att = ((inner - mean - hat * along) * hat_scale_ref[rows, :]).astype(BF16)
        for head in range(HEADS):
            vals, queries, keys = (
                qkv_ref[rows, part * width + head * HDIM : part * width + (head + 1) * HDIM]
                for part in range(3)
            )
            grad_o = grad_att[:, head * HDIM : (head + 1) * HDIM]
            grad_weight = dot(grad_o, vals, NT)
            grad_score = (grad_weight * slope_ref[tile * HEADS + head].astype(F32)).astype(BF16)
            weight_t = dot(vals, grad_o, NT)
            score_t = (weight_t * slope_t_ref[tile * HEADS + head].astype(F32)).astype(BF16)
            for part, value in (
                (1, dot(weight_t_ref[tile * HEADS + head], grad_o)),
                (2, dot(grad_score, keys)),
                (3, dot(score_t, queries)),
            ):
                first = part * width + head * HDIM
                active_ref[rows, first : first + HDIM] = value.astype(BF16)
    sums_ref[:, :width] = (dot(mixed_t_ref[...], grad_y_ref[...]) * factor).astype(BF16)
    gather = gather_of(ints_ref[:, :tokens], count)
    grad_normed = jnp.zeros((count, width), F32)
    for part in range(4):
        columns = slice(part * width, (part + 1) * width)
        summed = dot(gather, active_ref[:, columns])
        grad_hidden = (summed * rows_slope_ref[:, columns].astype(F32)).astype(BF16)
        sums_ref[:, (part + 1) * width : (part + 2) * width] = (
            dot(normed_t_ref[...], grad_hidden) * factor
        ).astype(BF16)
        grad_normed = grad_normed + dot(grad_hidden, weights_ref[:, columns], NT)
    hat = rows_hat_ref[...]
    gains = (jnp.sum(grad_normed * hat, axis=0, keepdims=True) * factor, gain_total * factor)
    plan.write(me_ref[0], sums_ref, part_refs)
    inner = grad_normed * gain_in
    mean = jnp.mean(inner, axis=-1, keepdims=True)
    along = jnp.mean(inner * hat, axis=-1, keepdims=True)
    row_grad = (inner - mean - hat * along) * rows_scale_ref[...] + dot(gather, grad_y_ref[...])
    places = table_ref.shape[0]
    spots = lax.broadcasted_iota(jnp.int32, (places, count), 0)
    hit = spots == jnp.broadcast_to(place_ref[...], (places, count))
    spread = jnp.where(hit, 1.0, 0.0).astype(BF16)
    table_ref[:, :width] = dot(spread, row_grad.astype(BF16)).astype(BF16)
    extra = plan.extra
    lanes = []
    for row in range(plan.capacity):
        first = row * plan.gain_lanes
        gain = gains[first // width][:, first % width : first % width + plan.gain_lanes]
        rest = extra - GAIN_AT - plan.gain_lanes
        row_parts = [jnp.zeros((1, GAIN_AT), F32), gain]
        lanes.append(jnp.concatenate(row_parts + [jnp.zeros((1, rest), F32)] * (rest > 0), axis=1))
    lanes = jnp.concatenate(lanes, axis=0).astype(BF16)
    repeat = lax.broadcasted_iota(jnp.int32, (places, plan.capacity), 0) % plan.capacity
    lane = lax.broadcasted_iota(jnp.int32, (places, plan.capacity), 1)
    repeat = jnp.where(repeat == lane, 1.0, 0.0).astype(BF16)
    table_ref[:, width:] = dot(repeat, lanes).astype(BF16)
    table_ref[:, width : width + LANES] += dot(spread, digits_ref[...]).astype(BF16)


class Plan:
    def __init__(self, dp_size, table_size, count, width):
        self.chunks = dp_size * table_size
        self.capacity = 2 * count // self.chunks
        self.row_groups = min(self.chunks, width // CHUNK_ROWS)
        self.column_groups = self.chunks // self.row_groups
        block = self.column_groups * LANES
        self.wide = -(-5 * width // block) * LANES
        self.gain_lanes = 2 * width // self.capacity
        self.extra = -(-(GAIN_AT + self.gain_lanes) // LANES) * LANES
        self.split = -(-self.wide // (2 * LANES)) * LANES
        self.sides = ((0, self.split), (self.split, self.wide - self.split))
        table_bits = [1 << bit for bit in range(1, table_size.bit_length() - 1)]
        dp_bits = [table_size << bit for bit in range(dp_size.bit_length() - 1)]
        self.near_steps = len(table_bits) + 1
        self.orders = (table_bits + dp_bits, dp_bits[:1] + table_bits + dp_bits[1:])

    def chunk_at(self, me, side, place):
        order = [1] + self.orders[side]
        mask = 0
        for step, bit in enumerate(order):
            if place >> (len(order) - 1 - step) & 1:
                mask ^= bit
        chunk = me ^ mask
        begin, size = self.sides[side]
        first = (chunk & (self.row_groups - 1)) * CHUNK_ROWS
        rows = pl.ds(pl.multiple_of(first, CHUNK_ROWS), CHUNK_ROWS)
        if self.column_groups == 1:
            return rows, slice(begin, begin + size)
        group = chunk >> (self.row_groups.bit_length() - 1)
        return rows, pl.ds(pl.multiple_of(group * self.wide + begin, LANES), size)

    def write(self, me, sums_ref, part_refs):
        half = self.chunks // 2
        for side in range(2):
            for place in range(self.chunks):
                out_ref = part_refs[2 * side + place // half]
                out_ref[place % half] = sums_ref[self.chunk_at(me, side, place)]

    def read(self, me, part_refs, sums_ref):
        half = self.chunks // 2
        for side in range(2):
            for place in range(self.chunks):
                in_ref = part_refs[2 * side + place // half]
                sums_ref[self.chunk_at(me, side, place)] = in_ref[place % half]


def table_body(plan, got_ref, out_ref, gain_in_ref, gain_out_ref):
    places, width = got_ref.shape[0], out_ref.shape[1]
    lane = lax.broadcasted_iota(jnp.int32, (16, LANES), 1)
    scale = jnp.where(lane == 0, 32.0, jnp.where(lane == 1, 1.0, 0.0)).astype(BF16)
    numbers = dot(scale, got_ref[:, width : width + LANES], NT)[0:1].astype(jnp.int32)
    step = 256
    for first in range(0, out_ref.shape[0], step):
        sub = lax.broadcasted_iota(jnp.int32, (step, places), 0) + first
        hit = jnp.where(sub == jnp.broadcast_to(numbers, (step, places)), 1.0, 0.0)
        out_ref[first : first + step, :] = dot(hit.astype(BF16), got_ref[:, :width])
    sub = lax.broadcasted_iota(jnp.int32, (16, places), 0)
    lane = lax.broadcasted_iota(jnp.int32, (16, places), 1) % plan.capacity
    total = dot(jnp.where(sub == lane, 1.0, 0.0).astype(BF16), got_ref[:, width:])
    for row in range(plan.capacity):
        first = row * plan.gain_lanes
        gain_ref = (gain_in_ref, gain_out_ref)[first // width]
        gain_ref[:, first % width : first % width + plan.gain_lanes] = total[
            row : row + 1, GAIN_AT : GAIN_AT + plan.gain_lanes
        ]


def widen_body(plan, me_ref, *refs):
    w_in_ref, w_out_ref, sums_ref = refs[4:]
    plan.read(me_ref[0], refs[:4], sums_ref)
    width = w_out_ref.shape[0]
    w_out_ref[...] = sums_ref[:, :width].astype(F32)
    w_in_ref[...] = sums_ref[:, width : 5 * width].astype(F32)


def add(left, right):
    return (left.astype(F32) + right.astype(F32)).astype(BF16)


def on_device(
    touched_rows,
    row_of_token,
    row_owner,
    owner_row,
    seq_blocks,
    seq_dest,
    grad_out,
    w_in,
    w_out,
    gain_in,
    gain_out,
):
    dp_size, table_size = lax.axis_size("dp"), lax.axis_size("table")
    both = ("dp", "table")
    count, width = touched_rows.shape
    tokens = row_of_token.shape[0]
    plan = Plan(dp_size, table_size, count, width)
    devices_all = plan.chunks
    total_factor = 1.0 / math.sqrt(grad_out.shape[0] * devices_all)
    gain_rows = jnp.stack([gain_in, gain_out])
    rows = jnp.concatenate([touched_rows, grad_out])
    weights = jnp.concatenate([w_in, w_out], axis=1)
    ints = jnp.concatenate([row_of_token, row_owner[:, 0], owner_row])[None, :]
    me = lax.axis_index(both).astype(jnp.int32)[None]

    def swap(values, mask):
        return lax.ppermute(values, both, [(here, here ^ mask) for here in range(devices_all)])

    def exchange(values, axes, groups):
        return lax.all_to_all(
            values, axes, split_axis=0, concat_axis=0, tiled=True, axis_index_groups=groups
        )

    peers = jnp.arange(dp_size, dtype=jnp.int32)
    own = jnp.sum(jnp.where(seq_dest[:, None] == peers, seq_blocks[:, None], 0), axis=0)
    lengths = jnp.where(peers[:, None] == lax.axis_index("dp"), own, 0)
    for bit in range(dp_size.bit_length() - 1):
        lengths = lengths + swap(lengths, table_size << bit)
    send = call(
        functools.partial(send_body, table_size, count),
        [shape_of((SLOT, width), BF16)] * dp_size,
        [SMEM] * 2 + [VMEM],
        scratch=[pltpu.SMEM((dp_size,), jnp.int32)],
    )(me, lengths, rows)
    got = list(send)
    for apart in reversed(range(1, dp_size)):
        got[apart] = swap(send[apart], apart * table_size)
    shapes = row_shapes(count, width)
    made = call(
        functools.partial(rows_body, plan.capacity),
        list(shapes.values()),
        [VMEM] * 4,
        flops=8 * count * width * width,
        moved=4_000_000,
    )(rows, weights, gain_rows, ints)
    saved = dict(zip(shapes, made), weights=weights)
    got[0], after = lax.optimization_barrier((got[0], ints))
    shapes = token_shapes(tokens, width)
    made = call(
        forward_body,
        list(shapes.values()),
        [VMEM] * 3,
        flops=4 * count * width * width * 10,
        moved=8_000_000,
        mebibytes=12 + tokens // 32,
    )(saved["rows_active"], gain_rows, after)
    saved |= dict(zip(shapes, made))

    outs = [shape_of((devices_all * plan.capacity, width + plan.extra), BF16)]
    for _, wide in plan.sides:
        outs += [shape_of((devices_all // 2, CHUNK_ROWS, wide), BF16)] * 2
    table_send, *parts = call(
        functools.partial(backward_body, plan, table_size, total_factor),
        outs,
        [SMEM] * 3 + [VMEM] * (2 + len(USED) + dp_size),
        flops=4 * count * width * width * 40,
        moved=12_000_000,
        mebibytes=12 + tokens // 32,
        scratch=[
            pltpu.VMEM((dp_size, SLOT, width), BF16),
            pltpu.VMEM((width, plan.column_groups * plan.wide), BF16),
            pltpu.VMEM((tokens, 4 * width), BF16),
            pltpu.VMEM((tokens, width), BF16),
        ],
    )(
        me,
        seq_dest,
        seq_blocks,
        ints,
        gain_rows,
        *(saved[name] for name in USED),
        *got,
    )

    def reduced(kept, mask):
        middle = kept.shape[0] // 2
        return add(kept[:middle], swap(kept[middle:], mask))

    def gathered(kept, mask):
        return jnp.concatenate([kept, swap(kept, mask)])

    sides = [add(parts[2 * side], swap(parts[2 * side + 1], 1)) for side in range(2)]
    *sides, table_send = lax.optimization_barrier((*sides, table_send))
    low = min(2, dp_size)
    high, inside = dp_size // low, low * table_size
    groups = [[upper * low + lower for upper in range(high)] for lower in range(low)]
    table_got = exchange(table_send.reshape(high, inside, plan.capacity, -1), "dp", groups)
    for step in range(plan.near_steps):
        sides = [reduced(sides[side], plan.orders[side][step]) for side in range(2)]
    kept = jnp.concatenate(sides, axis=2)
    kept, table_got = lax.optimization_barrier((kept, table_got))
    groups = [[upper * inside + lower for lower in range(inside)] for upper in range(high)]
    table_got = exchange(jnp.swapaxes(table_got, 0, 1), both, groups)
    for mask in plan.orders[0][plan.near_steps :]:
        kept = reduced(kept, mask)
    back = plan.orders[0][: plan.near_steps - 1 : -1]
    kept = gathered(kept, back[0])
    kept, table_got = lax.optimization_barrier((kept, table_got))
    table_part, grad_gain_in, grad_gain_out = call(
        functools.partial(table_body, plan),
        (
            shape_of((ROWS_DEV, width), F32),
            shape_of((1, width), F32),
            shape_of((1, width), F32),
        ),
        [VMEM],
    )(table_got.reshape(devices_all * plan.capacity, -1))
    for mask in back[1:]:
        kept = gathered(kept, mask)
    kept, table_part = lax.optimization_barrier((kept, table_part))
    sides = [kept[..., : plan.split], kept[..., plan.split :]]
    for step in reversed(range(plan.near_steps)):
        sides = [gathered(sides[side], plan.orders[side][step]) for side in range(2)]
    grad_w_in, grad_w_out = call(
        functools.partial(widen_body, plan),
        (shape_of(w_in.shape, F32), shape_of(w_out.shape, F32)),
        [SMEM] + [VMEM] * 4,
        scratch=[pltpu.VMEM((width, plan.column_groups * plan.wide), BF16)],
    )(me, sides[0], swap(sides[0], 1), sides[1], swap(sides[1], 1))
    return (table_part, grad_w_in, grad_w_out, grad_gain_in[0], grad_gain_out[0])


def solution(mesh):
    rows = P(("dp", "table"), None)
    flat = P(("dp", "table"))
    in_specs = (rows, flat, rows, flat, flat, flat, rows, P(), P(), P(), P())
    out_specs = (rows, P(), P(), P(), P())
    return jax.shard_map(
        on_device, mesh=mesh, in_specs=in_specs, out_specs=out_specs, check_vma=False
    )
```

```python
import functools
import math

import jax
import jax.numpy as jnp
from jax import lax
from jax.experimental import pallas as pl
from jax.experimental.pallas import tpu as pltpu
from jax.sharding import PartitionSpec as P

HEADS = 4
HDIM = 128
BLK = 16
LMAXB = 4
SLOT = LMAXB * BLK
ROWS_DEV = 1024
TILE = 2 * SLOT
LANES = 128
CHUNK_ROWS = 16
GAIN_AT = 64
EPSILON = 1e-05
F32 = jnp.float32
BF16 = jnp.bfloat16
VMEM = pl.BlockSpec(memory_space=pltpu.VMEM)
SMEM = pl.BlockSpec(memory_space=pltpu.SMEM)


def call(body, out_shape, in_specs, flops=0, moved=0, scratch=(), mebibytes=24):
    outs = jax.tree.map(lambda _: VMEM, out_shape)
    return pl.pallas_call(
        body,
        out_shape=out_shape,
        in_specs=in_specs,
        out_specs=outs,
        scratch_shapes=scratch,
        compiler_params=pltpu.CompilerParams(vmem_limit_bytes=mebibytes * 1024 * 1024),
        cost_estimate=pl.CostEstimate(flops=flops, bytes_accessed=moved, transcendentals=0),
    )


def shape_of(dims, dtype):
    return jax.ShapeDtypeStruct(dims, dtype)


def sigmoid(values):
    return 0.5 * jnp.tanh(0.5 * values) + 0.5


def dot(left, right, contract=((1,), (0,))):
    return lax.dot_general(left, right, (contract, ((), ())), preferred_element_type=F32)


NT = ((1,), (1,))
TN = ((0,), (0,))


def send_body(table_size, count, me_ref, lengths_ref, rows_ref, *refs):
    out_refs, begin_ref = refs[:-1], refs[-1]
    peers = len(out_refs)
    blocks = (rows_ref.shape[0] - count) // BLK
    me = me_ref[0] // table_size
    begin = jnp.int32(0)
    for peer in range(peers):
        begin_ref[peer] = begin
        begin = begin + lengths_ref[peer, me]
    for apart, out_ref in enumerate(out_refs):
        begin = begin_ref[me ^ apart]
        for inner in range(LMAXB):
            block = jnp.minimum(begin + inner, blocks - 1)
            rows = rows_ref[pl.ds(pl.multiple_of(count + block * BLK, BLK), BLK), :]
            out_ref[inner * BLK : (inner + 1) * BLK, :] = rows


def tile_mask():
    sub = lax.broadcasted_iota(jnp.int32, (TILE, TILE), 0)
    lane = lax.broadcasted_iota(jnp.int32, (TILE, TILE), 1)
    return (sub // SLOT == lane // SLOT) & (lane <= sub)


def row_shapes(count, width):
    return dict(
        rows_active=shape_of((count, 5 * width), BF16),
        normed_t=shape_of((width, count), BF16),
        rows_slope=shape_of((count, 4 * width), BF16),
        rows_hat=shape_of((count, width), F32),
        rows_scale=shape_of((count, 1), F32),
        place=shape_of((1, count), jnp.int32),
        digits=shape_of((count, LANES), BF16),
    )


def token_shapes(tokens, width):
    pairs = tokens // TILE * HEADS
    return dict(
        gate=shape_of((tokens, width), F32),
        hat=shape_of((tokens, width), F32),
        hat_scale=shape_of((tokens, 1), F32),
        qkv=shape_of((tokens, 3 * width), BF16),
        slope=shape_of((pairs, TILE, TILE), BF16),
        slope_t=shape_of((pairs, TILE, TILE), BF16),
        weight_t=shape_of((pairs, TILE, TILE), BF16),
        mixed_t=shape_of((width, tokens), BF16),
    )


def column_of(row):
    wide = jnp.broadcast_to(row.astype(F32), (8, row.shape[1])).T
    return wide[:, 0:1].astype(jnp.int32)


def rows_body(
    capacity,
    rows_ref,
    weights_ref,
    gains_ref,
    ints_ref,
    rows_active_ref,
    normed_t_ref,
    rows_slope_ref,
    rows_hat_ref,
    rows_scale_ref,
    place_ref,
    digits_ref,
):
    count, width = rows_hat_ref.shape
    tokens = ints_ref.shape[1] - 2 * count
    owner_row = ints_ref[:, tokens : tokens + count]
    across = jnp.broadcast_to(owner_row, (count, count))
    down = jnp.broadcast_to(column_of(owner_row), (count, count))
    sub = lax.broadcasted_iota(jnp.int32, (count, count), 0)
    lane = lax.broadcasted_iota(jnp.int32, (count, count), 1)
    earlier = jnp.where((across == down) & (sub < lane), 1.0, 0.0)
    rank = jnp.sum(earlier, axis=0, keepdims=True).astype(jnp.int32)
    place_ref[...] = owner_row * capacity + rank
    number = jnp.broadcast_to(column_of(ints_ref[:, tokens + count :]), (count, LANES))
    lane = lax.broadcasted_iota(jnp.int32, (count, LANES), 1)
    digits = jnp.where(lane == 0, number >> 5, jnp.where(lane == 1, number & 31, 0))
    digits_ref[...] = digits.astype(F32).astype(BF16)
    values = rows_ref[:count, :].astype(F32)
    shifted = values - jnp.mean(values, axis=-1, keepdims=True)
    scale = lax.rsqrt(jnp.mean(shifted * shifted, axis=-1, keepdims=True) + EPSILON)
    hat = shifted * scale
    rows_hat_ref[...] = hat
    rows_scale_ref[...] = scale
    normed = hat * gains_ref[0:1, :]
    normed_t_ref[...] = normed.T.astype(BF16)
    normed = normed.astype(BF16)
    for part in range(4):
        columns = slice(part * width, (part + 1) * width)
        hidden = dot(normed, weights_ref[:, columns])
        sigma = sigmoid(hidden)
        active = hidden * sigma
        slope = sigma * (1.0 + hidden * (1.0 - sigma))
        rows_slope_ref[:, columns] = slope.astype(BF16)
        high = active.astype(BF16)
        rows_active_ref[:, columns] = high
        if part == 0:
            rows_active_ref[:, 4 * width :] = (active - high.astype(F32)).astype(BF16)


def forward_body(
    rows_active_ref,
    gains_ref,
    ints_ref,
    gate_ref,
    hat_ref,
    hat_scale_ref,
    qkv_ref,
    slope_ref,
    slope_t_ref,
    weight_t_ref,
    mixed_t_ref,
):
    count = rows_active_ref.shape[0]
    tokens, width = gate_ref.shape
    items = column_of(ints_ref[:, :tokens])
    lane = lax.broadcasted_iota(jnp.int32, (tokens, count), 1)
    pick = jnp.where(lane == jnp.broadcast_to(items, (tokens, count)), 1.0, 0.0).astype(BF16)
    gate_ref[...] = dot(pick, rows_active_ref[:, :width]) + dot(
        pick, rows_active_ref[:, 4 * width :]
    )
    for part in range(3):
        columns = slice((part + 1) * width, (part + 2) * width)
        qkv_ref[:, part * width : (part + 1) * width] = dot(pick, rows_active_ref[:, columns]).astype(
            BF16
        )
    gain_out = gains_ref[1:2, :]
    mask = tile_mask()
    factor = HDIM ** (-0.5)
    for tile in range(tokens // TILE):
        rows = slice(tile * TILE, (tile + 1) * TILE)
        parts = []
        for head in range(HEADS):
            vals, queries, keys = (
                qkv_ref[rows, part * width + head * HDIM : part * width + (head + 1) * HDIM]
                for part in range(3)
            )
            score = dot(queries, keys, NT) * factor
            sigma = sigmoid(score)
            weight = jnp.where(mask, score * sigma, 0.0)
            slope = sigma * (1.0 + score * (1.0 - sigma)) * factor
            slope = jnp.where(mask, slope, 0.0)
            slope_ref[tile * HEADS + head] = slope.astype(BF16)
            slope_t_ref[tile * HEADS + head] = slope.T.astype(BF16)
            weight_t_ref[tile * HEADS + head] = weight.T.astype(BF16)
            parts.append(dot(weight.astype(BF16), vals))
        attended = jnp.concatenate(parts, axis=1)
        shifted = attended - jnp.mean(attended, axis=-1, keepdims=True)
        scale = lax.rsqrt(jnp.mean(shifted * shifted, axis=-1, keepdims=True) + EPSILON)
        hat = shifted * scale
        hat_ref[rows, :] = hat
        hat_scale_ref[rows, :] = scale
        mixed = hat * gain_out * gate_ref[rows, :]
        mixed_t_ref[:, rows] = mixed.T.astype(BF16)


def gather_of(items, count):
    tokens = items.shape[1]
    sub = lax.broadcasted_iota(jnp.int32, (count, tokens), 0)
    hit = sub == jnp.broadcast_to(items, (count, tokens))
    return jnp.where(hit, 1.0, 0.0).astype(BF16)


USED = (
    "weights",
    "hat",
    "gate",
    "hat_scale",
    "qkv",
    "slope",
    "slope_t",
    "weight_t",
    "mixed_t",
    "normed_t",
    "rows_slope",
    "rows_hat",
    "rows_scale",
    "place",
    "digits",
)


def backward_body(
    plan,
    table_size,
    factor,
    me_ref,
    dest_ref,
    blocks_ref,
    ints_ref,
    gains_ref,
    *refs,
):
    used, refs = dict(zip(USED, refs)), refs[len(USED) :]
    got_refs, (table_ref, *part_refs), (wide_ref, sums_ref, active_ref, grad_y_ref) = (
        refs[:-9],
        refs[-9:-4],
        refs[-4:],
    )
    weights_ref, hat_ref, gate_ref, hat_scale_ref, qkv_ref, slope_ref, slope_t_ref = (
        used[name] for name in USED[:7]
    )
    weight_t_ref, mixed_t_ref, normed_t_ref, rows_slope_ref = (used[name] for name in USED[7:11])
    rows_hat_ref, rows_scale_ref, place_ref, digits_ref = (used[name] for name in USED[11:])
    for apart, got_ref in enumerate(got_refs):
        wide_ref[apart] = got_ref[...]
    for slot in range(len(got_refs)):
        rows = wide_ref[dest_ref[slot] ^ (me_ref[0] // table_size)]
        live = lax.broadcasted_iota(jnp.int32, rows.shape, 0) < blocks_ref[slot] * BLK
        rows = jnp.where(live, rows.astype(F32), 0.0).astype(BF16)
        grad_y_ref[slot * SLOT : (slot + 1) * SLOT, :] = rows
    tokens, width = grad_y_ref.shape
    count = normed_t_ref.shape[1]
    gain_in, gain_out = gains_ref[0:1, :], gains_ref[1:2, :]
    gain_total = jnp.zeros((1, width), F32)
    for tile in range(tokens // TILE):
        rows = slice(tile * TILE, (tile + 1) * TILE)
        grad_mixed = dot(grad_y_ref[rows, :], weights_ref[:, 4 * width :], NT)
        hat = hat_ref[rows, :]
        active_ref[rows, :width] = (grad_mixed * hat * gain_out).astype(BF16)
        inner = grad_mixed * gate_ref[rows, :]
        gain_total = gain_total + jnp.sum(inner * hat, axis=0, keepdims=True)
        inner = inner * gain_out
        mean = jnp.mean(inner, axis=-1, keepdims=True)
        along = jnp.mean(inner * hat, axis=-1, keepdims=True)
        grad_att = ((inner - mean - hat * along) * hat_scale_ref[rows, :]).astype(BF16)
        for head in range(HEADS):
            vals, queries, keys = (
                qkv_ref[rows, part * width + head * HDIM : part * width + (head + 1) * HDIM]
                for part in range(3)
            )
            grad_o = grad_att[:, head * HDIM : (head + 1) * HDIM]
            grad_weight = dot(grad_o, vals, NT)
            grad_score = (grad_weight * slope_ref[tile * HEADS + head].astype(F32)).astype(BF16)
            weight_t = dot(vals, grad_o, NT)
            score_t = (weight_t * slope_t_ref[tile * HEADS + head].astype(F32)).astype(BF16)
            for part, value in (
                (1, dot(weight_t_ref[tile * HEADS + head], grad_o)),
                (2, dot(grad_score, keys)),
                (3, dot(score_t, queries)),
            ):
                first = part * width + head * HDIM
                active_ref[rows, first : first + HDIM] = value.astype(BF16)
    sums_ref[:, :width] = (dot(mixed_t_ref[...], grad_y_ref[...]) * factor).astype(BF16)
    gather = gather_of(ints_ref[:, :tokens], count)
    grad_normed = jnp.zeros((count, width), F32)
    for part in range(4):
        columns = slice(part * width, (part + 1) * width)
        summed = dot(gather, active_ref[:, columns])
        grad_hidden = (summed * rows_slope_ref[:, columns].astype(F32)).astype(BF16)
        sums_ref[:, (part + 1) * width : (part + 2) * width] = (
            dot(normed_t_ref[...], grad_hidden) * factor
        ).astype(BF16)
        grad_normed = grad_normed + dot(grad_hidden, weights_ref[:, columns], NT)
    hat = rows_hat_ref[...]
    gains = (jnp.sum(grad_normed * hat, axis=0, keepdims=True) * factor, gain_total * factor)
    plan.write(me_ref[0], sums_ref, part_refs)
    inner = grad_normed * gain_in
    mean = jnp.mean(inner, axis=-1, keepdims=True)
    along = jnp.mean(inner * hat, axis=-1, keepdims=True)
    row_grad = (inner - mean - hat * along) * rows_scale_ref[...] + dot(gather, grad_y_ref[...])
    places = table_ref.shape[0]
    spots = lax.broadcasted_iota(jnp.int32, (places, count), 0)
    hit = spots == jnp.broadcast_to(place_ref[...], (places, count))
    spread = jnp.where(hit, 1.0, 0.0).astype(BF16)
    table_ref[:, :width] = dot(spread, row_grad.astype(BF16)).astype(BF16)
    extra = plan.extra
    lanes = []
    for row in range(plan.capacity):
        first = row * plan.gain_lanes
        gain = gains[first // width][:, first % width : first % width + plan.gain_lanes]
        rest = extra - GAIN_AT - plan.gain_lanes
        row_parts = [jnp.zeros((1, GAIN_AT), F32), gain]
        lanes.append(jnp.concatenate(row_parts + [jnp.zeros((1, rest), F32)] * (rest > 0), axis=1))
    lanes = jnp.concatenate(lanes, axis=0).astype(BF16)
    repeat = lax.broadcasted_iota(jnp.int32, (places, plan.capacity), 0) % plan.capacity
    lane = lax.broadcasted_iota(jnp.int32, (places, plan.capacity), 1)
    repeat = jnp.where(repeat == lane, 1.0, 0.0).astype(BF16)
    table_ref[:, width:] = dot(repeat, lanes).astype(BF16)
    table_ref[:, width : width + LANES] += dot(spread, digits_ref[...]).astype(BF16)


class Plan:
    def __init__(self, dp_size, table_size, count, width):
        self.chunks = dp_size * table_size
        self.capacity = 2 * count // self.chunks
        self.row_groups = min(self.chunks, width // CHUNK_ROWS)
        self.column_groups = self.chunks // self.row_groups
        block = self.column_groups * LANES
        self.wide = -(-5 * width // block) * LANES
        self.gain_lanes = 2 * width // self.capacity
        self.extra = -(-(GAIN_AT + self.gain_lanes) // LANES) * LANES
        self.split = -(-self.wide // (2 * LANES)) * LANES
        self.sides = ((0, self.split), (self.split, self.wide - self.split))
        table_bits = [1 << bit for bit in range(1, table_size.bit_length() - 1)]
        dp_bits = [table_size << bit for bit in range(dp_size.bit_length() - 1)]
        self.near_steps = len(table_bits) + 1
        self.orders = (table_bits + dp_bits, dp_bits[:1] + table_bits + dp_bits[1:])

    def chunk_at(self, me, side, place):
        order = [1] + self.orders[side]
        mask = 0
        for step, bit in enumerate(order):
            if place >> (len(order) - 1 - step) & 1:
                mask ^= bit
        chunk = me ^ mask
        begin, size = self.sides[side]
        first = (chunk & (self.row_groups - 1)) * CHUNK_ROWS
        rows = pl.ds(pl.multiple_of(first, CHUNK_ROWS), CHUNK_ROWS)
        if self.column_groups == 1:
            return rows, slice(begin, begin + size)
        group = chunk >> (self.row_groups.bit_length() - 1)
        return rows, pl.ds(pl.multiple_of(group * self.wide + begin, LANES), size)

    def write(self, me, sums_ref, part_refs):
        half = self.chunks // 2
        for side in range(2):
            for place in range(self.chunks):
                out_ref = part_refs[2 * side + place // half]
                out_ref[place % half] = sums_ref[self.chunk_at(me, side, place)]

    def read(self, me, part_refs, sums_ref):
        half = self.chunks // 2
        for side in range(2):
            for place in range(self.chunks):
                in_ref = part_refs[2 * side + place // half]
                sums_ref[self.chunk_at(me, side, place)] = in_ref[place % half]


def table_body(plan, got_ref, out_ref, gain_in_ref, gain_out_ref):
    places, width = got_ref.shape[0], out_ref.shape[1]
    lane = lax.broadcasted_iota(jnp.int32, (16, LANES), 1)
    scale = jnp.where(lane == 0, 32.0, jnp.where(lane == 1, 1.0, 0.0)).astype(BF16)
    numbers = dot(scale, got_ref[:, width : width + LANES], NT)[0:1].astype(jnp.int32)
    step = 256
    for first in range(0, out_ref.shape[0], step):
        sub = lax.broadcasted_iota(jnp.int32, (step, places), 0) + first
        hit = jnp.where(sub == jnp.broadcast_to(numbers, (step, places)), 1.0, 0.0)
        out_ref[first : first + step, :] = dot(hit.astype(BF16), got_ref[:, :width])
    sub = lax.broadcasted_iota(jnp.int32, (16, places), 0)
    lane = lax.broadcasted_iota(jnp.int32, (16, places), 1) % plan.capacity
    total = dot(jnp.where(sub == lane, 1.0, 0.0).astype(BF16), got_ref[:, width:])
    for row in range(plan.capacity):
        first = row * plan.gain_lanes
        gain_ref = (gain_in_ref, gain_out_ref)[first // width]
        gain_ref[:, first % width : first % width + plan.gain_lanes] = total[
            row : row + 1, GAIN_AT : GAIN_AT + plan.gain_lanes
        ]


def widen_body(plan, me_ref, *refs):
    w_in_ref, w_out_ref, sums_ref = refs[4:]
    plan.read(me_ref[0], refs[:4], sums_ref)
    width = w_out_ref.shape[0]
    w_out_ref[...] = sums_ref[:, :width].astype(F32)
    w_in_ref[...] = sums_ref[:, width : 5 * width].astype(F32)


def add(left, right):
    return (left.astype(F32) + right.astype(F32)).astype(BF16)


def on_device(
    touched_rows,
    row_of_token,
    row_owner,
    owner_row,
    seq_blocks,
    seq_dest,
    grad_out,
    w_in,
    w_out,
    gain_in,
    gain_out,
):
    dp_size, table_size = lax.axis_size("dp"), lax.axis_size("table")
    both = ("dp", "table")
    count, width = touched_rows.shape
    tokens = row_of_token.shape[0]
    plan = Plan(dp_size, table_size, count, width)
    devices_all = plan.chunks
    total_factor = 1.0 / math.sqrt(grad_out.shape[0] * devices_all)
    gain_rows = jnp.stack([gain_in, gain_out])
    ints = jnp.concatenate([row_of_token, row_owner[:, 0], owner_row])[None, :]
    me = lax.axis_index(both).astype(jnp.int32)[None]

    def swap(values, mask):
        return lax.ppermute(values, both, [(here, here ^ mask) for here in range(devices_all)])

    def exchange(values, axes, groups):
        return lax.all_to_all(
            values, axes, split_axis=0, concat_axis=0, tiled=True, axis_index_groups=groups
        )

    peers = jnp.arange(dp_size, dtype=jnp.int32)
    own = jnp.sum(jnp.where(seq_dest[:, None] == peers, seq_blocks[:, None], 0), axis=0)
    lengths = jnp.where(peers[:, None] == lax.axis_index("dp"), own, 0)
    steps = [table_size << bit for bit in range(dp_size.bit_length() - 1)]
    for step, mask in enumerate(steps[::2]):
        pair = steps[2 * step + 1 : 2 * step + 2]
        came = [swap(lengths, mask)] + [swap(lengths, far) for far in pair]
        came += [swap(lengths, far ^ mask) for far in pair]
        lengths = lengths + sum(came)
        if step == 0:
            lengths, touched_rows = lax.optimization_barrier((lengths, touched_rows))
    rows = jnp.concatenate([touched_rows, grad_out])
    weights = jnp.concatenate([w_in, w_out], axis=1)
    send = call(
        functools.partial(send_body, table_size, count),
        [shape_of((SLOT, width), BF16)] * dp_size,
        [SMEM] * 2 + [VMEM],
        scratch=[pltpu.SMEM((dp_size,), jnp.int32)],
    )(me, lengths, rows)
    got = list(send)
    near, far = list(range(dp_size // 2 - 1, 0, -1)), list(range(dp_size - 1, dp_size // 2 - 1, -1))
    turns = far[:1] + [apart for pair in zip(far[1:], near) for apart in pair]
    for apart in turns:
        got[apart] = swap(send[apart], apart * table_size)
    shapes = row_shapes(count, width)
    made = call(
        functools.partial(rows_body, plan.capacity),
        list(shapes.values()),
        [VMEM] * 4,
        flops=8 * count * width * width,
        moved=4_000_000,
    )(rows, weights, gain_rows, ints)
    saved = dict(zip(shapes, made), weights=weights)
    got[0], after = lax.optimization_barrier((got[0], ints))
    shapes = token_shapes(tokens, width)
    made = call(
        forward_body,
        list(shapes.values()),
        [VMEM] * 3,
        flops=4 * count * width * width * 10,
        moved=8_000_000,
        mebibytes=12 + tokens // 32,
    )(saved["rows_active"], gain_rows, after)
    saved |= dict(zip(shapes, made))

    outs = [shape_of((devices_all * plan.capacity, width + plan.extra), BF16)]
    for _, wide in plan.sides:
        outs += [shape_of((devices_all // 2, CHUNK_ROWS, wide), BF16)] * 2
    table_send, *parts = call(
        functools.partial(backward_body, plan, table_size, total_factor),
        outs,
        [SMEM] * 3 + [VMEM] * (2 + len(USED) + dp_size),
        flops=4 * count * width * width * 40,
        moved=12_000_000,
        mebibytes=12 + tokens // 32,
        scratch=[
            pltpu.VMEM((dp_size, SLOT, width), BF16),
            pltpu.VMEM((width, plan.column_groups * plan.wide), BF16),
            pltpu.VMEM((tokens, 4 * width), BF16),
            pltpu.VMEM((tokens, width), BF16),
        ],
    )(
        me,
        seq_dest,
        seq_blocks,
        ints,
        gain_rows,
        *(saved[name] for name in USED),
        *got,
    )

    def reduced(kept, mask):
        middle = kept.shape[0] // 2
        return add(kept[:middle], swap(kept[middle:], mask))

    def gathered(kept, mask):
        return jnp.concatenate([kept, swap(kept, mask)])

    sides = [add(parts[2 * side], swap(parts[2 * side + 1], 1)) for side in range(2)]
    *sides, table_send = lax.optimization_barrier((*sides, table_send))
    low = min(2, dp_size)
    high, inside = dp_size // low, low * table_size
    groups = [[upper * low + lower for upper in range(high)] for lower in range(low)]
    table_got = exchange(table_send.reshape(high, inside, plan.capacity, -1), "dp", groups)
    for step in range(plan.near_steps):
        sides = [reduced(sides[side], plan.orders[side][step]) for side in range(2)]
    kept = jnp.concatenate(sides, axis=2)
    kept, table_got = lax.optimization_barrier((kept, table_got))
    groups = [[upper * inside + lower for lower in range(inside)] for upper in range(high)]
    table_got = exchange(jnp.swapaxes(table_got, 0, 1), both, groups)
    for mask in plan.orders[0][plan.near_steps :]:
        kept = reduced(kept, mask)
    back = plan.orders[0][: plan.near_steps - 1 : -1]
    kept = gathered(kept, back[0])
    kept, table_got = lax.optimization_barrier((kept, table_got))
    table_part, grad_gain_in, grad_gain_out = call(
        functools.partial(table_body, plan),
        (
            shape_of((ROWS_DEV, width), F32),
            shape_of((1, width), F32),
            shape_of((1, width), F32),
        ),
        [VMEM],
    )(table_got.reshape(devices_all * plan.capacity, -1))
    for mask in back[1:]:
        kept = gathered(kept, mask)
    kept, table_part = lax.optimization_barrier((kept, table_part))
    sides = [kept[..., : plan.split], kept[..., plan.split :]]
    for step in reversed(range(plan.near_steps)):
        sides = [gathered(sides[side], plan.orders[side][step]) for side in range(2)]
    grad_w_in, grad_w_out = call(
        functools.partial(widen_body, plan),
        (shape_of(w_in.shape, F32), shape_of(w_out.shape, F32)),
        [SMEM] + [VMEM] * 4,
        scratch=[pltpu.VMEM((width, plan.column_groups * plan.wide), BF16)],
    )(me, sides[0], swap(sides[0], 1), sides[1], swap(sides[1], 1))
    return (table_part, grad_w_in, grad_w_out, grad_gain_in[0], grad_gain_out[0])


def solution(mesh):
    rows = P(("dp", "table"), None)
    flat = P(("dp", "table"))
    in_specs = (rows, flat, rows, flat, flat, flat, rows, P(), P(), P(), P())
    out_specs = (rows, P(), P(), P(), P())
    return jax.shard_map(
        on_device, mesh=mesh, in_specs=in_specs, out_specs=out_specs, check_vma=False
    )
```

```python
import functools
import math

import jax
import jax.numpy as jnp
from jax import lax
from jax.experimental import pallas as pl
from jax.experimental.pallas import tpu as pltpu
from jax.sharding import PartitionSpec as P

HEADS = 4
HDIM = 128
BLK = 16
LMAXB = 4
SLOT = LMAXB * BLK
ROWS_DEV = 1024
TILE = 2 * SLOT
LANES = 128
CHUNK_ROWS = 16
GAIN_AT = 64
EPSILON = 1e-05
F32 = jnp.float32
BF16 = jnp.bfloat16
VMEM = pl.BlockSpec(memory_space=pltpu.VMEM)
SMEM = pl.BlockSpec(memory_space=pltpu.SMEM)


def call(body, out_shape, in_specs, flops=0, moved=0, scratch=(), mebibytes=24):
    outs = jax.tree.map(lambda _: VMEM, out_shape)
    return pl.pallas_call(
        body,
        out_shape=out_shape,
        in_specs=in_specs,
        out_specs=outs,
        scratch_shapes=scratch,
        compiler_params=pltpu.CompilerParams(vmem_limit_bytes=mebibytes * 1024 * 1024),
        cost_estimate=pl.CostEstimate(flops=flops, bytes_accessed=moved, transcendentals=0),
    )


def shape_of(dims, dtype):
    return jax.ShapeDtypeStruct(dims, dtype)


def sigmoid(values):
    return 0.5 * jnp.tanh(0.5 * values) + 0.5


def dot(left, right, contract=((1,), (0,))):
    return lax.dot_general(left, right, (contract, ((), ())), preferred_element_type=F32)


NT = ((1,), (1,))
TN = ((0,), (0,))


def slot_orders(peers):
    far = list(range(peers - 1, peers // 2 - 1, -1))
    near = list(range(peers // 2 - 1, 0, -1))
    return [0] + far + near, [0] + near + far


def send_body(table_size, count, me_ref, lengths_ref, rows_ref, *refs):
    out_refs, begin_ref = refs[:-1], refs[-1]
    peers = len(out_refs)
    blocks = (rows_ref.shape[0] - count) // BLK
    me = me_ref[0] // table_size
    begin = jnp.int32(0)
    for peer in range(peers):
        begin_ref[peer] = begin
        begin = begin + lengths_ref[peer, me]
    orders = slot_orders(peers)
    for turn, out_ref in enumerate(out_refs):
        apart = jnp.where((me_ref[0] & 1) == 0, orders[0][turn], orders[1][turn])
        begin = begin_ref[me ^ apart]
        for inner in range(LMAXB):
            block = jnp.minimum(begin + inner, blocks - 1)
            rows = rows_ref[pl.ds(pl.multiple_of(count + block * BLK, BLK), BLK), :]
            out_ref[inner * BLK : (inner + 1) * BLK, :] = rows


def tile_mask():
    sub = lax.broadcasted_iota(jnp.int32, (TILE, TILE), 0)
    lane = lax.broadcasted_iota(jnp.int32, (TILE, TILE), 1)
    return (sub // SLOT == lane // SLOT) & (lane <= sub)


def row_shapes(count, width):
    return dict(
        rows_active=shape_of((count, 5 * width), BF16),
        normed_t=shape_of((width, count), BF16),
        rows_slope=shape_of((count, 4 * width), BF16),
        rows_hat=shape_of((count, width), F32),
        rows_scale=shape_of((count, 1), F32),
        place=shape_of((1, count), jnp.int32),
        digits=shape_of((count, LANES), BF16),
    )


def token_shapes(tokens, width):
    pairs = tokens // TILE * HEADS
    return dict(
        gate=shape_of((tokens, width), F32),
        hat=shape_of((tokens, width), F32),
        hat_scale=shape_of((tokens, 1), F32),
        qkv=shape_of((tokens, 3 * width), BF16),
        slope=shape_of((pairs, TILE, TILE), BF16),
        slope_t=shape_of((pairs, TILE, TILE), BF16),
        weight_t=shape_of((pairs, TILE, TILE), BF16),
        mixed_t=shape_of((width, tokens), BF16),
    )


def column_of(row):
    wide = jnp.broadcast_to(row.astype(F32), (8, row.shape[1])).T
    return wide[:, 0:1].astype(jnp.int32)


def rows_body(
    capacity,
    rows_ref,
    weights_ref,
    gains_ref,
    ints_ref,
    rows_active_ref,
    normed_t_ref,
    rows_slope_ref,
    rows_hat_ref,
    rows_scale_ref,
    place_ref,
    digits_ref,
):
    count, width = rows_hat_ref.shape
    tokens = ints_ref.shape[1] - 2 * count
    owner_row = ints_ref[:, tokens : tokens + count]
    across = jnp.broadcast_to(owner_row, (count, count))
    down = jnp.broadcast_to(column_of(owner_row), (count, count))
    sub = lax.broadcasted_iota(jnp.int32, (count, count), 0)
    lane = lax.broadcasted_iota(jnp.int32, (count, count), 1)
    earlier = jnp.where((across == down) & (sub < lane), 1.0, 0.0)
    rank = jnp.sum(earlier, axis=0, keepdims=True).astype(jnp.int32)
    place_ref[...] = owner_row * capacity + rank
    number = jnp.broadcast_to(column_of(ints_ref[:, tokens + count :]), (count, LANES))
    lane = lax.broadcasted_iota(jnp.int32, (count, LANES), 1)
    digits = jnp.where(lane == 0, number >> 5, jnp.where(lane == 1, number & 31, 0))
    digits_ref[...] = digits.astype(F32).astype(BF16)
    values = rows_ref[:count, :].astype(F32)
    shifted = values - jnp.mean(values, axis=-1, keepdims=True)
    scale = lax.rsqrt(jnp.mean(shifted * shifted, axis=-1, keepdims=True) + EPSILON)
    hat = shifted * scale
    rows_hat_ref[...] = hat
    rows_scale_ref[...] = scale
    normed = hat * gains_ref[0:1, :]
    normed_t_ref[...] = normed.T.astype(BF16)
    normed = normed.astype(BF16)
    for part in range(4):
        columns = slice(part * width, (part + 1) * width)
        hidden = dot(normed, weights_ref[:, columns])
        sigma = sigmoid(hidden)
        active = hidden * sigma
        slope = sigma * (1.0 + hidden * (1.0 - sigma))
        rows_slope_ref[:, columns] = slope.astype(BF16)
        high = active.astype(BF16)
        rows_active_ref[:, columns] = high
        if part == 0:
            rows_active_ref[:, 4 * width :] = (active - high.astype(F32)).astype(BF16)


def forward_body(
    rows_active_ref,
    gains_ref,
    ints_ref,
    gate_ref,
    hat_ref,
    hat_scale_ref,
    qkv_ref,
    slope_ref,
    slope_t_ref,
    weight_t_ref,
    mixed_t_ref,
):
    count = rows_active_ref.shape[0]
    tokens, width = gate_ref.shape
    items = column_of(ints_ref[:, :tokens])
    lane = lax.broadcasted_iota(jnp.int32, (tokens, count), 1)
    pick = jnp.where(lane == jnp.broadcast_to(items, (tokens, count)), 1.0, 0.0).astype(BF16)
    gate_ref[...] = dot(pick, rows_active_ref[:, :width]) + dot(
        pick, rows_active_ref[:, 4 * width :]
    )
    for part in range(3):
        columns = slice((part + 1) * width, (part + 2) * width)
        qkv_ref[:, part * width : (part + 1) * width] = dot(pick, rows_active_ref[:, columns]).astype(
            BF16
        )
    gain_out = gains_ref[1:2, :]
    mask = tile_mask()
    factor = HDIM ** (-0.5)
    for tile in range(tokens // TILE):
        rows = slice(tile * TILE, (tile + 1) * TILE)
        parts = []
        for head in range(HEADS):
            vals, queries, keys = (
                qkv_ref[rows, part * width + head * HDIM : part * width + (head + 1) * HDIM]
                for part in range(3)
            )
            score = dot(queries, keys, NT) * factor
            sigma = sigmoid(score)
            weight = jnp.where(mask, score * sigma, 0.0)
            slope = sigma * (1.0 + score * (1.0 - sigma)) * factor
            slope = jnp.where(mask, slope, 0.0)
            slope_ref[tile * HEADS + head] = slope.astype(BF16)
            slope_t_ref[tile * HEADS + head] = slope.T.astype(BF16)
            weight_t_ref[tile * HEADS + head] = weight.T.astype(BF16)
            parts.append(dot(weight.astype(BF16), vals))
        attended = jnp.concatenate(parts, axis=1)
        shifted = attended - jnp.mean(attended, axis=-1, keepdims=True)
        scale = lax.rsqrt(jnp.mean(shifted * shifted, axis=-1, keepdims=True) + EPSILON)
        hat = shifted * scale
        hat_ref[rows, :] = hat
        hat_scale_ref[rows, :] = scale
        mixed = hat * gain_out * gate_ref[rows, :]
        mixed_t_ref[:, rows] = mixed.T.astype(BF16)


def gather_of(items, count):
    tokens = items.shape[1]
    sub = lax.broadcasted_iota(jnp.int32, (count, tokens), 0)
    hit = sub == jnp.broadcast_to(items, (count, tokens))
    return jnp.where(hit, 1.0, 0.0).astype(BF16)


USED = (
    "weights",
    "hat",
    "gate",
    "hat_scale",
    "qkv",
    "slope",
    "slope_t",
    "weight_t",
    "mixed_t",
    "normed_t",
    "rows_slope",
    "rows_hat",
    "rows_scale",
    "place",
    "digits",
)


def backward_body(
    plan,
    table_size,
    factor,
    me_ref,
    dest_ref,
    blocks_ref,
    ints_ref,
    gains_ref,
    *refs,
):
    used, refs = dict(zip(USED, refs)), refs[len(USED) :]
    got_refs, (table_ref, *part_refs), (wide_ref, sums_ref, active_ref, grad_y_ref) = (
        refs[:-9],
        refs[-9:-4],
        refs[-4:],
    )
    weights_ref, hat_ref, gate_ref, hat_scale_ref, qkv_ref, slope_ref, slope_t_ref = (
        used[name] for name in USED[:7]
    )
    weight_t_ref, mixed_t_ref, normed_t_ref, rows_slope_ref = (used[name] for name in USED[7:11])
    rows_hat_ref, rows_scale_ref, place_ref, digits_ref = (used[name] for name in USED[11:])
    orders = slot_orders(len(got_refs))
    for turn, got_ref in enumerate(got_refs):
        apart = jnp.where((me_ref[0] & 1) == 0, orders[0][turn], orders[1][turn])
        wide_ref[apart] = got_ref[...]
    for slot in range(len(got_refs)):
        rows = wide_ref[dest_ref[slot] ^ (me_ref[0] // table_size)]
        live = lax.broadcasted_iota(jnp.int32, rows.shape, 0) < blocks_ref[slot] * BLK
        rows = jnp.where(live, rows.astype(F32), 0.0).astype(BF16)
        grad_y_ref[slot * SLOT : (slot + 1) * SLOT, :] = rows
    tokens, width = grad_y_ref.shape
    count = normed_t_ref.shape[1]
    gain_in, gain_out = gains_ref[0:1, :], gains_ref[1:2, :]
    gain_total = jnp.zeros((1, width), F32)
    for tile in range(tokens // TILE):
        rows = slice(tile * TILE, (tile + 1) * TILE)
        grad_mixed = dot(grad_y_ref[rows, :], weights_ref[:, 4 * width :], NT)
        hat = hat_ref[rows, :]
        active_ref[rows, :width] = (grad_mixed * hat * gain_out).astype(BF16)
        inner = grad_mixed * gate_ref[rows, :]
        gain_total = gain_total + jnp.sum(inner * hat, axis=0, keepdims=True)
        inner = inner * gain_out
        mean = jnp.mean(inner, axis=-1, keepdims=True)
        along = jnp.mean(inner * hat, axis=-1, keepdims=True)
        grad_att = ((inner - mean - hat * along) * hat_scale_ref[rows, :]).astype(BF16)
        for head in range(HEADS):
            vals, queries, keys = (
                qkv_ref[rows, part * width + head * HDIM : part * width + (head + 1) * HDIM]
                for part in range(3)
            )
            grad_o = grad_att[:, head * HDIM : (head + 1) * HDIM]
            grad_weight = dot(grad_o, vals, NT)
            grad_score = (grad_weight * slope_ref[tile * HEADS + head].astype(F32)).astype(BF16)
            weight_t = dot(vals, grad_o, NT)
            score_t = (weight_t * slope_t_ref[tile * HEADS + head].astype(F32)).astype(BF16)
            for part, value in (
                (1, dot(weight_t_ref[tile * HEADS + head], grad_o)),
                (2, dot(grad_score, keys)),
                (3, dot(score_t, queries)),
            ):
                first = part * width + head * HDIM
                active_ref[rows, first : first + HDIM] = value.astype(BF16)
    sums_ref[:, :width] = (dot(mixed_t_ref[...], grad_y_ref[...]) * factor).astype(BF16)
    gather = gather_of(ints_ref[:, :tokens], count)
    grad_normed = jnp.zeros((count, width), F32)
    for part in range(4):
        columns = slice(part * width, (part + 1) * width)
        summed = dot(gather, active_ref[:, columns])
        grad_hidden = (summed * rows_slope_ref[:, columns].astype(F32)).astype(BF16)
        sums_ref[:, (part + 1) * width : (part + 2) * width] = (
            dot(normed_t_ref[...], grad_hidden) * factor
        ).astype(BF16)
        grad_normed = grad_normed + dot(grad_hidden, weights_ref[:, columns], NT)
    hat = rows_hat_ref[...]
    gains = (jnp.sum(grad_normed * hat, axis=0, keepdims=True) * factor, gain_total * factor)
    plan.write(me_ref[0], sums_ref, part_refs)
    inner = grad_normed * gain_in
    mean = jnp.mean(inner, axis=-1, keepdims=True)
    along = jnp.mean(inner * hat, axis=-1, keepdims=True)
    row_grad = (inner - mean - hat * along) * rows_scale_ref[...] + dot(gather, grad_y_ref[...])
    places = table_ref.shape[0]
    spots = lax.broadcasted_iota(jnp.int32, (places, count), 0)
    hit = spots == jnp.broadcast_to(place_ref[...], (places, count))
    spread = jnp.where(hit, 1.0, 0.0).astype(BF16)
    table_ref[:, :width] = dot(spread, row_grad.astype(BF16)).astype(BF16)
    extra = plan.extra
    lanes = []
    for row in range(plan.capacity):
        first = row * plan.gain_lanes
        gain = gains[first // width][:, first % width : first % width + plan.gain_lanes]
        rest = extra - GAIN_AT - plan.gain_lanes
        row_parts = [jnp.zeros((1, GAIN_AT), F32), gain]
        lanes.append(jnp.concatenate(row_parts + [jnp.zeros((1, rest), F32)] * (rest > 0), axis=1))
    lanes = jnp.concatenate(lanes, axis=0).astype(BF16)
    repeat = lax.broadcasted_iota(jnp.int32, (places, plan.capacity), 0) % plan.capacity
    lane = lax.broadcasted_iota(jnp.int32, (places, plan.capacity), 1)
    repeat = jnp.where(repeat == lane, 1.0, 0.0).astype(BF16)
    table_ref[:, width:] = dot(repeat, lanes).astype(BF16)
    table_ref[:, width : width + LANES] += dot(spread, digits_ref[...]).astype(BF16)


class Plan:
    def __init__(self, dp_size, table_size, count, width):
        self.chunks = dp_size * table_size
        self.capacity = 2 * count // self.chunks
        self.row_groups = min(self.chunks, width // CHUNK_ROWS)
        self.column_groups = self.chunks // self.row_groups
        block = self.column_groups * LANES
        self.wide = -(-5 * width // block) * LANES
        self.gain_lanes = 2 * width // self.capacity
        self.extra = -(-(GAIN_AT + self.gain_lanes) // LANES) * LANES
        first = -(-3 * self.wide // (5 * LANES)) * LANES
        self.split = -(-self.wide // (2 * LANES)) * LANES
        self.sides = ((0, first), (first, self.wide - first))
        self.halves = ((0, self.split), (self.split, self.wide - self.split))
        table_bits = [1 << bit for bit in range(1, table_size.bit_length() - 1)]
        dp_bits = [table_size << bit for bit in range(dp_size.bit_length() - 1)]
        self.near_steps = len(table_bits) + 1
        self.orders = (table_bits + dp_bits, dp_bits[:1] + table_bits + dp_bits[1:])

    def chunk_at(self, me, sides, side, place):
        order = [1] + self.orders[side]
        mask = 0
        for step, bit in enumerate(order):
            if place >> (len(order) - 1 - step) & 1:
                mask ^= bit
        chunk = me ^ mask
        begin, size = sides[side]
        first = (chunk & (self.row_groups - 1)) * CHUNK_ROWS
        rows = pl.ds(pl.multiple_of(first, CHUNK_ROWS), CHUNK_ROWS)
        if self.column_groups == 1:
            return rows, slice(begin, begin + size)
        group = chunk >> (self.row_groups.bit_length() - 1)
        return rows, pl.ds(pl.multiple_of(group * self.wide + begin, LANES), size)

    def write(self, me, sums_ref, part_refs):
        half = self.chunks // 2
        for side in range(2):
            for place in range(self.chunks):
                out_ref = part_refs[2 * side + place // half]
                out_ref[place % half] = sums_ref[self.chunk_at(me, self.sides, side, place)]

    def read(self, me, part_refs, sums_ref):
        half = self.chunks // 2
        for side in range(2):
            for place in range(self.chunks):
                in_ref = part_refs[2 * side + place // half]
                sums_ref[self.chunk_at(me, self.halves, side, place)] = in_ref[place % half]


def table_body(plan, got_ref, out_ref, gain_in_ref, gain_out_ref):
    places, width = got_ref.shape[0], out_ref.shape[1]
    lane = lax.broadcasted_iota(jnp.int32, (16, LANES), 1)
    scale = jnp.where(lane == 0, 32.0, jnp.where(lane == 1, 1.0, 0.0)).astype(BF16)
    numbers = dot(scale, got_ref[:, width : width + LANES], NT)[0:1].astype(jnp.int32)
    step = 256
    for first in range(0, out_ref.shape[0], step):
        sub = lax.broadcasted_iota(jnp.int32, (step, places), 0) + first
        hit = jnp.where(sub == jnp.broadcast_to(numbers, (step, places)), 1.0, 0.0)
        out_ref[first : first + step, :] = dot(hit.astype(BF16), got_ref[:, :width])
    sub = lax.broadcasted_iota(jnp.int32, (16, places), 0)
    lane = lax.broadcasted_iota(jnp.int32, (16, places), 1) % plan.capacity
    total = dot(jnp.where(sub == lane, 1.0, 0.0).astype(BF16), got_ref[:, width:])
    for row in range(plan.capacity):
        first = row * plan.gain_lanes
        gain_ref = (gain_in_ref, gain_out_ref)[first // width]
        gain_ref[:, first % width : first % width + plan.gain_lanes] = total[
            row : row + 1, GAIN_AT : GAIN_AT + plan.gain_lanes
        ]


def widen_body(plan, me_ref, *refs):
    w_in_ref, w_out_ref, sums_ref = refs[4:]
    plan.read(me_ref[0], refs[:4], sums_ref)
    width = w_out_ref.shape[0]
    w_out_ref[...] = sums_ref[:, :width].astype(F32)
    w_in_ref[...] = sums_ref[:, width : 5 * width].astype(F32)


def add(left, right):
    return (left.astype(F32) + right.astype(F32)).astype(BF16)


def on_device(
    touched_rows,
    row_of_token,
    row_owner,
    owner_row,
    seq_blocks,
    seq_dest,
    grad_out,
    w_in,
    w_out,
    gain_in,
    gain_out,
):
    dp_size, table_size = lax.axis_size("dp"), lax.axis_size("table")
    both = ("dp", "table")
    count, width = touched_rows.shape
    tokens = row_of_token.shape[0]
    plan = Plan(dp_size, table_size, count, width)
    devices_all = plan.chunks
    total_factor = 1.0 / math.sqrt(grad_out.shape[0] * devices_all)
    gain_rows = jnp.stack([gain_in, gain_out])
    ints = jnp.concatenate([row_of_token, row_owner[:, 0], owner_row])[None, :]
    me = lax.axis_index(both).astype(jnp.int32)[None]

    def swap(values, *masks):
        pairs = [(here, here ^ masks[here % len(masks)]) for here in range(devices_all)]
        return lax.ppermute(values, both, pairs)

    def exchange(values, axes, groups):
        return lax.all_to_all(
            values, axes, split_axis=0, concat_axis=0, tiled=True, axis_index_groups=groups
        )

    peers = jnp.arange(dp_size, dtype=jnp.int32)
    own = jnp.sum(jnp.where(seq_dest[:, None] == peers, seq_blocks[:, None], 0), axis=0)
    lengths = jnp.where(peers[:, None] == lax.axis_index("dp"), own, 0)
    steps = [table_size << bit for bit in range(dp_size.bit_length() - 1)]
    for step, mask in enumerate(steps[::2]):
        pair = steps[2 * step + 1 : 2 * step + 2]
        came = [swap(lengths, mask)] + [swap(lengths, far) for far in pair]
        came += [swap(lengths, far ^ mask) for far in pair]
        lengths = lengths + sum(came)
        if step == 0:
            lengths, touched_rows = lax.optimization_barrier((lengths, touched_rows))
    rows = jnp.concatenate([touched_rows, grad_out])
    weights = jnp.concatenate([w_in, w_out], axis=1)
    send = call(
        functools.partial(send_body, table_size, count),
        [shape_of((SLOT, width), BF16)] * dp_size,
        [SMEM] * 2 + [VMEM],
        scratch=[pltpu.SMEM((dp_size,), jnp.int32)],
    )(me, lengths, rows)
    got = list(send)
    orders = slot_orders(dp_size)
    for turn in range(1, dp_size):
        got[turn] = swap(send[turn], *(order[turn] * table_size for order in orders))
    shapes = row_shapes(count, width)
    made = call(
        functools.partial(rows_body, plan.capacity),
        list(shapes.values()),
        [VMEM] * 4,
        flops=8 * count * width * width,
        moved=4_000_000,
    )(rows, weights, gain_rows, ints)
    saved = dict(zip(shapes, made), weights=weights)
    got[0], after = lax.optimization_barrier((got[0], ints))
    shapes = token_shapes(tokens, width)
    made = call(
        forward_body,
        list(shapes.values()),
        [VMEM] * 3,
        flops=4 * count * width * width * 10,
        moved=8_000_000,
        mebibytes=12 + tokens // 32,
    )(saved["rows_active"], gain_rows, after)
    saved |= dict(zip(shapes, made))

    outs = [shape_of((devices_all * plan.capacity, width + plan.extra), BF16)]
    for _, wide in plan.sides:
        outs += [shape_of((devices_all // 2, CHUNK_ROWS, wide), BF16)] * 2
    table_send, *parts = call(
        functools.partial(backward_body, plan, table_size, total_factor),
        outs,
        [SMEM] * 3 + [VMEM] * (2 + len(USED) + dp_size),
        flops=4 * count * width * width * 40,
        moved=12_000_000,
        mebibytes=12 + tokens // 32,
        scratch=[
            pltpu.VMEM((dp_size, SLOT, width), BF16),
            pltpu.VMEM((width, plan.column_groups * plan.wide), BF16),
            pltpu.VMEM((tokens, 4 * width), BF16),
            pltpu.VMEM((tokens, width), BF16),
        ],
    )(
        me,
        seq_dest,
        seq_blocks,
        ints,
        gain_rows,
        *(saved[name] for name in USED),
        *got,
    )

    def reduced(kept, mask):
        middle = kept.shape[0] // 2
        return add(kept[:middle], swap(kept[middle:], mask))

    def gathered(kept, mask):
        return jnp.concatenate([kept, swap(kept, mask)])

    sides = [add(parts[2 * side], swap(parts[2 * side + 1], 1)) for side in range(2)]
    *sides, table_send = lax.optimization_barrier((*sides, table_send))
    low = min(2, dp_size)
    high, inside = dp_size // low, low * table_size
    groups = [[upper * low + lower for upper in range(high)] for lower in range(low)]
    table_got = exchange(table_send.reshape(high, inside, plan.capacity, -1), "dp", groups)
    for step in range(plan.near_steps):
        sides = [reduced(sides[side], plan.orders[side][step]) for side in range(2)]
    kept = jnp.concatenate(sides, axis=2)
    kept, table_got = lax.optimization_barrier((kept, table_got))
    groups = [[upper * inside + lower for lower in range(inside)] for upper in range(high)]
    table_got = exchange(jnp.swapaxes(table_got, 0, 1), both, groups)
    for mask in plan.orders[0][plan.near_steps :]:
        kept = reduced(kept, mask)
    back = plan.orders[0][: plan.near_steps - 1 : -1]
    kept = gathered(kept, back[0])
    kept, table_got = lax.optimization_barrier((kept, table_got))
    table_part, grad_gain_in, grad_gain_out = call(
        functools.partial(table_body, plan),
        (
            shape_of((ROWS_DEV, width), F32),
            shape_of((1, width), F32),
            shape_of((1, width), F32),
        ),
        [VMEM],
    )(table_got.reshape(devices_all * plan.capacity, -1))
    for mask in back[1:]:
        kept = gathered(kept, mask)
    kept, table_part = lax.optimization_barrier((kept, table_part))
    sides = [kept[..., : plan.split], kept[..., plan.split :]]
    for step in reversed(range(plan.near_steps)):
        sides = [gathered(sides[side], plan.orders[side][step]) for side in range(2)]
    grad_w_in, grad_w_out = call(
        functools.partial(widen_body, plan),
        (shape_of(w_in.shape, F32), shape_of(w_out.shape, F32)),
        [SMEM] + [VMEM] * 4,
        scratch=[pltpu.VMEM((width, plan.column_groups * plan.wide), BF16)],
    )(me, sides[0], swap(sides[0], 1), sides[1], swap(sides[1], 1))
    return (table_part, grad_w_in, grad_w_out, grad_gain_in[0], grad_gain_out[0])


def solution(mesh):
    rows = P(("dp", "table"), None)
    flat = P(("dp", "table"))
    in_specs = (rows, flat, rows, flat, flat, flat, rows, P(), P(), P(), P())
    out_specs = (rows, P(), P(), P(), P())
    return jax.shard_map(
        on_device, mesh=mesh, in_specs=in_specs, out_specs=out_specs, check_vma=False
    )
```

```python
import functools
import math

import jax
import jax.numpy as jnp
from jax import lax
from jax.experimental import pallas as pl
from jax.experimental.pallas import tpu as pltpu
from jax.sharding import PartitionSpec as P

HEADS = 4
HDIM = 128
BLK = 16
LMAXB = 4
SLOT = LMAXB * BLK
ROWS_DEV = 1024
TILE = 2 * SLOT
LANES = 128
CHUNK_ROWS = 16
GAIN_AT = 64
EPSILON = 1e-05
F32 = jnp.float32
BF16 = jnp.bfloat16
VMEM = pl.BlockSpec(memory_space=pltpu.VMEM)
SMEM = pl.BlockSpec(memory_space=pltpu.SMEM)
ANY = pl.BlockSpec(memory_space=pl.ANY)


def call(body, out_shape, in_specs, flops=0, moved=0, scratch=(), mebibytes=24):
    outs = jax.tree.map(lambda _: VMEM, out_shape)
    return pl.pallas_call(
        body,
        out_shape=out_shape,
        in_specs=in_specs,
        out_specs=outs,
        scratch_shapes=scratch,
        compiler_params=pltpu.CompilerParams(vmem_limit_bytes=mebibytes * 1024 * 1024),
        cost_estimate=pl.CostEstimate(flops=flops, bytes_accessed=moved, transcendentals=0),
    )


def shape_of(dims, dtype):
    return jax.ShapeDtypeStruct(dims, dtype)


def sigmoid(values):
    return 0.5 * jnp.tanh(0.5 * values) + 0.5


def dot(left, right, contract=((1,), (0,))):
    return lax.dot_general(left, right, (contract, ((), ())), preferred_element_type=F32)


NT = ((1,), (1,))
TN = ((0,), (0,))


def slot_orders(peers):
    far = list(range(peers - 1, peers // 2 - 1, -1))
    near = list(range(peers // 2 - 1, 0, -1))
    return [0] + far + near, [0] + near + far


def send_body(table_size, count, me_ref, lengths_ref, rows_ref, *refs):
    out_refs, begin_ref = refs[:-1], refs[-1]
    peers = len(out_refs)
    blocks = (rows_ref.shape[0] - count) // BLK
    me = me_ref[0] // table_size
    begin = jnp.int32(0)
    for peer in range(peers):
        begin_ref[peer] = begin
        begin = begin + lengths_ref[peer, me]
    orders = slot_orders(peers)
    for turn, out_ref in enumerate(out_refs):
        apart = jnp.where((me_ref[0] & 1) == 0, orders[0][turn], orders[1][turn])
        begin = begin_ref[me ^ apart]
        for inner in range(LMAXB):
            block = jnp.minimum(begin + inner, blocks - 1)
            rows = rows_ref[pl.ds(pl.multiple_of(count + block * BLK, BLK), BLK), :]
            out_ref[inner * BLK : (inner + 1) * BLK, :] = rows


def tile_mask():
    sub = lax.broadcasted_iota(jnp.int32, (TILE, TILE), 0)
    lane = lax.broadcasted_iota(jnp.int32, (TILE, TILE), 1)
    return (sub // SLOT == lane // SLOT) & (lane <= sub)


def row_shapes(count, width):
    return dict(
        rows_active=shape_of((count, 5 * width), BF16),
        normed_t=shape_of((width, count), BF16),
        rows_slope=shape_of((count, 4 * width), BF16),
        rows_hat=shape_of((count, width), F32),
        rows_scale=shape_of((count, 1), F32),
        place=shape_of((1, count), jnp.int32),
        digits=shape_of((count, LANES), BF16),
    )


def token_shapes(tokens, width):
    pairs = tokens // TILE * HEADS
    return dict(
        gate=shape_of((tokens, width), F32),
        hat=shape_of((tokens, width), F32),
        hat_scale=shape_of((tokens, 1), F32),
        qkv=shape_of((tokens, 3 * width), BF16),
        slope=shape_of((pairs, TILE, TILE), BF16),
        slope_t=shape_of((pairs, TILE, TILE), BF16),
        weight_t=shape_of((pairs, TILE, TILE), BF16),
        mixed_t=shape_of((width, tokens), BF16),
    )


def column_of(row):
    wide = jnp.broadcast_to(row.astype(F32), (8, row.shape[1])).T
    return wide[:, 0:1].astype(jnp.int32)


def rows_body(
    capacity,
    rows_ref,
    weights_ref,
    gains_ref,
    ints_ref,
    rows_active_ref,
    normed_t_ref,
    rows_slope_ref,
    rows_hat_ref,
    rows_scale_ref,
    place_ref,
    digits_ref,
):
    count, width = rows_hat_ref.shape
    tokens = ints_ref.shape[1] - 2 * count
    owner_row = ints_ref[:, tokens : tokens + count]
    across = jnp.broadcast_to(owner_row, (count, count))
    down = jnp.broadcast_to(column_of(owner_row), (count, count))
    sub = lax.broadcasted_iota(jnp.int32, (count, count), 0)
    lane = lax.broadcasted_iota(jnp.int32, (count, count), 1)
    earlier = jnp.where((across == down) & (sub < lane), 1.0, 0.0)
    rank = jnp.sum(earlier, axis=0, keepdims=True).astype(jnp.int32)
    place_ref[...] = owner_row * capacity + rank
    number = jnp.broadcast_to(column_of(ints_ref[:, tokens + count :]), (count, LANES))
    lane = lax.broadcasted_iota(jnp.int32, (count, LANES), 1)
    digits = jnp.where(lane == 0, number >> 5, jnp.where(lane == 1, number & 31, 0))
    digits_ref[...] = digits.astype(F32).astype(BF16)
    values = rows_ref[:count, :].astype(F32)
    shifted = values - jnp.mean(values, axis=-1, keepdims=True)
    scale = lax.rsqrt(jnp.mean(shifted * shifted, axis=-1, keepdims=True) + EPSILON)
    hat = shifted * scale
    rows_hat_ref[...] = hat
    rows_scale_ref[...] = scale
    normed = hat * gains_ref[0:1, :]
    normed_t_ref[...] = normed.T.astype(BF16)
    normed = normed.astype(BF16)
    for part in range(4):
        columns = slice(part * width, (part + 1) * width)
        hidden = dot(normed, weights_ref[:, columns])
        sigma = sigmoid(hidden)
        active = hidden * sigma
        slope = sigma * (1.0 + hidden * (1.0 - sigma))
        rows_slope_ref[:, columns] = slope.astype(BF16)
        high = active.astype(BF16)
        rows_active_ref[:, columns] = high
        if part == 0:
            rows_active_ref[:, 4 * width :] = (active - high.astype(F32)).astype(BF16)


def forward_body(
    rows_active_ref,
    gains_ref,
    ints_ref,
    gate_ref,
    hat_ref,
    hat_scale_ref,
    qkv_ref,
    slope_ref,
    slope_t_ref,
    weight_t_ref,
    mixed_t_ref,
):
    count = rows_active_ref.shape[0]
    tokens, width = gate_ref.shape
    items = column_of(ints_ref[:, :tokens])
    lane = lax.broadcasted_iota(jnp.int32, (tokens, count), 1)
    pick = jnp.where(lane == jnp.broadcast_to(items, (tokens, count)), 1.0, 0.0).astype(BF16)
    gate_ref[...] = dot(pick, rows_active_ref[:, :width]) + dot(
        pick, rows_active_ref[:, 4 * width :]
    )
    for part in range(3):
        columns = slice((part + 1) * width, (part + 2) * width)
        qkv_ref[:, part * width : (part + 1) * width] = dot(pick, rows_active_ref[:, columns]).astype(
            BF16
        )
    gain_out = gains_ref[1:2, :]
    mask = tile_mask()
    factor = HDIM ** (-0.5)
    for tile in range(tokens // TILE):
        rows = slice(tile * TILE, (tile + 1) * TILE)
        parts = []
        for head in range(HEADS):
            vals, queries, keys = (
                qkv_ref[rows, part * width + head * HDIM : part * width + (head + 1) * HDIM]
                for part in range(3)
            )
            score = dot(queries, keys, NT) * factor
            sigma = sigmoid(score)
            weight = jnp.where(mask, score * sigma, 0.0)
            slope = sigma * (1.0 + score * (1.0 - sigma)) * factor
            slope = jnp.where(mask, slope, 0.0)
            slope_ref[tile * HEADS + head] = slope.astype(BF16)
            slope_t_ref[tile * HEADS + head] = slope.T.astype(BF16)
            weight_t_ref[tile * HEADS + head] = weight.T.astype(BF16)
            parts.append(dot(weight.astype(BF16), vals))
        attended = jnp.concatenate(parts, axis=1)
        shifted = attended - jnp.mean(attended, axis=-1, keepdims=True)
        scale = lax.rsqrt(jnp.mean(shifted * shifted, axis=-1, keepdims=True) + EPSILON)
        hat = shifted * scale
        hat_ref[rows, :] = hat
        hat_scale_ref[rows, :] = scale
        mixed = hat * gain_out * gate_ref[rows, :]
        mixed_t_ref[:, rows] = mixed.T.astype(BF16)


def gather_of(items, count):
    tokens = items.shape[1]
    sub = lax.broadcasted_iota(jnp.int32, (count, tokens), 0)
    hit = sub == jnp.broadcast_to(items, (count, tokens))
    return jnp.where(hit, 1.0, 0.0).astype(BF16)


USED = (
    "weights",
    "hat",
    "gate",
    "hat_scale",
    "qkv",
    "slope",
    "slope_t",
    "weight_t",
    "mixed_t",
    "normed_t",
    "rows_slope",
    "rows_hat",
    "rows_scale",
    "place",
    "digits",
)


def backward_body(
    plan,
    table_size,
    factor,
    me_ref,
    dest_ref,
    blocks_ref,
    ints_ref,
    gains_ref,
    *refs,
):
    used, refs = dict(zip(USED, refs)), refs[len(USED) :]
    got_refs, (table_ref, *part_refs), (wide_ref, sums_ref, active_ref, grad_y_ref) = (
        refs[:-9],
        refs[-9:-4],
        refs[-4:],
    )
    weights_ref, hat_ref, gate_ref, hat_scale_ref, qkv_ref, slope_ref, slope_t_ref = (
        used[name] for name in USED[:7]
    )
    weight_t_ref, mixed_t_ref, normed_t_ref, rows_slope_ref = (used[name] for name in USED[7:11])
    rows_hat_ref, rows_scale_ref, place_ref, digits_ref = (used[name] for name in USED[11:])
    orders = slot_orders(len(got_refs))
    for turn, got_ref in enumerate(got_refs):
        apart = jnp.where((me_ref[0] & 1) == 0, orders[0][turn], orders[1][turn])
        wide_ref[apart] = got_ref[...]
    for slot in range(len(got_refs)):
        rows = wide_ref[dest_ref[slot] ^ (me_ref[0] // table_size)]
        live = lax.broadcasted_iota(jnp.int32, rows.shape, 0) < blocks_ref[slot] * BLK
        rows = jnp.where(live, rows.astype(F32), 0.0).astype(BF16)
        grad_y_ref[slot * SLOT : (slot + 1) * SLOT, :] = rows
    tokens, width = grad_y_ref.shape
    count = normed_t_ref.shape[1]
    gain_in, gain_out = gains_ref[0:1, :], gains_ref[1:2, :]
    gain_total = jnp.zeros((1, width), F32)
    for tile in range(tokens // TILE):
        rows = slice(tile * TILE, (tile + 1) * TILE)
        grad_mixed = dot(grad_y_ref[rows, :], weights_ref[:, 4 * width :], NT)
        hat = hat_ref[rows, :]
        active_ref[rows, :width] = (grad_mixed * hat * gain_out).astype(BF16)
        inner = grad_mixed * gate_ref[rows, :]
        gain_total = gain_total + jnp.sum(inner * hat, axis=0, keepdims=True)
        inner = inner * gain_out
        mean = jnp.mean(inner, axis=-1, keepdims=True)
        along = jnp.mean(inner * hat, axis=-1, keepdims=True)
        grad_att = ((inner - mean - hat * along) * hat_scale_ref[rows, :]).astype(BF16)
        for head in range(HEADS):
            vals, queries, keys = (
                qkv_ref[rows, part * width + head * HDIM : part * width + (head + 1) * HDIM]
                for part in range(3)
            )
            grad_o = grad_att[:, head * HDIM : (head + 1) * HDIM]
            grad_weight = dot(grad_o, vals, NT)
            grad_score = (grad_weight * slope_ref[tile * HEADS + head].astype(F32)).astype(BF16)
            weight_t = dot(vals, grad_o, NT)
            score_t = (weight_t * slope_t_ref[tile * HEADS + head].astype(F32)).astype(BF16)
            for part, value in (
                (1, dot(weight_t_ref[tile * HEADS + head], grad_o)),
                (2, dot(grad_score, keys)),
                (3, dot(score_t, queries)),
            ):
                first = part * width + head * HDIM
                active_ref[rows, first : first + HDIM] = value.astype(BF16)
    sums_ref[:, :width] = (dot(mixed_t_ref[...], grad_y_ref[...]) * factor).astype(BF16)
    gather = gather_of(ints_ref[:, :tokens], count)
    grad_normed = jnp.zeros((count, width), F32)
    for part in range(4):
        columns = slice(part * width, (part + 1) * width)
        summed = dot(gather, active_ref[:, columns])
        grad_hidden = (summed * rows_slope_ref[:, columns].astype(F32)).astype(BF16)
        sums_ref[:, (part + 1) * width : (part + 2) * width] = (
            dot(normed_t_ref[...], grad_hidden) * factor
        ).astype(BF16)
        grad_normed = grad_normed + dot(grad_hidden, weights_ref[:, columns], NT)
    hat = rows_hat_ref[...]
    gains = (jnp.sum(grad_normed * hat, axis=0, keepdims=True) * factor, gain_total * factor)
    plan.write(me_ref[0], sums_ref, part_refs)
    inner = grad_normed * gain_in
    mean = jnp.mean(inner, axis=-1, keepdims=True)
    along = jnp.mean(inner * hat, axis=-1, keepdims=True)
    row_grad = (inner - mean - hat * along) * rows_scale_ref[...] + dot(gather, grad_y_ref[...])
    places = table_ref.shape[0]
    spots = lax.broadcasted_iota(jnp.int32, (places, count), 0)
    hit = spots == jnp.broadcast_to(place_ref[...], (places, count))
    spread = jnp.where(hit, 1.0, 0.0).astype(BF16)
    table_ref[:, :width] = dot(spread, row_grad.astype(BF16)).astype(BF16)
    extra = plan.extra
    lanes = []
    for row in range(plan.capacity):
        first = row * plan.gain_lanes
        gain = gains[first // width][:, first % width : first % width + plan.gain_lanes]
        rest = extra - GAIN_AT - plan.gain_lanes
        row_parts = [jnp.zeros((1, GAIN_AT), F32), gain]
        lanes.append(jnp.concatenate(row_parts + [jnp.zeros((1, rest), F32)] * (rest > 0), axis=1))
    lanes = jnp.concatenate(lanes, axis=0).astype(BF16)
    repeat = lax.broadcasted_iota(jnp.int32, (places, plan.capacity), 0) % plan.capacity
    lane = lax.broadcasted_iota(jnp.int32, (places, plan.capacity), 1)
    repeat = jnp.where(repeat == lane, 1.0, 0.0).astype(BF16)
    table_ref[:, width:] = dot(repeat, lanes).astype(BF16)
    table_ref[:, width : width + LANES] += dot(spread, digits_ref[...]).astype(BF16)


class Plan:
    def __init__(self, dp_size, table_size, count, width):
        self.chunks = dp_size * table_size
        self.capacity = 2 * count // self.chunks
        self.row_groups = min(self.chunks, width // CHUNK_ROWS)
        self.column_groups = self.chunks // self.row_groups
        block = self.column_groups * LANES
        self.wide = -(-5 * width // block) * LANES
        self.gain_lanes = 2 * width // self.capacity
        self.extra = -(-(GAIN_AT + self.gain_lanes) // LANES) * LANES
        first = -(-3 * self.wide // (5 * LANES)) * LANES
        self.split = -(-self.wide // (2 * LANES)) * LANES
        self.sides = ((0, first), (first, self.wide - first))
        self.halves = ((0, self.split), (self.split, self.wide - self.split))
        table_bits = [1 << bit for bit in range(1, table_size.bit_length() - 1)]
        dp_bits = [table_size << bit for bit in range(dp_size.bit_length() - 1)]
        self.near_steps = len(table_bits) + 1
        self.orders = (table_bits + dp_bits, dp_bits[:1] + table_bits + dp_bits[1:])

    def chunk(self, me, side, place):
        order = [1] + self.orders[side]
        mask = 0
        for step, bit in enumerate(order):
            if place >> (len(order) - 1 - step) & 1:
                mask ^= bit
        return me ^ mask

    def columns(self, chunk, part):
        begin, size = part
        if self.column_groups == 1:
            return slice(begin, begin + size)
        group = chunk >> (self.row_groups.bit_length() - 1)
        return pl.ds(pl.multiple_of(group * self.wide + begin, LANES), size)

    def write(self, me, sums_ref, part_refs):
        half = self.chunks // 2
        for side in range(2):
            for place in range(self.chunks):
                chunk = self.chunk(me, side, place)
                first = pl.multiple_of((chunk & (self.row_groups - 1)) * CHUNK_ROWS, CHUNK_ROWS)
                rows = pl.ds(first, CHUNK_ROWS)
                out_ref = part_refs[2 * side + place // half]
                out_ref[place % half] = sums_ref[rows, self.columns(chunk, self.sides[side])]


def table_body(plan, got_ref, out_ref, gain_in_ref, gain_out_ref):
    places, width = got_ref.shape[0], out_ref.shape[1]
    lane = lax.broadcasted_iota(jnp.int32, (16, LANES), 1)
    scale = jnp.where(lane == 0, 32.0, jnp.where(lane == 1, 1.0, 0.0)).astype(BF16)
    numbers = dot(scale, got_ref[:, width : width + LANES], NT)[0:1].astype(jnp.int32)
    step = 256
    for first in range(0, out_ref.shape[0], step):
        sub = lax.broadcasted_iota(jnp.int32, (step, places), 0) + first
        hit = jnp.where(sub == jnp.broadcast_to(numbers, (step, places)), 1.0, 0.0)
        out_ref[first : first + step, :] = dot(hit.astype(BF16), got_ref[:, :width])
    sub = lax.broadcasted_iota(jnp.int32, (16, places), 0)
    lane = lax.broadcasted_iota(jnp.int32, (16, places), 1) % plan.capacity
    total = dot(jnp.where(sub == lane, 1.0, 0.0).astype(BF16), got_ref[:, width:])
    for row in range(plan.capacity):
        first = row * plan.gain_lanes
        gain_ref = (gain_in_ref, gain_out_ref)[first // width]
        gain_ref[:, first % width : first % width + plan.gain_lanes] = total[
            row : row + 1, GAIN_AT : GAIN_AT + plan.gain_lanes
        ]


def widen_body(plan, came, me_ref, left_ref, right_ref, *refs):
    w_in_ref, w_out_ref, stage_ref, sems = refs[-4:]
    side = (me_ref[0] & 1) ^ came
    half, blocks = plan.chunks // 2, plan.row_groups // 2
    for part, in_ref in enumerate((left_ref, right_ref)):
        for place in range(half):
            chunk = plan.chunk(me_ref[0], part, came * half + place)
            row = (chunk & (plan.row_groups - 1)) >> 1
            rows = pl.ds(pl.multiple_of(row * CHUNK_ROWS, CHUNK_ROWS), CHUNK_ROWS)
            stage_ref[rows, plan.columns(chunk, plan.halves[part])] = in_ref[place].astype(F32)
    split = w_out_ref.shape[1]
    copies = []
    for block in range(blocks):
        first = pl.multiple_of((2 * block + side) * CHUNK_ROWS, CHUNK_ROWS)
        here = stage_ref.at[pl.ds(block * CHUNK_ROWS, CHUNK_ROWS)]
        there = pl.ds(first, CHUNK_ROWS)
        copies += [
            pltpu.make_async_copy(here.at[:, split:], w_in_ref.at[there], sems.at[0, block]),
            pltpu.make_async_copy(here.at[:, :split], w_out_ref.at[there], sems.at[1, block]),
        ]
    for copy in copies:
        copy.start()
    for copy in copies:
        copy.wait()


def add(left, right):
    return (left.astype(F32) + right.astype(F32)).astype(BF16)


def on_device(
    touched_rows,
    row_of_token,
    row_owner,
    owner_row,
    seq_blocks,
    seq_dest,
    grad_out,
    w_in,
    w_out,
    gain_in,
    gain_out,
):
    dp_size, table_size = lax.axis_size("dp"), lax.axis_size("table")
    both = ("dp", "table")
    count, width = touched_rows.shape
    tokens = row_of_token.shape[0]
    plan = Plan(dp_size, table_size, count, width)
    devices_all = plan.chunks
    total_factor = 1.0 / math.sqrt(grad_out.shape[0] * devices_all)
    gain_rows = jnp.stack([gain_in, gain_out])
    ints = jnp.concatenate([row_of_token, row_owner[:, 0], owner_row])[None, :]
    me = lax.axis_index(both).astype(jnp.int32)[None]

    def swap(values, *masks):
        pairs = [(here, here ^ masks[here % len(masks)]) for here in range(devices_all)]
        return lax.ppermute(values, both, pairs)

    def exchange(values, axes, groups):
        return lax.all_to_all(
            values, axes, split_axis=0, concat_axis=0, tiled=True, axis_index_groups=groups
        )

    peers = jnp.arange(dp_size, dtype=jnp.int32)
    own = jnp.sum(jnp.where(seq_dest[:, None] == peers, seq_blocks[:, None], 0), axis=0)
    lengths = jnp.where(peers[:, None] == lax.axis_index("dp"), own, 0)
    steps = [table_size << bit for bit in range(dp_size.bit_length() - 1)]
    for step, mask in enumerate(steps[::2]):
        pair = steps[2 * step + 1 : 2 * step + 2]
        came = [swap(lengths, mask)] + [swap(lengths, far) for far in pair]
        came += [swap(lengths, far ^ mask) for far in pair]
        lengths = lengths + sum(came)
        if step == 0:
            lengths, touched_rows = lax.optimization_barrier((lengths, touched_rows))
    rows = jnp.concatenate([touched_rows, grad_out])
    weights = jnp.concatenate([w_in, w_out], axis=1)
    send = call(
        functools.partial(send_body, table_size, count),
        [shape_of((SLOT, width), BF16)] * dp_size,
        [SMEM] * 2 + [VMEM],
        scratch=[pltpu.SMEM((dp_size,), jnp.int32)],
    )(me, lengths, rows)
    got = list(send)
    orders = slot_orders(dp_size)
    for turn in range(1, dp_size):
        got[turn] = swap(send[turn], *(order[turn] * table_size for order in orders))
    shapes = row_shapes(count, width)
    made = call(
        functools.partial(rows_body, plan.capacity),
        list(shapes.values()),
        [VMEM] * 4,
        flops=8 * count * width * width,
        moved=4_000_000,
    )(rows, weights, gain_rows, ints)
    saved = dict(zip(shapes, made), weights=weights)
    got[0], after = lax.optimization_barrier((got[0], ints))
    shapes = token_shapes(tokens, width)
    made = call(
        forward_body,
        list(shapes.values()),
        [VMEM] * 3,
        flops=4 * count * width * width * 10,
        moved=8_000_000,
        mebibytes=12 + tokens // 32,
    )(saved["rows_active"], gain_rows, after)
    saved |= dict(zip(shapes, made))

    outs = [shape_of((devices_all * plan.capacity, width + plan.extra), BF16)]
    for _, wide in plan.sides:
        outs += [shape_of((devices_all // 2, CHUNK_ROWS, wide), BF16)] * 2
    table_send, *parts = call(
        functools.partial(backward_body, plan, table_size, total_factor),
        outs,
        [SMEM] * 3 + [VMEM] * (2 + len(USED) + dp_size),
        flops=4 * count * width * width * 40,
        moved=12_000_000,
        mebibytes=12 + tokens // 32,
        scratch=[
            pltpu.VMEM((dp_size, SLOT, width), BF16),
            pltpu.VMEM((width, plan.column_groups * plan.wide), BF16),
            pltpu.VMEM((tokens, 4 * width), BF16),
            pltpu.VMEM((tokens, width), BF16),
        ],
    )(
        me,
        seq_dest,
        seq_blocks,
        ints,
        gain_rows,
        *(saved[name] for name in USED),
        *got,
    )

    def reduced(kept, mask):
        middle = kept.shape[0] // 2
        return add(kept[:middle], swap(kept[middle:], mask))

    def gathered(kept, mask):
        return jnp.concatenate([kept, swap(kept, mask)])

    sides = [add(parts[2 * side], swap(parts[2 * side + 1], 1)) for side in range(2)]
    *sides, table_send = lax.optimization_barrier((*sides, table_send))
    low = min(2, dp_size)
    high, inside = dp_size // low, low * table_size
    groups = [[upper * low + lower for upper in range(high)] for lower in range(low)]
    table_got = exchange(table_send.reshape(high, inside, plan.capacity, -1), "dp", groups)
    for step in range(plan.near_steps):
        sides = [reduced(sides[side], plan.orders[side][step]) for side in range(2)]
    kept = jnp.concatenate(sides, axis=2)
    away = plan.orders[0][plan.near_steps :]
    kept = reduced(kept, away[0])
    kept, table_got = lax.optimization_barrier((kept, table_got))
    groups = [[upper * inside + lower for lower in range(inside)] for upper in range(high)]
    table_got = exchange(jnp.swapaxes(table_got, 0, 1), both, groups)
    for mask in away[1:]:
        kept = reduced(kept, mask)
    back = plan.orders[0][: plan.near_steps - 1 : -1]
    kept = gathered(kept, back[0])
    kept, table_got = lax.optimization_barrier((kept, table_got))
    table_part, grad_gain_in, grad_gain_out = call(
        functools.partial(table_body, plan),
        (
            shape_of((ROWS_DEV, width), F32),
            shape_of((1, width), F32),
            shape_of((1, width), F32),
        ),
        [VMEM],
    )(table_got.reshape(devices_all * plan.capacity, -1))
    for mask in back[1:]:
        kept = gathered(kept, mask)
    kept, table_part = lax.optimization_barrier((kept, table_part))
    sides = [kept[..., : plan.split], kept[..., plan.split :]]
    for step in reversed(range(plan.near_steps)):
        sides = [gathered(sides[side], plan.orders[side][step]) for side in range(2)]
    came = [swap(side, 1) for side in sides]
    rows = width // 2
    outs = [shape_of(w_in.shape, F32), shape_of(w_out.shape, F32)]
    for turn, parts in enumerate((sides, came)):
        written = () if turn == 0 else (grad_w_in, grad_w_out)
        grad_w_in, grad_w_out = pl.pallas_call(
            functools.partial(widen_body, plan, turn),
            out_shape=outs,
            in_specs=[SMEM] + [VMEM] * 2 + [ANY] * len(written),
            out_specs=[ANY] * 2,
            scratch_shapes=[
                pltpu.VMEM((rows, 5 * width), F32),
                pltpu.SemaphoreType.DMA((2, plan.row_groups // 2)),
            ],
            input_output_aliases={3: 0, 4: 1} if written else {},
            compiler_params=pltpu.CompilerParams(vmem_limit_bytes=24 * 1024 * 1024),
            cost_estimate=pl.CostEstimate(flops=0, bytes_accessed=4_000_000, transcendentals=0),
        )(me, *parts, *written)
    return (table_part, grad_w_in, grad_w_out, grad_gain_in[0], grad_gain_out[0])


def solution(mesh):
    rows = P(("dp", "table"), None)
    flat = P(("dp", "table"))
    in_specs = (rows, flat, rows, flat, flat, flat, rows, P(), P(), P(), P())
    out_specs = (rows, P(), P(), P(), P())
    return jax.shard_map(
        on_device, mesh=mesh, in_specs=in_specs, out_specs=out_specs, check_vma=False
    )
```

```python
import functools
import math

import jax
import jax.numpy as jnp
from jax import lax
from jax.experimental import pallas as pl
from jax.experimental.pallas import tpu as pltpu
from jax.sharding import PartitionSpec as P

HEADS = 4
HDIM = 128
BLK = 16
LMAXB = 4
SLOT = LMAXB * BLK
ROWS_DEV = 1024
TILE = 2 * SLOT
LANES = 128
CHUNK_ROWS = 16
GAIN_AT = 64
EPSILON = 1e-05
F32 = jnp.float32
BF16 = jnp.bfloat16
VMEM = pl.BlockSpec(memory_space=pltpu.VMEM)
SMEM = pl.BlockSpec(memory_space=pltpu.SMEM)
ANY = pl.BlockSpec(memory_space=pl.ANY)


def call(body, out_shape, in_specs, flops=0, moved=0, scratch=(), mebibytes=24):
    outs = jax.tree.map(lambda _: VMEM, out_shape)
    return pl.pallas_call(
        body,
        out_shape=out_shape,
        in_specs=in_specs,
        out_specs=outs,
        scratch_shapes=scratch,
        compiler_params=pltpu.CompilerParams(vmem_limit_bytes=mebibytes * 1024 * 1024),
        cost_estimate=pl.CostEstimate(flops=flops, bytes_accessed=moved, transcendentals=0),
    )


def shape_of(dims, dtype):
    return jax.ShapeDtypeStruct(dims, dtype)


def sigmoid(values):
    return 0.5 * jnp.tanh(0.5 * values) + 0.5


def dot(left, right, contract=((1,), (0,))):
    return lax.dot_general(left, right, (contract, ((), ())), preferred_element_type=F32)


NT = ((1,), (1,))
TN = ((0,), (0,))


def slot_orders(peers):
    far = list(range(peers - 1, peers // 2 - 1, -1))
    near = list(range(peers // 2 - 1, 0, -1))
    return [0] + far + near, [0] + near + far


def send_body(table_size, count, me_ref, lengths_ref, rows_ref, *refs):
    out_refs, begin_ref = refs[:-1], refs[-1]
    peers = len(out_refs)
    blocks = (rows_ref.shape[0] - count) // BLK
    me = me_ref[0] // table_size
    begin = jnp.int32(0)
    for peer in range(peers):
        begin_ref[peer] = begin
        begin = begin + lengths_ref[peer, me]
    orders = slot_orders(peers)
    for turn, out_ref in enumerate(out_refs):
        apart = jnp.where((me_ref[0] & 1) == 0, orders[0][turn], orders[1][turn])
        begin = begin_ref[me ^ apart]
        for inner in range(LMAXB):
            block = jnp.minimum(begin + inner, blocks - 1)
            rows = rows_ref[pl.ds(pl.multiple_of(count + block * BLK, BLK), BLK), :]
            out_ref[inner * BLK : (inner + 1) * BLK, :] = rows


def tile_mask():
    sub = lax.broadcasted_iota(jnp.int32, (TILE, TILE), 0)
    lane = lax.broadcasted_iota(jnp.int32, (TILE, TILE), 1)
    return (sub // SLOT == lane // SLOT) & (lane <= sub)


def row_shapes(count, width):
    return dict(
        rows_active=shape_of((count, 5 * width), BF16),
        normed_t=shape_of((width, count), BF16),
        rows_slope=shape_of((count, 4 * width), BF16),
        rows_hat=shape_of((count, width), F32),
        rows_scale=shape_of((count, 1), F32),
        place=shape_of((1, count), jnp.int32),
        digits=shape_of((count, LANES), BF16),
    )


def token_shapes(tokens, width):
    pairs = tokens // TILE * HEADS
    return dict(
        gate=shape_of((tokens, width), F32),
        hat=shape_of((tokens, width), F32),
        hat_scale=shape_of((tokens, 1), F32),
        qkv=shape_of((tokens, 3 * width), BF16),
        slope=shape_of((pairs, TILE, TILE), BF16),
        slope_t=shape_of((pairs, TILE, TILE), BF16),
        weight_t=shape_of((pairs, TILE, TILE), BF16),
        mixed_t=shape_of((width, tokens), BF16),
    )


def column_of(row):
    wide = jnp.broadcast_to(row.astype(F32), (8, row.shape[1])).T
    return wide[:, 0:1].astype(jnp.int32)


def rows_body(
    capacity,
    rows_ref,
    weights_ref,
    gains_ref,
    ints_ref,
    rows_active_ref,
    normed_t_ref,
    rows_slope_ref,
    rows_hat_ref,
    rows_scale_ref,
    place_ref,
    digits_ref,
):
    count, width = rows_hat_ref.shape
    tokens = ints_ref.shape[1] - 2 * count
    owner_row = ints_ref[:, tokens : tokens + count]
    across = jnp.broadcast_to(owner_row, (count, count))
    down = jnp.broadcast_to(column_of(owner_row), (count, count))
    sub = lax.broadcasted_iota(jnp.int32, (count, count), 0)
    lane = lax.broadcasted_iota(jnp.int32, (count, count), 1)
    earlier = jnp.where((across == down) & (sub < lane), 1.0, 0.0)
    rank = jnp.sum(earlier, axis=0, keepdims=True).astype(jnp.int32)
    place_ref[...] = owner_row * capacity + rank
    number = jnp.broadcast_to(column_of(ints_ref[:, tokens + count :]), (count, LANES))
    lane = lax.broadcasted_iota(jnp.int32, (count, LANES), 1)
    digits = jnp.where(lane == 0, number >> 5, jnp.where(lane == 1, number & 31, 0))
    digits_ref[...] = digits.astype(F32).astype(BF16)
    values = rows_ref[:count, :].astype(F32)
    shifted = values - jnp.mean(values, axis=-1, keepdims=True)
    scale = lax.rsqrt(jnp.mean(shifted * shifted, axis=-1, keepdims=True) + EPSILON)
    hat = shifted * scale
    rows_hat_ref[...] = hat
    rows_scale_ref[...] = scale
    normed = hat * gains_ref[0:1, :]
    normed_t_ref[...] = normed.T.astype(BF16)
    normed = normed.astype(BF16)
    for part in range(4):
        columns = slice(part * width, (part + 1) * width)
        hidden = dot(normed, weights_ref[:, columns])
        sigma = sigmoid(hidden)
        active = hidden * sigma
        slope = sigma * (1.0 + hidden * (1.0 - sigma))
        rows_slope_ref[:, columns] = slope.astype(BF16)
        high = active.astype(BF16)
        rows_active_ref[:, columns] = high
        if part == 0:
            rows_active_ref[:, 4 * width :] = (active - high.astype(F32)).astype(BF16)


def forward_body(
    rows_active_ref,
    gains_ref,
    ints_ref,
    gate_ref,
    hat_ref,
    hat_scale_ref,
    qkv_ref,
    slope_ref,
    slope_t_ref,
    weight_t_ref,
    mixed_t_ref,
):
    count = rows_active_ref.shape[0]
    tokens, width = gate_ref.shape
    items = column_of(ints_ref[:, :tokens])
    lane = lax.broadcasted_iota(jnp.int32, (tokens, count), 1)
    pick = jnp.where(lane == jnp.broadcast_to(items, (tokens, count)), 1.0, 0.0).astype(BF16)
    gate_ref[...] = dot(pick, rows_active_ref[:, :width]) + dot(
        pick, rows_active_ref[:, 4 * width :]
    )
    for part in range(3):
        columns = slice((part + 1) * width, (part + 2) * width)
        qkv_ref[:, part * width : (part + 1) * width] = dot(pick, rows_active_ref[:, columns]).astype(
            BF16
        )
    gain_out = gains_ref[1:2, :]
    mask = tile_mask()
    factor = HDIM ** (-0.5)
    for tile in range(tokens // TILE):
        rows = slice(tile * TILE, (tile + 1) * TILE)
        parts = []
        for head in range(HEADS):
            vals, queries, keys = (
                qkv_ref[rows, part * width + head * HDIM : part * width + (head + 1) * HDIM]
                for part in range(3)
            )
            score = dot(queries, keys, NT) * factor
            sigma = sigmoid(score)
            weight = jnp.where(mask, score * sigma, 0.0)
            slope = sigma * (1.0 + score * (1.0 - sigma)) * factor
            slope = jnp.where(mask, slope, 0.0)
            slope_ref[tile * HEADS + head] = slope.astype(BF16)
            slope_t_ref[tile * HEADS + head] = slope.T.astype(BF16)
            weight_t_ref[tile * HEADS + head] = weight.T.astype(BF16)
            parts.append(dot(weight.astype(BF16), vals))
        attended = jnp.concatenate(parts, axis=1)
        shifted = attended - jnp.mean(attended, axis=-1, keepdims=True)
        scale = lax.rsqrt(jnp.mean(shifted * shifted, axis=-1, keepdims=True) + EPSILON)
        hat = shifted * scale
        hat_ref[rows, :] = hat
        hat_scale_ref[rows, :] = scale
        mixed = hat * gain_out * gate_ref[rows, :]
        mixed_t_ref[:, rows] = mixed.T.astype(BF16)


def gather_of(items, count):
    tokens = items.shape[1]
    sub = lax.broadcasted_iota(jnp.int32, (count, tokens), 0)
    hit = sub == jnp.broadcast_to(items, (count, tokens))
    return jnp.where(hit, 1.0, 0.0).astype(BF16)


USED = (
    "weights",
    "hat",
    "gate",
    "hat_scale",
    "qkv",
    "slope",
    "slope_t",
    "weight_t",
    "mixed_t",
    "normed_t",
    "rows_slope",
    "rows_hat",
    "rows_scale",
    "place",
    "digits",
)


def backward_body(
    plan,
    table_size,
    factor,
    me_ref,
    dest_ref,
    blocks_ref,
    ints_ref,
    gains_ref,
    *refs,
):
    used, refs = dict(zip(USED, refs)), refs[len(USED) :]
    got_refs, (table_ref, *part_refs), (wide_ref, sums_ref, active_ref, grad_y_ref) = (
        refs[:-9],
        refs[-9:-4],
        refs[-4:],
    )
    weights_ref, hat_ref, gate_ref, hat_scale_ref, qkv_ref, slope_ref, slope_t_ref = (
        used[name] for name in USED[:7]
    )
    weight_t_ref, mixed_t_ref, normed_t_ref, rows_slope_ref = (used[name] for name in USED[7:11])
    rows_hat_ref, rows_scale_ref, place_ref, digits_ref = (used[name] for name in USED[11:])
    orders = slot_orders(len(got_refs))
    for turn, got_ref in enumerate(got_refs):
        apart = jnp.where((me_ref[0] & 1) == 0, orders[0][turn], orders[1][turn])
        wide_ref[apart] = got_ref[...]
    for slot in range(len(got_refs)):
        rows = wide_ref[dest_ref[slot] ^ (me_ref[0] // table_size)]
        live = lax.broadcasted_iota(jnp.int32, rows.shape, 0) < blocks_ref[slot] * BLK
        rows = jnp.where(live, rows.astype(F32), 0.0).astype(BF16)
        grad_y_ref[slot * SLOT : (slot + 1) * SLOT, :] = rows
    tokens, width = grad_y_ref.shape
    count = normed_t_ref.shape[1]
    gain_in, gain_out = gains_ref[0:1, :], gains_ref[1:2, :]
    gain_total = jnp.zeros((1, width), F32)
    for tile in range(tokens // TILE):
        rows = slice(tile * TILE, (tile + 1) * TILE)
        grad_mixed = dot(grad_y_ref[rows, :], weights_ref[:, 4 * width :], NT)
        hat = hat_ref[rows, :]
        active_ref[rows, :width] = (grad_mixed * hat * gain_out).astype(BF16)
        inner = grad_mixed * gate_ref[rows, :]
        gain_total = gain_total + jnp.sum(inner * hat, axis=0, keepdims=True)
        inner = inner * gain_out
        mean = jnp.mean(inner, axis=-1, keepdims=True)
        along = jnp.mean(inner * hat, axis=-1, keepdims=True)
        grad_att = ((inner - mean - hat * along) * hat_scale_ref[rows, :]).astype(BF16)
        for head in range(HEADS):
            vals, queries, keys = (
                qkv_ref[rows, part * width + head * HDIM : part * width + (head + 1) * HDIM]
                for part in range(3)
            )
            grad_o = grad_att[:, head * HDIM : (head + 1) * HDIM]
            grad_weight = dot(grad_o, vals, NT)
            grad_score = (grad_weight * slope_ref[tile * HEADS + head].astype(F32)).astype(BF16)
            weight_t = dot(vals, grad_o, NT)
            score_t = (weight_t * slope_t_ref[tile * HEADS + head].astype(F32)).astype(BF16)
            for part, value in (
                (1, dot(weight_t_ref[tile * HEADS + head], grad_o)),
                (2, dot(grad_score, keys)),
                (3, dot(score_t, queries)),
            ):
                first = part * width + head * HDIM
                active_ref[rows, first : first + HDIM] = value.astype(BF16)
    sums_ref[:, :width] = (dot(mixed_t_ref[...], grad_y_ref[...]) * factor).astype(BF16)
    gather = gather_of(ints_ref[:, :tokens], count)
    grad_normed = jnp.zeros((count, width), F32)
    for part in range(4):
        columns = slice(part * width, (part + 1) * width)
        summed = dot(gather, active_ref[:, columns])
        grad_hidden = (summed * rows_slope_ref[:, columns].astype(F32)).astype(BF16)
        sums_ref[:, (part + 1) * width : (part + 2) * width] = (
            dot(normed_t_ref[...], grad_hidden) * factor
        ).astype(BF16)
        grad_normed = grad_normed + dot(grad_hidden, weights_ref[:, columns], NT)
    hat = rows_hat_ref[...]
    gains = (jnp.sum(grad_normed * hat, axis=0, keepdims=True) * factor, gain_total * factor)
    plan.write(me_ref[0], sums_ref, part_refs)
    inner = grad_normed * gain_in
    mean = jnp.mean(inner, axis=-1, keepdims=True)
    along = jnp.mean(inner * hat, axis=-1, keepdims=True)
    row_grad = (inner - mean - hat * along) * rows_scale_ref[...] + dot(gather, grad_y_ref[...])
    places = table_ref.shape[0]
    spots = lax.broadcasted_iota(jnp.int32, (places, count), 0)
    hit = spots == jnp.broadcast_to(place_ref[...], (places, count))
    spread = jnp.where(hit, 1.0, 0.0).astype(BF16)
    table_ref[:, :width] = dot(spread, row_grad.astype(BF16)).astype(BF16)
    extra = plan.extra
    lanes = []
    for row in range(plan.capacity):
        first = row * plan.gain_lanes
        gain = gains[first // width][:, first % width : first % width + plan.gain_lanes]
        rest = extra - GAIN_AT - plan.gain_lanes
        row_parts = [jnp.zeros((1, GAIN_AT), F32), gain]
        lanes.append(jnp.concatenate(row_parts + [jnp.zeros((1, rest), F32)] * (rest > 0), axis=1))
    lanes = jnp.concatenate(lanes, axis=0).astype(BF16)
    repeat = lax.broadcasted_iota(jnp.int32, (places, plan.capacity), 0) % plan.capacity
    lane = lax.broadcasted_iota(jnp.int32, (places, plan.capacity), 1)
    repeat = jnp.where(repeat == lane, 1.0, 0.0).astype(BF16)
    table_ref[:, width:] = dot(repeat, lanes).astype(BF16)
    table_ref[:, width : width + LANES] += dot(spread, digits_ref[...]).astype(BF16)


class Plan:
    def __init__(self, dp_size, table_size, count, width):
        self.chunks = dp_size * table_size
        self.capacity = 2 * count // self.chunks
        self.row_groups = min(self.chunks, width // CHUNK_ROWS)
        self.column_groups = self.chunks // self.row_groups
        block = self.column_groups * LANES
        self.wide = -(-5 * width // block) * LANES
        self.gain_lanes = 2 * width // self.capacity
        self.extra = -(-(GAIN_AT + self.gain_lanes) // LANES) * LANES
        first = -(-3 * self.wide // (5 * LANES)) * LANES
        self.split = -(-self.wide // (2 * LANES)) * LANES
        self.sides = ((0, first), (first, self.wide - first))
        self.halves = ((0, self.split), (self.split, self.wide - self.split))
        table_bits = [1 << bit for bit in range(1, table_size.bit_length() - 1)]
        dp_bits = [table_size << bit for bit in range(dp_size.bit_length() - 1)]
        self.near_steps = len(table_bits) + 1
        self.orders = (table_bits + dp_bits, dp_bits[:1] + table_bits + dp_bits[1:])

    def chunk(self, me, side, place):
        order = [1] + self.orders[side]
        mask = 0
        for step, bit in enumerate(order):
            if place >> (len(order) - 1 - step) & 1:
                mask ^= bit
        return me ^ mask

    def columns(self, chunk, part):
        begin, size = part
        if self.column_groups == 1:
            return slice(begin, begin + size)
        group = chunk >> (self.row_groups.bit_length() - 1)
        return pl.ds(pl.multiple_of(group * self.wide + begin, LANES), size)

    def write(self, me, sums_ref, part_refs):
        half = self.chunks // 2
        for side in range(2):
            for place in range(self.chunks):
                chunk = self.chunk(me, side, place)
                first = pl.multiple_of((chunk & (self.row_groups - 1)) * CHUNK_ROWS, CHUNK_ROWS)
                rows = pl.ds(first, CHUNK_ROWS)
                out_ref = part_refs[2 * side + place // half]
                out_ref[place % half] = sums_ref[rows, self.columns(chunk, self.sides[side])]


def table_body(plan, got_ref, out_ref, gain_in_ref, gain_out_ref):
    places, width = got_ref.shape[0], out_ref.shape[1]
    lane = lax.broadcasted_iota(jnp.int32, (16, LANES), 1)
    scale = jnp.where(lane == 0, 32.0, jnp.where(lane == 1, 1.0, 0.0)).astype(BF16)
    numbers = dot(scale, got_ref[:, width : width + LANES], NT)[0:1].astype(jnp.int32)
    step = 256
    for first in range(0, out_ref.shape[0], step):
        sub = lax.broadcasted_iota(jnp.int32, (step, places), 0) + first
        hit = jnp.where(sub == jnp.broadcast_to(numbers, (step, places)), 1.0, 0.0)
        out_ref[first : first + step, :] = dot(hit.astype(BF16), got_ref[:, :width])
    sub = lax.broadcasted_iota(jnp.int32, (16, places), 0)
    lane = lax.broadcasted_iota(jnp.int32, (16, places), 1) % plan.capacity
    total = dot(jnp.where(sub == lane, 1.0, 0.0).astype(BF16), got_ref[:, width:])
    for row in range(plan.capacity):
        first = row * plan.gain_lanes
        gain_ref = (gain_in_ref, gain_out_ref)[first // width]
        gain_ref[:, first % width : first % width + plan.gain_lanes] = total[
            row : row + 1, GAIN_AT : GAIN_AT + plan.gain_lanes
        ]


def widen_body(plan, came, me_ref, left_ref, right_ref, *refs):
    w_in_ref, w_out_ref, stage_ref, sems = refs[-4:]
    half, split = plan.chunks // 2, w_out_ref.shape[1]
    copies = []

    def send(rows, there, first, size, sem):
        for out_ref, begin, end in ((w_out_ref, 0, split), (w_in_ref, split, stage_ref.shape[1])):
            low, high = max(first, begin), min(first + size, end)
            if low < high:
                here = stage_ref.at[rows, low:high]
                target = out_ref.at[there, low - begin : high - begin]
                copies.append(pltpu.make_async_copy(here, target, sem.at[int(begin > 0)]))
                copies[-1].start()

    for part, in_ref in enumerate((left_ref, right_ref)):
        for place in range(half):
            chunk = plan.chunk(me_ref[0], part, came * half + place)
            row = (chunk & (plan.row_groups - 1)) >> 1
            rows = pl.ds(pl.multiple_of(row * CHUNK_ROWS, CHUNK_ROWS), CHUNK_ROWS)
            stage_ref[rows, plan.columns(chunk, plan.halves[part])] = in_ref[place].astype(F32)
            if plan.column_groups == 1:
                there = pl.ds(pl.multiple_of(chunk * CHUNK_ROWS, CHUNK_ROWS), CHUNK_ROWS)
                send(rows, there, *plan.halves[part], sems.at[part, place])
    if plan.column_groups > 1:
        side = (me_ref[0] & 1) ^ came
        for block in range(plan.row_groups // 2):
            first = pl.multiple_of((2 * block + side) * CHUNK_ROWS, CHUNK_ROWS)
            rows = pl.ds(block * CHUNK_ROWS, CHUNK_ROWS)
            there = pl.ds(first, CHUNK_ROWS)
            send(rows, there, 0, stage_ref.shape[1], sems.at[0, block])
    for copy in copies:
        copy.wait()


def add(left, right):
    return (left.astype(F32) + right.astype(F32)).astype(BF16)


def on_device(
    touched_rows,
    row_of_token,
    row_owner,
    owner_row,
    seq_blocks,
    seq_dest,
    grad_out,
    w_in,
    w_out,
    gain_in,
    gain_out,
):
    dp_size, table_size = lax.axis_size("dp"), lax.axis_size("table")
    both = ("dp", "table")
    count, width = touched_rows.shape
    tokens = row_of_token.shape[0]
    plan = Plan(dp_size, table_size, count, width)
    devices_all = plan.chunks
    total_factor = 1.0 / math.sqrt(grad_out.shape[0] * devices_all)
    gain_rows = jnp.stack([gain_in, gain_out])
    ints = jnp.concatenate([row_of_token, row_owner[:, 0], owner_row])[None, :]
    me = lax.axis_index(both).astype(jnp.int32)[None]

    def swap(values, *masks):
        pairs = [(here, here ^ masks[here % len(masks)]) for here in range(devices_all)]
        return lax.ppermute(values, both, pairs)

    def exchange(values, axes, groups):
        return lax.all_to_all(
            values, axes, split_axis=0, concat_axis=0, tiled=True, axis_index_groups=groups
        )

    peers = jnp.arange(dp_size, dtype=jnp.int32)
    own = jnp.sum(jnp.where(seq_dest[:, None] == peers, seq_blocks[:, None], 0), axis=0)
    lengths = jnp.where(peers[:, None] == lax.axis_index("dp"), own, 0)
    steps = [table_size << bit for bit in range(dp_size.bit_length() - 1)]
    for step, mask in enumerate(steps[::2]):
        pair = steps[2 * step + 1 : 2 * step + 2]
        came = [swap(lengths, mask)] + [swap(lengths, far) for far in pair]
        came += [swap(lengths, far ^ mask) for far in pair]
        lengths = lengths + sum(came)
        if step == 0:
            lengths, touched_rows = lax.optimization_barrier((lengths, touched_rows))
    rows = jnp.concatenate([touched_rows, grad_out])
    weights = jnp.concatenate([w_in, w_out], axis=1)
    send = call(
        functools.partial(send_body, table_size, count),
        [shape_of((SLOT, width), BF16)] * dp_size,
        [SMEM] * 2 + [VMEM],
        scratch=[pltpu.SMEM((dp_size,), jnp.int32)],
    )(me, lengths, rows)
    got = list(send)
    orders = slot_orders(dp_size)
    for turn in range(1, dp_size):
        got[turn] = swap(send[turn], *(order[turn] * table_size for order in orders))
    shapes = row_shapes(count, width)
    made = call(
        functools.partial(rows_body, plan.capacity),
        list(shapes.values()),
        [VMEM] * 4,
        flops=8 * count * width * width,
        moved=4_000_000,
    )(rows, weights, gain_rows, ints)
    saved = dict(zip(shapes, made), weights=weights)
    got[0], after = lax.optimization_barrier((got[0], ints))
    shapes = token_shapes(tokens, width)
    made = call(
        forward_body,
        list(shapes.values()),
        [VMEM] * 3,
        flops=4 * count * width * width * 10,
        moved=8_000_000,
        mebibytes=12 + tokens // 32,
    )(saved["rows_active"], gain_rows, after)
    saved |= dict(zip(shapes, made))

    outs = [shape_of((devices_all * plan.capacity, width + plan.extra), BF16)]
    for _, wide in plan.sides:
        outs += [shape_of((devices_all // 2, CHUNK_ROWS, wide), BF16)] * 2
    table_send, *parts = call(
        functools.partial(backward_body, plan, table_size, total_factor),
        outs,
        [SMEM] * 3 + [VMEM] * (2 + len(USED) + dp_size),
        flops=4 * count * width * width * 40,
        moved=12_000_000,
        mebibytes=12 + tokens // 32,
        scratch=[
            pltpu.VMEM((dp_size, SLOT, width), BF16),
            pltpu.VMEM((width, plan.column_groups * plan.wide), BF16),
            pltpu.VMEM((tokens, 4 * width), BF16),
            pltpu.VMEM((tokens, width), BF16),
        ],
    )(
        me,
        seq_dest,
        seq_blocks,
        ints,
        gain_rows,
        *(saved[name] for name in USED),
        *got,
    )

    def reduced(kept, mask):
        middle = kept.shape[0] // 2
        return add(kept[:middle], swap(kept[middle:], mask))

    def gathered(kept, mask):
        return jnp.concatenate([kept, swap(kept, mask)])

    sides = [add(parts[2 * side], swap(parts[2 * side + 1], 1)) for side in range(2)]
    *sides, table_send = lax.optimization_barrier((*sides, table_send))
    low = min(2, dp_size)
    high, inside = dp_size // low, low * table_size
    groups = [[upper * low + lower for upper in range(high)] for lower in range(low)]
    table_got = exchange(table_send.reshape(high, inside, plan.capacity, -1), "dp", groups)
    for step in range(plan.near_steps):
        sides = [reduced(sides[side], plan.orders[side][step]) for side in range(2)]
    kept = jnp.concatenate(sides, axis=2)
    away = plan.orders[0][plan.near_steps :]
    kept = reduced(kept, away[0])
    kept, table_got = lax.optimization_barrier((kept, table_got))
    groups = [[upper * inside + lower for lower in range(inside)] for upper in range(high)]
    table_got = exchange(jnp.swapaxes(table_got, 0, 1), both, groups)
    for mask in away[1:]:
        kept = reduced(kept, mask)
    table_part, grad_gain_in, grad_gain_out = call(
        functools.partial(table_body, plan),
        (
            shape_of((ROWS_DEV, width), F32),
            shape_of((1, width), F32),
            shape_of((1, width), F32),
        ),
        [VMEM],
    )(table_got.reshape(devices_all * plan.capacity, -1))
    for mask in reversed(away):
        kept = gathered(kept, mask)
    sides = [kept[..., : plan.split], kept[..., plan.split :]]
    for step in reversed(range(plan.near_steps)):
        if step == 0:
            *sides, table_part = lax.optimization_barrier((*sides, table_part))
        sides = [gathered(sides[side], plan.orders[side][step]) for side in range(2)]
    came = [swap(side, 1) for side in sides]
    rows = width // 2
    outs = [shape_of(w_in.shape, F32), shape_of(w_out.shape, F32)]
    for turn, parts in enumerate((sides, came)):
        written = () if turn == 0 else (grad_w_in, grad_w_out)
        grad_w_in, grad_w_out = pl.pallas_call(
            functools.partial(widen_body, plan, turn),
            out_shape=outs,
            in_specs=[SMEM] + [VMEM] * 2 + [ANY] * len(written),
            out_specs=[ANY] * 2,
            scratch_shapes=[
                pltpu.VMEM((rows, 5 * width), F32),
                pltpu.SemaphoreType.DMA((2, plan.row_groups // 2, 2)),
            ],
            input_output_aliases={3: 0, 4: 1} if written else {},
            compiler_params=pltpu.CompilerParams(vmem_limit_bytes=24 * 1024 * 1024),
            cost_estimate=pl.CostEstimate(flops=0, bytes_accessed=4_000_000, transcendentals=0),
        )(me, *parts, *written)
    return (table_part, grad_w_in, grad_w_out, grad_gain_in[0], grad_gain_out[0])


def solution(mesh):
    rows = P(("dp", "table"), None)
    flat = P(("dp", "table"))
    in_specs = (rows, flat, rows, flat, flat, flat, rows, P(), P(), P(), P())
    out_specs = (rows, P(), P(), P(), P())
    return jax.shard_map(
        on_device, mesh=mesh, in_specs=in_specs, out_specs=out_specs, check_vma=False
    )
```

```python
import functools
import math

import jax
import jax.numpy as jnp
from jax import lax
from jax.experimental import pallas as pl
from jax.experimental.pallas import tpu as pltpu
from jax.sharding import PartitionSpec as P

HEADS = 4
HDIM = 128
BLK = 16
LMAXB = 4
SLOT = LMAXB * BLK
ROWS_DEV = 1024
TILE = 2 * SLOT
LANES = 128
CHUNK_ROWS = 16
GAIN_AT = 64
EPSILON = 1e-05
F32 = jnp.float32
BF16 = jnp.bfloat16
VMEM = pl.BlockSpec(memory_space=pltpu.VMEM)
SMEM = pl.BlockSpec(memory_space=pltpu.SMEM)
ANY = pl.BlockSpec(memory_space=pl.ANY)


def call(body, out_shape, in_specs, flops=0, moved=0, scratch=(), mebibytes=24):
    outs = jax.tree.map(lambda _: VMEM, out_shape)
    return pl.pallas_call(
        body,
        out_shape=out_shape,
        in_specs=in_specs,
        out_specs=outs,
        scratch_shapes=scratch,
        compiler_params=pltpu.CompilerParams(vmem_limit_bytes=mebibytes * 1024 * 1024),
        cost_estimate=pl.CostEstimate(flops=flops, bytes_accessed=moved, transcendentals=0),
    )


def shape_of(dims, dtype):
    return jax.ShapeDtypeStruct(dims, dtype)


def sigmoid(values):
    return 0.5 * jnp.tanh(0.5 * values) + 0.5


def dot(left, right, contract=((1,), (0,))):
    return lax.dot_general(left, right, (contract, ((), ())), preferred_element_type=F32)


NT = ((1,), (1,))
TN = ((0,), (0,))


def slot_orders(peers):
    far = list(range(peers - 1, peers // 2 - 1, -1))
    near = list(range(peers // 2 - 1, 0, -1))
    return [0] + far + near, [0] + near + far


def send_body(table_size, count, me_ref, lengths_ref, rows_ref, *refs):
    out_refs, begin_ref = refs[:-1], refs[-1]
    peers = len(out_refs)
    blocks = (rows_ref.shape[0] - count) // BLK
    me = me_ref[0] // table_size
    begin = jnp.int32(0)
    for peer in range(peers):
        begin_ref[peer] = begin
        begin = begin + lengths_ref[peer, me]
    orders = slot_orders(peers)
    for turn, out_ref in enumerate(out_refs):
        apart = jnp.where((me_ref[0] & 1) == 0, orders[0][turn], orders[1][turn])
        begin = begin_ref[me ^ apart]
        for inner in range(LMAXB):
            block = jnp.minimum(begin + inner, blocks - 1)
            rows = rows_ref[pl.ds(pl.multiple_of(count + block * BLK, BLK), BLK), :]
            out_ref[inner * BLK : (inner + 1) * BLK, :] = rows


def tile_mask():
    sub = lax.broadcasted_iota(jnp.int32, (TILE, TILE), 0)
    lane = lax.broadcasted_iota(jnp.int32, (TILE, TILE), 1)
    return (sub // SLOT == lane // SLOT) & (lane <= sub)


def row_shapes(count, width):
    return dict(
        rows_active=shape_of((count, 5 * width), BF16),
        normed_t=shape_of((width, count), BF16),
        rows_slope=shape_of((count, 4 * width), BF16),
        rows_hat=shape_of((count, width), F32),
        rows_scale=shape_of((count, 1), F32),
        place=shape_of((1, count), jnp.int32),
        digits=shape_of((count, LANES), BF16),
    )


def token_shapes(tokens, width):
    pairs = tokens // TILE * HEADS
    return dict(
        gate=shape_of((tokens, width), F32),
        hat=shape_of((tokens, width), F32),
        hat_scale=shape_of((tokens, 1), F32),
        qkv=shape_of((tokens, 3 * width), BF16),
        slope=shape_of((pairs, TILE, TILE), BF16),
        slope_t=shape_of((pairs, TILE, TILE), BF16),
        weight_t=shape_of((pairs, TILE, TILE), BF16),
        mixed_t=shape_of((width, tokens), BF16),
    )


def column_of(row):
    wide = jnp.broadcast_to(row.astype(F32), (8, row.shape[1])).T
    return wide[:, 0:1].astype(jnp.int32)


def rows_body(
    capacity,
    rows_ref,
    weights_ref,
    gains_ref,
    ints_ref,
    rows_active_ref,
    normed_t_ref,
    rows_slope_ref,
    rows_hat_ref,
    rows_scale_ref,
    place_ref,
    digits_ref,
):
    count, width = rows_hat_ref.shape
    tokens = ints_ref.shape[1] - 2 * count
    owner_row = ints_ref[:, tokens : tokens + count]
    across = jnp.broadcast_to(owner_row, (count, count))
    down = jnp.broadcast_to(column_of(owner_row), (count, count))
    sub = lax.broadcasted_iota(jnp.int32, (count, count), 0)
    lane = lax.broadcasted_iota(jnp.int32, (count, count), 1)
    earlier = jnp.where((across == down) & (sub < lane), 1.0, 0.0)
    rank = jnp.sum(earlier, axis=0, keepdims=True).astype(jnp.int32)
    place_ref[...] = owner_row * capacity + rank
    number = jnp.broadcast_to(column_of(ints_ref[:, tokens + count :]), (count, LANES))
    lane = lax.broadcasted_iota(jnp.int32, (count, LANES), 1)
    digits = jnp.where(lane == 0, number >> 5, jnp.where(lane == 1, number & 31, 0))
    digits_ref[...] = digits.astype(F32).astype(BF16)
    values = rows_ref[:count, :].astype(F32)
    shifted = values - jnp.mean(values, axis=-1, keepdims=True)
    scale = lax.rsqrt(jnp.mean(shifted * shifted, axis=-1, keepdims=True) + EPSILON)
    hat = shifted * scale
    rows_hat_ref[...] = hat
    rows_scale_ref[...] = scale
    normed = hat * gains_ref[0:1, :]
    normed_t_ref[...] = normed.T.astype(BF16)
    normed = normed.astype(BF16)
    for part in range(4):
        columns = slice(part * width, (part + 1) * width)
        hidden = dot(normed, weights_ref[:, columns])
        sigma = sigmoid(hidden)
        active = hidden * sigma
        slope = sigma * (1.0 + hidden * (1.0 - sigma))
        rows_slope_ref[:, columns] = slope.astype(BF16)
        high = active.astype(BF16)
        rows_active_ref[:, columns] = high
        if part == 0:
            rows_active_ref[:, 4 * width :] = (active - high.astype(F32)).astype(BF16)


def forward_body(
    rows_active_ref,
    gains_ref,
    ints_ref,
    gate_ref,
    hat_ref,
    hat_scale_ref,
    qkv_ref,
    slope_ref,
    slope_t_ref,
    weight_t_ref,
    mixed_t_ref,
):
    count = rows_active_ref.shape[0]
    tokens, width = gate_ref.shape
    items = column_of(ints_ref[:, :tokens])
    lane = lax.broadcasted_iota(jnp.int32, (tokens, count), 1)
    pick = jnp.where(lane == jnp.broadcast_to(items, (tokens, count)), 1.0, 0.0).astype(BF16)
    gate_ref[...] = dot(pick, rows_active_ref[:, :width]) + dot(
        pick, rows_active_ref[:, 4 * width :]
    )
    for part in range(3):
        columns = slice((part + 1) * width, (part + 2) * width)
        qkv_ref[:, part * width : (part + 1) * width] = dot(pick, rows_active_ref[:, columns]).astype(
            BF16
        )
    gain_out = gains_ref[1:2, :]
    mask = tile_mask()
    factor = HDIM ** (-0.5)
    for tile in range(tokens // TILE):
        rows = slice(tile * TILE, (tile + 1) * TILE)
        parts = []
        for head in range(HEADS):
            vals, queries, keys = (
                qkv_ref[rows, part * width + head * HDIM : part * width + (head + 1) * HDIM]
                for part in range(3)
            )
            score = dot(queries, keys, NT) * factor
            sigma = sigmoid(score)
            weight = jnp.where(mask, score * sigma, 0.0)
            slope = sigma * (1.0 + score * (1.0 - sigma)) * factor
            slope = jnp.where(mask, slope, 0.0)
            slope_ref[tile * HEADS + head] = slope.astype(BF16)
            slope_t_ref[tile * HEADS + head] = slope.T.astype(BF16)
            weight_t_ref[tile * HEADS + head] = weight.T.astype(BF16)
            parts.append(dot(weight.astype(BF16), vals))
        attended = jnp.concatenate(parts, axis=1)
        shifted = attended - jnp.mean(attended, axis=-1, keepdims=True)
        scale = lax.rsqrt(jnp.mean(shifted * shifted, axis=-1, keepdims=True) + EPSILON)
        hat = shifted * scale
        hat_ref[rows, :] = hat
        hat_scale_ref[rows, :] = scale
        mixed = hat * gain_out * gate_ref[rows, :]
        mixed_t_ref[:, rows] = mixed.T.astype(BF16)


def gather_of(items, count):
    tokens = items.shape[1]
    sub = lax.broadcasted_iota(jnp.int32, (count, tokens), 0)
    hit = sub == jnp.broadcast_to(items, (count, tokens))
    return jnp.where(hit, 1.0, 0.0).astype(BF16)


USED = (
    "weights",
    "hat",
    "gate",
    "hat_scale",
    "qkv",
    "slope",
    "slope_t",
    "weight_t",
    "mixed_t",
    "normed_t",
    "rows_slope",
    "rows_hat",
    "rows_scale",
    "place",
    "digits",
)


def backward_body(
    plan,
    table_size,
    factor,
    me_ref,
    dest_ref,
    blocks_ref,
    ints_ref,
    gains_ref,
    *refs,
):
    used, refs = dict(zip(USED, refs)), refs[len(USED) :]
    got_refs, (table_ref, *part_refs), (wide_ref, sums_ref, active_ref, grad_y_ref) = (
        refs[:-9],
        refs[-9:-4],
        refs[-4:],
    )
    weights_ref, hat_ref, gate_ref, hat_scale_ref, qkv_ref, slope_ref, slope_t_ref = (
        used[name] for name in USED[:7]
    )
    weight_t_ref, mixed_t_ref, normed_t_ref, rows_slope_ref = (used[name] for name in USED[7:11])
    rows_hat_ref, rows_scale_ref, place_ref, digits_ref = (used[name] for name in USED[11:])
    orders = slot_orders(len(got_refs))
    for turn, got_ref in enumerate(got_refs):
        apart = jnp.where((me_ref[0] & 1) == 0, orders[0][turn], orders[1][turn])
        wide_ref[apart] = got_ref[...]
    for slot in range(len(got_refs)):
        rows = wide_ref[dest_ref[slot] ^ (me_ref[0] // table_size)]
        live = lax.broadcasted_iota(jnp.int32, rows.shape, 0) < blocks_ref[slot] * BLK
        rows = jnp.where(live, rows.astype(F32), 0.0).astype(BF16)
        grad_y_ref[slot * SLOT : (slot + 1) * SLOT, :] = rows
    tokens, width = grad_y_ref.shape
    count = normed_t_ref.shape[1]
    gain_in, gain_out = gains_ref[0:1, :], gains_ref[1:2, :]
    gain_total = jnp.zeros((1, width), F32)
    for tile in range(tokens // TILE):
        rows = slice(tile * TILE, (tile + 1) * TILE)
        grad_mixed = dot(grad_y_ref[rows, :], weights_ref[:, 4 * width :], NT)
        hat = hat_ref[rows, :]
        active_ref[rows, :width] = (grad_mixed * hat * gain_out).astype(BF16)
        inner = grad_mixed * gate_ref[rows, :]
        gain_total = gain_total + jnp.sum(inner * hat, axis=0, keepdims=True)
        inner = inner * gain_out
        mean = jnp.mean(inner, axis=-1, keepdims=True)
        along = jnp.mean(inner * hat, axis=-1, keepdims=True)
        grad_att = ((inner - mean - hat * along) * hat_scale_ref[rows, :]).astype(BF16)
        for head in range(HEADS):
            vals, queries, keys = (
                qkv_ref[rows, part * width + head * HDIM : part * width + (head + 1) * HDIM]
                for part in range(3)
            )
            grad_o = grad_att[:, head * HDIM : (head + 1) * HDIM]
            grad_weight = dot(grad_o, vals, NT)
            grad_score = (grad_weight * slope_ref[tile * HEADS + head].astype(F32)).astype(BF16)
            weight_t = dot(vals, grad_o, NT)
            score_t = (weight_t * slope_t_ref[tile * HEADS + head].astype(F32)).astype(BF16)
            for part, value in (
                (1, dot(weight_t_ref[tile * HEADS + head], grad_o)),
                (2, dot(grad_score, keys)),
                (3, dot(score_t, queries)),
            ):
                first = part * width + head * HDIM
                active_ref[rows, first : first + HDIM] = value.astype(BF16)
    sums_ref[:, :width] = (dot(mixed_t_ref[...], grad_y_ref[...]) * factor).astype(BF16)
    gather = gather_of(ints_ref[:, :tokens], count)
    grad_normed = jnp.zeros((count, width), F32)
    for part in range(4):
        columns = slice(part * width, (part + 1) * width)
        summed = dot(gather, active_ref[:, columns])
        grad_hidden = (summed * rows_slope_ref[:, columns].astype(F32)).astype(BF16)
        sums_ref[:, (part + 1) * width : (part + 2) * width] = (
            dot(normed_t_ref[...], grad_hidden) * factor
        ).astype(BF16)
        grad_normed = grad_normed + dot(grad_hidden, weights_ref[:, columns], NT)
    hat = rows_hat_ref[...]
    gains = (jnp.sum(grad_normed * hat, axis=0, keepdims=True) * factor, gain_total * factor)
    plan.write(me_ref[0], sums_ref, part_refs)
    inner = grad_normed * gain_in
    mean = jnp.mean(inner, axis=-1, keepdims=True)
    along = jnp.mean(inner * hat, axis=-1, keepdims=True)
    row_grad = (inner - mean - hat * along) * rows_scale_ref[...] + dot(gather, grad_y_ref[...])
    places = table_ref.shape[0]
    spots = lax.broadcasted_iota(jnp.int32, (places, count), 0)
    hit = spots == jnp.broadcast_to(place_ref[...], (places, count))
    spread = jnp.where(hit, 1.0, 0.0).astype(BF16)
    table_ref[:, :width] = dot(spread, row_grad.astype(BF16)).astype(BF16)
    extra = plan.extra
    lanes = []
    for row in range(plan.capacity):
        first = row * plan.gain_lanes
        gain = gains[first // width][:, first % width : first % width + plan.gain_lanes]
        rest = extra - GAIN_AT - plan.gain_lanes
        row_parts = [jnp.zeros((1, GAIN_AT), F32), gain]
        lanes.append(jnp.concatenate(row_parts + [jnp.zeros((1, rest), F32)] * (rest > 0), axis=1))
    lanes = jnp.concatenate(lanes, axis=0).astype(BF16)
    repeat = lax.broadcasted_iota(jnp.int32, (places, plan.capacity), 0) % plan.capacity
    lane = lax.broadcasted_iota(jnp.int32, (places, plan.capacity), 1)
    repeat = jnp.where(repeat == lane, 1.0, 0.0).astype(BF16)
    table_ref[:, width:] = dot(repeat, lanes).astype(BF16)
    table_ref[:, width : width + LANES] += dot(spread, digits_ref[...]).astype(BF16)


class Plan:
    def __init__(self, dp_size, table_size, count, width):
        self.chunks = dp_size * table_size
        self.capacity = 2 * count // self.chunks
        self.row_groups = min(self.chunks, width // CHUNK_ROWS)
        self.column_groups = self.chunks // self.row_groups
        block = self.column_groups * LANES
        self.wide = -(-5 * width // block) * LANES
        self.gain_lanes = 2 * width // self.capacity
        self.extra = -(-(GAIN_AT + self.gain_lanes) // LANES) * LANES
        first = -(-13 * self.wide // (20 * LANES)) * LANES
        self.split = -(-self.wide // (2 * LANES)) * LANES
        self.sides = ((0, first), (first, self.wide - first))
        self.halves = ((0, self.split), (self.split, self.wide - self.split))
        table_bits = [1 << bit for bit in range(1, table_size.bit_length() - 1)]
        dp_bits = [table_size << bit for bit in range(dp_size.bit_length() - 1)]
        self.near_steps = len(table_bits) + 1
        self.orders = (table_bits + dp_bits, dp_bits[:1] + table_bits + dp_bits[1:])

    def chunk(self, me, side, place):
        order = [1] + self.orders[side]
        mask = 0
        for step, bit in enumerate(order):
            if place >> (len(order) - 1 - step) & 1:
                mask ^= bit
        return me ^ mask

    def columns(self, chunk, part):
        begin, size = part
        if self.column_groups == 1:
            return slice(begin, begin + size)
        group = chunk >> (self.row_groups.bit_length() - 1)
        return pl.ds(pl.multiple_of(group * self.wide + begin, LANES), size)

    def write(self, me, sums_ref, part_refs):
        half = self.chunks // 2
        for side in range(2):
            for place in range(self.chunks):
                chunk = self.chunk(me, side, place)
                first = pl.multiple_of((chunk & (self.row_groups - 1)) * CHUNK_ROWS, CHUNK_ROWS)
                rows = pl.ds(first, CHUNK_ROWS)
                out_ref = part_refs[2 * side + place // half]
                out_ref[place % half] = sums_ref[rows, self.columns(chunk, self.sides[side])]


def table_body(plan, got_ref, out_ref, gain_in_ref, gain_out_ref):
    places, width = got_ref.shape[0], out_ref.shape[1]
    lane = lax.broadcasted_iota(jnp.int32, (16, LANES), 1)
    scale = jnp.where(lane == 0, 32.0, jnp.where(lane == 1, 1.0, 0.0)).astype(BF16)
    numbers = dot(scale, got_ref[:, width : width + LANES], NT)[0:1].astype(jnp.int32)
    step = 256
    for first in range(0, out_ref.shape[0], step):
        sub = lax.broadcasted_iota(jnp.int32, (step, places), 0) + first
        hit = jnp.where(sub == jnp.broadcast_to(numbers, (step, places)), 1.0, 0.0)
        out_ref[first : first + step, :] = dot(hit.astype(BF16), got_ref[:, :width])
    sub = lax.broadcasted_iota(jnp.int32, (16, places), 0)
    lane = lax.broadcasted_iota(jnp.int32, (16, places), 1) % plan.capacity
    total = dot(jnp.where(sub == lane, 1.0, 0.0).astype(BF16), got_ref[:, width:])
    for row in range(plan.capacity):
        first = row * plan.gain_lanes
        gain_ref = (gain_in_ref, gain_out_ref)[first // width]
        gain_ref[:, first % width : first % width + plan.gain_lanes] = total[
            row : row + 1, GAIN_AT : GAIN_AT + plan.gain_lanes
        ]


def widen_body(plan, came, me_ref, left_ref, right_ref, *refs):
    w_in_ref, w_out_ref, stage_ref, sems = refs[-4:]
    side = (me_ref[0] & 1) ^ came
    half, blocks = plan.chunks // 2, plan.row_groups // 2
    for part, in_ref in enumerate((left_ref, right_ref)):
        for place in range(half):
            chunk = plan.chunk(me_ref[0], part, came * half + place)
            row = (chunk & (plan.row_groups - 1)) >> 1
            rows = pl.ds(pl.multiple_of(row * CHUNK_ROWS, CHUNK_ROWS), CHUNK_ROWS)
            stage_ref[rows, plan.columns(chunk, plan.halves[part])] = in_ref[place].astype(F32)
    split = w_out_ref.shape[1]
    copies = []
    for block in range(blocks):
        first = pl.multiple_of((2 * block + side) * CHUNK_ROWS, CHUNK_ROWS)
        here = stage_ref.at[pl.ds(block * CHUNK_ROWS, CHUNK_ROWS)]
        there = pl.ds(first, CHUNK_ROWS)
        copies += [
            pltpu.make_async_copy(here.at[:, split:], w_in_ref.at[there], sems.at[0, block]),
            pltpu.make_async_copy(here.at[:, :split], w_out_ref.at[there], sems.at[1, block]),
        ]
    for copy in copies:
        copy.start()
    for copy in copies:
        copy.wait()


def add(left, right):
    return (left.astype(F32) + right.astype(F32)).astype(BF16)


def on_device(
    touched_rows,
    row_of_token,
    row_owner,
    owner_row,
    seq_blocks,
    seq_dest,
    grad_out,
    w_in,
    w_out,
    gain_in,
    gain_out,
):
    dp_size, table_size = lax.axis_size("dp"), lax.axis_size("table")
    both = ("dp", "table")
    count, width = touched_rows.shape
    tokens = row_of_token.shape[0]
    plan = Plan(dp_size, table_size, count, width)
    devices_all = plan.chunks
    total_factor = 1.0 / math.sqrt(grad_out.shape[0] * devices_all)
    gain_rows = jnp.stack([gain_in, gain_out])
    ints = jnp.concatenate([row_of_token, row_owner[:, 0], owner_row])[None, :]
    me = lax.axis_index(both).astype(jnp.int32)[None]

    def swap(values, *masks):
        pairs = [(here, here ^ masks[here % len(masks)]) for here in range(devices_all)]
        return lax.ppermute(values, both, pairs)

    def exchange(values, axes, groups):
        return lax.all_to_all(
            values, axes, split_axis=0, concat_axis=0, tiled=True, axis_index_groups=groups
        )

    peers = jnp.arange(dp_size, dtype=jnp.int32)
    own = jnp.sum(jnp.where(seq_dest[:, None] == peers, seq_blocks[:, None], 0), axis=0)
    lengths = jnp.where(peers[:, None] == lax.axis_index("dp"), own, 0)
    steps = [table_size << bit for bit in range(dp_size.bit_length() - 1)]
    for step, mask in enumerate(steps[::2]):
        pair = steps[2 * step + 1 : 2 * step + 2]
        came = [swap(lengths, mask)] + [swap(lengths, far) for far in pair]
        came += [swap(lengths, far ^ mask) for far in pair]
        lengths = lengths + sum(came)
        if step == 0:
            lengths, touched_rows = lax.optimization_barrier((lengths, touched_rows))
    rows = jnp.concatenate([touched_rows, grad_out])
    weights = jnp.concatenate([w_in, w_out], axis=1)
    shapes = row_shapes(count, width)
    made = call(
        functools.partial(rows_body, plan.capacity),
        list(shapes.values()),
        [VMEM] * 4,
        flops=8 * count * width * width,
        moved=4_000_000,
    )(rows, weights, gain_rows, ints)
    saved = dict(zip(shapes, made), weights=weights)
    lengths, saved["rows_active"] = lax.optimization_barrier((lengths, saved["rows_active"]))
    send = call(
        functools.partial(send_body, table_size, count),
        [shape_of((SLOT, width), BF16)] * dp_size,
        [SMEM] * 2 + [VMEM],
        scratch=[pltpu.SMEM((dp_size,), jnp.int32)],
    )(me, lengths, rows)
    got = list(send)
    orders = slot_orders(dp_size)
    for turn in range(1, dp_size):
        got[turn] = swap(send[turn], *(order[turn] * table_size for order in orders))
    got[0], after = lax.optimization_barrier((got[0], ints))
    shapes = token_shapes(tokens, width)
    made = call(
        forward_body,
        list(shapes.values()),
        [VMEM] * 3,
        flops=4 * count * width * width * 10,
        moved=8_000_000,
        mebibytes=12 + tokens // 32,
    )(saved["rows_active"], gain_rows, after)
    saved |= dict(zip(shapes, made))

    outs = [shape_of((devices_all * plan.capacity, width + plan.extra), BF16)]
    for _, wide in plan.sides:
        outs += [shape_of((devices_all // 2, CHUNK_ROWS, wide), BF16)] * 2
    table_send, *parts = call(
        functools.partial(backward_body, plan, table_size, total_factor),
        outs,
        [SMEM] * 3 + [VMEM] * (2 + len(USED) + dp_size),
        flops=4 * count * width * width * 40,
        moved=12_000_000,
        mebibytes=12 + tokens // 32,
        scratch=[
            pltpu.VMEM((dp_size, SLOT, width), BF16),
            pltpu.VMEM((width, plan.column_groups * plan.wide), BF16),
            pltpu.VMEM((tokens, 4 * width), BF16),
            pltpu.VMEM((tokens, width), BF16),
        ],
    )(
        me,
        seq_dest,
        seq_blocks,
        ints,
        gain_rows,
        *(saved[name] for name in USED),
        *got,
    )

    def reduced(kept, mask):
        middle = kept.shape[0] // 2
        return add(kept[:middle], swap(kept[middle:], mask))

    def gathered(kept, mask):
        return jnp.concatenate([kept, swap(kept, mask)])

    sides = [add(parts[2 * side], swap(parts[2 * side + 1], 1)) for side in range(2)]
    *sides, table_send = lax.optimization_barrier((*sides, table_send))
    low = min(2, dp_size)
    high, inside = dp_size // low, low * table_size
    groups = [[upper * low + lower for upper in range(high)] for lower in range(low)]
    table_got = exchange(table_send.reshape(high, inside, plan.capacity, -1), "dp", groups)
    for step in range(plan.near_steps):
        sides = [reduced(sides[side], plan.orders[side][step]) for side in range(2)]
    kept = jnp.concatenate(sides, axis=2)
    away = plan.orders[0][plan.near_steps :]
    kept = reduced(kept, away[0])
    kept, table_got = lax.optimization_barrier((kept, table_got))
    groups = [[upper * inside + lower for lower in range(inside)] for upper in range(high)]
    table_got = exchange(jnp.swapaxes(table_got, 0, 1), both, groups)
    for mask in away[1:]:
        kept = reduced(kept, mask)
    back = plan.orders[0][: plan.near_steps - 1 : -1]
    kept = gathered(kept, back[0])
    kept, table_got = lax.optimization_barrier((kept, table_got))
    table_part, grad_gain_in, grad_gain_out = call(
        functools.partial(table_body, plan),
        (
            shape_of((ROWS_DEV, width), F32),
            shape_of((1, width), F32),
            shape_of((1, width), F32),
        ),
        [VMEM],
    )(table_got.reshape(devices_all * plan.capacity, -1))
    for mask in back[1:]:
        kept = gathered(kept, mask)
    kept, table_part = lax.optimization_barrier((kept, table_part))
    sides = [kept[..., : plan.split], kept[..., plan.split :]]
    for step in reversed(range(plan.near_steps)):
        sides = [gathered(sides[side], plan.orders[side][step]) for side in range(2)]
    came = [swap(side, 1) for side in sides]
    rows = width // 2
    outs = [shape_of(w_in.shape, F32), shape_of(w_out.shape, F32)]
    for turn, parts in enumerate((sides, came)):
        written = () if turn == 0 else (grad_w_in, grad_w_out)
        grad_w_in, grad_w_out = pl.pallas_call(
            functools.partial(widen_body, plan, turn),
            out_shape=outs,
            in_specs=[SMEM] + [VMEM] * 2 + [ANY] * len(written),
            out_specs=[ANY] * 2,
            scratch_shapes=[
                pltpu.VMEM((rows, 5 * width), F32),
                pltpu.SemaphoreType.DMA((2, plan.row_groups // 2)),
            ],
            input_output_aliases={3: 0, 4: 1} if written else {},
            compiler_params=pltpu.CompilerParams(vmem_limit_bytes=24 * 1024 * 1024),
            cost_estimate=pl.CostEstimate(flops=0, bytes_accessed=4_000_000, transcendentals=0),
        )(me, *parts, *written)
    return (table_part, grad_w_in, grad_w_out, grad_gain_in[0], grad_gain_out[0])


def solution(mesh):
    rows = P(("dp", "table"), None)
    flat = P(("dp", "table"))
    in_specs = (rows, flat, rows, flat, flat, flat, rows, P(), P(), P(), P())
    out_specs = (rows, P(), P(), P(), P())
    return jax.shard_map(
        on_device, mesh=mesh, in_specs=in_specs, out_specs=out_specs, check_vma=False
    )
```

```python
import functools
import math

import jax
import jax.numpy as jnp
from jax import lax
from jax.experimental import pallas as pl
from jax.experimental.pallas import tpu as pltpu
from jax.sharding import PartitionSpec as P

HEADS = 4
HDIM = 128
BLK = 16
LMAXB = 4
SLOT = LMAXB * BLK
ROWS_DEV = 1024
TILE = 2 * SLOT
LANES = 128
CHUNK_ROWS = 16
GAIN_AT = 64
EPSILON = 1e-05
F32 = jnp.float32
BF16 = jnp.bfloat16
VMEM = pl.BlockSpec(memory_space=pltpu.VMEM)
SMEM = pl.BlockSpec(memory_space=pltpu.SMEM)
ANY = pl.BlockSpec(memory_space=pl.ANY)


def call(body, out_shape, in_specs, flops=0, moved=0, scratch=(), mebibytes=24):
    outs = jax.tree.map(lambda _: VMEM, out_shape)
    return pl.pallas_call(
        body,
        out_shape=out_shape,
        in_specs=in_specs,
        out_specs=outs,
        scratch_shapes=scratch,
        compiler_params=pltpu.CompilerParams(vmem_limit_bytes=mebibytes * 1024 * 1024),
        cost_estimate=pl.CostEstimate(flops=flops, bytes_accessed=moved, transcendentals=0),
    )


def shape_of(dims, dtype):
    return jax.ShapeDtypeStruct(dims, dtype)


def sigmoid(values):
    return 0.5 * jnp.tanh(0.5 * values) + 0.5


def dot(left, right, contract=((1,), (0,))):
    return lax.dot_general(left, right, (contract, ((), ())), preferred_element_type=F32)


NT = ((1,), (1,))
TN = ((0,), (0,))


def slot_orders(peers):
    far = list(range(peers - 1, peers // 2 - 1, -1))
    near = list(range(peers // 2 - 1, 0, -1))
    return [0] + far + near, [0] + near + far


def send_body(table_size, count, me_ref, lengths_ref, rows_ref, *refs):
    out_refs, begin_ref = refs[:-1], refs[-1]
    peers = len(out_refs)
    blocks = (rows_ref.shape[0] - count) // BLK
    me = me_ref[0] // table_size
    begin = jnp.int32(0)
    for peer in range(peers):
        begin_ref[peer] = begin
        begin = begin + lengths_ref[peer, me]
    orders = slot_orders(peers)
    for turn, out_ref in enumerate(out_refs):
        apart = jnp.where((me_ref[0] & 1) == 0, orders[0][turn], orders[1][turn])
        begin = begin_ref[me ^ apart]
        for inner in range(LMAXB):
            block = jnp.minimum(begin + inner, blocks - 1)
            rows = rows_ref[pl.ds(pl.multiple_of(count + block * BLK, BLK), BLK), :]
            out_ref[inner * BLK : (inner + 1) * BLK, :] = rows


def tile_mask():
    sub = lax.broadcasted_iota(jnp.int32, (TILE, TILE), 0)
    lane = lax.broadcasted_iota(jnp.int32, (TILE, TILE), 1)
    return (sub // SLOT == lane // SLOT) & (lane <= sub)


def row_shapes(count, width):
    return dict(
        rows_active=shape_of((count, 5 * width), BF16),
        normed_t=shape_of((width, count), BF16),
        rows_slope=shape_of((count, 4 * width), BF16),
        rows_hat=shape_of((count, width), F32),
        rows_scale=shape_of((count, 1), F32),
        place=shape_of((1, count), jnp.int32),
        digits=shape_of((count, LANES), BF16),
    )


def token_shapes(tokens, width):
    pairs = tokens // TILE * HEADS
    return dict(
        gate=shape_of((tokens, width), F32),
        hat=shape_of((tokens, width), F32),
        hat_scale=shape_of((tokens, 1), F32),
        qkv=shape_of((tokens, 3 * width), BF16),
        slope=shape_of((pairs, TILE, TILE), BF16),
        slope_t=shape_of((pairs, TILE, TILE), BF16),
        weight_t=shape_of((pairs, TILE, TILE), BF16),
        mixed_t=shape_of((width, tokens), BF16),
    )


def column_of(row):
    wide = jnp.broadcast_to(row.astype(F32), (8, row.shape[1])).T
    return wide[:, 0:1].astype(jnp.int32)


def rows_body(
    capacity,
    rows_ref,
    weights_ref,
    gains_ref,
    ints_ref,
    rows_active_ref,
    normed_t_ref,
    rows_slope_ref,
    rows_hat_ref,
    rows_scale_ref,
    place_ref,
    digits_ref,
):
    count, width = rows_hat_ref.shape
    tokens = ints_ref.shape[1] - 2 * count
    owner_row = ints_ref[:, tokens : tokens + count]
    across = jnp.broadcast_to(owner_row, (count, count))
    down = jnp.broadcast_to(column_of(owner_row), (count, count))
    sub = lax.broadcasted_iota(jnp.int32, (count, count), 0)
    lane = lax.broadcasted_iota(jnp.int32, (count, count), 1)
    earlier = jnp.where((across == down) & (sub < lane), 1.0, 0.0)
    rank = jnp.sum(earlier, axis=0, keepdims=True).astype(jnp.int32)
    place_ref[...] = owner_row * capacity + rank
    number = jnp.broadcast_to(column_of(ints_ref[:, tokens + count :]), (count, LANES))
    lane = lax.broadcasted_iota(jnp.int32, (count, LANES), 1)
    digits = jnp.where(lane == 0, number >> 5, jnp.where(lane == 1, number & 31, 0))
    digits_ref[...] = digits.astype(F32).astype(BF16)
    values = rows_ref[:count, :].astype(F32)
    shifted = values - jnp.mean(values, axis=-1, keepdims=True)
    scale = lax.rsqrt(jnp.mean(shifted * shifted, axis=-1, keepdims=True) + EPSILON)
    hat = shifted * scale
    rows_hat_ref[...] = hat
    rows_scale_ref[...] = scale
    normed = hat * gains_ref[0:1, :]
    normed_t_ref[...] = normed.T.astype(BF16)
    normed = normed.astype(BF16)
    for part in range(4):
        columns = slice(part * width, (part + 1) * width)
        hidden = dot(normed, weights_ref[:, columns])
        sigma = sigmoid(hidden)
        active = hidden * sigma
        slope = sigma * (1.0 + hidden * (1.0 - sigma))
        rows_slope_ref[:, columns] = slope.astype(BF16)
        high = active.astype(BF16)
        rows_active_ref[:, columns] = high
        if part == 0:
            rows_active_ref[:, 4 * width :] = (active - high.astype(F32)).astype(BF16)


def forward_body(
    rows_active_ref,
    gains_ref,
    ints_ref,
    gate_ref,
    hat_ref,
    hat_scale_ref,
    qkv_ref,
    slope_ref,
    slope_t_ref,
    weight_t_ref,
    mixed_t_ref,
):
    count = rows_active_ref.shape[0]
    tokens, width = gate_ref.shape
    items = column_of(ints_ref[:, :tokens])
    lane = lax.broadcasted_iota(jnp.int32, (tokens, count), 1)
    pick = jnp.where(lane == jnp.broadcast_to(items, (tokens, count)), 1.0, 0.0).astype(BF16)
    gate_ref[...] = dot(pick, rows_active_ref[:, :width]) + dot(
        pick, rows_active_ref[:, 4 * width :]
    )
    for part in range(3):
        columns = slice((part + 1) * width, (part + 2) * width)
        qkv_ref[:, part * width : (part + 1) * width] = dot(pick, rows_active_ref[:, columns]).astype(
            BF16
        )
    gain_out = gains_ref[1:2, :]
    mask = tile_mask()
    factor = HDIM ** (-0.5)
    for tile in range(tokens // TILE):
        rows = slice(tile * TILE, (tile + 1) * TILE)
        parts = []
        for head in range(HEADS):
            vals, queries, keys = (
                qkv_ref[rows, part * width + head * HDIM : part * width + (head + 1) * HDIM]
                for part in range(3)
            )
            score = dot(queries, keys, NT) * factor
            sigma = sigmoid(score)
            weight = jnp.where(mask, score * sigma, 0.0)
            slope = sigma * (1.0 + score * (1.0 - sigma)) * factor
            slope = jnp.where(mask, slope, 0.0)
            slope_ref[tile * HEADS + head] = slope.astype(BF16)
            slope_t_ref[tile * HEADS + head] = slope.T.astype(BF16)
            weight_t_ref[tile * HEADS + head] = weight.T.astype(BF16)
            parts.append(dot(weight.astype(BF16), vals))
        attended = jnp.concatenate(parts, axis=1)
        shifted = attended - jnp.mean(attended, axis=-1, keepdims=True)
        scale = lax.rsqrt(jnp.mean(shifted * shifted, axis=-1, keepdims=True) + EPSILON)
        hat = shifted * scale
        hat_ref[rows, :] = hat
        hat_scale_ref[rows, :] = scale
        mixed = hat * gain_out * gate_ref[rows, :]
        mixed_t_ref[:, rows] = mixed.T.astype(BF16)


def gather_of(items, count):
    tokens = items.shape[1]
    sub = lax.broadcasted_iota(jnp.int32, (count, tokens), 0)
    hit = sub == jnp.broadcast_to(items, (count, tokens))
    return jnp.where(hit, 1.0, 0.0).astype(BF16)


USED = (
    "weights",
    "hat",
    "gate",
    "hat_scale",
    "qkv",
    "slope",
    "slope_t",
    "weight_t",
    "mixed_t",
    "normed_t",
    "rows_slope",
    "rows_hat",
    "rows_scale",
    "place",
    "digits",
)


def backward_body(
    plan,
    table_size,
    factor,
    me_ref,
    dest_ref,
    blocks_ref,
    ints_ref,
    gains_ref,
    *refs,
):
    used, refs = dict(zip(USED, refs)), refs[len(USED) :]
    got_refs, (table_ref, *part_refs), (wide_ref, sums_ref, active_ref, grad_y_ref) = (
        refs[:-9],
        refs[-9:-4],
        refs[-4:],
    )
    weights_ref, hat_ref, gate_ref, hat_scale_ref, qkv_ref, slope_ref, slope_t_ref = (
        used[name] for name in USED[:7]
    )
    weight_t_ref, mixed_t_ref, normed_t_ref, rows_slope_ref = (used[name] for name in USED[7:11])
    rows_hat_ref, rows_scale_ref, place_ref, digits_ref = (used[name] for name in USED[11:])
    orders = slot_orders(len(got_refs))
    for turn, got_ref in enumerate(got_refs):
        apart = jnp.where((me_ref[0] & 1) == 0, orders[0][turn], orders[1][turn])
        wide_ref[apart] = got_ref[...]
    for slot in range(len(got_refs)):
        rows = wide_ref[dest_ref[slot] ^ (me_ref[0] // table_size)]
        live = lax.broadcasted_iota(jnp.int32, rows.shape, 0) < blocks_ref[slot] * BLK
        rows = jnp.where(live, rows.astype(F32), 0.0).astype(BF16)
        grad_y_ref[slot * SLOT : (slot + 1) * SLOT, :] = rows
    tokens, width = grad_y_ref.shape
    count = normed_t_ref.shape[1]
    gain_in, gain_out = gains_ref[0:1, :], gains_ref[1:2, :]
    gain_total = jnp.zeros((1, width), F32)
    for tile in range(tokens // TILE):
        rows = slice(tile * TILE, (tile + 1) * TILE)
        grad_mixed = dot(grad_y_ref[rows, :], weights_ref[:, 4 * width :], NT)
        hat = hat_ref[rows, :]
        active_ref[rows, :width] = (grad_mixed * hat * gain_out).astype(BF16)
        inner = grad_mixed * gate_ref[rows, :]
        gain_total = gain_total + jnp.sum(inner * hat, axis=0, keepdims=True)
        inner = inner * gain_out
        mean = jnp.mean(inner, axis=-1, keepdims=True)
        along = jnp.mean(inner * hat, axis=-1, keepdims=True)
        grad_att = ((inner - mean - hat * along) * hat_scale_ref[rows, :]).astype(BF16)
        for head in range(HEADS):
            vals, queries, keys = (
                qkv_ref[rows, part * width + head * HDIM : part * width + (head + 1) * HDIM]
                for part in range(3)
            )
            grad_o = grad_att[:, head * HDIM : (head + 1) * HDIM]
            grad_weight = dot(grad_o, vals, NT)
            grad_score = (grad_weight * slope_ref[tile * HEADS + head].astype(F32)).astype(BF16)
            weight_t = dot(vals, grad_o, NT)
            score_t = (weight_t * slope_t_ref[tile * HEADS + head].astype(F32)).astype(BF16)
            for part, value in (
                (1, dot(weight_t_ref[tile * HEADS + head], grad_o)),
                (2, dot(grad_score, keys)),
                (3, dot(score_t, queries)),
            ):
                first = part * width + head * HDIM
                active_ref[rows, first : first + HDIM] = value.astype(BF16)
    sums_ref[:, :width] = (dot(mixed_t_ref[...], grad_y_ref[...]) * factor).astype(BF16)
    gather = gather_of(ints_ref[:, :tokens], count)
    grad_normed = jnp.zeros((count, width), F32)
    for part in range(4):
        columns = slice(part * width, (part + 1) * width)
        summed = dot(gather, active_ref[:, columns])
        grad_hidden = (summed * rows_slope_ref[:, columns].astype(F32)).astype(BF16)
        sums_ref[:, (part + 1) * width : (part + 2) * width] = (
            dot(normed_t_ref[...], grad_hidden) * factor
        ).astype(BF16)
        grad_normed = grad_normed + dot(grad_hidden, weights_ref[:, columns], NT)
    hat = rows_hat_ref[...]
    gains = (jnp.sum(grad_normed * hat, axis=0, keepdims=True) * factor, gain_total * factor)
    plan.write(me_ref[0], sums_ref, part_refs)
    inner = grad_normed * gain_in
    mean = jnp.mean(inner, axis=-1, keepdims=True)
    along = jnp.mean(inner * hat, axis=-1, keepdims=True)
    row_grad = (inner - mean - hat * along) * rows_scale_ref[...] + dot(gather, grad_y_ref[...])
    places = table_ref.shape[0]
    spots = lax.broadcasted_iota(jnp.int32, (places, count), 0)
    hit = spots == jnp.broadcast_to(place_ref[...], (places, count))
    spread = jnp.where(hit, 1.0, 0.0).astype(BF16)
    table_ref[:, :width] = dot(spread, row_grad.astype(BF16)).astype(BF16)
    extra = plan.extra
    lanes = []
    for row in range(plan.capacity):
        first = row * plan.gain_lanes
        gain = gains[first // width][:, first % width : first % width + plan.gain_lanes]
        rest = extra - GAIN_AT - plan.gain_lanes
        row_parts = [jnp.zeros((1, GAIN_AT), F32), gain]
        lanes.append(jnp.concatenate(row_parts + [jnp.zeros((1, rest), F32)] * (rest > 0), axis=1))
    lanes = jnp.concatenate(lanes, axis=0).astype(BF16)
    repeat = lax.broadcasted_iota(jnp.int32, (places, plan.capacity), 0) % plan.capacity
    lane = lax.broadcasted_iota(jnp.int32, (places, plan.capacity), 1)
    repeat = jnp.where(repeat == lane, 1.0, 0.0).astype(BF16)
    table_ref[:, width:] = dot(repeat, lanes).astype(BF16)
    table_ref[:, width : width + LANES] += dot(spread, digits_ref[...]).astype(BF16)


class Plan:
    def __init__(self, dp_size, table_size, count, width):
        self.chunks = dp_size * table_size
        self.capacity = 2 * count // self.chunks
        self.row_groups = min(self.chunks, width // CHUNK_ROWS)
        self.column_groups = self.chunks // self.row_groups
        block = self.column_groups * LANES
        self.wide = -(-5 * width // block) * LANES
        self.gain_lanes = 2 * width // self.capacity
        self.extra = -(-(GAIN_AT + self.gain_lanes) // LANES) * LANES
        self.split = -(-self.wide // (2 * LANES)) * LANES
        self.halves = ((0, self.split), (self.split, self.wide - self.split))
        table_bits = [1 << bit for bit in range(1, table_size.bit_length() - 1)]
        dp_bits = [table_size << bit for bit in range(dp_size.bit_length() - 1)]
        self.near_steps = len(table_bits) + 1
        self.orders = (table_bits + dp_bits, dp_bits[:1] + table_bits + dp_bits[1:])

    def chunk(self, me, side, place):
        order = [1] + self.orders[side]
        mask = 0
        for step, bit in enumerate(order):
            if place >> (len(order) - 1 - step) & 1:
                mask ^= bit
        return me ^ mask

    def columns(self, chunk, part):
        begin, size = part
        if self.column_groups == 1:
            return slice(begin, begin + size)
        group = chunk >> (self.row_groups.bit_length() - 1)
        return pl.ds(pl.multiple_of(group * self.wide + begin, LANES), size)

    def write(self, me, sums_ref, part_refs):
        half = self.chunks // 2
        for side in range(2):
            for place in range(self.chunks):
                chunk = self.chunk(me, side, place)
                first = pl.multiple_of((chunk & (self.row_groups - 1)) * CHUNK_ROWS, CHUNK_ROWS)
                rows = pl.ds(first, CHUNK_ROWS)
                out_ref = part_refs[2 * side + place // half]
                out_ref[place % half] = sums_ref[rows, self.columns(chunk, self.halves[side])]


def table_body(plan, got_ref, out_ref, gain_in_ref, gain_out_ref):
    places, width = got_ref.shape[0], out_ref.shape[1]
    lane = lax.broadcasted_iota(jnp.int32, (16, LANES), 1)
    scale = jnp.where(lane == 0, 32.0, jnp.where(lane == 1, 1.0, 0.0)).astype(BF16)
    numbers = dot(scale, got_ref[:, width : width + LANES], NT)[0:1].astype(jnp.int32)
    step = 256
    for first in range(0, out_ref.shape[0], step):
        sub = lax.broadcasted_iota(jnp.int32, (step, places), 0) + first
        hit = jnp.where(sub == jnp.broadcast_to(numbers, (step, places)), 1.0, 0.0)
        out_ref[first : first + step, :] = dot(hit.astype(BF16), got_ref[:, :width])
    sub = lax.broadcasted_iota(jnp.int32, (16, places), 0)
    lane = lax.broadcasted_iota(jnp.int32, (16, places), 1) % plan.capacity
    total = dot(jnp.where(sub == lane, 1.0, 0.0).astype(BF16), got_ref[:, width:])
    for row in range(plan.capacity):
        first = row * plan.gain_lanes
        gain_ref = (gain_in_ref, gain_out_ref)[first // width]
        gain_ref[:, first % width : first % width + plan.gain_lanes] = total[
            row : row + 1, GAIN_AT : GAIN_AT + plan.gain_lanes
        ]


def widen_body(plan, came, me_ref, left_ref, right_ref, *refs):
    w_in_ref, w_out_ref, stage_ref, sems = refs[-4:]
    side = (me_ref[0] & 1) ^ came
    half, blocks = plan.chunks // 2, plan.row_groups // 2
    for part, in_ref in enumerate((left_ref, right_ref)):
        for place in range(half):
            chunk = plan.chunk(me_ref[0], part, came * half + place)
            row = (chunk & (plan.row_groups - 1)) >> 1
            rows = pl.ds(pl.multiple_of(row * CHUNK_ROWS, CHUNK_ROWS), CHUNK_ROWS)
            stage_ref[rows, plan.columns(chunk, plan.halves[part])] = in_ref[place].astype(F32)
    split = w_out_ref.shape[1]
    copies = []
    for block in range(blocks):
        first = pl.multiple_of((2 * block + side) * CHUNK_ROWS, CHUNK_ROWS)
        here = stage_ref.at[pl.ds(block * CHUNK_ROWS, CHUNK_ROWS)]
        there = pl.ds(first, CHUNK_ROWS)
        copies += [
            pltpu.make_async_copy(here.at[:, split:], w_in_ref.at[there], sems.at[0, block]),
            pltpu.make_async_copy(here.at[:, :split], w_out_ref.at[there], sems.at[1, block]),
        ]
    for copy in copies:
        copy.start()
    for copy in copies:
        copy.wait()


def add(left, right):
    return (left.astype(F32) + right.astype(F32)).astype(BF16)


def on_device(
    touched_rows,
    row_of_token,
    row_owner,
    owner_row,
    seq_blocks,
    seq_dest,
    grad_out,
    w_in,
    w_out,
    gain_in,
    gain_out,
):
    dp_size, table_size = lax.axis_size("dp"), lax.axis_size("table")
    both = ("dp", "table")
    count, width = touched_rows.shape
    tokens = row_of_token.shape[0]
    plan = Plan(dp_size, table_size, count, width)
    devices_all = plan.chunks
    total_factor = 1.0 / math.sqrt(grad_out.shape[0] * devices_all)
    gain_rows = jnp.stack([gain_in, gain_out])
    ints = jnp.concatenate([row_of_token, row_owner[:, 0], owner_row])[None, :]
    me = lax.axis_index(both).astype(jnp.int32)[None]

    def swap(values, *masks):
        pairs = [(here, here ^ masks[here % len(masks)]) for here in range(devices_all)]
        return lax.ppermute(values, both, pairs)

    def exchange(values, axes, groups):
        return lax.all_to_all(
            values, axes, split_axis=0, concat_axis=0, tiled=True, axis_index_groups=groups
        )

    peers = jnp.arange(dp_size, dtype=jnp.int32)
    own = jnp.sum(jnp.where(seq_dest[:, None] == peers, seq_blocks[:, None], 0), axis=0)
    lengths = jnp.where(peers[:, None] == lax.axis_index("dp"), own, 0)
    steps = [table_size << bit for bit in range(dp_size.bit_length() - 1)]
    for step, mask in enumerate(steps[::2]):
        pair = steps[2 * step + 1 : 2 * step + 2]
        came = [swap(lengths, mask)] + [swap(lengths, far) for far in pair]
        came += [swap(lengths, far ^ mask) for far in pair]
        lengths = lengths + sum(came)
        if step == 0:
            lengths, touched_rows = lax.optimization_barrier((lengths, touched_rows))
    rows = jnp.concatenate([touched_rows, grad_out])
    weights = jnp.concatenate([w_in, w_out], axis=1)
    send = call(
        functools.partial(send_body, table_size, count),
        [shape_of((SLOT, width), BF16)] * dp_size,
        [SMEM] * 2 + [VMEM],
        scratch=[pltpu.SMEM((dp_size,), jnp.int32)],
    )(me, lengths, rows)
    got = list(send)
    orders = slot_orders(dp_size)
    for turn in range(1, dp_size):
        got[turn] = swap(send[turn], *(order[turn] * table_size for order in orders))
    shapes = row_shapes(count, width)
    made = call(
        functools.partial(rows_body, plan.capacity),
        list(shapes.values()),
        [VMEM] * 4,
        flops=8 * count * width * width,
        moved=4_000_000,
    )(rows, weights, gain_rows, ints)
    saved = dict(zip(shapes, made), weights=weights)
    got[0], after = lax.optimization_barrier((got[0], ints))
    shapes = token_shapes(tokens, width)
    made = call(
        forward_body,
        list(shapes.values()),
        [VMEM] * 3,
        flops=4 * count * width * width * 10,
        moved=8_000_000,
        mebibytes=12 + tokens // 32,
    )(saved["rows_active"], gain_rows, after)
    saved |= dict(zip(shapes, made))

    outs = [shape_of((devices_all * plan.capacity, width + plan.extra), BF16)]
    for _, wide in plan.halves:
        outs += [shape_of((devices_all // 2, CHUNK_ROWS, wide), BF16)] * 2
    table_send, *parts = call(
        functools.partial(backward_body, plan, table_size, total_factor),
        outs,
        [SMEM] * 3 + [VMEM] * (2 + len(USED) + dp_size),
        flops=4 * count * width * width * 40,
        moved=12_000_000,
        mebibytes=12 + tokens // 32,
        scratch=[
            pltpu.VMEM((dp_size, SLOT, width), BF16),
            pltpu.VMEM((width, plan.column_groups * plan.wide), BF16),
            pltpu.VMEM((tokens, 4 * width), BF16),
            pltpu.VMEM((tokens, width), BF16),
        ],
    )(
        me,
        seq_dest,
        seq_blocks,
        ints,
        gain_rows,
        *(saved[name] for name in USED),
        *got,
    )

    def reduced(kept, mask):
        middle = kept.shape[0] // 2
        return add(kept[:middle], swap(kept[middle:], mask))

    def gathered(kept, mask):
        return jnp.concatenate([kept, swap(kept, mask)])

    sides = [add(parts[2 * side], swap(parts[2 * side + 1], 1)) for side in range(2)]
    *sides, table_send = lax.optimization_barrier((*sides, table_send))
    low = min(2, dp_size)
    high, inside = dp_size // low, low * table_size
    groups = [[upper * low + lower for upper in range(high)] for lower in range(low)]
    table_got = exchange(table_send.reshape(high, inside, plan.capacity, -1), "dp", groups)
    for step in range(plan.near_steps):
        sides = [reduced(sides[side], plan.orders[side][step]) for side in range(2)]
    kept = jnp.concatenate(sides, axis=2)
    away = plan.orders[0][plan.near_steps :]
    kept = reduced(kept, away[0])
    kept, table_got = lax.optimization_barrier((kept, table_got))
    groups = [[upper * inside + lower for lower in range(inside)] for upper in range(high)]
    table_got = exchange(jnp.swapaxes(table_got, 0, 1), both, groups)
    for mask in away[1:]:
        kept = reduced(kept, mask)
    back = plan.orders[0][: plan.near_steps - 1 : -1]
    kept = gathered(kept, back[0])
    kept, table_got = lax.optimization_barrier((kept, table_got))
    table_part, grad_gain_in, grad_gain_out = call(
        functools.partial(table_body, plan),
        (
            shape_of((ROWS_DEV, width), F32),
            shape_of((1, width), F32),
            shape_of((1, width), F32),
        ),
        [VMEM],
    )(table_got.reshape(devices_all * plan.capacity, -1))
    for mask in back[1:]:
        kept = gathered(kept, mask)
    kept, table_part = lax.optimization_barrier((kept, table_part))
    sides = [kept[..., : plan.split], kept[..., plan.split :]]
    for step in reversed(range(plan.near_steps)):
        sides = [gathered(sides[side], plan.orders[side][step]) for side in range(2)]
    came = [swap(side, 1) for side in sides]
    rows = width // 2
    outs = [shape_of(w_in.shape, F32), shape_of(w_out.shape, F32)]
    for turn, parts in enumerate((sides, came)):
        written = () if turn == 0 else (grad_w_in, grad_w_out)
        grad_w_in, grad_w_out = pl.pallas_call(
            functools.partial(widen_body, plan, turn),
            out_shape=outs,
            in_specs=[SMEM] + [VMEM] * 2 + [ANY] * len(written),
            out_specs=[ANY] * 2,
            scratch_shapes=[
                pltpu.VMEM((rows, 5 * width), F32),
                pltpu.SemaphoreType.DMA((2, plan.row_groups // 2)),
            ],
            input_output_aliases={3: 0, 4: 1} if written else {},
            compiler_params=pltpu.CompilerParams(vmem_limit_bytes=24 * 1024 * 1024),
            cost_estimate=pl.CostEstimate(flops=0, bytes_accessed=4_000_000, transcendentals=0),
        )(me, *parts, *written)
    return (table_part, grad_w_in, grad_w_out, grad_gain_in[0], grad_gain_out[0])


def solution(mesh):
    rows = P(("dp", "table"), None)
    flat = P(("dp", "table"))
    in_specs = (rows, flat, rows, flat, flat, flat, rows, P(), P(), P(), P())
    out_specs = (rows, P(), P(), P(), P())
    return jax.shard_map(
        on_device, mesh=mesh, in_specs=in_specs, out_specs=out_specs, check_vma=False
    )
```

```python
import functools
import math

import jax
import jax.numpy as jnp
from jax import lax
from jax.experimental import pallas as pl
from jax.experimental.pallas import tpu as pltpu
from jax.sharding import PartitionSpec as P

HEADS = 4
HDIM = 128
BLK = 16
LMAXB = 4
SLOT = LMAXB * BLK
ROWS_DEV = 1024
TILE = 2 * SLOT
LANES = 128
CHUNK_ROWS = 16
GAIN_AT = 64
EPSILON = 1e-05
F32 = jnp.float32
BF16 = jnp.bfloat16
VMEM = pl.BlockSpec(memory_space=pltpu.VMEM)
SMEM = pl.BlockSpec(memory_space=pltpu.SMEM)
ANY = pl.BlockSpec(memory_space=pl.ANY)


def call(body, out_shape, in_specs, flops=0, moved=0, scratch=(), mebibytes=24):
    outs = jax.tree.map(lambda _: VMEM, out_shape)
    return pl.pallas_call(
        body,
        out_shape=out_shape,
        in_specs=in_specs,
        out_specs=outs,
        scratch_shapes=scratch,
        compiler_params=pltpu.CompilerParams(vmem_limit_bytes=mebibytes * 1024 * 1024),
        cost_estimate=pl.CostEstimate(flops=flops, bytes_accessed=moved, transcendentals=0),
    )


def shape_of(dims, dtype):
    return jax.ShapeDtypeStruct(dims, dtype)


def sigmoid(values):
    return 0.5 * jnp.tanh(0.5 * values) + 0.5


def dot(left, right, contract=((1,), (0,))):
    return lax.dot_general(left, right, (contract, ((), ())), preferred_element_type=F32)


NT = ((1,), (1,))
TN = ((0,), (0,))


def slot_orders(peers):
    far = list(range(peers - 1, peers // 2 - 1, -1))
    near = list(range(peers // 2 - 1, 0, -1))
    return [0] + far + near, [0] + near + far


def send_body(table_size, count, me_ref, lengths_ref, rows_ref, *refs):
    out_refs, begin_ref = refs[:-1], refs[-1]
    peers = len(out_refs)
    blocks = (rows_ref.shape[0] - count) // BLK
    me = me_ref[0] // table_size
    begin = jnp.int32(0)
    for peer in range(peers):
        begin_ref[peer] = begin
        begin = begin + lengths_ref[peer, me]
    orders = slot_orders(peers)
    for turn, out_ref in enumerate(out_refs):
        apart = jnp.where((me_ref[0] & 1) == 0, orders[0][turn], orders[1][turn])
        begin = begin_ref[me ^ apart]
        for inner in range(LMAXB):
            block = jnp.minimum(begin + inner, blocks - 1)
            rows = rows_ref[pl.ds(pl.multiple_of(count + block * BLK, BLK), BLK), :]
            out_ref[inner * BLK : (inner + 1) * BLK, :] = rows


def tile_mask():
    sub = lax.broadcasted_iota(jnp.int32, (TILE, TILE), 0)
    lane = lax.broadcasted_iota(jnp.int32, (TILE, TILE), 1)
    return (sub // SLOT == lane // SLOT) & (lane <= sub)


def row_shapes(count, width):
    return dict(
        rows_active=shape_of((count, 5 * width), BF16),
        normed_t=shape_of((width, count), BF16),
        rows_slope=shape_of((count, 4 * width), BF16),
        rows_hat=shape_of((count, width), F32),
        rows_scale=shape_of((count, 1), F32),
        place=shape_of((1, count), jnp.int32),
        digits=shape_of((count, LANES), BF16),
    )


def token_shapes(tokens, width):
    pairs = tokens // TILE * HEADS
    return dict(
        gate=shape_of((tokens, width), F32),
        hat=shape_of((tokens, width), F32),
        hat_scale=shape_of((tokens, 1), F32),
        qkv=shape_of((tokens, 3 * width), BF16),
        slope=shape_of((pairs, TILE, TILE), BF16),
        slope_t=shape_of((pairs, TILE, TILE), BF16),
        weight_t=shape_of((pairs, TILE, TILE), BF16),
        mixed_t=shape_of((width, tokens), BF16),
    )


def column_of(row):
    wide = jnp.broadcast_to(row.astype(F32), (8, row.shape[1])).T
    return wide[:, 0:1].astype(jnp.int32)


def rows_body(
    capacity,
    rows_ref,
    weights_ref,
    gains_ref,
    ints_ref,
    rows_active_ref,
    normed_t_ref,
    rows_slope_ref,
    rows_hat_ref,
    rows_scale_ref,
    place_ref,
    digits_ref,
):
    count, width = rows_hat_ref.shape
    tokens = ints_ref.shape[1] - 2 * count
    owner_row = ints_ref[:, tokens : tokens + count]
    across = jnp.broadcast_to(owner_row, (count, count))
    down = jnp.broadcast_to(column_of(owner_row), (count, count))
    sub = lax.broadcasted_iota(jnp.int32, (count, count), 0)
    lane = lax.broadcasted_iota(jnp.int32, (count, count), 1)
    earlier = jnp.where((across == down) & (sub < lane), 1.0, 0.0)
    rank = jnp.sum(earlier, axis=0, keepdims=True).astype(jnp.int32)
    place_ref[...] = owner_row * capacity + rank
    number = jnp.broadcast_to(column_of(ints_ref[:, tokens + count :]), (count, LANES))
    lane = lax.broadcasted_iota(jnp.int32, (count, LANES), 1)
    digits = jnp.where(lane == 0, number >> 5, jnp.where(lane == 1, number & 31, 0))
    digits_ref[...] = digits.astype(F32).astype(BF16)
    values = rows_ref[:count, :].astype(F32)
    shifted = values - jnp.mean(values, axis=-1, keepdims=True)
    scale = lax.rsqrt(jnp.mean(shifted * shifted, axis=-1, keepdims=True) + EPSILON)
    hat = shifted * scale
    rows_hat_ref[...] = hat
    rows_scale_ref[...] = scale
    normed = hat * gains_ref[0:1, :]
    normed_t_ref[...] = normed.T.astype(BF16)
    normed = normed.astype(BF16)
    for part in range(4):
        columns = slice(part * width, (part + 1) * width)
        hidden = dot(normed, weights_ref[:, columns])
        sigma = sigmoid(hidden)
        active = hidden * sigma
        slope = sigma * (1.0 + hidden * (1.0 - sigma))
        rows_slope_ref[:, columns] = slope.astype(BF16)
        high = active.astype(BF16)
        rows_active_ref[:, columns] = high
        if part == 0:
            rows_active_ref[:, 4 * width :] = (active - high.astype(F32)).astype(BF16)


def forward_body(
    rows_active_ref,
    gains_ref,
    ints_ref,
    gate_ref,
    hat_ref,
    hat_scale_ref,
    qkv_ref,
    slope_ref,
    slope_t_ref,
    weight_t_ref,
    mixed_t_ref,
):
    count = rows_active_ref.shape[0]
    tokens, width = gate_ref.shape
    items = column_of(ints_ref[:, :tokens])
    lane = lax.broadcasted_iota(jnp.int32, (tokens, count), 1)
    pick = jnp.where(lane == jnp.broadcast_to(items, (tokens, count)), 1.0, 0.0).astype(BF16)
    gate_ref[...] = dot(pick, rows_active_ref[:, :width]) + dot(
        pick, rows_active_ref[:, 4 * width :]
    )
    for part in range(3):
        columns = slice((part + 1) * width, (part + 2) * width)
        qkv_ref[:, part * width : (part + 1) * width] = dot(pick, rows_active_ref[:, columns]).astype(
            BF16
        )
    gain_out = gains_ref[1:2, :]
    mask = tile_mask()
    factor = HDIM ** (-0.5)
    for tile in range(tokens // TILE):
        rows = slice(tile * TILE, (tile + 1) * TILE)
        parts = []
        for head in range(HEADS):
            vals, queries, keys = (
                qkv_ref[rows, part * width + head * HDIM : part * width + (head + 1) * HDIM]
                for part in range(3)
            )
            score = dot(queries, keys, NT) * factor
            sigma = sigmoid(score)
            weight = jnp.where(mask, score * sigma, 0.0)
            slope = sigma * (1.0 + score * (1.0 - sigma)) * factor
            slope = jnp.where(mask, slope, 0.0)
            slope_ref[tile * HEADS + head] = slope.astype(BF16)
            slope_t_ref[tile * HEADS + head] = slope.T.astype(BF16)
            weight_t_ref[tile * HEADS + head] = weight.T.astype(BF16)
            parts.append(dot(weight.astype(BF16), vals))
        attended = jnp.concatenate(parts, axis=1)
        shifted = attended - jnp.mean(attended, axis=-1, keepdims=True)
        scale = lax.rsqrt(jnp.mean(shifted * shifted, axis=-1, keepdims=True) + EPSILON)
        hat = shifted * scale
        hat_ref[rows, :] = hat
        hat_scale_ref[rows, :] = scale
        mixed = hat * gain_out * gate_ref[rows, :]
        mixed_t_ref[:, rows] = mixed.T.astype(BF16)


def gather_of(items, count):
    tokens = items.shape[1]
    sub = lax.broadcasted_iota(jnp.int32, (count, tokens), 0)
    hit = sub == jnp.broadcast_to(items, (count, tokens))
    return jnp.where(hit, 1.0, 0.0).astype(BF16)


USED = (
    "weights",
    "hat",
    "gate",
    "hat_scale",
    "qkv",
    "slope",
    "slope_t",
    "weight_t",
    "mixed_t",
    "normed_t",
    "rows_slope",
    "rows_hat",
    "rows_scale",
    "place",
    "digits",
)


def backward_body(
    plan,
    table_size,
    factor,
    me_ref,
    dest_ref,
    blocks_ref,
    ints_ref,
    gains_ref,
    *refs,
):
    used, refs = dict(zip(USED, refs)), refs[len(USED) :]
    got_refs, (table_ref, *part_refs), (wide_ref, sums_ref, active_ref, grad_y_ref) = (
        refs[:-9],
        refs[-9:-4],
        refs[-4:],
    )
    weights_ref, hat_ref, gate_ref, hat_scale_ref, qkv_ref, slope_ref, slope_t_ref = (
        used[name] for name in USED[:7]
    )
    weight_t_ref, mixed_t_ref, normed_t_ref, rows_slope_ref = (used[name] for name in USED[7:11])
    rows_hat_ref, rows_scale_ref, place_ref, digits_ref = (used[name] for name in USED[11:])
    orders = slot_orders(len(got_refs))
    for turn, got_ref in enumerate(got_refs):
        apart = jnp.where((me_ref[0] & 1) == 0, orders[0][turn], orders[1][turn])
        wide_ref[apart] = got_ref[...]
    for slot in range(len(got_refs)):
        rows = wide_ref[dest_ref[slot] ^ (me_ref[0] // table_size)]
        live = lax.broadcasted_iota(jnp.int32, rows.shape, 0) < blocks_ref[slot] * BLK
        rows = jnp.where(live, rows.astype(F32), 0.0).astype(BF16)
        grad_y_ref[slot * SLOT : (slot + 1) * SLOT, :] = rows
    tokens, width = grad_y_ref.shape
    count = normed_t_ref.shape[1]
    gain_in, gain_out = gains_ref[0:1, :], gains_ref[1:2, :]
    gain_total = jnp.zeros((1, width), F32)
    for tile in range(tokens // TILE):
        rows = slice(tile * TILE, (tile + 1) * TILE)
        grad_mixed = dot(grad_y_ref[rows, :], weights_ref[:, 4 * width :], NT)
        hat = hat_ref[rows, :]
        active_ref[rows, :width] = (grad_mixed * hat * gain_out).astype(BF16)
        inner = grad_mixed * gate_ref[rows, :]
        gain_total = gain_total + jnp.sum(inner * hat, axis=0, keepdims=True)
        inner = inner * gain_out
        mean = jnp.mean(inner, axis=-1, keepdims=True)
        along = jnp.mean(inner * hat, axis=-1, keepdims=True)
        grad_att = ((inner - mean - hat * along) * hat_scale_ref[rows, :]).astype(BF16)
        for head in range(HEADS):
            vals, queries, keys = (
                qkv_ref[rows, part * width + head * HDIM : part * width + (head + 1) * HDIM]
                for part in range(3)
            )
            grad_o = grad_att[:, head * HDIM : (head + 1) * HDIM]
            grad_weight = dot(grad_o, vals, NT)
            grad_score = (grad_weight * slope_ref[tile * HEADS + head].astype(F32)).astype(BF16)
            weight_t = dot(vals, grad_o, NT)
            score_t = (weight_t * slope_t_ref[tile * HEADS + head].astype(F32)).astype(BF16)
            for part, value in (
                (1, dot(weight_t_ref[tile * HEADS + head], grad_o)),
                (2, dot(grad_score, keys)),
                (3, dot(score_t, queries)),
            ):
                first = part * width + head * HDIM
                active_ref[rows, first : first + HDIM] = value.astype(BF16)
    sums_ref[:, :width] = (dot(mixed_t_ref[...], grad_y_ref[...]) * factor).astype(BF16)
    gather = gather_of(ints_ref[:, :tokens], count)
    grad_normed = jnp.zeros((count, width), F32)
    for part in range(4):
        columns = slice(part * width, (part + 1) * width)
        summed = dot(gather, active_ref[:, columns])
        grad_hidden = (summed * rows_slope_ref[:, columns].astype(F32)).astype(BF16)
        sums_ref[:, (part + 1) * width : (part + 2) * width] = (
            dot(normed_t_ref[...], grad_hidden) * factor
        ).astype(BF16)
        grad_normed = grad_normed + dot(grad_hidden, weights_ref[:, columns], NT)
    hat = rows_hat_ref[...]
    gains = (jnp.sum(grad_normed * hat, axis=0, keepdims=True) * factor, gain_total * factor)
    plan.write(me_ref[0], sums_ref, part_refs)
    inner = grad_normed * gain_in
    mean = jnp.mean(inner, axis=-1, keepdims=True)
    along = jnp.mean(inner * hat, axis=-1, keepdims=True)
    row_grad = (inner - mean - hat * along) * rows_scale_ref[...] + dot(gather, grad_y_ref[...])
    places = table_ref.shape[0]
    spots = lax.broadcasted_iota(jnp.int32, (places, count), 0)
    hit = spots == jnp.broadcast_to(place_ref[...], (places, count))
    spread = jnp.where(hit, 1.0, 0.0).astype(BF16)
    table_ref[:, :width] = dot(spread, row_grad.astype(BF16)).astype(BF16)
    extra = plan.extra
    lanes = []
    for row in range(plan.capacity):
        first = row * plan.gain_lanes
        gain = gains[first // width][:, first % width : first % width + plan.gain_lanes]
        rest = extra - GAIN_AT - plan.gain_lanes
        row_parts = [jnp.zeros((1, GAIN_AT), F32), gain]
        lanes.append(jnp.concatenate(row_parts + [jnp.zeros((1, rest), F32)] * (rest > 0), axis=1))
    lanes = jnp.concatenate(lanes, axis=0).astype(BF16)
    repeat = lax.broadcasted_iota(jnp.int32, (places, plan.capacity), 0) % plan.capacity
    lane = lax.broadcasted_iota(jnp.int32, (places, plan.capacity), 1)
    repeat = jnp.where(repeat == lane, 1.0, 0.0).astype(BF16)
    table_ref[:, width:] = dot(repeat, lanes).astype(BF16)
    table_ref[:, width : width + LANES] += dot(spread, digits_ref[...]).astype(BF16)


class Plan:
    def __init__(self, dp_size, table_size, count, width):
        self.chunks = dp_size * table_size
        self.capacity = 2 * count // self.chunks
        self.row_groups = min(self.chunks, width // CHUNK_ROWS)
        self.column_groups = self.chunks // self.row_groups
        block = self.column_groups * LANES
        self.wide = -(-5 * width // block) * LANES
        self.gain_lanes = 2 * width // self.capacity
        self.extra = -(-(GAIN_AT + self.gain_lanes) // LANES) * LANES
        first = -(-3 * self.wide // (5 * LANES)) * LANES
        self.split = -(-self.wide // (2 * LANES)) * LANES
        self.sides = ((0, first), (first, self.wide - first))
        self.halves = ((0, self.split), (self.split, self.wide - self.split))
        table_bits = [1 << bit for bit in range(1, table_size.bit_length() - 1)]
        dp_bits = [table_size << bit for bit in range(dp_size.bit_length() - 1)]
        self.near_steps = len(table_bits) + 1
        self.orders = (table_bits + dp_bits, dp_bits[:1] + table_bits + dp_bits[1:])

    def chunk(self, me, side, place):
        order = [1] + self.orders[side]
        mask = 0
        for step, bit in enumerate(order):
            if place >> (len(order) - 1 - step) & 1:
                mask ^= bit
        return me ^ mask

    def columns(self, chunk, part):
        begin, size = part
        if self.column_groups == 1:
            return slice(begin, begin + size)
        group = chunk >> (self.row_groups.bit_length() - 1)
        return pl.ds(pl.multiple_of(group * self.wide + begin, LANES), size)

    def write(self, me, sums_ref, part_refs):
        half = self.chunks // 2
        for side in range(2):
            for place in range(self.chunks):
                chunk = self.chunk(me, side, place)
                first = pl.multiple_of((chunk & (self.row_groups - 1)) * CHUNK_ROWS, CHUNK_ROWS)
                rows = pl.ds(first, CHUNK_ROWS)
                out_ref = part_refs[2 * side + place // half]
                out_ref[place % half] = sums_ref[rows, self.columns(chunk, self.sides[side])]


def table_body(plan, got_ref, out_ref, gain_in_ref, gain_out_ref):
    places, width = got_ref.shape[0], out_ref.shape[1]
    lane = lax.broadcasted_iota(jnp.int32, (16, LANES), 1)
    scale = jnp.where(lane == 0, 32.0, jnp.where(lane == 1, 1.0, 0.0)).astype(BF16)
    numbers = dot(scale, got_ref[:, width : width + LANES], NT)[0:1].astype(jnp.int32)
    step = 256
    for first in range(0, out_ref.shape[0], step):
        sub = lax.broadcasted_iota(jnp.int32, (step, places), 0) + first
        hit = jnp.where(sub == jnp.broadcast_to(numbers, (step, places)), 1.0, 0.0)
        out_ref[first : first + step, :] = dot(hit.astype(BF16), got_ref[:, :width])
    sub = lax.broadcasted_iota(jnp.int32, (16, places), 0)
    lane = lax.broadcasted_iota(jnp.int32, (16, places), 1) % plan.capacity
    total = dot(jnp.where(sub == lane, 1.0, 0.0).astype(BF16), got_ref[:, width:])
    for row in range(plan.capacity):
        first = row * plan.gain_lanes
        gain_ref = (gain_in_ref, gain_out_ref)[first // width]
        gain_ref[:, first % width : first % width + plan.gain_lanes] = total[
            row : row + 1, GAIN_AT : GAIN_AT + plan.gain_lanes
        ]


def widen_body(plan, came, me_ref, left_ref, right_ref, *refs):
    w_in_ref, w_out_ref, stage_ref, sems = refs[-4:]
    side = (me_ref[0] & 1) ^ came
    half, blocks = plan.chunks // 2, plan.row_groups // 2
    for part, in_ref in enumerate((left_ref, right_ref)):
        for place in range(half):
            chunk = plan.chunk(me_ref[0], part, came * half + place)
            row = (chunk & (plan.row_groups - 1)) >> 1
            rows = pl.ds(pl.multiple_of(row * CHUNK_ROWS, CHUNK_ROWS), CHUNK_ROWS)
            stage_ref[rows, plan.columns(chunk, plan.halves[part])] = in_ref[place].astype(F32)
    split = w_out_ref.shape[1]
    copies = []
    for block in range(blocks):
        first = pl.multiple_of((2 * block + side) * CHUNK_ROWS, CHUNK_ROWS)
        here = stage_ref.at[pl.ds(block * CHUNK_ROWS, CHUNK_ROWS)]
        there = pl.ds(first, CHUNK_ROWS)
        copies += [
            pltpu.make_async_copy(here.at[:, split:], w_in_ref.at[there], sems.at[0, block]),
            pltpu.make_async_copy(here.at[:, :split], w_out_ref.at[there], sems.at[1, block]),
        ]
    for copy in copies:
        copy.start()
    for copy in copies:
        copy.wait()


def add(left, right):
    return (left.astype(F32) + right.astype(F32)).astype(BF16)


def on_device(
    touched_rows,
    row_of_token,
    row_owner,
    owner_row,
    seq_blocks,
    seq_dest,
    grad_out,
    w_in,
    w_out,
    gain_in,
    gain_out,
):
    dp_size, table_size = lax.axis_size("dp"), lax.axis_size("table")
    both = ("dp", "table")
    count, width = touched_rows.shape
    tokens = row_of_token.shape[0]
    plan = Plan(dp_size, table_size, count, width)
    devices_all = plan.chunks
    total_factor = 1.0 / math.sqrt(grad_out.shape[0] * devices_all)
    gain_rows = jnp.stack([gain_in, gain_out])
    ints = jnp.concatenate([row_of_token, row_owner[:, 0], owner_row])[None, :]
    me = lax.axis_index(both).astype(jnp.int32)[None]

    def swap(values, *masks):
        pairs = [(here, here ^ masks[here % len(masks)]) for here in range(devices_all)]
        return lax.ppermute(values, both, pairs)

    def exchange(values, axes, groups):
        return lax.all_to_all(
            values, axes, split_axis=0, concat_axis=0, tiled=True, axis_index_groups=groups
        )

    peers = jnp.arange(dp_size, dtype=jnp.int32)
    own = jnp.sum(jnp.where(seq_dest[:, None] == peers, seq_blocks[:, None], 0), axis=0)
    lengths = jnp.where(peers[:, None] == lax.axis_index("dp"), own, 0)
    steps = [table_size << bit for bit in range(dp_size.bit_length() - 1)]
    for step, mask in enumerate(steps[::2]):
        pair = steps[2 * step + 1 : 2 * step + 2]
        came = [swap(lengths, mask)] + [swap(lengths, far) for far in pair]
        came += [swap(lengths, far ^ mask) for far in pair]
        lengths = lengths + sum(came)
        if step == 0:
            lengths, touched_rows = lax.optimization_barrier((lengths, touched_rows))
    rows = jnp.concatenate([touched_rows, grad_out])
    weights = jnp.concatenate([w_in, w_out], axis=1)
    send = call(
        functools.partial(send_body, table_size, count),
        [shape_of((SLOT, width), BF16)] * dp_size,
        [SMEM] * 2 + [VMEM],
        scratch=[pltpu.SMEM((dp_size,), jnp.int32)],
    )(me, lengths, rows)
    got = list(send)
    orders = slot_orders(dp_size)
    for turn in range(1, dp_size):
        got[turn] = swap(send[turn], *(order[turn] * table_size for order in orders))
    shapes = row_shapes(count, width)
    made = call(
        functools.partial(rows_body, plan.capacity),
        list(shapes.values()),
        [VMEM] * 4,
        flops=8 * count * width * width,
        moved=4_000_000,
    )(rows, weights, gain_rows, ints)
    saved = dict(zip(shapes, made), weights=weights)
    got[0], after = lax.optimization_barrier((got[0], ints))
    shapes = token_shapes(tokens, width)
    made = call(
        forward_body,
        list(shapes.values()),
        [VMEM] * 3,
        flops=4 * count * width * width * 10,
        moved=8_000_000,
        mebibytes=12 + tokens // 32,
    )(saved["rows_active"], gain_rows, after)
    saved |= dict(zip(shapes, made))

    outs = [shape_of((devices_all * plan.capacity, width + plan.extra), BF16)]
    for _, wide in plan.sides:
        outs += [shape_of((devices_all // 2, CHUNK_ROWS, wide), BF16)] * 2
    table_send, *parts = call(
        functools.partial(backward_body, plan, table_size, total_factor),
        outs,
        [SMEM] * 3 + [VMEM] * (2 + len(USED) + dp_size),
        flops=4 * count * width * width * 40,
        moved=12_000_000,
        mebibytes=12 + tokens // 32,
        scratch=[
            pltpu.VMEM((dp_size, SLOT, width), BF16),
            pltpu.VMEM((width, plan.column_groups * plan.wide), BF16),
            pltpu.VMEM((tokens, 4 * width), BF16),
            pltpu.VMEM((tokens, width), BF16),
        ],
    )(
        me,
        seq_dest,
        seq_blocks,
        ints,
        gain_rows,
        *(saved[name] for name in USED),
        *got,
    )

    def reduced(kept, mask):
        middle = kept.shape[0] // 2
        return add(kept[:middle], swap(kept[middle:], mask))

    def gathered(kept, mask):
        return jnp.concatenate([kept, swap(kept, mask)])

    sides = [add(parts[2 * side], swap(parts[2 * side + 1], 1)) for side in range(2)]
    *sides, table_send = lax.optimization_barrier((*sides, table_send))
    low = min(2, dp_size)
    high, inside = dp_size // low, low * table_size
    groups = [[upper * low + lower for upper in range(high)] for lower in range(low)]
    table_got = exchange(table_send.reshape(high, inside, plan.capacity, -1), "dp", groups)
    for step in range(plan.near_steps):
        sides = [reduced(sides[side], plan.orders[side][step]) for side in range(2)]
    kept = jnp.concatenate(sides, axis=2)
    away = plan.orders[0][plan.near_steps :]
    kept = reduced(kept, away[0])
    kept, table_got = lax.optimization_barrier((kept, table_got))
    groups = [[upper * inside + lower for lower in range(inside)] for upper in range(high)]
    table_got = exchange(jnp.swapaxes(table_got, 0, 1), both, groups)
    for mask in away[1:]:
        kept = reduced(kept, mask)
    for mask in reversed(away):
        kept = gathered(kept, mask)
    kept, table_got = lax.optimization_barrier((kept, table_got))
    table_part, grad_gain_in, grad_gain_out = call(
        functools.partial(table_body, plan),
        (
            shape_of((ROWS_DEV, width), F32),
            shape_of((1, width), F32),
            shape_of((1, width), F32),
        ),
        [VMEM],
    )(table_got.reshape(devices_all * plan.capacity, -1))
    sides = [kept[..., : plan.split], kept[..., plan.split :]]
    for step in reversed(range(plan.near_steps)):
        if step == 0:
            *sides, table_part = lax.optimization_barrier((*sides, table_part))
        sides = [gathered(sides[side], plan.orders[side][step]) for side in range(2)]
    came = [swap(side, 1) for side in sides]
    rows = width // 2
    outs = [shape_of(w_in.shape, F32), shape_of(w_out.shape, F32)]
    for turn, parts in enumerate((sides, came)):
        written = () if turn == 0 else (grad_w_in, grad_w_out)
        grad_w_in, grad_w_out = pl.pallas_call(
            functools.partial(widen_body, plan, turn),
            out_shape=outs,
            in_specs=[SMEM] + [VMEM] * 2 + [ANY] * len(written),
            out_specs=[ANY] * 2,
            scratch_shapes=[
                pltpu.VMEM((rows, 5 * width), F32),
                pltpu.SemaphoreType.DMA((2, plan.row_groups // 2)),
            ],
            input_output_aliases={3: 0, 4: 1} if written else {},
            compiler_params=pltpu.CompilerParams(vmem_limit_bytes=24 * 1024 * 1024),
            cost_estimate=pl.CostEstimate(flops=0, bytes_accessed=4_000_000, transcendentals=0),
        )(me, *parts, *written)
    return (table_part, grad_w_in, grad_w_out, grad_gain_in[0], grad_gain_out[0])


def solution(mesh):
    rows = P(("dp", "table"), None)
    flat = P(("dp", "table"))
    in_specs = (rows, flat, rows, flat, flat, flat, rows, P(), P(), P(), P())
    out_specs = (rows, P(), P(), P(), P())
    return jax.shard_map(
        on_device, mesh=mesh, in_specs=in_specs, out_specs=out_specs, check_vma=False
    )
```

```python
import functools
import math

import jax
import jax.numpy as jnp
from jax import lax
from jax.experimental import pallas as pl
from jax.experimental.pallas import tpu as pltpu
from jax.sharding import PartitionSpec as P

HEADS = 4
HDIM = 128
BLK = 16
LMAXB = 4
SLOT = LMAXB * BLK
ROWS_DEV = 1024
TILE = 2 * SLOT
LANES = 128
CHUNK_ROWS = 16
GAIN_AT = 64
EPSILON = 1e-05
F32 = jnp.float32
BF16 = jnp.bfloat16
VMEM = pl.BlockSpec(memory_space=pltpu.VMEM)
SMEM = pl.BlockSpec(memory_space=pltpu.SMEM)
ANY = pl.BlockSpec(memory_space=pl.ANY)


def call(body, out_shape, in_specs, flops=0, moved=0, scratch=(), mebibytes=24):
    outs = jax.tree.map(lambda _: VMEM, out_shape)
    return pl.pallas_call(
        body,
        out_shape=out_shape,
        in_specs=in_specs,
        out_specs=outs,
        scratch_shapes=scratch,
        compiler_params=pltpu.CompilerParams(vmem_limit_bytes=mebibytes * 1024 * 1024),
        cost_estimate=pl.CostEstimate(flops=flops, bytes_accessed=moved, transcendentals=0),
    )


def shape_of(dims, dtype):
    return jax.ShapeDtypeStruct(dims, dtype)


def sigmoid(values):
    return 0.5 * jnp.tanh(0.5 * values) + 0.5


def dot(left, right, contract=((1,), (0,))):
    return lax.dot_general(left, right, (contract, ((), ())), preferred_element_type=F32)


NT = ((1,), (1,))
TN = ((0,), (0,))


def slot_orders(peers):
    far = list(range(peers - 1, peers // 2 - 1, -1))
    near = list(range(peers // 2 - 1, 0, -1))
    return [0] + far + near, [0] + near + far


def send_body(table_size, count, me_ref, lengths_ref, rows_ref, *refs):
    out_refs, begin_ref = refs[:-1], refs[-1]
    peers = len(out_refs)
    blocks = (rows_ref.shape[0] - count) // BLK
    me = me_ref[0] // table_size
    begin = jnp.int32(0)
    for peer in range(peers):
        begin_ref[peer] = begin
        begin = begin + lengths_ref[peer, me]
    orders = slot_orders(peers)
    for turn, out_ref in enumerate(out_refs):
        apart = jnp.where((me_ref[0] & 1) == 0, orders[0][turn], orders[1][turn])
        begin = begin_ref[me ^ apart]
        for inner in range(LMAXB):
            block = jnp.minimum(begin + inner, blocks - 1)
            rows = rows_ref[pl.ds(pl.multiple_of(count + block * BLK, BLK), BLK), :]
            out_ref[inner * BLK : (inner + 1) * BLK, :] = rows


def tile_mask():
    sub = lax.broadcasted_iota(jnp.int32, (TILE, TILE), 0)
    lane = lax.broadcasted_iota(jnp.int32, (TILE, TILE), 1)
    return (sub // SLOT == lane // SLOT) & (lane <= sub)


def row_shapes(count, width):
    return dict(
        rows_active=shape_of((count, 5 * width), BF16),
        normed_t=shape_of((width, count), BF16),
        rows_slope=shape_of((count, 4 * width), BF16),
        rows_hat=shape_of((count, width), F32),
        rows_scale=shape_of((count, 1), F32),
        place=shape_of((1, count), jnp.int32),
        digits=shape_of((count, LANES), BF16),
    )


def token_shapes(tokens, width):
    pairs = tokens // TILE * HEADS
    return dict(
        gate=shape_of((tokens, width), F32),
        hat=shape_of((tokens, width), F32),
        hat_scale=shape_of((tokens, 1), F32),
        qkv=shape_of((tokens, 3 * width), BF16),
        slope=shape_of((pairs, TILE, TILE), BF16),
        slope_t=shape_of((pairs, TILE, TILE), BF16),
        weight_t=shape_of((pairs, TILE, TILE), BF16),
        mixed_t=shape_of((width, tokens), BF16),
    )


def column_of(row):
    wide = jnp.broadcast_to(row.astype(F32), (8, row.shape[1])).T
    return wide[:, 0:1].astype(jnp.int32)


def rows_body(
    capacity,
    rows_ref,
    weights_ref,
    gains_ref,
    ints_ref,
    rows_active_ref,
    normed_t_ref,
    rows_slope_ref,
    rows_hat_ref,
    rows_scale_ref,
    place_ref,
    digits_ref,
):
    count, width = rows_hat_ref.shape
    tokens = ints_ref.shape[1] - 2 * count
    owner_row = ints_ref[:, tokens : tokens + count]
    across = jnp.broadcast_to(owner_row, (count, count))
    down = jnp.broadcast_to(column_of(owner_row), (count, count))
    sub = lax.broadcasted_iota(jnp.int32, (count, count), 0)
    lane = lax.broadcasted_iota(jnp.int32, (count, count), 1)
    earlier = jnp.where((across == down) & (sub < lane), 1.0, 0.0)
    rank = jnp.sum(earlier, axis=0, keepdims=True).astype(jnp.int32)
    place_ref[...] = owner_row * capacity + rank
    number = jnp.broadcast_to(column_of(ints_ref[:, tokens + count :]), (count, LANES))
    lane = lax.broadcasted_iota(jnp.int32, (count, LANES), 1)
    digits = jnp.where(lane == 0, number >> 5, jnp.where(lane == 1, number & 31, 0))
    digits_ref[...] = digits.astype(F32).astype(BF16)
    values = rows_ref[:count, :].astype(F32)
    shifted = values - jnp.mean(values, axis=-1, keepdims=True)
    scale = lax.rsqrt(jnp.mean(shifted * shifted, axis=-1, keepdims=True) + EPSILON)
    hat = shifted * scale
    rows_hat_ref[...] = hat
    rows_scale_ref[...] = scale
    normed = hat * gains_ref[0:1, :]
    normed_t_ref[...] = normed.T.astype(BF16)
    normed = normed.astype(BF16)
    for part in range(4):
        columns = slice(part * width, (part + 1) * width)
        hidden = dot(normed, weights_ref[:, columns])
        sigma = sigmoid(hidden)
        active = hidden * sigma
        slope = sigma * (1.0 + hidden * (1.0 - sigma))
        rows_slope_ref[:, columns] = slope.astype(BF16)
        high = active.astype(BF16)
        rows_active_ref[:, columns] = high
        if part == 0:
            rows_active_ref[:, 4 * width :] = (active - high.astype(F32)).astype(BF16)


def forward_body(
    rows_active_ref,
    gains_ref,
    ints_ref,
    gate_ref,
    hat_ref,
    hat_scale_ref,
    qkv_ref,
    slope_ref,
    slope_t_ref,
    weight_t_ref,
    mixed_t_ref,
):
    count = rows_active_ref.shape[0]
    tokens, width = gate_ref.shape
    items = column_of(ints_ref[:, :tokens])
    lane = lax.broadcasted_iota(jnp.int32, (tokens, count), 1)
    pick = jnp.where(lane == jnp.broadcast_to(items, (tokens, count)), 1.0, 0.0).astype(BF16)
    gate_ref[...] = dot(pick, rows_active_ref[:, :width]) + dot(
        pick, rows_active_ref[:, 4 * width :]
    )
    for part in range(3):
        columns = slice((part + 1) * width, (part + 2) * width)
        qkv_ref[:, part * width : (part + 1) * width] = dot(pick, rows_active_ref[:, columns]).astype(
            BF16
        )
    gain_out = gains_ref[1:2, :]
    mask = tile_mask()
    factor = HDIM ** (-0.5)
    for tile in range(tokens // TILE):
        rows = slice(tile * TILE, (tile + 1) * TILE)
        parts = []
        for head in range(HEADS):
            vals, queries, keys = (
                qkv_ref[rows, part * width + head * HDIM : part * width + (head + 1) * HDIM]
                for part in range(3)
            )
            score = dot(queries, keys, NT) * factor
            sigma = sigmoid(score)
            weight = jnp.where(mask, score * sigma, 0.0)
            slope = sigma * (1.0 + score * (1.0 - sigma)) * factor
            slope = jnp.where(mask, slope, 0.0)
            slope_ref[tile * HEADS + head] = slope.astype(BF16)
            slope_t_ref[tile * HEADS + head] = slope.T.astype(BF16)
            weight_t_ref[tile * HEADS + head] = weight.T.astype(BF16)
            parts.append(dot(weight.astype(BF16), vals))
        attended = jnp.concatenate(parts, axis=1)
        shifted = attended - jnp.mean(attended, axis=-1, keepdims=True)
        scale = lax.rsqrt(jnp.mean(shifted * shifted, axis=-1, keepdims=True) + EPSILON)
        hat = shifted * scale
        hat_ref[rows, :] = hat
        hat_scale_ref[rows, :] = scale
        mixed = hat * gain_out * gate_ref[rows, :]
        mixed_t_ref[:, rows] = mixed.T.astype(BF16)


def gather_of(items, count):
    tokens = items.shape[1]
    sub = lax.broadcasted_iota(jnp.int32, (count, tokens), 0)
    hit = sub == jnp.broadcast_to(items, (count, tokens))
    return jnp.where(hit, 1.0, 0.0).astype(BF16)


USED = (
    "weights",
    "hat",
    "gate",
    "hat_scale",
    "qkv",
    "slope",
    "slope_t",
    "weight_t",
    "mixed_t",
    "normed_t",
    "rows_slope",
    "rows_hat",
    "rows_scale",
    "place",
    "digits",
)


def backward_body(
    plan,
    table_size,
    factor,
    me_ref,
    dest_ref,
    blocks_ref,
    ints_ref,
    gains_ref,
    *refs,
):
    used, refs = dict(zip(USED, refs)), refs[len(USED) :]
    got_refs, (table_ref, *part_refs), (wide_ref, sums_ref, active_ref, grad_y_ref) = (
        refs[:-9],
        refs[-9:-4],
        refs[-4:],
    )
    weights_ref, hat_ref, gate_ref, hat_scale_ref, qkv_ref, slope_ref, slope_t_ref = (
        used[name] for name in USED[:7]
    )
    weight_t_ref, mixed_t_ref, normed_t_ref, rows_slope_ref = (used[name] for name in USED[7:11])
    rows_hat_ref, rows_scale_ref, place_ref, digits_ref = (used[name] for name in USED[11:])
    orders = slot_orders(len(got_refs))
    for turn, got_ref in enumerate(got_refs):
        apart = jnp.where((me_ref[0] & 1) == 0, orders[0][turn], orders[1][turn])
        wide_ref[apart] = got_ref[...]
    for slot in range(len(got_refs)):
        rows = wide_ref[dest_ref[slot] ^ (me_ref[0] // table_size)]
        live = lax.broadcasted_iota(jnp.int32, rows.shape, 0) < blocks_ref[slot] * BLK
        rows = jnp.where(live, rows.astype(F32), 0.0).astype(BF16)
        grad_y_ref[slot * SLOT : (slot + 1) * SLOT, :] = rows
    tokens, width = grad_y_ref.shape
    count = normed_t_ref.shape[1]
    gain_in, gain_out = gains_ref[0:1, :], gains_ref[1:2, :]
    gain_total = jnp.zeros((1, width), F32)
    for tile in range(tokens // TILE):
        rows = slice(tile * TILE, (tile + 1) * TILE)
        grad_mixed = dot(grad_y_ref[rows, :], weights_ref[:, 4 * width :], NT)
        hat = hat_ref[rows, :]
        active_ref[rows, :width] = (grad_mixed * hat * gain_out).astype(BF16)
        inner = grad_mixed * gate_ref[rows, :]
        gain_total = gain_total + jnp.sum(inner * hat, axis=0, keepdims=True)
        inner = inner * gain_out
        mean = jnp.mean(inner, axis=-1, keepdims=True)
        along = jnp.mean(inner * hat, axis=-1, keepdims=True)
        grad_att = ((inner - mean - hat * along) * hat_scale_ref[rows, :]).astype(BF16)
        for head in range(HEADS):
            vals, queries, keys = (
                qkv_ref[rows, part * width + head * HDIM : part * width + (head + 1) * HDIM]
                for part in range(3)
            )
            grad_o = grad_att[:, head * HDIM : (head + 1) * HDIM]
            grad_weight = dot(grad_o, vals, NT)
            grad_score = (grad_weight * slope_ref[tile * HEADS + head].astype(F32)).astype(BF16)
            weight_t = dot(vals, grad_o, NT)
            score_t = (weight_t * slope_t_ref[tile * HEADS + head].astype(F32)).astype(BF16)
            for part, value in (
                (1, dot(weight_t_ref[tile * HEADS + head], grad_o)),
                (2, dot(grad_score, keys)),
                (3, dot(score_t, queries)),
            ):
                first = part * width + head * HDIM
                active_ref[rows, first : first + HDIM] = value.astype(BF16)
    sums_ref[:, :width] = (dot(mixed_t_ref[...], grad_y_ref[...]) * factor).astype(BF16)
    gather = gather_of(ints_ref[:, :tokens], count)
    grad_normed = jnp.zeros((count, width), F32)
    for part in range(4):
        columns = slice(part * width, (part + 1) * width)
        summed = dot(gather, active_ref[:, columns])
        grad_hidden = (summed * rows_slope_ref[:, columns].astype(F32)).astype(BF16)
        sums_ref[:, (part + 1) * width : (part + 2) * width] = (
            dot(normed_t_ref[...], grad_hidden) * factor
        ).astype(BF16)
        grad_normed = grad_normed + dot(grad_hidden, weights_ref[:, columns], NT)
    hat = rows_hat_ref[...]
    gains = (jnp.sum(grad_normed * hat, axis=0, keepdims=True) * factor, gain_total * factor)
    plan.write(me_ref[0], sums_ref, part_refs)
    inner = grad_normed * gain_in
    mean = jnp.mean(inner, axis=-1, keepdims=True)
    along = jnp.mean(inner * hat, axis=-1, keepdims=True)
    row_grad = (inner - mean - hat * along) * rows_scale_ref[...] + dot(gather, grad_y_ref[...])
    places = table_ref.shape[0]
    spots = lax.broadcasted_iota(jnp.int32, (places, count), 0)
    hit = spots == jnp.broadcast_to(place_ref[...], (places, count))
    spread = jnp.where(hit, 1.0, 0.0).astype(BF16)
    table_ref[:, :width] = dot(spread, row_grad.astype(BF16)).astype(BF16)
    extra = plan.extra
    lanes = []
    for row in range(plan.capacity):
        first = row * plan.gain_lanes
        gain = gains[first // width][:, first % width : first % width + plan.gain_lanes]
        rest = extra - GAIN_AT - plan.gain_lanes
        row_parts = [jnp.zeros((1, GAIN_AT), F32), gain]
        lanes.append(jnp.concatenate(row_parts + [jnp.zeros((1, rest), F32)] * (rest > 0), axis=1))
    lanes = jnp.concatenate(lanes, axis=0).astype(BF16)
    repeat = lax.broadcasted_iota(jnp.int32, (places, plan.capacity), 0) % plan.capacity
    lane = lax.broadcasted_iota(jnp.int32, (places, plan.capacity), 1)
    repeat = jnp.where(repeat == lane, 1.0, 0.0).astype(BF16)
    table_ref[:, width:] = dot(repeat, lanes).astype(BF16)
    table_ref[:, width : width + LANES] += dot(spread, digits_ref[...]).astype(BF16)


class Plan:
    def __init__(self, dp_size, table_size, count, width):
        self.chunks = dp_size * table_size
        self.capacity = 2 * count // self.chunks
        self.row_groups = min(self.chunks, width // CHUNK_ROWS)
        self.column_groups = self.chunks // self.row_groups
        block = self.column_groups * LANES
        self.wide = -(-5 * width // block) * LANES
        self.gain_lanes = 2 * width // self.capacity
        self.extra = -(-(GAIN_AT + self.gain_lanes) // LANES) * LANES
        first = -(-3 * self.wide // (5 * LANES)) * LANES
        self.split = -(-self.wide // (2 * LANES)) * LANES
        self.sides = ((0, first), (first, self.wide - first))
        self.halves = ((0, self.split), (self.split, self.wide - self.split))
        table_bits = [1 << bit for bit in range(1, table_size.bit_length() - 1)]
        dp_bits = [table_size << bit for bit in range(dp_size.bit_length() - 1)]
        self.near_steps = len(table_bits) + 1
        self.orders = (table_bits + dp_bits, dp_bits[:1] + table_bits + dp_bits[1:])

    def chunk(self, me, side, place):
        order = [1] + self.orders[side]
        mask = 0
        for step, bit in enumerate(order):
            if place >> (len(order) - 1 - step) & 1:
                mask ^= bit
        return me ^ mask

    def columns(self, chunk, part):
        begin, size = part
        if self.column_groups == 1:
            return slice(begin, begin + size)
        group = chunk >> (self.row_groups.bit_length() - 1)
        return pl.ds(pl.multiple_of(group * self.wide + begin, LANES), size)

    def write(self, me, sums_ref, part_refs):
        half = self.chunks // 2
        for side in range(2):
            for place in range(self.chunks):
                chunk = self.chunk(me, side, place)
                first = pl.multiple_of((chunk & (self.row_groups - 1)) * CHUNK_ROWS, CHUNK_ROWS)
                rows = pl.ds(first, CHUNK_ROWS)
                out_ref = part_refs[2 * side + place // half]
                out_ref[place % half] = sums_ref[rows, self.columns(chunk, self.sides[side])]


def table_body(plan, got_ref, out_ref, gain_in_ref, gain_out_ref):
    places, width = got_ref.shape[0], out_ref.shape[1]
    lane = lax.broadcasted_iota(jnp.int32, (16, LANES), 1)
    scale = jnp.where(lane == 0, 32.0, jnp.where(lane == 1, 1.0, 0.0)).astype(BF16)
    numbers = dot(scale, got_ref[:, width : width + LANES], NT)[0:1].astype(jnp.int32)
    step = 256
    for first in range(0, out_ref.shape[0], step):
        sub = lax.broadcasted_iota(jnp.int32, (step, places), 0) + first
        hit = jnp.where(sub == jnp.broadcast_to(numbers, (step, places)), 1.0, 0.0)
        out_ref[first : first + step, :] = dot(hit.astype(BF16), got_ref[:, :width])
    sub = lax.broadcasted_iota(jnp.int32, (16, places), 0)
    lane = lax.broadcasted_iota(jnp.int32, (16, places), 1) % plan.capacity
    total = dot(jnp.where(sub == lane, 1.0, 0.0).astype(BF16), got_ref[:, width:])
    for row in range(plan.capacity):
        first = row * plan.gain_lanes
        gain_ref = (gain_in_ref, gain_out_ref)[first // width]
        gain_ref[:, first % width : first % width + plan.gain_lanes] = total[
            row : row + 1, GAIN_AT : GAIN_AT + plan.gain_lanes
        ]


def widen_body(plan, came, me_ref, left_ref, right_ref, *refs):
    w_in_ref, w_out_ref, stage_ref, sems = refs[-4:]
    side = (me_ref[0] & 1) ^ came
    half, blocks = plan.chunks // 2, plan.row_groups // 2
    for part, in_ref in enumerate((left_ref, right_ref)):
        for place in range(half):
            chunk = plan.chunk(me_ref[0], part, came * half + place)
            row = (chunk & (plan.row_groups - 1)) >> 1
            rows = pl.ds(pl.multiple_of(row * CHUNK_ROWS, CHUNK_ROWS), CHUNK_ROWS)
            stage_ref[rows, plan.columns(chunk, plan.halves[part])] = in_ref[place].astype(F32)
    split = w_out_ref.shape[1]
    copies = []
    for block in range(blocks):
        first = pl.multiple_of((2 * block + side) * CHUNK_ROWS, CHUNK_ROWS)
        here = stage_ref.at[pl.ds(block * CHUNK_ROWS, CHUNK_ROWS)]
        there = pl.ds(first, CHUNK_ROWS)
        copies += [
            pltpu.make_async_copy(here.at[:, split:], w_in_ref.at[there], sems.at[0, block]),
            pltpu.make_async_copy(here.at[:, :split], w_out_ref.at[there], sems.at[1, block]),
        ]
    for copy in copies:
        copy.start()
    for copy in copies:
        copy.wait()


def add(left, right):
    return (left.astype(F32) + right.astype(F32)).astype(BF16)


def on_device(
    touched_rows,
    row_of_token,
    row_owner,
    owner_row,
    seq_blocks,
    seq_dest,
    grad_out,
    w_in,
    w_out,
    gain_in,
    gain_out,
):
    dp_size, table_size = lax.axis_size("dp"), lax.axis_size("table")
    both = ("dp", "table")
    count, width = touched_rows.shape
    tokens = row_of_token.shape[0]
    plan = Plan(dp_size, table_size, count, width)
    devices_all = plan.chunks
    total_factor = 1.0 / math.sqrt(grad_out.shape[0] * devices_all)
    gain_rows = jnp.stack([gain_in, gain_out])
    ints = jnp.concatenate([row_of_token, row_owner[:, 0], owner_row])[None, :]
    me = lax.axis_index(both).astype(jnp.int32)[None]

    def swap(values, *masks):
        pairs = [(here, here ^ masks[here % len(masks)]) for here in range(devices_all)]
        return lax.ppermute(values, both, pairs)

    def exchange(values, axes, groups):
        return lax.all_to_all(
            values, axes, split_axis=0, concat_axis=0, tiled=True, axis_index_groups=groups
        )

    peers = jnp.arange(dp_size, dtype=jnp.int32)
    own = jnp.sum(jnp.where(seq_dest[:, None] == peers, seq_blocks[:, None], 0), axis=0)
    lengths = jnp.where(peers[:, None] == lax.axis_index("dp"), own, 0)
    steps = [table_size << bit for bit in range(dp_size.bit_length() - 1)]
    for step, mask in enumerate(steps[::2]):
        pair = steps[2 * step + 1 : 2 * step + 2]
        came = [swap(lengths, mask)] + [swap(lengths, far) for far in pair]
        came += [swap(lengths, far ^ mask) for far in pair]
        lengths = lengths + sum(came)
        if step == 0:
            lengths, touched_rows = lax.optimization_barrier((lengths, touched_rows))
    rows = jnp.concatenate([touched_rows, grad_out])
    weights = jnp.concatenate([w_in, w_out], axis=1)
    shapes = row_shapes(count, width)
    made = call(
        functools.partial(rows_body, plan.capacity),
        list(shapes.values()),
        [VMEM] * 4,
        flops=8 * count * width * width,
        moved=4_000_000,
    )(rows, weights, gain_rows, ints)
    saved = dict(zip(shapes, made), weights=weights)
    lengths, saved["rows_active"] = lax.optimization_barrier((lengths, saved["rows_active"]))
    send = call(
        functools.partial(send_body, table_size, count),
        [shape_of((SLOT, width), BF16)] * dp_size,
        [SMEM] * 2 + [VMEM],
        scratch=[pltpu.SMEM((dp_size,), jnp.int32)],
    )(me, lengths, rows)
    got = list(send)
    orders = slot_orders(dp_size)
    for turn in range(1, dp_size):
        got[turn] = swap(send[turn], *(order[turn] * table_size for order in orders))
    got[0], after = lax.optimization_barrier((got[0], ints))
    shapes = token_shapes(tokens, width)
    made = call(
        forward_body,
        list(shapes.values()),
        [VMEM] * 3,
        flops=4 * count * width * width * 10,
        moved=8_000_000,
        mebibytes=12 + tokens // 32,
    )(saved["rows_active"], gain_rows, after)
    saved |= dict(zip(shapes, made))

    outs = [shape_of((devices_all * plan.capacity, width + plan.extra), BF16)]
    for _, wide in plan.sides:
        outs += [shape_of((devices_all // 2, CHUNK_ROWS, wide), BF16)] * 2
    table_send, *parts = call(
        functools.partial(backward_body, plan, table_size, total_factor),
        outs,
        [SMEM] * 3 + [VMEM] * (2 + len(USED) + dp_size),
        flops=4 * count * width * width * 40,
        moved=12_000_000,
        mebibytes=12 + tokens // 32,
        scratch=[
            pltpu.VMEM((dp_size, SLOT, width), BF16),
            pltpu.VMEM((width, plan.column_groups * plan.wide), BF16),
            pltpu.VMEM((tokens, 4 * width), BF16),
            pltpu.VMEM((tokens, width), BF16),
        ],
    )(
        me,
        seq_dest,
        seq_blocks,
        ints,
        gain_rows,
        *(saved[name] for name in USED),
        *got,
    )

    def reduced(kept, mask):
        middle = kept.shape[0] // 2
        return add(kept[:middle], swap(kept[middle:], mask))

    def gathered(kept, mask):
        return jnp.concatenate([kept, swap(kept, mask)])

    sides = [add(parts[2 * side], swap(parts[2 * side + 1], 1)) for side in range(2)]
    *sides, table_send = lax.optimization_barrier((*sides, table_send))
    low = min(2, dp_size)
    high, inside = dp_size // low, low * table_size
    groups = [[upper * low + lower for upper in range(high)] for lower in range(low)]
    table_got = exchange(table_send.reshape(high, inside, plan.capacity, -1), "dp", groups)
    for step in range(plan.near_steps):
        sides = [reduced(sides[side], plan.orders[side][step]) for side in range(2)]
    kept = jnp.concatenate(sides, axis=2)
    away = plan.orders[0][plan.near_steps :]
    kept = reduced(kept, away[0])
    kept, table_got = lax.optimization_barrier((kept, table_got))
    groups = [[upper * inside + lower for lower in range(inside)] for upper in range(high)]
    table_got = exchange(jnp.swapaxes(table_got, 0, 1), both, groups)
    for mask in away[1:]:
        kept = reduced(kept, mask)
    back = plan.orders[0][: plan.near_steps - 1 : -1]
    kept = gathered(kept, back[0])
    kept, table_got = lax.optimization_barrier((kept, table_got))
    table_part, grad_gain_in, grad_gain_out = call(
        functools.partial(table_body, plan),
        (
            shape_of((ROWS_DEV, width), F32),
            shape_of((1, width), F32),
            shape_of((1, width), F32),
        ),
        [VMEM],
    )(table_got.reshape(devices_all * plan.capacity, -1))
    for mask in back[1:]:
        kept = gathered(kept, mask)
    kept, table_part = lax.optimization_barrier((kept, table_part))
    sides = [kept[..., : plan.split], kept[..., plan.split :]]
    for step in reversed(range(plan.near_steps)):
        sides = [gathered(sides[side], plan.orders[side][step]) for side in range(2)]
    came = [swap(side, 1) for side in sides]
    rows = width // 2
    outs = [shape_of(w_in.shape, F32), shape_of(w_out.shape, F32)]
    for turn, parts in enumerate((sides, came)):
        written = () if turn == 0 else (grad_w_in, grad_w_out)
        grad_w_in, grad_w_out = pl.pallas_call(
            functools.partial(widen_body, plan, turn),
            out_shape=outs,
            in_specs=[SMEM] + [VMEM] * 2 + [ANY] * len(written),
            out_specs=[ANY] * 2,
            scratch_shapes=[
                pltpu.VMEM((rows, 5 * width), F32),
                pltpu.SemaphoreType.DMA((2, plan.row_groups // 2)),
            ],
            input_output_aliases={3: 0, 4: 1} if written else {},
            compiler_params=pltpu.CompilerParams(vmem_limit_bytes=24 * 1024 * 1024),
            cost_estimate=pl.CostEstimate(flops=0, bytes_accessed=4_000_000, transcendentals=0),
        )(me, *parts, *written)
    return (table_part, grad_w_in, grad_w_out, grad_gain_in[0], grad_gain_out[0])


def solution(mesh):
    rows = P(("dp", "table"), None)
    flat = P(("dp", "table"))
    in_specs = (rows, flat, rows, flat, flat, flat, rows, P(), P(), P(), P())
    out_specs = (rows, P(), P(), P(), P())
    return jax.shard_map(
        on_device, mesh=mesh, in_specs=in_specs, out_specs=out_specs, check_vma=False
    )
```
